32 devices in a mesh: ctx: 16 (over z, x, core), tp: 2 (over y).
Axes of the slice: x: 2, y: 2, z: 4, core: 2. Of those that a mesh axis runs over, the one named last changes fastest.
Arguments:
- features: bfloat16 [32, 196, 1152], P('ctx', None, 'tp'), may hold values from -6 to 6
- group_kernel: bfloat16 [9, 1152, 48], P(None, 'tp'), may hold values from -0.3125 to 0.3125
- squeeze_in: bfloat16 [1152, 288], P('tp'), may hold values from -0.75 to 0.75
- squeeze_out: bfloat16 [288, 1152], P(None, 'tp'), may hold values from -0.75 to 0.75
- sampler_kernel: bfloat16 [1152, 8, 1152], P('ctx', None, 'tp'), may hold values from -0.0625 to 0.0625
- readout_kernel: bfloat16 [1152, 8192], P('ctx', 'tp'), may hold values from -0.1875 to 0.1875
- frame_clip: int32 [32], replicated, may hold values from 0 to 3, as said below
- clip_keep: int32 [4], replicated, may hold values from 1 to 512, as said below
- token_cotangent: bfloat16 [1024, 8192], P('ctx', 'tp'), may hold values from -6 to 6
Outputs:
- llm_tokens: bfloat16 [1024, 8192], P('ctx', 'tp')
- grad_features: bfloat16 [32, 196, 1152], P('ctx', None, 'tp')
The draws below stay inside these ranges and needn't reach their ends.
Inputs may be any that keep to these rules, and one draw needn't show every extreme that they name: `frame_clip`: clip ids start at 0 and never fall along the frames; every clip covers an even number of frames from 2 to 16 and starts at an even frame; some clip covers 16. `clip_keep`: each clip keeps at least one and at most 8 * 8 times half its frames of its tokens; the clip of 16 frames keeps all of its tokens, and some clip keeps a single token.
All inputs are finite; a program needn't handle non-finite values.
Results may differ from the reference program's by a relative error of at most 0.009.
Values may be sent and summed in bfloat16 or wider, within the bound.
No kernel may reach another device: no remote copies, remote signals or barrier semaphores. Data moves between devices by JAX's collectives and lax.ppermute only.
A program may use at most 128 MiB of HBM per device.

```python
import jax
import jax.numpy as jnp
from jax import lax

C = 1152
H = 8192
G = 48
SIDE = 14
R = 288
OUT_SIDE = 8
CELLS = 196
FRAMES = 32
CLIPS = 4
TOKENS = 1024
N_CTX = 16


def clip_order(key):
    return jax.random.permutation(jax.random.fold_in(key, 9), CLIPS)


def clip_lengths(key):
    halves = jax.random.randint(jax.random.fold_in(key, 7), (CLIPS // 2,), -3, 4)
    paired = jnp.stack([4 + halves, 4 - halves], axis=1).reshape(CLIPS).astype(jnp.int32)
    fixed_head = jnp.array([8, 2, 3, 3], dtype=jnp.int32)
    joined = jnp.concatenate([fixed_head, paired[4:]])
    return joined[clip_order(key)]


def clip_marks(key):
    fixed_head = jnp.array([2, 1, 0, 0], dtype=jnp.int32)
    joined = jnp.concatenate([fixed_head, jnp.zeros((CLIPS - 4,), jnp.int32)])
    return joined[clip_order(key)]


def pair_clips(key):
    lengths = clip_lengths(key)
    ends = jnp.cumsum(lengths)
    slots = jnp.arange(FRAMES // 2, dtype=jnp.int32)
    return jnp.sum((ends[None, :] <= slots[:, None]).astype(jnp.int32), axis=1).astype(jnp.int32)


def draw_frame_clip(key, part):
    return jnp.repeat(pair_clips(key), 2).astype(jnp.int32)


def draw_clip_keep(key, part):
    produced = clip_lengths(key) * (OUT_SIDE * OUT_SIDE)
    marks = clip_marks(key)
    picked = jax.random.randint(jax.random.fold_in(key, 11), (CLIPS,), 1, 2 * produced)
    kept = jnp.minimum(picked, produced)
    kept = jnp.where(marks == 2, produced, kept)
    kept = jnp.where(marks == 1, jnp.ones_like(kept), kept)
    return kept.astype(jnp.int32)


def shard_levels(key, shape, cuts, low, largest):
    def one(dim, blocks):
        steps = jax.random.uniform(jax.random.fold_in(jax.random.fold_in(key, 6), dim), (blocks,), jnp.float32, low / len(cuts), largest / len(cuts))
        return jnp.repeat(jnp.exp(steps), shape[dim] // blocks).reshape((-1,) + (1,) * (len(shape) - dim - 1))

    factor_of = one(*cuts[0])
    for cut in cuts[1:]:
        factor_of = factor_of * one(*cut)
    return factor_of


def bell_draw(own_key, shape, scale, reach, pieces=(), held_as=jnp.bfloat16):
    values = scale * jax.random.normal(own_key, shape, jnp.float32)
    if pieces:
        values = values * shard_levels(own_key, shape, pieces, -0.22, 0.18)
    return jnp.clip(values, -reach, reach).astype(held_as)


def setup_inputs(seed: int = 0) -> dict:
    key_list = jax.random.split(jax.random.key(seed), 10)
    return {
        "features": bell_draw(key_list[0], (FRAMES, CELLS, C), 1.0, 6.0, ((0, 16), (2, 2))),
        "group_kernel": bell_draw(key_list[1], (9, C, G), (9 * G) ** -0.5, 0.3125, ((1, 2),)),
        "squeeze_in": bell_draw(key_list[2], (C, R), (C // 16) ** -0.5, 0.75, ((0, 2),)),
        "squeeze_out": bell_draw(key_list[3], (R, C), (R // 4) ** -0.5, 0.75, ((1, 2),)),
        "sampler_kernel": bell_draw(key_list[4], (C, 8, C), (8 * C) ** -0.5, 0.0625, ((0, 16), (2, 2))),
        "readout_kernel": bell_draw(key_list[5], (C, H), C ** -0.5, 0.1875, ((0, 16), (1, 2))),
        "frame_clip": draw_frame_clip(jax.random.fold_in(key_list[9], 71), 0),
        "clip_keep": draw_clip_keep(jax.random.fold_in(key_list[9], 71), 0),
        "token_cotangent": bell_draw(key_list[8], (TOKENS, H), 1.0, 6.0, ((0, 16), (1, 2))),
    }


def silu_slope(values):
    sigma = jax.nn.sigmoid(values)
    return sigma * (1.0 + values * (1.0 - sigma))


def grouped_forward(frames_grid, group_kernel):
    count, side, _, chans = frames_grid.shape
    width = group_kernel.shape[2]
    groups = chans // width
    padded = jnp.pad(frames_grid, ((0, 0), (1, 1), (1, 1), (0, 0)))
    kernel = group_kernel.reshape(9, groups, width, width).astype(jnp.float32)
    total = jnp.zeros((count, side, side, groups, width), jnp.float32)
    for kernel_tap in range(9):
        row_shift, col_shift = divmod(kernel_tap, 3)
        window = padded[:, row_shift:row_shift + side, col_shift:col_shift + side]
        window = window.reshape(count, side, side, groups, width).astype(jnp.float32)
        total = total + jnp.einsum("fyxgi,gio->fyxgo", window, kernel[kernel_tap])
    return total.reshape(count, side, side, chans)


def grouped_backward(grad_grid, group_kernel):
    count, side, _, chans = grad_grid.shape
    width = group_kernel.shape[2]
    groups = chans // width
    kernel = group_kernel.reshape(9, groups, width, width).astype(jnp.float32)
    source = grad_grid.reshape(count, side, side, groups, width).astype(jnp.float32)
    total = jnp.zeros((count, side + 2, side + 2, chans), jnp.float32)
    for kernel_tap in range(9):
        row_shift, col_shift = divmod(kernel_tap, 3)
        spread = jnp.einsum("fyxgo,gio->fyxgi", source, kernel[kernel_tap]).reshape(count, side, side, chans)
        total = total + jnp.pad(spread, ((0, 0), (row_shift, 2 - row_shift), (col_shift, 2 - col_shift), (0, 0)))
    return total[:, 1:side + 1, 1:side + 1]


def make_patches(prev_odd, even):
    stacked = jnp.stack([prev_odd, even], axis=1)
    stacked = jnp.pad(stacked, ((0, 0), (0, 0), (1, 1), (1, 1), (0, 0)))
    pairs, _, padded_side, _, chans = stacked.shape
    half = padded_side // 2
    shaped = stacked.reshape(pairs, 2, half, 2, half, 2, chans).transpose(0, 2, 4, 1, 3, 5, 6)
    return shaped.reshape(pairs * half * half, 8 * chans)


def unpatch(grad_rows, pairs, side, chans):
    half = side // 2 + 1
    shaped = grad_rows.reshape(pairs, half, half, 2, 2, 2, chans).transpose(0, 3, 1, 4, 2, 5, 6)
    shaped = shaped.reshape(pairs, 2, 2 * half, 2 * half, chans)
    return shaped[:, :, 1:side + 1, 1:side + 1]


def reorder(rows):
    width = rows.shape[1]
    return rows.reshape(N_CTX, N_CTX, -1, width).transpose(1, 0, 2, 3).reshape(-1, width)


def reference(features, group_kernel, squeeze_in, squeeze_out, sampler_kernel, readout_kernel, frame_clip, clip_keep, token_cotangent):
    highest = lax.Precision.HIGHEST
    frames, cells, chans = features.shape
    pairs = frames // 2
    grid = features.reshape(frames, SIDE, SIDE, chans)
    conv_out = grouped_forward(grid, group_kernel)
    active = jax.nn.silu(conv_out)
    pooled = jnp.mean(active, axis=(1, 2))
    squeezed = jnp.dot(pooled, squeeze_in.astype(jnp.float32), precision=highest)
    relaxed = jax.nn.silu(squeezed)
    excite = jax.nn.sigmoid(jnp.dot(relaxed, squeeze_out.astype(jnp.float32), precision=highest))
    hidden = (grid.astype(jnp.float32) + active * excite[:, None, None, :]).astype(jnp.bfloat16)
    same_clip = frame_clip[1:-1:2] == frame_clip[2::2]
    pair_mask = jnp.concatenate([jnp.zeros((1,), bool), same_clip]).astype(jnp.float32)
    even = hidden[0::2]
    odd = hidden[1::2]
    prev_odd = jnp.concatenate([jnp.zeros_like(odd[:1]), odd[:-1]], axis=0)
    prev_odd = prev_odd * pair_mask.astype(jnp.bfloat16)[:, None, None, None]
    patches = make_patches(prev_odd, even)
    sampler_rows = sampler_kernel.reshape(chans, 8 * chans)
    pre = jnp.dot(patches, sampler_rows.T, preferred_element_type=jnp.float32)
    act = jax.nn.silu(pre).astype(jnp.bfloat16)
    per_frame = OUT_SIDE * OUT_SIDE
    pair_clip = frame_clip[0::2]
    clip_ids = jnp.arange(clip_keep.shape[0], dtype=jnp.int32)
    start_pair = jnp.sum((pair_clip[None, :] < clip_ids[:, None]).astype(jnp.int32), axis=1)
    own_start = start_pair[pair_clip]
    own_keep = clip_keep[pair_clip]
    pair_index = jnp.arange(pairs, dtype=jnp.int32)
    position = (pair_index - own_start)[:, None] * per_frame + jnp.arange(per_frame, dtype=jnp.int32)[None, :]
    live = (position < own_keep[:, None]).reshape(-1).astype(jnp.bfloat16)
    tokens = jnp.dot(act, readout_kernel, preferred_element_type=jnp.float32).astype(jnp.bfloat16) * live[:, None]
    llm_tokens = reorder(tokens)
    back = reorder(token_cotangent) * live[:, None]
    grad_act = jnp.dot(back, readout_kernel.T, preferred_element_type=jnp.float32)
    grad_pre = (grad_act * silu_slope(pre)).astype(jnp.bfloat16)
    grad_patches = jnp.dot(grad_pre, sampler_rows, preferred_element_type=jnp.float32)
    grad_taps = unpatch(grad_patches, pairs, SIDE, chans)
    leading = grad_taps[:, 0] * pair_mask[:, None, None, None]
    grad_even = grad_taps[:, 1]
    grad_odd = jnp.concatenate([leading[1:], jnp.zeros_like(leading[:1])], axis=0)
    grad_hidden = jnp.stack([grad_even, grad_odd], axis=1).reshape(frames, SIDE, SIDE, chans)
    grad_excite = jnp.sum(grad_hidden * active, axis=(1, 2))
    grad_inner = grad_excite * excite * (1.0 - excite)
    grad_relaxed = jnp.dot(grad_inner, squeeze_out.astype(jnp.float32).T, precision=highest)
    grad_squeezed = grad_relaxed * silu_slope(squeezed)
    grad_pooled = jnp.dot(grad_squeezed, squeeze_in.astype(jnp.float32).T, precision=highest)
    grad_active = grad_hidden * excite[:, None, None, :] + grad_pooled[:, None, None, :] / cells
    grad_conv = (grad_active * silu_slope(conv_out)).astype(jnp.bfloat16)
    grad_grid = grad_hidden + grouped_backward(grad_conv, group_kernel)
    grad_features = grad_grid.astype(jnp.bfloat16).reshape(frames, cells, chans)
    return llm_tokens, grad_features
```

```python
import jax
import jax.numpy as jnp
from jax import lax
from jax.sharding import PartitionSpec as P

SIDE = 14
OUT_SIDE = 8


def shifted(value, axis, by):
    count = lax.axis_size(axis)
    pairs = [(i, i + by) for i in range(count) if 0 <= i + by < count]
    return lax.ppermute(value, axis, pairs)


def silu_slope(values):
    sigma = jax.nn.sigmoid(values)
    return sigma * (1.0 + values * (1.0 - sigma))


def grouped_forward(frames_grid, group_kernel):
    count, side, _, chans = frames_grid.shape
    width = group_kernel.shape[2]
    groups = chans // width
    padded = jnp.pad(frames_grid, ((0, 0), (1, 1), (1, 1), (0, 0)))
    kernel = group_kernel.reshape(9, groups, width, width)
    total = jnp.zeros((count, side, side, groups, width), jnp.float32)
    for kernel_tap in range(9):
        row_shift, col_shift = divmod(kernel_tap, 3)
        window = padded[:, row_shift : row_shift + side, col_shift : col_shift + side]
        window = window.reshape(count, side, side, groups, width)
        total = total + jnp.einsum(
            "fyxgi,gio->fyxgo", window, kernel[kernel_tap], preferred_element_type=jnp.float32
        )
    return total.reshape(count, side, side, chans)


def grouped_backward(grad_grid, group_kernel):
    count, side, _, chans = grad_grid.shape
    width = group_kernel.shape[2]
    groups = chans // width
    kernel = group_kernel.reshape(9, groups, width, width)
    source = grad_grid.reshape(count, side, side, groups, width)
    total = jnp.zeros((count, side + 2, side + 2, chans), jnp.float32)
    for kernel_tap in range(9):
        row_shift, col_shift = divmod(kernel_tap, 3)
        spread = jnp.einsum(
            "fyxgo,gio->fyxgi", source, kernel[kernel_tap], preferred_element_type=jnp.float32
        )
        spread = spread.reshape(count, side, side, chans)
        total = total + jnp.pad(
            spread, ((0, 0), (row_shift, 2 - row_shift), (col_shift, 2 - col_shift), (0, 0))
        )
    return total[:, 1 : side + 1, 1 : side + 1]


def make_patches(prev_odd, even):
    stacked = jnp.stack([prev_odd, even], axis=1)
    stacked = jnp.pad(stacked, ((0, 0), (0, 0), (1, 1), (1, 1), (0, 0)))
    pairs, _, padded_side, _, chans = stacked.shape
    half = padded_side // 2
    shaped = stacked.reshape(pairs, 2, half, 2, half, 2, chans).transpose(0, 2, 4, 1, 3, 5, 6)
    return shaped.reshape(pairs * half * half, 8 * chans)


def unpatch(grad_rows, pairs, side, chans):
    half = side // 2 + 1
    shaped = grad_rows.reshape(pairs, half, half, 2, 2, 2, chans).transpose(0, 3, 1, 4, 2, 5, 6)
    shaped = shaped.reshape(pairs, 2, 2 * half, 2 * half, chans)
    return shaped[:, :, 1 : side + 1, 1 : side + 1]


def contract_last(left, right):
    return lax.dot_general(
        left, right, (((1,), (1,)), ((), ())), preferred_element_type=jnp.float32
    )


def per_device(
    features,
    group_kernel,
    squeeze_in,
    squeeze_out,
    sampler_kernel,
    readout_kernel,
    frame_clip,
    clip_keep,
    token_cotangent,
):
    highest = lax.Precision.HIGHEST
    shard_index = lax.axis_index("ctx")
    frames_dev, cells, chans = features.shape
    pairs_dev = frames_dev // 2
    grid = features.reshape(frames_dev, SIDE, SIDE, chans)
    conv_out = grouped_forward(grid, group_kernel)
    active = jax.nn.silu(conv_out)
    pooled = jnp.mean(active, axis=(1, 2))
    squeezed = lax.psum(jnp.dot(pooled, squeeze_in.astype(jnp.float32), precision=highest), "tp")
    relaxed = jax.nn.silu(squeezed)
    excite = jax.nn.sigmoid(jnp.dot(relaxed, squeeze_out.astype(jnp.float32), precision=highest))
    hidden = (grid.astype(jnp.float32) + active * excite[:, None, None, :]).astype(jnp.bfloat16)
    count = lax.axis_size("ctx")
    same_core = [list(range(0, count, 2)), list(range(1, count, 2))]
    swap_core = [(i, i ^ 1) for i in range(count)]
    flat_sampler = sampler_kernel.reshape(sampler_kernel.shape[0], 8 * chans)
    readouts = [lax.all_gather(readout_kernel, "ctx", axis=0, tiled=True, axis_index_groups=same_core)]
    samplers = [lax.all_gather(flat_sampler, "ctx", axis=0, tiled=True, axis_index_groups=same_core)]
    readouts.append(lax.ppermute(readouts[0], "ctx", swap_core))
    samplers.append(lax.ppermute(samplers[0], "ctx", swap_core))
    halo_frame = shifted(hidden[-1], "ctx", 1)
    local_clip = lax.dynamic_slice_in_dim(frame_clip, shard_index * frames_dev, frames_dev)
    edge_clip = lax.dynamic_slice_in_dim(
        frame_clip, jnp.maximum(shard_index * frames_dev - 1, 0), 1
    )
    first_keep = jnp.logical_and(shard_index > 0, edge_clip[0] == local_clip[0])
    later_keep = local_clip[1:-1:2] == local_clip[2::2]
    pair_mask = jnp.concatenate([first_keep[None], later_keep]).astype(jnp.float32)
    even = hidden[0::2]
    odd = hidden[1::2]
    prev_odd = jnp.concatenate([halo_frame[None], odd[:-1]], axis=0)
    prev_odd = prev_odd * pair_mask.astype(jnp.bfloat16)[:, None, None, None]
    patches = make_patches(prev_odd, even)
    per_frame = OUT_SIDE * OUT_SIDE
    pair_clip = frame_clip[0::2]
    clip_ids = jnp.arange(clip_keep.shape[0], dtype=jnp.int32)
    start_pair = jnp.sum((pair_clip[None, :] < clip_ids[:, None]).astype(jnp.int32), axis=1)
    own_clip = local_clip[0::2]
    one_hot = (own_clip[:, None] == clip_ids[None, :]).astype(jnp.int32)
    own_start = jnp.sum(one_hot * start_pair[None, :], axis=1)
    own_keep = jnp.sum(one_hot * clip_keep[None, :], axis=1)
    pair_index = shard_index * pairs_dev + jnp.arange(pairs_dev, dtype=jnp.int32)
    position = (pair_index - own_start)[:, None] * per_frame + jnp.arange(
        per_frame, dtype=jnp.int32
    )[None, :]
    live = (position < own_keep[:, None]).reshape(-1).astype(jnp.bfloat16)
    pre = lax.psum(jnp.concatenate([contract_last(patches, part) for part in samplers], axis=1), "tp")
    act = jax.nn.silu(pre).astype(jnp.bfloat16)
    tokens = (
        sum(
            jnp.dot(piece, part, preferred_element_type=jnp.float32)
            for piece, part in zip(jnp.split(act, 2, axis=1), readouts)
        ).astype(jnp.bfloat16)
        * live[:, None]
    )
    llm_tokens = lax.all_to_all(tokens, "ctx", split_axis=0, concat_axis=0, tiled=True)
    back = (
        lax.all_to_all(token_cotangent, "ctx", split_axis=0, concat_axis=0, tiled=True)
        * live[:, None]
    )
    grad_act = lax.psum(jnp.concatenate([contract_last(back, part) for part in readouts], axis=1), "tp")
    grad_pre = (grad_act * silu_slope(pre)).astype(jnp.bfloat16)
    grad_patches = sum(
        jnp.dot(piece, part, preferred_element_type=jnp.float32)
        for piece, part in zip(jnp.split(grad_pre, 2, axis=1), samplers)
    )
    grad_taps = unpatch(grad_patches, pairs_dev, SIDE, chans)
    leading = grad_taps[:, 0] * pair_mask[:, None, None, None]
    incoming = shifted(leading[0].astype(jnp.bfloat16), "ctx", -1).astype(jnp.float32)
    grad_even = grad_taps[:, 1]
    grad_odd = jnp.concatenate([leading[1:], incoming[None]], axis=0)
    grad_hidden = jnp.stack([grad_even, grad_odd], axis=1).reshape(frames_dev, SIDE, SIDE, chans)
    grad_excite = jnp.sum(grad_hidden * active, axis=(1, 2))
    grad_inner = grad_excite * excite * (1.0 - excite)
    grad_relaxed = lax.psum(
        jnp.dot(grad_inner, squeeze_out.astype(jnp.float32).T, precision=highest), "tp"
    )
    grad_squeezed = grad_relaxed * silu_slope(squeezed)
    grad_pooled = jnp.dot(grad_squeezed, squeeze_in.astype(jnp.float32).T, precision=highest)
    grad_active = grad_hidden * excite[:, None, None, :] + grad_pooled[:, None, None, :] / cells
    grad_conv = (grad_active * silu_slope(conv_out)).astype(jnp.bfloat16)
    grad_grid = grad_hidden + grouped_backward(grad_conv, group_kernel)
    grad_features = grad_grid.astype(jnp.bfloat16).reshape(frames_dev, cells, chans)
    return (llm_tokens, grad_features)


def solution(mesh):
    placed = (
        P("ctx", None, "tp"),
        P(None, "tp", None),
        P("tp", None),
        P(None, "tp"),
        P("ctx", None, "tp"),
        P("ctx", "tp"),
        P(),
        P(),
        P("ctx", "tp"),
    )
    return jax.shard_map(
        per_device,
        mesh=mesh,
        in_specs=placed,
        out_specs=(P("ctx", "tp"), P("ctx", None, "tp")),
        check_vma=False,
    )
```

```python
import jax
import jax.numpy as jnp
from jax import lax
from jax.sharding import PartitionSpec as P

SIDE = 14
OUT_SIDE = 8


def shifted(value, axis, by):
    count = lax.axis_size(axis)
    pairs = [(i, i + by) for i in range(count) if 0 <= i + by < count]
    return lax.ppermute(value, axis, pairs)


def ring_order(chips):
    return list(range(0, chips, 2)) + list(range(1, chips, 2))[::-1]


def ring_pairs(count, by):
    order = ring_order(count // 2)
    pairs = []
    for place, chip in enumerate(order):
        target = order[(place + by) % len(order)]
        pairs += [(2 * chip, 2 * target), (2 * chip + 1, 2 * target + 1)]
    return pairs


def swap_cores(value):
    return lax.ppermute(value, "ctx", [(i, i ^ 1) for i in range(lax.axis_size("ctx"))])


def sum_tp(value):
    size = lax.axis_size("tp")
    reach = 1
    while reach < size:
        value = value + lax.ppermute(value, "tp", [(i, i ^ reach) for i in range(size)])
        reach *= 2
    return value


def ring_gather(samplers, readouts):
    count = lax.axis_size("ctx")
    chips = count // 2
    onward, backward = ring_pairs(count, 1), ring_pairs(count, -1)
    groups = [([samplers], [readouts])]
    up_s = down_s = samplers
    up_r = down_r = readouts
    for step in range(1, chips // 2):
        up_r, down_r = lax.ppermute(up_r, "ctx", onward), lax.ppermute(down_r, "ctx", backward)
        up_s, down_s = lax.ppermute(up_s, "ctx", onward), lax.ppermute(down_s, "ctx", backward)
        groups.append(([up_s, down_s], [up_r, down_r]))
    up_s = lax.ppermute(up_s, "ctx", onward)
    down_r = lax.ppermute(down_r, "ctx", backward)
    groups.append(([up_s], [down_r]))
    return groups


def silu_slope(values):
    sigma = jax.nn.sigmoid(values)
    return sigma * (1.0 + values * (1.0 - sigma))


def grouped_forward(frames_grid, group_kernel):
    count, side, _, chans = frames_grid.shape
    width = group_kernel.shape[2]
    groups = chans // width
    padded = jnp.pad(frames_grid, ((0, 0), (1, 1), (1, 1), (0, 0)))
    kernel = group_kernel.reshape(9, groups, width, width)
    total = jnp.zeros((count, side, side, groups, width), jnp.float32)
    for kernel_tap in range(9):
        row_shift, col_shift = divmod(kernel_tap, 3)
        window = padded[:, row_shift : row_shift + side, col_shift : col_shift + side]
        window = window.reshape(count, side, side, groups, width)
        total = total + jnp.einsum(
            "fyxgi,gio->fyxgo", window, kernel[kernel_tap], preferred_element_type=jnp.float32
        )
    return total.reshape(count, side, side, chans)


def grouped_backward(grad_grid, group_kernel):
    count, side, _, chans = grad_grid.shape
    width = group_kernel.shape[2]
    groups = chans // width
    kernel = group_kernel.reshape(9, groups, width, width)
    source = grad_grid.reshape(count, side, side, groups, width)
    total = jnp.zeros((count, side + 2, side + 2, chans), jnp.float32)
    for kernel_tap in range(9):
        row_shift, col_shift = divmod(kernel_tap, 3)
        spread = jnp.einsum(
            "fyxgo,gio->fyxgi", source, kernel[kernel_tap], preferred_element_type=jnp.float32
        )
        spread = spread.reshape(count, side, side, chans)
        total = total + jnp.pad(
            spread, ((0, 0), (row_shift, 2 - row_shift), (col_shift, 2 - col_shift), (0, 0))
        )
    return total[:, 1 : side + 1, 1 : side + 1]


def make_patches(prev_odd, even):
    stacked = jnp.stack([prev_odd, even], axis=1)
    stacked = jnp.pad(stacked, ((0, 0), (0, 0), (1, 1), (1, 1), (0, 0)))
    pairs, _, padded_side, _, chans = stacked.shape
    half = padded_side // 2
    shaped = stacked.reshape(pairs, 2, half, 2, half, 2, chans).transpose(0, 2, 4, 1, 3, 5, 6)
    return shaped.reshape(pairs * half * half, 8 * chans)


def unpatch(grad_rows, pairs, side, chans):
    half = side // 2 + 1
    shaped = grad_rows.reshape(pairs, half, half, 2, 2, 2, chans).transpose(0, 3, 1, 4, 2, 5, 6)
    shaped = shaped.reshape(pairs, 2, 2 * half, 2 * half, chans)
    return shaped[:, :, 1 : side + 1, 1 : side + 1]


def contract_last(left, right):
    return lax.dot_general(
        left, right, (((1,), (1,)), ((), ())), preferred_element_type=jnp.float32
    )


def per_device(
    features,
    group_kernel,
    squeeze_in,
    squeeze_out,
    sampler_kernel,
    readout_kernel,
    frame_clip,
    clip_keep,
    token_cotangent,
):
    highest = lax.Precision.HIGHEST
    shard_index = lax.axis_index("ctx")
    frames_dev, cells, chans = features.shape
    pairs_dev = frames_dev // 2
    grid = features.reshape(frames_dev, SIDE, SIDE, chans)
    conv_out = grouped_forward(grid, group_kernel)
    active = jax.nn.silu(conv_out)
    pooled = jnp.mean(active, axis=(1, 2))
    squeezed = lax.psum(jnp.dot(pooled, squeeze_in.astype(jnp.float32), precision=highest), "tp")
    relaxed = jax.nn.silu(squeezed)
    excite = jax.nn.sigmoid(jnp.dot(relaxed, squeeze_out.astype(jnp.float32), precision=highest))
    hidden = (grid.astype(jnp.float32) + active * excite[:, None, None, :]).astype(jnp.bfloat16)
    flat_sampler = sampler_kernel.reshape(sampler_kernel.shape[0], 8 * chans)
    groups = ring_gather(flat_sampler, readout_kernel)
    halo_frame = shifted(hidden[-1], "ctx", 1)
    local_clip = lax.dynamic_slice_in_dim(frame_clip, shard_index * frames_dev, frames_dev)
    edge_clip = lax.dynamic_slice_in_dim(
        frame_clip, jnp.maximum(shard_index * frames_dev - 1, 0), 1
    )
    first_keep = jnp.logical_and(shard_index > 0, edge_clip[0] == local_clip[0])
    later_keep = local_clip[1:-1:2] == local_clip[2::2]
    pair_mask = jnp.concatenate([first_keep[None], later_keep]).astype(jnp.float32)
    even = hidden[0::2]
    odd = hidden[1::2]
    prev_odd = jnp.concatenate([halo_frame[None], odd[:-1]], axis=0)
    prev_odd = prev_odd * pair_mask.astype(jnp.bfloat16)[:, None, None, None]
    patches = make_patches(prev_odd, even)
    per_frame = OUT_SIDE * OUT_SIDE
    pair_clip = frame_clip[0::2]
    clip_ids = jnp.arange(clip_keep.shape[0], dtype=jnp.int32)
    start_pair = jnp.sum((pair_clip[None, :] < clip_ids[:, None]).astype(jnp.int32), axis=1)
    own_clip = local_clip[0::2]
    one_hot = (own_clip[:, None] == clip_ids[None, :]).astype(jnp.int32)
    own_start = jnp.sum(one_hot * start_pair[None, :], axis=1)
    own_keep = jnp.sum(one_hot * clip_keep[None, :], axis=1)
    pair_index = shard_index * pairs_dev + jnp.arange(pairs_dev, dtype=jnp.int32)
    position = (pair_index - own_start)[:, None] * per_frame + jnp.arange(
        per_frame, dtype=jnp.int32
    )[None, :]
    live = (position < own_keep[:, None]).reshape(-1).astype(jnp.bfloat16)
    back = (
        lax.all_to_all(token_cotangent, "ctx", split_axis=0, concat_axis=0, tiled=True)
        * live[:, None]
    )
    rows = back.shape[0]
    both_patches = jnp.concatenate([patches, swap_cores(patches)], axis=0)
    both_back = jnp.concatenate([back, swap_cores(back)], axis=0)
    both_tokens = both_grads = 0.0
    for group_s, group_r in groups:
        partial = jnp.concatenate(
            [contract_last(both_patches, part) for part in group_s]
            + [contract_last(both_back, part) for part in group_r],
            axis=1,
        )
        pre, grad_act = jnp.split(sum_tp(partial), 2, axis=1)
        act = jax.nn.silu(pre).astype(jnp.bfloat16)
        grad_pre = (grad_act * silu_slope(pre)).astype(jnp.bfloat16)
        for piece, part in zip(jnp.split(act, len(group_r), axis=1), group_r):
            both_tokens += jnp.dot(piece, part, preferred_element_type=jnp.float32)
        for piece, part in zip(jnp.split(grad_pre, len(group_s), axis=1), group_s):
            both_grads += jnp.dot(piece, part, preferred_element_type=jnp.float32)
    grad_patches = both_grads[:rows] + swap_cores(both_grads[rows:])
    tokens = (both_tokens[:rows] + swap_cores(both_tokens[rows:])).astype(jnp.bfloat16) * live[:, None]
    llm_tokens = lax.all_to_all(tokens, "ctx", split_axis=0, concat_axis=0, tiled=True)
    grad_taps = unpatch(grad_patches, pairs_dev, SIDE, chans)
    leading = grad_taps[:, 0] * pair_mask[:, None, None, None]
    incoming = shifted(leading[0].astype(jnp.bfloat16), "ctx", -1).astype(jnp.float32)
    grad_even = grad_taps[:, 1]
    grad_odd = jnp.concatenate([leading[1:], incoming[None]], axis=0)
    grad_hidden = jnp.stack([grad_even, grad_odd], axis=1).reshape(frames_dev, SIDE, SIDE, chans)
    grad_excite = jnp.sum(grad_hidden * active, axis=(1, 2))
    grad_inner = grad_excite * excite * (1.0 - excite)
    grad_relaxed = lax.psum(
        jnp.dot(grad_inner, squeeze_out.astype(jnp.float32).T, precision=highest), "tp"
    )
    grad_squeezed = grad_relaxed * silu_slope(squeezed)
    grad_pooled = jnp.dot(grad_squeezed, squeeze_in.astype(jnp.float32).T, precision=highest)
    grad_active = grad_hidden * excite[:, None, None, :] + grad_pooled[:, None, None, :] / cells
    grad_conv = (grad_active * silu_slope(conv_out)).astype(jnp.bfloat16)
    grad_grid = grad_hidden + grouped_backward(grad_conv, group_kernel)
    grad_features = grad_grid.astype(jnp.bfloat16).reshape(frames_dev, cells, chans)
    return (llm_tokens, grad_features)


def solution(mesh):
    placed = (
        P("ctx", None, "tp"),
        P(None, "tp", None),
        P("tp", None),
        P(None, "tp"),
        P("ctx", None, "tp"),
        P("ctx", "tp"),
        P(),
        P(),
        P("ctx", "tp"),
    )
    return jax.shard_map(
        per_device,
        mesh=mesh,
        in_specs=placed,
        out_specs=(P("ctx", "tp"), P("ctx", None, "tp")),
        check_vma=False,
    )
```

```python
import jax
import jax.numpy as jnp
from jax import lax
from jax.experimental import pallas as pl
from jax.experimental.pallas import tpu as pltpu
from jax.sharding import PartitionSpec as P

SIDE = 14
OUT_SIDE = 8
WIDE = 16
FRAME_ROWS = WIDE * WIDE
EDGE = 8
LANES = 128
VMEM_BYTES = 40 * 2**20


def whole_call(kernel, outs, scratch, flops, moved):
    return pl.pallas_call(
        kernel,
        out_shape=outs,
        scratch_shapes=scratch,
        compiler_params=pltpu.CompilerParams(vmem_limit_bytes=VMEM_BYTES),
        cost_estimate=pl.CostEstimate(flops=flops, bytes_accessed=moved, transcendentals=0),
    )


def silu_slope(values):
    sigma = jax.nn.sigmoid(values)
    return sigma * (1.0 + values * (1.0 - sigma))


def inside(rows):
    row = lax.broadcasted_iota(jnp.int32, (rows, 1), 0)
    across, down = row & (WIDE - 1), (row // WIDE) & (WIDE - 1)
    good = (across >= 1) & (across <= SIDE) & (down >= 1) & (down <= SIDE)
    return good.astype(jnp.float32)


def channel_blocks(chans, width):
    span = 4 * width
    blocks = []
    for low in range(0, chans, span):
        high = min(chans, low + span)
        blocks.append((low, high, low // LANES * LANES, min(chans, -(-high // LANES) * LANES)))
    return blocks


def block_tools(block, width):
    low, high, start, end = block
    size = end - start
    out_lane = lax.broadcasted_iota(jnp.int32, (width, size), 1) + start
    within = lax.broadcasted_iota(jnp.int32, (width, size), 0)
    lane = lax.broadcasted_iota(jnp.int32, (size, size), 1) + start
    row = lax.broadcasted_iota(jnp.int32, (size, size), 0) + start
    spread = jnp.zeros((width, size), jnp.float32)
    same = jnp.zeros((size, size), jnp.float32)
    for first in range(low, high, width):
        spread += (out_lane == within + first).astype(jnp.float32)
        in_lane = (lane >= first) & (lane < first + width)
        in_row = (row >= first) & (row < first + width)
        same += (in_lane & in_row).astype(jnp.float32)
    return spread.astype(jnp.bfloat16), same


def dense_tap(group_ref, tap, block, spread, same):
    _, _, start, end = block
    full = jnp.dot(group_ref[tap, start:end, :], spread, preferred_element_type=jnp.float32)
    return (full * same).astype(jnp.bfloat16)


def store_shifts(wide_ref, shift_ref, sign):
    rows = shift_ref.shape[1]
    for col in range(3):
        at = EDGE + sign * (col - 1)
        shift_ref[col] = wide_ref[at : at + rows, :].astype(jnp.bfloat16)


def conv_kernel(feat_ref, group_ref, squeeze_ref, conv_ref, pad_ref, sq_ref, flat_ref, wide_ref, shift_ref):
    frames, _, chans = feat_ref.shape
    width = group_ref.shape[2]
    rows = frames * FRAME_ROWS
    wide_ref[...] = jnp.zeros_like(wide_ref)
    for frame in range(frames):
        flat_ref[...] = feat_ref[frame].astype(jnp.float32)
        for y in range(SIDE):
            at = EDGE + frame * FRAME_ROWS + (y + 1) * WIDE + 1
            wide_ref[at : at + SIDE, :] = flat_ref[y * SIDE : (y + 1) * SIDE, :]
    store_shifts(wide_ref, shift_ref, 1)
    pad_ref[...] = shift_ref[1]
    conv_ref[...] = jnp.zeros_like(conv_ref)
    body = rows - 2 * WIDE
    for block in channel_blocks(chans, width):
        _, _, start, end = block
        spread, same = block_tools(block, width)
        total = jnp.zeros((body, end - start), jnp.float32)
        for tap in range(9):
            down, across = divmod(tap, 3)
            weights = dense_tap(group_ref, tap, block, spread, same)
            source = shift_ref[across, down * WIDE : down * WIDE + body, start:end]
            total += jnp.dot(source, weights, preferred_element_type=jnp.float32)
        conv_ref[WIDE : WIDE + body, start:end] += total
    conv = conv_ref[...] * inside(rows)
    conv_ref[...] = conv
    active = conv * jax.nn.sigmoid(conv)
    pooled = jnp.concatenate(
        [
            jnp.sum(active[f * FRAME_ROWS : (f + 1) * FRAME_ROWS], axis=0, keepdims=True)
            for f in range(frames)
        ],
        axis=0,
    ) * (1.0 / (SIDE * SIDE))
    sq_ref[...] = jnp.dot(
        pooled, squeeze_ref[...].astype(jnp.float32), precision=lax.Precision.HIGHEST
    )


def hidden_kernel(conv_ref, pad_ref, sq_ref, expand_ref, even_ref, odd_ref, excite_ref):
    squeezed = sq_ref[...]
    relaxed = squeezed * jax.nn.sigmoid(squeezed)
    excite = jax.nn.sigmoid(
        jnp.dot(relaxed, expand_ref[...].astype(jnp.float32), precision=lax.Precision.HIGHEST)
    )
    excite_ref[...] = excite
    for frame, out_ref in enumerate((even_ref, odd_ref)):
        rows = slice(frame * FRAME_ROWS, (frame + 1) * FRAME_ROWS)
        conv = conv_ref[rows, :]
        active = conv * jax.nn.sigmoid(conv)
        hidden = pad_ref[rows, :].astype(jnp.float32) + active * excite[frame : frame + 1]
        out_ref[...] = hidden.astype(jnp.bfloat16)


def select_rows(to_patches):
    shape = (FRAME_ROWS, FRAME_ROWS)
    out_row = lax.broadcasted_iota(jnp.int32, shape, 0)
    in_row = lax.broadcasted_iota(jnp.int32, shape, 1)
    patch_row, frame_row = (out_row, in_row) if to_patches else (in_row, out_row)
    down, across = patch_row >> 7, (patch_row >> 6) & 1
    a, b = (patch_row >> 3) & 7, patch_row & 7
    return ((2 * a + down) * WIDE + 2 * b + across == frame_row).astype(jnp.float32)


def patch_kernel(mask_ref, halo_ref, even_ref, out_ref):
    chans = halo_ref.shape[1]
    per_frame = OUT_SIDE * OUT_SIDE
    select = select_rows(True).astype(jnp.bfloat16)
    for frame, source in enumerate((halo_ref, even_ref)):
        rows = jnp.dot(select, source[...], preferred_element_type=jnp.float32)
        if frame == 0:
            rows = rows * mask_ref[0, 0]
        rows = rows.astype(jnp.bfloat16)
        for tap in range(4):
            at = (frame * 4 + tap) * chans
            out_ref[:, at : at + chans] = rows[tap * per_frame : (tap + 1) * per_frame]


def unpatch_kernel(mask_ref, own_ref, mate_ref, lead_ref, even_ref):
    chans = lead_ref.shape[1]
    select = select_rows(False)
    frames = []
    for frame in range(2):
        pieces = []
        for tap in range(frame * 4, frame * 4 + 4):
            lanes = slice(tap * chans, (tap + 1) * chans)
            pieces.append(own_ref[:, lanes] + mate_ref[:, lanes])
        frames.append(
            jnp.dot(select, jnp.concatenate(pieces, axis=0), precision=lax.Precision.HIGHEST)
        )
    good = inside(FRAME_ROWS)
    lead_ref[...] = (frames[0] * (good * mask_ref[0, 0])).astype(jnp.bfloat16)
    even_ref[...] = frames[1] * good


def excite_grad_kernel(even_ref, odd_ref, conv_ref, excite_ref, expand_ref, out_ref):
    sums = []
    for frame, grad_ref in enumerate((even_ref, odd_ref)):
        conv = conv_ref[frame * FRAME_ROWS : (frame + 1) * FRAME_ROWS, :]
        active = conv * jax.nn.sigmoid(conv)
        sums.append(jnp.sum(grad_ref[...].astype(jnp.float32) * active, axis=0, keepdims=True))
    excite = excite_ref[...]
    inner = jnp.concatenate(sums, axis=0) * excite * (1.0 - excite)
    out_ref[...] = lax.dot_general(
        inner,
        expand_ref[...].astype(jnp.float32),
        (((1,), (1,)), ((), ())),
        precision=lax.Precision.HIGHEST,
        preferred_element_type=jnp.float32,
    )


def conv_grad_kernel(
    even_ref, odd_ref, conv_ref, excite_ref, sq_ref, relaxed_ref, squeeze_ref, group_ref,
    out_ref, flat_ref, wide_ref, shift_ref, grad_ref,
):
    frames, _, chans = out_ref.shape
    width = group_ref.shape[2]
    rows = frames * FRAME_ROWS
    grad_squeezed = relaxed_ref[...] * silu_slope(sq_ref[...])
    pooled = lax.dot_general(
        grad_squeezed,
        squeeze_ref[...].astype(jnp.float32),
        (((1,), (1,)), ((), ())),
        precision=lax.Precision.HIGHEST,
        preferred_element_type=jnp.float32,
    ) * (1.0 / (SIDE * SIDE))
    wide_ref[0:EDGE, :] = jnp.zeros((EDGE, chans), jnp.float32)
    wide_ref[EDGE + rows :, :] = jnp.zeros((EDGE, chans), jnp.float32)
    good = inside(FRAME_ROWS)
    for frame, source in enumerate((even_ref, odd_ref)):
        at = frame * FRAME_ROWS
        grad = source[...].astype(jnp.float32)
        grad_ref[at : at + FRAME_ROWS, :] = grad
        active = grad * excite_ref[frame : frame + 1, :] + pooled[frame : frame + 1]
        slope = silu_slope(conv_ref[at : at + FRAME_ROWS, :])
        wide_ref[EDGE + at : EDGE + at + FRAME_ROWS, :] = active * slope * good
    store_shifts(wide_ref, shift_ref, -1)
    body = rows - 2 * WIDE
    for block in channel_blocks(chans, width):
        _, _, start, end = block
        spread, same = block_tools(block, width)
        total = jnp.zeros((body, end - start), jnp.float32)
        for tap in range(9):
            down, across = divmod(tap, 3)
            weights = dense_tap(group_ref, tap, block, spread, same)
            at = (2 - down) * WIDE
            source = shift_ref[across, at : at + body, start:end]
            total += lax.dot_general(
                source, weights, (((1,), (1,)), ((), ())), preferred_element_type=jnp.float32
            )
        grad_ref[WIDE : WIDE + body, start:end] += total
    for frame in range(frames):
        for y in range(SIDE):
            at = frame * FRAME_ROWS + (y + 1) * WIDE + 1
            flat_ref[y * SIDE : (y + 1) * SIDE, :] = grad_ref[at : at + SIDE, :]
        out_ref[frame] = flat_ref[...].astype(jnp.bfloat16)


def f32(*shape):
    return jax.ShapeDtypeStruct(shape, jnp.float32)


def bf16(*shape):
    return jax.ShapeDtypeStruct(shape, jnp.bfloat16)


def conv_forward(features, group_kernel, squeeze_in):
    frames, cells, chans = features.shape
    rows = frames * FRAME_ROWS
    return whole_call(
        conv_kernel,
        (f32(rows, chans), bf16(rows, chans), f32(frames, squeeze_in.shape[1])),
        [
            pltpu.VMEM((cells, chans), jnp.float32),
            pltpu.VMEM((rows + 2 * EDGE, chans), jnp.float32),
            pltpu.VMEM((3, rows, chans), jnp.bfloat16),
        ],
        rows * chans * 256 * 18 * 2,
        rows * chans * 8 + 9 * chans * 256,
    )(features, group_kernel, squeeze_in)


def hidden_frames(conv, padded, squeezed, squeeze_out):
    rows, chans = conv.shape
    return whole_call(
        hidden_kernel,
        (bf16(FRAME_ROWS, chans), bf16(FRAME_ROWS, chans), f32(rows // FRAME_ROWS, chans)),
        [],
        rows * chans * 10,
        rows * chans * 8,
    )(conv, padded, squeezed, squeeze_out)


def vmem_specs(count):
    return [pl.BlockSpec(memory_space=pltpu.SMEM)] + [pl.BlockSpec(memory_space=pltpu.VMEM)] * count


def take_patches(mask, halo, even):
    chans = even.shape[1]
    return pl.pallas_call(
        patch_kernel,
        out_shape=bf16(OUT_SIDE * OUT_SIDE, 8 * chans),
        in_specs=vmem_specs(2),
        compiler_params=pltpu.CompilerParams(vmem_limit_bytes=VMEM_BYTES),
        cost_estimate=pl.CostEstimate(
            flops=8 * FRAME_ROWS * chans, bytes_accessed=8 * FRAME_ROWS * chans, transcendentals=0
        ),
    )(mask, halo, even)


def return_patches(mask, own, mate, chans):
    return pl.pallas_call(
        unpatch_kernel,
        out_shape=(bf16(FRAME_ROWS, chans), f32(FRAME_ROWS, chans)),
        in_specs=vmem_specs(2),
        compiler_params=pltpu.CompilerParams(vmem_limit_bytes=VMEM_BYTES),
        cost_estimate=pl.CostEstimate(
            flops=8 * FRAME_ROWS * chans, bytes_accessed=24 * FRAME_ROWS * chans, transcendentals=0
        ),
    )(mask, own, mate)


def excite_grad(even, odd, conv, excite, squeeze_out):
    rows, chans = conv.shape
    return whole_call(
        excite_grad_kernel,
        f32(rows // FRAME_ROWS, squeeze_out.shape[0]),
        [],
        rows * chans * 10,
        rows * chans * 7,
    )(even, odd, conv, excite, squeeze_out)


def conv_backward(even, odd, conv, excite, squeezed, grad_relaxed, squeeze_in, group_kernel):
    rows, chans = conv.shape
    frames = rows // FRAME_ROWS
    return whole_call(
        conv_grad_kernel,
        bf16(frames, SIDE * SIDE, chans),
        [
            pltpu.VMEM((SIDE * SIDE, chans), jnp.float32),
            pltpu.VMEM((rows + 2 * EDGE, chans), jnp.float32),
            pltpu.VMEM((3, rows, chans), jnp.bfloat16),
            pltpu.VMEM((rows, chans), jnp.float32),
        ],
        rows * chans * 256 * 18 * 2,
        rows * chans * 10 + 9 * chans * 256,
    )(even, odd, conv, excite, squeezed, grad_relaxed, squeeze_in, group_kernel)


def shifted(value, axis, by):
    count = lax.axis_size(axis)
    pairs = [(i, i + by) for i in range(count) if 0 <= i + by < count]
    return lax.ppermute(value, axis, pairs)


def ring_order(chips):
    return list(range(0, chips, 2)) + list(range(1, chips, 2))[::-1]


def ring_pairs(count, by):
    order = ring_order(count // 2)
    pairs = []
    for place, chip in enumerate(order):
        target = order[(place + by) % len(order)]
        pairs += [(2 * chip, 2 * target), (2 * chip + 1, 2 * target + 1)]
    return pairs


def swap_cores(value):
    return lax.ppermute(value, "ctx", [(i, i ^ 1) for i in range(lax.axis_size("ctx"))])


def sum_tp(value):
    size = lax.axis_size("tp")
    reach = 1
    while reach < size:
        value = value + lax.ppermute(value, "tp", [(i, i ^ reach) for i in range(size)])
        reach *= 2
    return value


def ring_gather(samplers, readouts):
    count = lax.axis_size("ctx")
    chips = count // 2
    onward, backward = ring_pairs(count, 1), ring_pairs(count, -1)
    groups = [([samplers], [readouts])]
    up_s = down_s = samplers
    up_r = down_r = readouts
    for step in range(1, chips // 2):
        up_r, down_r = lax.ppermute(up_r, "ctx", onward), lax.ppermute(down_r, "ctx", backward)
        up_s, down_s = lax.ppermute(up_s, "ctx", onward), lax.ppermute(down_s, "ctx", backward)
        groups.append(([up_s, down_s], [up_r, down_r]))
    up_s = lax.ppermute(up_s, "ctx", onward)
    down_r = lax.ppermute(down_r, "ctx", backward)
    groups.append(([up_s], [down_r]))
    return groups


def contract_last(left, right):
    return lax.dot_general(
        left, right, (((1,), (1,)), ((), ())), preferred_element_type=jnp.float32
    )


def per_device(
    features,
    group_kernel,
    squeeze_in,
    squeeze_out,
    sampler_kernel,
    readout_kernel,
    frame_clip,
    clip_keep,
    token_cotangent,
):
    shard_index = lax.axis_index("ctx")
    frames_dev, cells, chans = features.shape
    pairs_dev = frames_dev // 2
    flat_sampler = sampler_kernel.reshape(sampler_kernel.shape[0], 8 * chans)
    groups = ring_gather(flat_sampler, readout_kernel)

    local_clip = lax.dynamic_slice_in_dim(frame_clip, shard_index * frames_dev, frames_dev)
    edge_clip = lax.dynamic_slice_in_dim(
        frame_clip, jnp.maximum(shard_index * frames_dev - 1, 0), 1
    )
    first_keep = jnp.logical_and(shard_index > 0, edge_clip[0] == local_clip[0])
    mask = first_keep.astype(jnp.float32).reshape(1, 1)
    per_frame = OUT_SIDE * OUT_SIDE
    pair_clip = frame_clip[0::2]
    clip_ids = jnp.arange(clip_keep.shape[0], dtype=jnp.int32)
    start_pair = jnp.sum((pair_clip[None, :] < clip_ids[:, None]).astype(jnp.int32), axis=1)
    own_clip = local_clip[0::2]
    one_hot = (own_clip[:, None] == clip_ids[None, :]).astype(jnp.int32)
    own_start = jnp.sum(one_hot * start_pair[None, :], axis=1)
    own_keep = jnp.sum(one_hot * clip_keep[None, :], axis=1)
    pair_index = shard_index * pairs_dev + jnp.arange(pairs_dev, dtype=jnp.int32)
    position = (pair_index - own_start)[:, None] * per_frame + jnp.arange(
        per_frame, dtype=jnp.int32
    )[None, :]
    live = (position < own_keep[:, None]).reshape(-1).astype(jnp.bfloat16)

    back = (
        lax.all_to_all(token_cotangent, "ctx", split_axis=0, concat_axis=0, tiled=True)
        * live[:, None]
    )
    rows = back.shape[0]
    both_back = jnp.concatenate([back, swap_cores(back)], axis=0)

    conv, padded, squeezed = conv_forward(features, group_kernel, squeeze_in)
    squeezed = sum_tp(squeezed)
    even, odd, excite = hidden_frames(conv, padded, squeezed, squeeze_out)
    patches = take_patches(mask, shifted(odd, "ctx", 1), even)
    both_patches = jnp.concatenate([patches, swap_cores(patches)], axis=0)

    both_tokens = both_grads = 0.0
    for group_s, group_r in groups:
        partial = jnp.concatenate(
            [contract_last(both_patches, part) for part in group_s]
            + [contract_last(both_back, part) for part in group_r],
            axis=1,
        )
        pre, grad_act = jnp.split(sum_tp(partial), 2, axis=1)
        act = jax.nn.silu(pre).astype(jnp.bfloat16)
        grad_pre = (grad_act * silu_slope(pre)).astype(jnp.bfloat16)
        for piece, part in zip(jnp.split(act, len(group_r), axis=1), group_r):
            both_tokens += jnp.dot(piece, part, preferred_element_type=jnp.float32)
        for piece, part in zip(jnp.split(grad_pre, len(group_s), axis=1), group_s):
            both_grads += jnp.dot(piece, part, preferred_element_type=jnp.float32)
    lead, grad_even = return_patches(mask, both_grads[:rows], swap_cores(both_grads[rows:]), chans)
    grad_odd = shifted(lead, "ctx", -1)
    grad_relaxed = sum_tp(excite_grad(grad_even, grad_odd, conv, excite, squeeze_out))
    grad_features = conv_backward(
        grad_even, grad_odd, conv, excite, squeezed, grad_relaxed, squeeze_in, group_kernel
    )
    tokens = (both_tokens[:rows] + swap_cores(both_tokens[rows:])).astype(jnp.bfloat16) * live[:, None]
    llm_tokens = lax.all_to_all(tokens, "ctx", split_axis=0, concat_axis=0, tiled=True)
    return (llm_tokens, grad_features)


def solution(mesh):
    placed = (
        P("ctx", None, "tp"),
        P(None, "tp", None),
        P("tp", None),
        P(None, "tp"),
        P("ctx", None, "tp"),
        P("ctx", "tp"),
        P(),
        P(),
        P("ctx", "tp"),
    )
    return jax.shard_map(
        per_device,
        mesh=mesh,
        in_specs=placed,
        out_specs=(P("ctx", "tp"), P("ctx", None, "tp")),
        check_vma=False,
    )
```

```python
import functools

import jax
import jax.numpy as jnp
from jax import lax
from jax.experimental import pallas as pl
from jax.experimental.pallas import tpu as pltpu
from jax.sharding import PartitionSpec as P

SIDE = 14
OUT_SIDE = 8
WIDE = 16
FRAME_ROWS = WIDE * WIDE
EDGE = 8
LANES = 128
VMEM_BYTES = 40 * 2**20
FREE = pl.CostEstimate(flops=0, bytes_accessed=0, transcendentals=0)


def whole_call(kernel, outs, scratch, cost=FREE):
    return pl.pallas_call(
        kernel,
        out_shape=outs,
        scratch_shapes=scratch,
        compiler_params=pltpu.CompilerParams(vmem_limit_bytes=VMEM_BYTES),
        cost_estimate=cost,
    )


def contract_last(left, right):
    return lax.dot_general(
        left, right, (((1,), (1,)), ((), ())), preferred_element_type=jnp.float32
    )


def contract_exact(left, right):
    return lax.dot_general(
        left,
        right,
        (((1,), (1,)), ((), ())),
        precision=lax.Precision.HIGHEST,
        preferred_element_type=jnp.float32,
    )


def silu_slope(values):
    sigma = jax.nn.sigmoid(values)
    return sigma * (1.0 + values * (1.0 - sigma))


def inside(rows):
    row = lax.broadcasted_iota(jnp.int32, (rows, 1), 0)
    across, down = row & (WIDE - 1), (row // WIDE) & (WIDE - 1)
    good = (across >= 1) & (across <= SIDE) & (down >= 1) & (down <= SIDE)
    return good.astype(jnp.float32)


def channel_blocks(chans, width):
    span = 4 * width
    blocks = []
    for low in range(0, chans, span):
        high = min(chans, low + span)
        blocks.append((low, high, low // LANES * LANES, min(chans, -(-high // LANES) * LANES)))
    return blocks


def block_tools(block, width):
    low, high, start, end = block
    size = end - start
    out_row = lax.broadcasted_iota(jnp.int32, (size, width), 0) + start
    within = lax.broadcasted_iota(jnp.int32, (size, width), 1)
    lane = lax.broadcasted_iota(jnp.int32, (size, size), 1) + start
    row = lax.broadcasted_iota(jnp.int32, (size, size), 0) + start
    spread = jnp.zeros((size, width), jnp.float32)
    same = jnp.zeros((size, size), jnp.float32)
    for first in range(low, high, width):
        spread += (out_row == within + first).astype(jnp.float32)
        in_lane = (lane >= first) & (lane < first + width)
        in_row = (row >= first) & (row < first + width)
        same += (in_lane & in_row).astype(jnp.float32)
    return spread.astype(jnp.bfloat16), same


def dense_tap(group_ref, tap, block, spread, same):
    _, _, start, end = block
    full = jnp.dot(spread, group_ref[tap, :, start:end], preferred_element_type=jnp.float32)
    return (full * same).astype(jnp.bfloat16)


def store_shifts(wide_ref, shift_ref, sign):
    rows = shift_ref.shape[1]
    for col in range(3):
        at = EDGE + sign * (col - 1)
        shift_ref[col] = wide_ref[at : at + rows, :].astype(jnp.bfloat16)


def conv_kernel(feat_ref, group_ref, squeeze_ref, conv_ref, pad_ref, sq_ref, flat_ref, wide_ref, shift_ref):
    frames, _, chans = feat_ref.shape
    width = group_ref.shape[1]
    rows = frames * FRAME_ROWS
    wide_ref[...] = jnp.zeros_like(wide_ref)
    for frame in range(frames):
        flat_ref[...] = feat_ref[frame].astype(jnp.float32)
        for y in range(SIDE):
            at = EDGE + frame * FRAME_ROWS + (y + 1) * WIDE + 1
            wide_ref[at : at + SIDE, :] = flat_ref[y * SIDE : (y + 1) * SIDE, :]
    store_shifts(wide_ref, shift_ref, 1)
    pad_ref[...] = shift_ref[1]
    conv_ref[...] = jnp.zeros_like(conv_ref)
    body = rows - 2 * WIDE
    for block in channel_blocks(chans, width):
        _, _, start, end = block
        spread, same = block_tools(block, width)
        total = jnp.zeros((body, end - start), jnp.float32)
        for tap in range(9):
            down, across = divmod(tap, 3)
            weights = dense_tap(group_ref, tap, block, spread, same)
            source = shift_ref[across, down * WIDE : down * WIDE + body, start:end]
            total += contract_last(source, weights)
        conv_ref[WIDE : WIDE + body, start:end] += total
    conv = conv_ref[...] * inside(rows)
    conv_ref[...] = conv
    active = conv * jax.nn.sigmoid(conv)
    pooled = jnp.concatenate(
        [
            jnp.sum(active[f * FRAME_ROWS : (f + 1) * FRAME_ROWS], axis=0, keepdims=True)
            for f in range(frames)
        ],
        axis=0,
    ) * (1.0 / (SIDE * SIDE))
    sq_ref[...] = contract_exact(pooled, squeeze_ref[...].astype(jnp.float32))


def hidden_kernel(conv_ref, pad_ref, sq_ref, expand_ref, even_ref, odd_ref, excite_ref):
    squeezed = sq_ref[...]
    relaxed = squeezed * jax.nn.sigmoid(squeezed)
    excite = jax.nn.sigmoid(
        jnp.dot(relaxed, expand_ref[...].astype(jnp.float32), precision=lax.Precision.HIGHEST)
    )
    excite_ref[...] = excite
    for frame, out_ref in enumerate((even_ref, odd_ref)):
        rows = slice(frame * FRAME_ROWS, (frame + 1) * FRAME_ROWS)
        conv = conv_ref[rows, :]
        active = conv * jax.nn.sigmoid(conv)
        hidden = pad_ref[rows, :].astype(jnp.float32) + active * excite[frame : frame + 1]
        out_ref[...] = hidden.astype(jnp.bfloat16)


def select_rows(to_patches):
    shape = (FRAME_ROWS, FRAME_ROWS)
    out_row = lax.broadcasted_iota(jnp.int32, shape, 0)
    in_row = lax.broadcasted_iota(jnp.int32, shape, 1)
    patch_row, frame_row = (out_row, in_row) if to_patches else (in_row, out_row)
    down, across = patch_row >> 7, (patch_row >> 6) & 1
    a, b = (patch_row >> 3) & 7, patch_row & 7
    return ((2 * a + down) * WIDE + 2 * b + across == frame_row).astype(jnp.float32)


def patch_kernel(mask_ref, halo_ref, even_ref, out_ref):
    chans = halo_ref.shape[1]
    per_frame = OUT_SIDE * OUT_SIDE
    select = select_rows(True).astype(jnp.bfloat16)
    for frame, source in enumerate((halo_ref, even_ref)):
        rows = jnp.dot(select, source[...], preferred_element_type=jnp.float32)
        if frame == 0:
            rows = rows * mask_ref[0, 0]
        rows = rows.astype(jnp.bfloat16)
        for tap in range(4):
            at = (frame * 4 + tap) * chans
            out_ref[:, at : at + chans] = rows[tap * per_frame : (tap + 1) * per_frame]


def unpatch_kernel(mask_ref, own_ref, mate_ref, lead_ref, even_ref):
    chans = lead_ref.shape[1]
    select = select_rows(False)
    frames = []
    for frame in range(2):
        pieces = []
        for tap in range(frame * 4, frame * 4 + 4):
            lanes = slice(tap * chans, (tap + 1) * chans)
            pieces.append(own_ref[:, lanes] + mate_ref[:, lanes])
        frames.append(
            jnp.dot(select, jnp.concatenate(pieces, axis=0), precision=lax.Precision.HIGHEST)
        )
    good = inside(FRAME_ROWS)
    lead_ref[...] = (frames[0] * (good * mask_ref[0, 0])).astype(jnp.bfloat16)
    even_ref[...] = frames[1] * good


def excite_grad_kernel(even_ref, odd_ref, conv_ref, excite_ref, expand_ref, out_ref):
    sums = []
    for frame, grad_ref in enumerate((even_ref, odd_ref)):
        conv = conv_ref[frame * FRAME_ROWS : (frame + 1) * FRAME_ROWS, :]
        active = conv * jax.nn.sigmoid(conv)
        sums.append(jnp.sum(grad_ref[...].astype(jnp.float32) * active, axis=0, keepdims=True))
    excite = excite_ref[...]
    inner = jnp.concatenate(sums, axis=0) * excite * (1.0 - excite)
    out_ref[...] = contract_exact(inner, expand_ref[...].astype(jnp.float32))


def conv_grad_kernel(
    even_ref, odd_ref, conv_ref, excite_ref, sq_ref, relaxed_ref, squeeze_ref, group_ref,
    out_ref, flat_ref, wide_ref, shift_ref, grad_ref,
):
    frames, _, chans = out_ref.shape
    width = group_ref.shape[1]
    rows = frames * FRAME_ROWS
    grad_squeezed = relaxed_ref[...] * silu_slope(sq_ref[...])
    pooled = jnp.dot(
        grad_squeezed, squeeze_ref[...].astype(jnp.float32), precision=lax.Precision.HIGHEST
    ) * (1.0 / (SIDE * SIDE))
    wide_ref[0:EDGE, :] = jnp.zeros((EDGE, chans), jnp.float32)
    wide_ref[EDGE + rows :, :] = jnp.zeros((EDGE, chans), jnp.float32)
    good = inside(FRAME_ROWS)
    for frame, source in enumerate((even_ref, odd_ref)):
        at = frame * FRAME_ROWS
        grad = source[...].astype(jnp.float32)
        grad_ref[at : at + FRAME_ROWS, :] = grad
        active = grad * excite_ref[frame : frame + 1, :] + pooled[frame : frame + 1]
        slope = silu_slope(conv_ref[at : at + FRAME_ROWS, :])
        wide_ref[EDGE + at : EDGE + at + FRAME_ROWS, :] = active * slope * good
    store_shifts(wide_ref, shift_ref, -1)
    body = rows - 2 * WIDE
    for block in channel_blocks(chans, width):
        _, _, start, end = block
        spread, same = block_tools(block, width)
        total = jnp.zeros((body, end - start), jnp.float32)
        for tap in range(9):
            down, across = divmod(tap, 3)
            weights = dense_tap(group_ref, tap, block, spread, same)
            at = (2 - down) * WIDE
            source = shift_ref[across, at : at + body, start:end]
            total += jnp.dot(source, weights, preferred_element_type=jnp.float32)
        grad_ref[WIDE : WIDE + body, start:end] += total
    for frame in range(frames):
        for y in range(SIDE):
            at = frame * FRAME_ROWS + (y + 1) * WIDE + 1
            flat_ref[y * SIDE : (y + 1) * SIDE, :] = grad_ref[at : at + SIDE, :]
        out_ref[frame] = flat_ref[...].astype(jnp.bfloat16)


def f32(*shape):
    return jax.ShapeDtypeStruct(shape, jnp.float32)


def bf16(*shape):
    return jax.ShapeDtypeStruct(shape, jnp.bfloat16)


def conv_forward(features, group_kernel, squeeze_in):
    frames, cells, chans = features.shape
    rows = frames * FRAME_ROWS
    return whole_call(
        conv_kernel,
        (f32(rows, chans), bf16(rows, chans), f32(frames, squeeze_in.shape[0])),
        [
            pltpu.VMEM((cells, chans), jnp.float32),
            pltpu.VMEM((rows + 2 * EDGE, chans), jnp.float32),
            pltpu.VMEM((3, rows, chans), jnp.bfloat16),
        ],
    )(features, group_kernel, squeeze_in)


def hidden_frames(conv, padded, squeezed, squeeze_out):
    rows, chans = conv.shape
    return whole_call(
        hidden_kernel,
        (bf16(FRAME_ROWS, chans), bf16(FRAME_ROWS, chans), f32(rows // FRAME_ROWS, chans)),
        [],
    )(conv, padded, squeezed, squeeze_out)


def vmem_specs(count):
    return [pl.BlockSpec(memory_space=pltpu.SMEM)] + [pl.BlockSpec(memory_space=pltpu.VMEM)] * count


def take_patches(mask, halo, even):
    chans = even.shape[1]
    return pl.pallas_call(
        patch_kernel,
        out_shape=bf16(OUT_SIDE * OUT_SIDE, 8 * chans),
        in_specs=vmem_specs(2),
        compiler_params=pltpu.CompilerParams(vmem_limit_bytes=VMEM_BYTES),
        cost_estimate=FREE,
    )(mask, halo, even)


def return_patches(mask, own, mate, chans):
    return pl.pallas_call(
        unpatch_kernel,
        out_shape=(bf16(FRAME_ROWS, chans), f32(FRAME_ROWS, chans)),
        in_specs=vmem_specs(2),
        compiler_params=pltpu.CompilerParams(vmem_limit_bytes=VMEM_BYTES),
        cost_estimate=FREE,
    )(mask, own, mate)


def excite_grad(even, odd, conv, excite, squeeze_out):
    rows, chans = conv.shape
    return whole_call(
        excite_grad_kernel,
        f32(rows // FRAME_ROWS, squeeze_out.shape[0]),
        [],
    )(even, odd, conv, excite, squeeze_out)


def conv_backward(even, odd, conv, excite, squeezed, grad_relaxed, squeeze_in, group_kernel):
    rows, chans = conv.shape
    frames = rows // FRAME_ROWS
    return whole_call(
        conv_grad_kernel,
        bf16(frames, SIDE * SIDE, chans),
        [
            pltpu.VMEM((SIDE * SIDE, chans), jnp.float32),
            pltpu.VMEM((rows + 2 * EDGE, chans), jnp.float32),
            pltpu.VMEM((3, rows, chans), jnp.bfloat16),
            pltpu.VMEM((rows, chans), jnp.float32),
        ],
        pl.CostEstimate(flops=rows * chans * 9216, bytes_accessed=16 * rows * chans, transcendentals=0),
    )(even, odd, conv, excite, squeezed, grad_relaxed, squeeze_in, group_kernel)


def shifted(value, axis, by):
    count = lax.axis_size(axis)
    pairs = [(i, i + by) for i in range(count) if 0 <= i + by < count]
    return lax.ppermute(value, axis, pairs)


def ring_order(chips):
    return list(range(0, chips, 2)) + list(range(1, chips, 2))[::-1]


def ring_pairs(count, by):
    order = ring_order(count // 2)
    pairs = []
    for place, chip in enumerate(order):
        target = order[(place + by) % len(order)]
        pairs += [(2 * chip, 2 * target), (2 * chip + 1, 2 * target + 1)]
    return pairs


def swap_cores(value):
    return lax.ppermute(value, "ctx", [(i, i ^ 1) for i in range(lax.axis_size("ctx"))])


def tp_terms(value):
    size = lax.axis_size("tp")
    reach, other = 1, None
    while reach < size:
        value = value if other is None else value + other
        other = lax.ppermute(value, "tp", [(i, i ^ reach) for i in range(size)])
        reach *= 2
    return value, jnp.zeros_like(value) if other is None else other


def sum_tp(value):
    value, other = tp_terms(value)
    return value + other


def ring_step(blocks):
    count = lax.axis_size("ctx")
    onward, backward = ring_pairs(count, 1), ring_pairs(count, -1)
    up_s, up_r, down_s, down_r = blocks
    send = lambda value, pairs: None if value is None else lax.ppermute(value, "ctx", pairs)
    up_r, down_r = send(up_r, onward), send(down_r, backward)
    up_s, down_s = send(up_s, onward), send(down_s, backward)
    return up_s, up_r, down_s, down_r


def tie(*values):
    return lax.optimization_barrier(values)


def sums_kernel(count, *refs):
    patch_ref, back_ref, *blocks, out_ref = refs
    products = [contract_last(patch_ref[...], ref[...]) for ref in blocks[:count]]
    products += [contract_last(back_ref[...], ref[...]) for ref in blocks[count:]]
    out_ref[...] = jnp.concatenate(products, axis=1)


def totals_kernel(count, backward, first, *refs):
    sums = refs[0][...] + refs[1][...]
    blocks, refs = refs[2 : 2 + count], refs[2 + count :]
    before, after = refs[:-2], refs[-2:]
    depth = sums.shape[1] // 2
    pre, grad_act = sums[:, :depth], sums[:, depth:]
    factor = grad_act * silu_slope(pre) if backward else pre * jax.nn.sigmoid(pre)
    factor = factor.astype(jnp.bfloat16)
    width = depth // count
    total = 0.0
    for place, ref in enumerate(blocks):
        piece = factor[:, place * width : (place + 1) * width]
        total += jnp.dot(piece, ref[...], preferred_element_type=jnp.float32)
    rows = after[0].shape[0]
    for half, ref in enumerate(after):
        value = total[half * rows : (half + 1) * rows]
        ref[...] = value if first else before[half][...] + value


def partial_sums(patches, back, samplers, readouts):
    count, width = len(samplers), samplers[0].shape[0]
    return whole_call(
        functools.partial(sums_kernel, count), f32(patches.shape[0], 2 * count * width), []
    )(patches, back, *samplers, *readouts)


def add_products(sums, blocks, before, backward):
    rows, columns = sums[0].shape[0] // 2, blocks[0].shape[1]
    kernel = functools.partial(totals_kernel, len(blocks), backward, not before)
    return whole_call(kernel, (f32(rows, columns),) * 2, [])(*sums, *blocks, *before)


def per_device(
    features,
    group_kernel,
    squeeze_in,
    squeeze_out,
    sampler_kernel,
    readout_kernel,
    frame_clip,
    clip_keep,
    token_cotangent,
):
    shard_index = lax.axis_index("ctx")
    frames_dev, cells, chans = features.shape
    pairs_dev = frames_dev // 2
    flat_sampler = sampler_kernel.reshape(sampler_kernel.shape[0], 8 * chans)
    blocks = ring_step((flat_sampler, readout_kernel) * 2)
    group_kernel = jnp.swapaxes(group_kernel, 1, 2)
    squeeze_in = squeeze_in.T

    local_clip = lax.dynamic_slice_in_dim(frame_clip, shard_index * frames_dev, frames_dev)
    edge_clip = lax.dynamic_slice_in_dim(
        frame_clip, jnp.maximum(shard_index * frames_dev - 1, 0), 1
    )
    first_keep = jnp.logical_and(shard_index > 0, edge_clip[0] == local_clip[0])
    mask = first_keep.astype(jnp.float32).reshape(1, 1)
    per_frame = OUT_SIDE * OUT_SIDE
    pair_clip = frame_clip[0::2]
    clip_ids = jnp.arange(clip_keep.shape[0], dtype=jnp.int32)
    start_pair = jnp.sum((pair_clip[None, :] < clip_ids[:, None]).astype(jnp.int32), axis=1)
    own_clip = local_clip[0::2]
    one_hot = (own_clip[:, None] == clip_ids[None, :]).astype(jnp.int32)
    own_start = jnp.sum(one_hot * start_pair[None, :], axis=1)
    own_keep = jnp.sum(one_hot * clip_keep[None, :], axis=1)
    pair_index = shard_index * pairs_dev + jnp.arange(pairs_dev, dtype=jnp.int32)
    position = (pair_index - own_start)[:, None] * per_frame + jnp.arange(
        per_frame, dtype=jnp.int32
    )[None, :]
    live = (position < own_keep[:, None]).reshape(-1).astype(jnp.bfloat16)

    back = (
        lax.all_to_all(token_cotangent, "ctx", split_axis=0, concat_axis=0, tiled=True)
        * live[:, None]
    )
    both_back = jnp.concatenate([back, swap_cores(back)], axis=0)

    conv, padded, squeezed = conv_forward(features, group_kernel, squeeze_in)
    squeezed = sum_tp(squeezed)
    even, odd, excite = hidden_frames(conv, padded, squeezed, squeeze_out)
    patches = take_patches(mask, shifted(odd, "ctx", 1), even)
    both_patches = jnp.concatenate([patches, swap_cores(patches)], axis=0)

    steps = lax.axis_size("ctx") // 4
    samplers, readouts = [flat_sampler], [readout_kernel]
    tokens = grads = ()
    for step in range(1, steps + 1):
        here = blocks
        if step < steps:
            samplers, readouts = samplers + [here[0], here[2]], readouts + [here[1], here[3]]
            if step == 1:
                *here, even = tie(*here, even)
            elif step > 2:
                *here, token_own, token_mate, grad_own, grad_mate = tie(*here, *tokens, *grads)
                tokens, grads = (token_own, token_mate), (grad_own, grad_mate)
            if step == steps - 1:
                here = here[0], None, None, here[3]
            blocks = ring_step(here)
        else:
            samplers, readouts = samplers + [here[0]], readouts + [here[3]]
        sums = tp_terms(partial_sums(both_patches, both_back, samplers, readouts))
        tokens = add_products(sums, readouts, tokens, False)
        grads = add_products(sums, samplers, grads, True)
        samplers, readouts = [], []
    lead, grad_even = return_patches(mask, grads[0], swap_cores(grads[1]), chans)
    token_own, token_mate, lead = tie(*tokens, lead)
    grad_odd = shifted(lead, "ctx", -1)
    grad_relaxed = sum_tp(excite_grad(grad_even, grad_odd, conv, excite, squeeze_out))
    tokens = (token_own + swap_cores(token_mate)).astype(jnp.bfloat16) * live[:, None]
    tokens, grad_relaxed = tie(tokens, grad_relaxed)
    llm_tokens = lax.all_to_all(tokens, "ctx", split_axis=0, concat_axis=0, tiled=True)
    grad_features = conv_backward(
        grad_even, grad_odd, conv, excite, squeezed, grad_relaxed, squeeze_in, group_kernel
    )
    return (llm_tokens, grad_features)


def solution(mesh):
    placed = (
        P("ctx", None, "tp"),
        P(None, "tp", None),
        P("tp", None),
        P(None, "tp"),
        P("ctx", None, "tp"),
        P("ctx", "tp"),
        P(),
        P(),
        P("ctx", "tp"),
    )
    return jax.shard_map(
        per_device,
        mesh=mesh,
        in_specs=placed,
        out_specs=(P("ctx", "tp"), P("ctx", None, "tp")),
        check_vma=False,
    )
```

```python
import functools

import jax
import jax.numpy as jnp
from jax import lax
from jax.experimental import pallas as pl
from jax.experimental.pallas import tpu as pltpu
from jax.sharding import PartitionSpec as P

SIDE = 14
OUT_SIDE = 8
WIDE = 16
FRAME_ROWS = WIDE * WIDE
EDGE = 8
LANES = 128
VMEM_BYTES = 20 * 2**20
FREE = pl.CostEstimate(flops=0, bytes_accessed=0, transcendentals=0)


def whole_call(kernel, outs, scratch, cost=FREE):
    return pl.pallas_call(
        kernel,
        out_shape=outs,
        scratch_shapes=scratch,
        compiler_params=pltpu.CompilerParams(vmem_limit_bytes=VMEM_BYTES),
        cost_estimate=cost,
    )


def contract_last(left, right):
    return lax.dot_general(
        left, right, (((1,), (1,)), ((), ())), preferred_element_type=jnp.float32
    )


def contract_exact(left, right):
    return lax.dot_general(
        left,
        right,
        (((1,), (1,)), ((), ())),
        precision=lax.Precision.HIGHEST,
        preferred_element_type=jnp.float32,
    )


def silu_slope(values):
    sigma = jax.nn.sigmoid(values)
    return sigma * (1.0 + values * (1.0 - sigma))


def inside(rows):
    row = lax.broadcasted_iota(jnp.int32, (rows, 1), 0)
    across, down = row & (WIDE - 1), (row // WIDE) & (WIDE - 1)
    good = (across >= 1) & (across <= SIDE) & (down >= 1) & (down <= SIDE)
    return good.astype(jnp.float32)


def channel_blocks(chans, width):
    span = 4 * width
    blocks = []
    for low in range(0, chans, span):
        high = min(chans, low + span)
        blocks.append((low, high, low // LANES * LANES, min(chans, -(-high // LANES) * LANES)))
    return blocks


def block_tools(block, width):
    low, high, start, end = block
    size = end - start
    out_row = lax.broadcasted_iota(jnp.int32, (size, width), 0) + start
    within = lax.broadcasted_iota(jnp.int32, (size, width), 1)
    lane = lax.broadcasted_iota(jnp.int32, (size, size), 1) + start
    row = lax.broadcasted_iota(jnp.int32, (size, size), 0) + start
    spread = jnp.zeros((size, width), jnp.float32)
    same = jnp.zeros((size, size), jnp.float32)
    for first in range(low, high, width):
        spread += (out_row == within + first).astype(jnp.float32)
        in_lane = (lane >= first) & (lane < first + width)
        in_row = (row >= first) & (row < first + width)
        same += (in_lane & in_row).astype(jnp.float32)
    return spread.astype(jnp.bfloat16), same


def dense_tap(group_ref, tap, block, spread, same):
    _, _, start, end = block
    full = jnp.dot(spread, group_ref[tap, :, start:end], preferred_element_type=jnp.float32)
    return (full * same).astype(jnp.bfloat16)


def store_shifts(wide_ref, shift_ref, sign):
    rows = shift_ref.shape[1]
    for col in range(3):
        at = EDGE + sign * (col - 1)
        shift_ref[col] = wide_ref[at : at + rows, :].astype(jnp.bfloat16)


def conv_kernel(feat_ref, group_ref, squeeze_ref, conv_ref, pad_ref, sq_ref, flat_ref, wide_ref, shift_ref):
    frames, _, chans = feat_ref.shape
    width = group_ref.shape[1]
    rows = frames * FRAME_ROWS
    wide_ref[...] = jnp.zeros_like(wide_ref)
    for frame in range(frames):
        flat_ref[...] = feat_ref[frame].astype(jnp.float32)
        for y in range(SIDE):
            at = EDGE + frame * FRAME_ROWS + (y + 1) * WIDE + 1
            wide_ref[at : at + SIDE, :] = flat_ref[y * SIDE : (y + 1) * SIDE, :]
    store_shifts(wide_ref, shift_ref, 1)
    pad_ref[...] = shift_ref[1]
    conv_ref[...] = jnp.zeros_like(conv_ref)
    body = rows - 2 * WIDE
    for block in channel_blocks(chans, width):
        _, _, start, end = block
        spread, same = block_tools(block, width)
        total = jnp.zeros((body, end - start), jnp.float32)
        for tap in range(9):
            down, across = divmod(tap, 3)
            weights = dense_tap(group_ref, tap, block, spread, same)
            source = shift_ref[across, down * WIDE : down * WIDE + body, start:end]
            total += contract_last(source, weights)
        conv_ref[WIDE : WIDE + body, start:end] += total
    conv = conv_ref[...] * inside(rows)
    conv_ref[...] = conv
    active = conv * jax.nn.sigmoid(conv)
    pooled = jnp.concatenate(
        [
            jnp.sum(active[f * FRAME_ROWS : (f + 1) * FRAME_ROWS], axis=0, keepdims=True)
            for f in range(frames)
        ],
        axis=0,
    ) * (1.0 / (SIDE * SIDE))
    sq_ref[...] = contract_exact(pooled, squeeze_ref[...].astype(jnp.float32))


def hidden_kernel(conv_ref, pad_ref, sq_ref, expand_ref, even_ref, odd_ref, excite_ref):
    squeezed = sq_ref[...]
    relaxed = squeezed * jax.nn.sigmoid(squeezed)
    excite = jax.nn.sigmoid(
        jnp.dot(relaxed, expand_ref[...].astype(jnp.float32), precision=lax.Precision.HIGHEST)
    )
    excite_ref[...] = excite
    for frame, out_ref in enumerate((even_ref, odd_ref)):
        rows = slice(frame * FRAME_ROWS, (frame + 1) * FRAME_ROWS)
        conv = conv_ref[rows, :]
        active = conv * jax.nn.sigmoid(conv)
        hidden = pad_ref[rows, :].astype(jnp.float32) + active * excite[frame : frame + 1]
        out_ref[...] = hidden.astype(jnp.bfloat16)


def select_rows(to_patches):
    shape = (FRAME_ROWS, FRAME_ROWS)
    out_row = lax.broadcasted_iota(jnp.int32, shape, 0)
    in_row = lax.broadcasted_iota(jnp.int32, shape, 1)
    patch_row, frame_row = (out_row, in_row) if to_patches else (in_row, out_row)
    down, across = patch_row >> 7, (patch_row >> 6) & 1
    a, b = (patch_row >> 3) & 7, patch_row & 7
    return ((2 * a + down) * WIDE + 2 * b + across == frame_row).astype(jnp.float32)


def facts_kernel(clip_ref, keep_ref, out_ref):
    shard = lax.axis_index("ctx")
    frames = clip_ref.shape[0]
    out_ref[0] = shard % 2
    for block in range(2):
        pair = shard // 2 * 2 + block
        clip = clip_ref[2 * pair]
        start = jnp.int32(0)
        for other in range(0, frames, 2):
            start += jnp.where(clip_ref[other] < clip, 1, 0)
        out_ref[1 + block] = keep_ref[clip] - (pair - start) * (OUT_SIDE * OUT_SIDE)
    before = clip_ref[jnp.maximum(2 * shard - 1, 0)]
    out_ref[3] = jnp.where((shard > 0) & (before == clip_ref[2 * shard]), 1, 0)


def token_place(row, core, unit):
    per_block = OUT_SIDE * OUT_SIDE
    within = row % per_block
    block = (within // unit) % 2
    target_core = jnp.where(row < per_block, core, 1 - core)
    return block, unit * (2 * (within // (2 * unit)) + target_core) + within % unit


def reorder_matrix(core, unit, to_sent):
    shape = (2 * OUT_SIDE * OUT_SIDE,) * 2
    out_row = lax.broadcasted_iota(jnp.int32, shape, 0)
    in_row = lax.broadcasted_iota(jnp.int32, shape, 1)
    sent, natural = (out_row, in_row) if to_sent else (in_row, out_row)
    block, token = token_place(sent, core, unit)
    source = jnp.where(block == core, 0, OUT_SIDE * OUT_SIDE) + token
    return (source == natural).astype(jnp.bfloat16)


def order_kernel(unit, facts_ref, own_ref, mate_ref, out_ref):
    rows = jnp.concatenate([own_ref[...], mate_ref[...]], axis=0)
    matrix = reorder_matrix(facts_ref[0], unit, True)
    out_ref[...] = jnp.dot(matrix, rows, preferred_element_type=jnp.float32).astype(jnp.bfloat16)


def patch_kernel(facts_ref, halo_ref, even_ref, out_ref):
    chans = halo_ref.shape[1]
    per_frame = OUT_SIDE * OUT_SIDE
    select = select_rows(True).astype(jnp.bfloat16)
    for frame, source in enumerate((halo_ref, even_ref)):
        rows = jnp.dot(select, source[...], preferred_element_type=jnp.float32)
        if frame == 0:
            rows = rows * facts_ref[3].astype(jnp.float32)
        rows = rows.astype(jnp.bfloat16)
        for tap in range(4):
            at = (frame * 4 + tap) * chans
            out_ref[:, at : at + chans] = rows[tap * per_frame : (tap + 1) * per_frame]


def unpatch_kernel(facts_ref, own_ref, mate_ref, lead_ref, even_ref):
    chans = lead_ref.shape[1]
    select = select_rows(False)
    frames = []
    for frame in range(2):
        pieces = []
        for tap in range(frame * 4, frame * 4 + 4):
            lanes = slice(tap * chans, (tap + 1) * chans)
            pieces.append(own_ref[:, lanes] + mate_ref[:, lanes])
        frames.append(
            jnp.dot(select, jnp.concatenate(pieces, axis=0), precision=lax.Precision.HIGHEST)
        )
    good = inside(FRAME_ROWS)
    lead_ref[...] = (frames[0] * (good * facts_ref[3].astype(jnp.float32))).astype(jnp.bfloat16)
    even_ref[...] = frames[1] * good


def excite_grad_kernel(even_ref, odd_ref, conv_ref, excite_ref, expand_ref, out_ref):
    sums = []
    for frame, grad_ref in enumerate((even_ref, odd_ref)):
        conv = conv_ref[frame * FRAME_ROWS : (frame + 1) * FRAME_ROWS, :]
        active = conv * jax.nn.sigmoid(conv)
        sums.append(jnp.sum(grad_ref[...].astype(jnp.float32) * active, axis=0, keepdims=True))
    excite = excite_ref[...]
    inner = jnp.concatenate(sums, axis=0) * excite * (1.0 - excite)
    out_ref[...] = contract_exact(inner, expand_ref[...].astype(jnp.float32))


def conv_grad_kernel(
    even_ref, odd_ref, conv_ref, excite_ref, sq_ref, relaxed_ref, squeeze_ref, group_ref,
    out_ref, flat_ref, wide_ref, shift_ref, grad_ref,
):
    frames, _, chans = out_ref.shape
    width = group_ref.shape[1]
    rows = frames * FRAME_ROWS
    grad_squeezed = relaxed_ref[...] * silu_slope(sq_ref[...])
    pooled = jnp.dot(
        grad_squeezed, squeeze_ref[...].astype(jnp.float32), precision=lax.Precision.HIGHEST
    ) * (1.0 / (SIDE * SIDE))
    wide_ref[0:EDGE, :] = jnp.zeros((EDGE, chans), jnp.float32)
    wide_ref[EDGE + rows :, :] = jnp.zeros((EDGE, chans), jnp.float32)
    good = inside(FRAME_ROWS)
    for frame, source in enumerate((even_ref, odd_ref)):
        at = frame * FRAME_ROWS
        grad = source[...].astype(jnp.float32)
        grad_ref[at : at + FRAME_ROWS, :] = grad
        active = grad * excite_ref[frame : frame + 1, :] + pooled[frame : frame + 1]
        slope = silu_slope(conv_ref[at : at + FRAME_ROWS, :])
        wide_ref[EDGE + at : EDGE + at + FRAME_ROWS, :] = active * slope * good
    store_shifts(wide_ref, shift_ref, -1)
    body = rows - 2 * WIDE
    for block in channel_blocks(chans, width):
        _, _, start, end = block
        spread, same = block_tools(block, width)
        total = jnp.zeros((body, end - start), jnp.float32)
        for tap in range(9):
            down, across = divmod(tap, 3)
            weights = dense_tap(group_ref, tap, block, spread, same)
            at = (2 - down) * WIDE
            source = shift_ref[across, at : at + body, start:end]
            total += jnp.dot(source, weights, preferred_element_type=jnp.float32)
        grad_ref[WIDE : WIDE + body, start:end] += total
    for frame in range(frames):
        for y in range(SIDE):
            at = frame * FRAME_ROWS + (y + 1) * WIDE + 1
            flat_ref[y * SIDE : (y + 1) * SIDE, :] = grad_ref[at : at + SIDE, :]
        out_ref[frame] = flat_ref[...].astype(jnp.bfloat16)


def f32(*shape):
    return jax.ShapeDtypeStruct(shape, jnp.float32)


def bf16(*shape):
    return jax.ShapeDtypeStruct(shape, jnp.bfloat16)


def conv_forward(features, group_kernel, squeeze_in):
    frames, cells, chans = features.shape
    rows = frames * FRAME_ROWS
    return whole_call(
        conv_kernel,
        (f32(rows, chans), bf16(rows, chans), f32(frames, squeeze_in.shape[0])),
        [
            pltpu.VMEM((cells, chans), jnp.float32),
            pltpu.VMEM((rows + 2 * EDGE, chans), jnp.float32),
            pltpu.VMEM((3, rows, chans), jnp.bfloat16),
        ],
    )(features, group_kernel, squeeze_in)


def hidden_frames(conv, padded, squeezed, squeeze_out):
    rows, chans = conv.shape
    return whole_call(
        hidden_kernel,
        (bf16(FRAME_ROWS, chans), bf16(FRAME_ROWS, chans), f32(rows // FRAME_ROWS, chans)),
        [],
    )(conv, padded, squeezed, squeeze_out)


def vmem_specs(count):
    return [pl.BlockSpec(memory_space=pltpu.SMEM)] + [pl.BlockSpec(memory_space=pltpu.VMEM)] * count


def facts_of(frame_clip, clip_keep):
    smem = pl.BlockSpec(memory_space=pltpu.SMEM)
    return pl.pallas_call(
        facts_kernel,
        out_shape=jax.ShapeDtypeStruct((4,), jnp.int32),
        in_specs=[smem, smem],
        out_specs=smem,
        cost_estimate=FREE,
    )(frame_clip, clip_keep)


def order_rows(facts, own, mate, unit):
    rows, columns = own.shape
    return pl.pallas_call(
        functools.partial(order_kernel, unit),
        out_shape=bf16(2 * rows, columns),
        in_specs=vmem_specs(2),
        compiler_params=pltpu.CompilerParams(vmem_limit_bytes=VMEM_BYTES),
        cost_estimate=FREE,
    )(facts, own, mate)


def take_patches(facts, halo, even):
    chans = even.shape[1]
    return pl.pallas_call(
        patch_kernel,
        out_shape=bf16(OUT_SIDE * OUT_SIDE, 8 * chans),
        in_specs=vmem_specs(2),
        compiler_params=pltpu.CompilerParams(vmem_limit_bytes=VMEM_BYTES),
        cost_estimate=FREE,
    )(facts, halo, even)


def return_patches(facts, own, mate, chans):
    return pl.pallas_call(
        unpatch_kernel,
        out_shape=(bf16(FRAME_ROWS, chans), f32(FRAME_ROWS, chans)),
        in_specs=vmem_specs(2),
        compiler_params=pltpu.CompilerParams(vmem_limit_bytes=VMEM_BYTES),
        cost_estimate=FREE,
    )(facts, own, mate)


def excite_grad(even, odd, conv, excite, squeeze_out):
    rows, chans = conv.shape
    return whole_call(
        excite_grad_kernel,
        f32(rows // FRAME_ROWS, squeeze_out.shape[0]),
        [],
    )(even, odd, conv, excite, squeeze_out)


def conv_backward(even, odd, conv, excite, squeezed, grad_relaxed, squeeze_in, group_kernel):
    rows, chans = conv.shape
    frames = rows // FRAME_ROWS
    return whole_call(
        conv_grad_kernel,
        bf16(frames, SIDE * SIDE, chans),
        [
            pltpu.VMEM((SIDE * SIDE, chans), jnp.float32),
            pltpu.VMEM((rows + 2 * EDGE, chans), jnp.float32),
            pltpu.VMEM((3, rows, chans), jnp.bfloat16),
            pltpu.VMEM((rows, chans), jnp.float32),
        ],
        pl.CostEstimate(flops=rows * chans * 9216, bytes_accessed=16 * rows * chans, transcendentals=0),
    )(even, odd, conv, excite, squeezed, grad_relaxed, squeeze_in, group_kernel)


def shifted(value, axis, by):
    count = lax.axis_size(axis)
    pairs = [(i, i + by) for i in range(count) if 0 <= i + by < count]
    return lax.ppermute(value, axis, pairs)


def ring_order(chips):
    return list(range(0, chips, 2)) + list(range(1, chips, 2))[::-1]


def ring_pairs(count, by):
    order = ring_order(count // 2)
    pairs = []
    for place, chip in enumerate(order):
        target = order[(place + by) % len(order)]
        pairs += [(2 * chip, 2 * target), (2 * chip + 1, 2 * target + 1)]
    return pairs


def swap_cores(value):
    return lax.ppermute(value, "ctx", [(i, i ^ 1) for i in range(lax.axis_size("ctx"))])


def tp_terms(value):
    size = lax.axis_size("tp")
    reach, other = 1, None
    while reach < size:
        value = value if other is None else value + other
        other = lax.ppermute(value, "tp", [(i, i ^ reach) for i in range(size)])
        reach *= 2
    return value, jnp.zeros_like(value) if other is None else other


def sum_tp(value):
    value, other = tp_terms(value)
    return value + other


def ring_step(blocks):
    count = lax.axis_size("ctx")
    onward, backward = ring_pairs(count, 1), ring_pairs(count, -1)
    up_s, up_r, down_s, down_r = blocks
    send = lambda value, pairs: None if value is None else lax.ppermute(value, "ctx", pairs)
    up_r, down_r = send(up_r, onward), send(down_r, backward)
    up_s, down_s = send(up_s, onward), send(down_s, backward)
    return up_s, up_r, down_s, down_r


def tie(*values):
    return lax.optimization_barrier(values)


def sums_kernel(count, patch_ref, keep_ref, send_ref, *refs):
    *blocks, out_ref = refs
    products = [contract_last(patch_ref[...], ref[...]) for ref in blocks[:count]]
    back = jnp.concatenate([keep_ref[...], send_ref[...]], axis=0)
    products += [contract_last(back, ref[...]) for ref in blocks[count:]]
    out_ref[...] = jnp.concatenate(products, axis=1)


def totals_kernel(count, unit, backward, first, facts_ref, *refs):
    sums = refs[0][...] + refs[1][...]
    blocks, refs = refs[2 : 2 + count], refs[2 + count :]
    before, after = refs[:-2], refs[-2:]
    rows, depth = sums.shape[0], sums.shape[1] // 2
    pre, grad_act = sums[:, :depth], sums[:, depth:]
    core = facts_ref[0]
    block, token = token_place(lax.broadcasted_iota(jnp.int32, (rows, 1), 0), core, unit)
    live = (token < jnp.where(block == 0, facts_ref[1], facts_ref[2])).astype(jnp.float32)
    factor = grad_act * silu_slope(pre) if backward else pre * jax.nn.sigmoid(pre)
    factor = (factor * live).astype(jnp.bfloat16)
    if backward:
        matrix = reorder_matrix(core, unit, False)
        factor = jnp.dot(matrix, factor, preferred_element_type=jnp.float32).astype(jnp.bfloat16)
    width = depth // count
    total = 0.0
    for place, ref in enumerate(blocks):
        piece = factor[:, place * width : (place + 1) * width]
        total += jnp.dot(piece, ref[...], preferred_element_type=jnp.float32)
    for half, ref in enumerate(after):
        value = total[half * rows // 2 : (half + 1) * rows // 2]
        ref[...] = value if first else before[half][...] + value


def partial_sums(patches, back, samplers, readouts):
    count, width = len(samplers), samplers[0].shape[0]
    return whole_call(
        functools.partial(sums_kernel, count), f32(patches.shape[0], 2 * count * width), []
    )(patches, *back, *samplers, *readouts)


def add_products(facts, sums, blocks, before, unit, backward):
    rows, columns = sums[0].shape[0] // 2, blocks[0].shape[1]
    kernel = functools.partial(totals_kernel, len(blocks), unit, backward, not before)
    operands = (*sums, *blocks, *before)
    return pl.pallas_call(
        kernel,
        out_shape=(f32(rows, columns),) * 2,
        in_specs=vmem_specs(len(operands)),
        compiler_params=pltpu.CompilerParams(vmem_limit_bytes=VMEM_BYTES),
        cost_estimate=FREE,
    )(facts, *operands)


def chips_exchange(value):
    count = lax.axis_size("ctx")
    groups = [list(range(core, count, 2)) for core in range(2)]
    return lax.all_to_all(
        value, "ctx", split_axis=0, concat_axis=0, tiled=True, axis_index_groups=groups
    )


def per_device(
    features,
    group_kernel,
    squeeze_in,
    squeeze_out,
    sampler_kernel,
    readout_kernel,
    frame_clip,
    clip_keep,
    token_cotangent,
):
    chans = features.shape[2]
    count = lax.axis_size("ctx")
    steps, unit = count // 4, OUT_SIDE * OUT_SIDE // count
    flat_sampler = sampler_kernel.reshape(sampler_kernel.shape[0], 8 * chans)
    blocks = ring_step((flat_sampler, readout_kernel) * 2)
    group_kernel = jnp.swapaxes(group_kernel, 1, 2)
    squeeze_in = squeeze_in.T
    facts = facts_of(frame_clip, clip_keep)

    conv, padded, squeezed = conv_forward(features, group_kernel, squeeze_in)
    token_cotangent, squeezed = tie(token_cotangent, squeezed)
    back = chips_exchange(token_cotangent)
    squeezed = sum_tp(squeezed)
    even, odd, excite = hidden_frames(conv, padded, squeezed, squeeze_out)
    halo = shifted(odd, "ctx", 1)
    halo, *blocks = tie(halo, *blocks)
    patches = take_patches(facts, halo, even)
    patches = order_rows(facts, patches, swap_cores(patches), unit)
    back = (back, swap_cores(back))

    samplers, readouts = [flat_sampler], [readout_kernel]
    tokens = grads = ()
    for step in range(1, steps + 1):
        here = blocks
        if step < steps:
            samplers, readouts = samplers + [here[0], here[2]], readouts + [here[1], here[3]]
            if step == steps - 1:
                *here, token_keep, token_send, grad_own, grad_mate = tie(*here, *tokens, *grads)
                tokens, grads = (token_keep, token_send), (grad_own, grad_mate)
                here = here[0], None, None, here[3]
            blocks = ring_step(here)
        else:
            samplers, readouts = samplers + [here[0]], readouts + [here[3]]
        if step >= steps - 2:
            sums = tp_terms(partial_sums(patches, back, samplers, readouts))
            tokens = add_products(facts, sums, readouts, tokens, unit, False)
            grads = add_products(facts, sums, samplers, grads, unit, True)
            samplers, readouts = [], []
    lead, grad_even = return_patches(facts, grads[0], swap_cores(grads[1]), chans)
    token_keep, token_send, lead = tie(*tokens, lead)
    grad_odd = shifted(lead, "ctx", -1)
    tokens = (token_keep + swap_cores(token_send)).astype(jnp.bfloat16)
    tokens, grad_odd = tie(tokens, grad_odd)
    llm_tokens = chips_exchange(tokens)
    grad_relaxed = sum_tp(excite_grad(grad_even, grad_odd, conv, excite, squeeze_out))
    grad_features = conv_backward(
        grad_even, grad_odd, conv, excite, squeezed, grad_relaxed, squeeze_in, group_kernel
    )
    return (llm_tokens, grad_features)


def solution(mesh):
    placed = (
        P("ctx", None, "tp"),
        P(None, "tp", None),
        P("tp", None),
        P(None, "tp"),
        P("ctx", None, "tp"),
        P("ctx", "tp"),
        P(),
        P(),
        P("ctx", "tp"),
    )
    return jax.shard_map(
        per_device,
        mesh=mesh,
        in_specs=placed,
        out_specs=(P("ctx", "tp"), P("ctx", None, "tp")),
        check_vma=False,
    )
```

```python
import functools

import jax
import jax.numpy as jnp
from jax import lax
from jax.experimental import pallas as pl
from jax.experimental.pallas import tpu as pltpu
from jax.sharding import PartitionSpec as P

SIDE = 14
OUT_SIDE = 8
WIDE = 16
FRAME_ROWS = WIDE * WIDE
EDGE = 8
LANES = 128
VMEM_BYTES = 20 * 2**20
FREE = pl.CostEstimate(flops=0, bytes_accessed=0, transcendentals=0)


def whole_call(kernel, outs, scratch, cost=FREE):
    return pl.pallas_call(
        kernel,
        out_shape=outs,
        scratch_shapes=scratch,
        compiler_params=pltpu.CompilerParams(vmem_limit_bytes=VMEM_BYTES),
        cost_estimate=cost,
    )


def contract_last(left, right):
    return lax.dot_general(
        left, right, (((1,), (1,)), ((), ())), preferred_element_type=jnp.float32
    )


def contract_exact(left, right):
    return lax.dot_general(
        left,
        right,
        (((1,), (1,)), ((), ())),
        precision=lax.Precision.HIGHEST,
        preferred_element_type=jnp.float32,
    )


def silu_slope(values):
    sigma = jax.nn.sigmoid(values)
    return sigma * (1.0 + values * (1.0 - sigma))


def inside(rows):
    row = lax.broadcasted_iota(jnp.int32, (rows, 1), 0)
    across, down = row & (WIDE - 1), (row // WIDE) & (WIDE - 1)
    good = (across >= 1) & (across <= SIDE) & (down >= 1) & (down <= SIDE)
    return good.astype(jnp.float32)


def channel_blocks(chans, width):
    span = 4 * width
    blocks = []
    for low in range(0, chans, span):
        high = min(chans, low + span)
        blocks.append((low, high, low // LANES * LANES, min(chans, -(-high // LANES) * LANES)))
    return blocks


def block_tools(block, width):
    low, high, start, end = block
    size = end - start
    out_row = lax.broadcasted_iota(jnp.int32, (size, width), 0) + start
    within = lax.broadcasted_iota(jnp.int32, (size, width), 1)
    lane = lax.broadcasted_iota(jnp.int32, (size, size), 1) + start
    row = lax.broadcasted_iota(jnp.int32, (size, size), 0) + start
    spread = jnp.zeros((size, width), jnp.float32)
    same = jnp.zeros((size, size), jnp.float32)
    for first in range(low, high, width):
        spread += (out_row == within + first).astype(jnp.float32)
        in_lane = (lane >= first) & (lane < first + width)
        in_row = (row >= first) & (row < first + width)
        same += (in_lane & in_row).astype(jnp.float32)
    return spread.astype(jnp.bfloat16), same


def dense_tap(group_ref, tap, block, spread, same):
    _, _, start, end = block
    full = jnp.dot(spread, group_ref[tap, :, start:end], preferred_element_type=jnp.float32)
    return (full * same).astype(jnp.bfloat16)


def store_shifts(wide_ref, shift_ref, sign):
    rows = shift_ref.shape[1]
    for col in range(3):
        at = EDGE + sign * (col - 1)
        shift_ref[col] = wide_ref[at : at + rows, :].astype(jnp.bfloat16)


def conv_kernel(feat_ref, group_ref, squeeze_ref, *refs):
    conv_ref, pad_ref, sq_ref, *dense_refs, flat_ref, wide_ref, shift_ref = refs
    frames, _, chans = feat_ref.shape
    width = group_ref.shape[1]
    rows = frames * FRAME_ROWS
    wide_ref[...] = jnp.zeros_like(wide_ref)
    for frame in range(frames):
        flat_ref[...] = feat_ref[frame].astype(jnp.float32)
        for y in range(SIDE):
            at = EDGE + frame * FRAME_ROWS + (y + 1) * WIDE + 1
            wide_ref[at : at + SIDE, :] = flat_ref[y * SIDE : (y + 1) * SIDE, :]
    store_shifts(wide_ref, shift_ref, 1)
    pad_ref[...] = shift_ref[1]
    conv_ref[...] = jnp.zeros_like(conv_ref)
    body = rows - 2 * WIDE
    for block, dense_ref in zip(channel_blocks(chans, width), dense_refs):
        _, _, start, end = block
        spread, same = block_tools(block, width)
        total = jnp.zeros((body, end - start), jnp.float32)
        for tap in range(9):
            down, across = divmod(tap, 3)
            weights = dense_tap(group_ref, tap, block, spread, same)
            dense_ref[tap] = weights
            source = shift_ref[across, down * WIDE : down * WIDE + body, start:end]
            total += contract_last(source, weights)
        conv_ref[WIDE : WIDE + body, start:end] += total
    conv = conv_ref[...] * inside(rows)
    conv_ref[...] = conv
    active = conv * jax.nn.sigmoid(conv)
    pooled = jnp.concatenate(
        [
            jnp.sum(active[f * FRAME_ROWS : (f + 1) * FRAME_ROWS], axis=0, keepdims=True)
            for f in range(frames)
        ],
        axis=0,
    ) * (1.0 / (SIDE * SIDE))
    sq_ref[...] = contract_exact(pooled, squeeze_ref[...].astype(jnp.float32))


def hidden_kernel(
    conv_ref, pad_ref, sq_ref, expand_ref, even_ref, odd_ref, excite_ref, active_ref, slope_ref
):
    squeezed = sq_ref[...]
    relaxed = squeezed * jax.nn.sigmoid(squeezed)
    excite = jax.nn.sigmoid(
        jnp.dot(relaxed, expand_ref[...].astype(jnp.float32), precision=lax.Precision.HIGHEST)
    )
    excite_ref[...] = excite
    good = inside(FRAME_ROWS)
    for frame, out_ref in enumerate((even_ref, odd_ref)):
        rows = slice(frame * FRAME_ROWS, (frame + 1) * FRAME_ROWS)
        conv = conv_ref[rows, :]
        sigma = jax.nn.sigmoid(conv)
        active = conv * sigma
        active_ref[rows, :] = active
        slope_ref[rows, :] = sigma * (1.0 + conv * (1.0 - sigma)) * good
        hidden = pad_ref[rows, :].astype(jnp.float32) + active * excite[frame : frame + 1]
        out_ref[...] = hidden.astype(jnp.bfloat16)


def select_rows(to_patches):
    shape = (FRAME_ROWS, FRAME_ROWS)
    out_row = lax.broadcasted_iota(jnp.int32, shape, 0)
    in_row = lax.broadcasted_iota(jnp.int32, shape, 1)
    patch_row, frame_row = (out_row, in_row) if to_patches else (in_row, out_row)
    down, across = patch_row >> 7, (patch_row >> 6) & 1
    a, b = (patch_row >> 3) & 7, patch_row & 7
    return ((2 * a + down) * WIDE + 2 * b + across == frame_row).astype(jnp.float32)


def facts_kernel(clip_ref, keep_ref, out_ref):
    shard = lax.axis_index("ctx")
    frames = clip_ref.shape[0]
    out_ref[0] = shard % 2
    for block in range(2):
        pair = shard // 2 * 2 + block
        clip = clip_ref[2 * pair]
        start = jnp.int32(0)
        for other in range(0, frames, 2):
            start += jnp.where(clip_ref[other] < clip, 1, 0)
        out_ref[1 + block] = keep_ref[clip] - (pair - start) * (OUT_SIDE * OUT_SIDE)
    before = clip_ref[jnp.maximum(2 * shard - 1, 0)]
    out_ref[3] = jnp.where((shard > 0) & (before == clip_ref[2 * shard]), 1, 0)


def token_place(row, core, unit):
    per_block = OUT_SIDE * OUT_SIDE
    within = row % per_block
    block = (within // unit) % 2
    target_core = jnp.where(row < per_block, core, 1 - core)
    return block, unit * (2 * (within // (2 * unit)) + target_core) + within % unit


def reorder_matrix(core, unit, to_sent):
    shape = (2 * OUT_SIDE * OUT_SIDE,) * 2
    out_row = lax.broadcasted_iota(jnp.int32, shape, 0)
    in_row = lax.broadcasted_iota(jnp.int32, shape, 1)
    sent, natural = (out_row, in_row) if to_sent else (in_row, out_row)
    block, token = token_place(sent, core, unit)
    source = jnp.where(block == core, 0, OUT_SIDE * OUT_SIDE) + token
    return (source == natural).astype(jnp.bfloat16)


def order_kernel(unit, facts_ref, own_ref, mate_ref, out_ref):
    rows = jnp.concatenate([own_ref[...], mate_ref[...]], axis=0)
    matrix = reorder_matrix(facts_ref[0], unit, True)
    out_ref[...] = jnp.dot(matrix, rows, preferred_element_type=jnp.float32).astype(jnp.bfloat16)


def patch_kernel(facts_ref, halo_ref, even_ref, out_ref):
    chans = halo_ref.shape[1]
    per_frame = OUT_SIDE * OUT_SIDE
    select = select_rows(True).astype(jnp.bfloat16)
    for frame, source in enumerate((halo_ref, even_ref)):
        rows = jnp.dot(select, source[...], preferred_element_type=jnp.float32)
        if frame == 0:
            rows = rows * facts_ref[3].astype(jnp.float32)
        rows = rows.astype(jnp.bfloat16)
        for tap in range(4):
            at = (frame * 4 + tap) * chans
            out_ref[:, at : at + chans] = rows[tap * per_frame : (tap + 1) * per_frame]


def unpatch_kernel(facts_ref, own_ref, mate_ref, lead_ref, even_ref):
    chans = lead_ref.shape[1]
    select = select_rows(False)
    frames = []
    for frame in range(2):
        pieces = []
        for tap in range(frame * 4, frame * 4 + 4):
            lanes = slice(tap * chans, (tap + 1) * chans)
            pieces.append(own_ref[:, lanes] + mate_ref[:, lanes])
        frames.append(
            jnp.dot(select, jnp.concatenate(pieces, axis=0), precision=lax.Precision.HIGHEST)
        )
    good = inside(FRAME_ROWS)
    lead_ref[...] = (frames[0] * (good * facts_ref[3].astype(jnp.float32))).astype(jnp.bfloat16)
    even_ref[...] = frames[1] * good


def excite_grad_kernel(even_ref, odd_ref, active_ref, excite_ref, expand_ref, out_ref):
    sums = []
    for frame, grad_ref in enumerate((even_ref, odd_ref)):
        active = active_ref[frame * FRAME_ROWS : (frame + 1) * FRAME_ROWS, :]
        sums.append(jnp.sum(grad_ref[...].astype(jnp.float32) * active, axis=0, keepdims=True))
    excite = excite_ref[...]
    inner = jnp.concatenate(sums, axis=0) * excite * (1.0 - excite)
    out_ref[...] = contract_exact(inner, expand_ref[...].astype(jnp.float32))


def conv_grad_kernel(
    width, even_ref, odd_ref, slope_ref, excite_ref, sq_ref, relaxed_ref, squeeze_ref, *refs
):
    *dense_refs, out_ref, flat_ref, wide_ref, shift_ref, grad_ref = refs
    frames, _, chans = out_ref.shape
    rows = frames * FRAME_ROWS
    grad_squeezed = relaxed_ref[...] * silu_slope(sq_ref[...])
    pooled = jnp.dot(
        grad_squeezed, squeeze_ref[...].astype(jnp.float32), precision=lax.Precision.HIGHEST
    ) * (1.0 / (SIDE * SIDE))
    wide_ref[0:EDGE, :] = jnp.zeros((EDGE, chans), jnp.float32)
    wide_ref[EDGE + rows :, :] = jnp.zeros((EDGE, chans), jnp.float32)
    for frame, source in enumerate((even_ref, odd_ref)):
        at = frame * FRAME_ROWS
        grad = source[...].astype(jnp.float32)
        grad_ref[at : at + FRAME_ROWS, :] = grad
        active = grad * excite_ref[frame : frame + 1, :] + pooled[frame : frame + 1]
        slope = slope_ref[at : at + FRAME_ROWS, :]
        wide_ref[EDGE + at : EDGE + at + FRAME_ROWS, :] = active * slope
    store_shifts(wide_ref, shift_ref, -1)
    body = rows - 2 * WIDE
    for block, dense_ref in zip(channel_blocks(chans, width), dense_refs):
        _, _, start, end = block
        total = jnp.zeros((body, end - start), jnp.float32)
        for tap in range(9):
            down, across = divmod(tap, 3)
            at = (2 - down) * WIDE
            source = shift_ref[across, at : at + body, start:end]
            total += jnp.dot(source, dense_ref[tap], preferred_element_type=jnp.float32)
        grad_ref[WIDE : WIDE + body, start:end] += total
    for frame in range(frames):
        for y in range(SIDE):
            at = frame * FRAME_ROWS + (y + 1) * WIDE + 1
            flat_ref[y * SIDE : (y + 1) * SIDE, :] = grad_ref[at : at + SIDE, :]
        out_ref[frame] = flat_ref[...].astype(jnp.bfloat16)


def f32(*shape):
    return jax.ShapeDtypeStruct(shape, jnp.float32)


def bf16(*shape):
    return jax.ShapeDtypeStruct(shape, jnp.bfloat16)


def conv_forward(features, group_kernel, squeeze_in):
    frames, cells, chans = features.shape
    rows = frames * FRAME_ROWS
    return whole_call(
        conv_kernel,
        (f32(rows, chans), bf16(rows, chans), f32(frames, squeeze_in.shape[0]))
        + tuple(
            bf16(9, end - start, end - start)
            for _, _, start, end in channel_blocks(chans, group_kernel.shape[1])
        ),
        [
            pltpu.VMEM((cells, chans), jnp.float32),
            pltpu.VMEM((rows + 2 * EDGE, chans), jnp.float32),
            pltpu.VMEM((3, rows, chans), jnp.bfloat16),
        ],
    )(features, group_kernel, squeeze_in)


def hidden_frames(conv, padded, squeezed, squeeze_out):
    rows, chans = conv.shape
    return whole_call(
        hidden_kernel,
        (bf16(FRAME_ROWS, chans),) * 2
        + (f32(rows // FRAME_ROWS, chans), f32(rows, chans), f32(rows, chans)),
        [],
    )(conv, padded, squeezed, squeeze_out)


def vmem_specs(count):
    return [pl.BlockSpec(memory_space=pltpu.SMEM)] + [pl.BlockSpec(memory_space=pltpu.VMEM)] * count


def facts_of(frame_clip, clip_keep):
    smem = pl.BlockSpec(memory_space=pltpu.SMEM)
    return pl.pallas_call(
        facts_kernel,
        out_shape=jax.ShapeDtypeStruct((4,), jnp.int32),
        in_specs=[smem, smem],
        out_specs=smem,
        cost_estimate=FREE,
    )(frame_clip, clip_keep)


def order_rows(facts, own, mate, unit):
    rows, columns = own.shape
    return pl.pallas_call(
        functools.partial(order_kernel, unit),
        out_shape=bf16(2 * rows, columns),
        in_specs=vmem_specs(2),
        compiler_params=pltpu.CompilerParams(vmem_limit_bytes=VMEM_BYTES),
        cost_estimate=FREE,
    )(facts, own, mate)


def take_patches(facts, halo, even):
    chans = even.shape[1]
    return pl.pallas_call(
        patch_kernel,
        out_shape=bf16(OUT_SIDE * OUT_SIDE, 8 * chans),
        in_specs=vmem_specs(2),
        compiler_params=pltpu.CompilerParams(vmem_limit_bytes=VMEM_BYTES),
        cost_estimate=FREE,
    )(facts, halo, even)


def return_patches(facts, own, mate, chans):
    return pl.pallas_call(
        unpatch_kernel,
        out_shape=(bf16(FRAME_ROWS, chans), f32(FRAME_ROWS, chans)),
        in_specs=vmem_specs(2),
        compiler_params=pltpu.CompilerParams(vmem_limit_bytes=VMEM_BYTES),
        cost_estimate=FREE,
    )(facts, own, mate)


def excite_grad(even, odd, active, excite, squeeze_out):
    rows, chans = active.shape
    return whole_call(
        excite_grad_kernel,
        f32(rows // FRAME_ROWS, squeeze_out.shape[0]),
        [],
    )(even, odd, active, excite, squeeze_out)


def conv_backward(even, odd, slope, excite, squeezed, grad_relaxed, squeeze_in, dense, width):
    rows, chans = slope.shape
    frames = rows // FRAME_ROWS
    return whole_call(
        functools.partial(conv_grad_kernel, width),
        bf16(frames, SIDE * SIDE, chans),
        [
            pltpu.VMEM((SIDE * SIDE, chans), jnp.float32),
            pltpu.VMEM((rows + 2 * EDGE, chans), jnp.float32),
            pltpu.VMEM((3, rows, chans), jnp.bfloat16),
            pltpu.VMEM((rows, chans), jnp.float32),
        ],
        pl.CostEstimate(flops=rows * chans * 9216, bytes_accessed=16 * rows * chans, transcendentals=0),
    )(even, odd, slope, excite, squeezed, grad_relaxed, squeeze_in, *dense)


def shifted(value, axis, by):
    count = lax.axis_size(axis)
    pairs = [(i, i + by) for i in range(count) if 0 <= i + by < count]
    return lax.ppermute(value, axis, pairs)


def ring_order(chips):
    return list(range(0, chips, 2)) + list(range(1, chips, 2))[::-1]


def ring_pairs(count, by):
    order = ring_order(count // 2)
    pairs = []
    for place, chip in enumerate(order):
        target = order[(place + by) % len(order)]
        pairs += [(2 * chip, 2 * target), (2 * chip + 1, 2 * target + 1)]
    return pairs


def swap_cores(value):
    return lax.ppermute(value, "ctx", [(i, i ^ 1) for i in range(lax.axis_size("ctx"))])


def tp_terms(value):
    size = lax.axis_size("tp")
    reach, other = 1, None
    while reach < size:
        value = value if other is None else value + other
        other = lax.ppermute(value, "tp", [(i, i ^ reach) for i in range(size)])
        reach *= 2
    return value, jnp.zeros_like(value) if other is None else other


def sum_tp(value):
    value, other = tp_terms(value)
    return value + other


def ring_step(blocks):
    count = lax.axis_size("ctx")
    onward, backward = ring_pairs(count, 1), ring_pairs(count, -1)
    up_s, up_r, down_s, down_r = blocks
    send = lambda value, pairs: None if value is None else lax.ppermute(value, "ctx", pairs)
    up_r, down_r = send(up_r, onward), send(down_r, backward)
    up_s, down_s = send(up_s, onward), send(down_s, backward)
    return up_s, up_r, down_s, down_r


def tie(*values):
    return lax.optimization_barrier(values)


def sums_kernel(count, patch_ref, keep_ref, send_ref, *refs):
    *blocks, out_ref = refs
    products = [contract_last(patch_ref[...], ref[...]) for ref in blocks[:count]]
    back = jnp.concatenate([keep_ref[...], send_ref[...]], axis=0)
    products += [contract_last(back, ref[...]) for ref in blocks[count:]]
    out_ref[...] = jnp.concatenate(products, axis=1)


def totals_kernel(count, unit, backward, first, facts_ref, *refs):
    sums = refs[0][...] + refs[1][...]
    blocks, refs = refs[2 : 2 + count], refs[2 + count :]
    before, after = refs[:-2], refs[-2:]
    rows, depth = sums.shape[0], sums.shape[1] // 2
    pre, grad_act = sums[:, :depth], sums[:, depth:]
    core = facts_ref[0]
    block, token = token_place(lax.broadcasted_iota(jnp.int32, (rows, 1), 0), core, unit)
    live = (token < jnp.where(block == 0, facts_ref[1], facts_ref[2])).astype(jnp.float32)
    factor = grad_act * silu_slope(pre) if backward else pre * jax.nn.sigmoid(pre)
    factor = (factor * live).astype(jnp.bfloat16)
    if backward:
        matrix = reorder_matrix(core, unit, False)
        factor = jnp.dot(matrix, factor, preferred_element_type=jnp.float32).astype(jnp.bfloat16)
    width = depth // count
    total = 0.0
    for place, ref in enumerate(blocks):
        piece = factor[:, place * width : (place + 1) * width]
        total += jnp.dot(piece, ref[...], preferred_element_type=jnp.float32)
    for half, ref in enumerate(after):
        value = total[half * rows // 2 : (half + 1) * rows // 2]
        ref[...] = value if first else before[half][...] + value


def partial_sums(patches, back, samplers, readouts):
    count, width = len(samplers), samplers[0].shape[0]
    return whole_call(
        functools.partial(sums_kernel, count), f32(patches.shape[0], 2 * count * width), []
    )(patches, *back, *samplers, *readouts)


def add_products(facts, sums, blocks, before, unit, backward):
    rows, columns = sums[0].shape[0] // 2, blocks[0].shape[1]
    kernel = functools.partial(totals_kernel, len(blocks), unit, backward, not before)
    operands = (*sums, *blocks, *before)
    return pl.pallas_call(
        kernel,
        out_shape=(f32(rows, columns),) * 2,
        in_specs=vmem_specs(len(operands)),
        compiler_params=pltpu.CompilerParams(vmem_limit_bytes=VMEM_BYTES),
        cost_estimate=FREE,
    )(facts, *operands)


def chips_exchange(value):
    count = lax.axis_size("ctx")
    groups = [list(range(core, count, 2)) for core in range(2)]
    return lax.all_to_all(
        value, "ctx", split_axis=0, concat_axis=0, tiled=True, axis_index_groups=groups
    )


def per_device(
    features,
    group_kernel,
    squeeze_in,
    squeeze_out,
    sampler_kernel,
    readout_kernel,
    frame_clip,
    clip_keep,
    token_cotangent,
):
    chans, width = features.shape[2], group_kernel.shape[2]
    count = lax.axis_size("ctx")
    steps, unit = count // 4, OUT_SIDE * OUT_SIDE // count
    flat_sampler = sampler_kernel.reshape(sampler_kernel.shape[0], 8 * chans)
    blocks = ring_step((flat_sampler, readout_kernel) * 2)
    group_kernel = jnp.swapaxes(group_kernel, 1, 2)
    squeeze_in = squeeze_in.T
    facts = facts_of(frame_clip, clip_keep)

    conv, padded, squeezed, *dense = conv_forward(features, group_kernel, squeeze_in)
    token_cotangent, squeezed = tie(token_cotangent, squeezed)
    back = chips_exchange(token_cotangent)
    squeezed = sum_tp(squeezed)
    even, odd, excite, active, slope = hidden_frames(conv, padded, squeezed, squeeze_out)
    halo = shifted(odd, "ctx", 1)

    samplers, readouts = [flat_sampler], [readout_kernel]
    tokens = grads = ()
    for step in range(1, steps + 1):
        if step == 1:
            *blocks, even = tie(*blocks, even)
        if step == 2:
            up_s, up_r, down_s, down_r = blocks
            halo, up_s, down_s = tie(halo, up_s, down_s)
            blocks = up_s, up_r, down_s, down_r
            patches = take_patches(facts, halo, even)
            patches = order_rows(facts, patches, swap_cores(patches), unit)
            back = (back, swap_cores(back))
        here = blocks
        if step < steps:
            samplers, readouts = samplers + [here[0], here[2]], readouts + [here[1], here[3]]
            if step == steps - 1:
                *here, token_keep, token_send, grad_own, grad_mate = tie(*here, *tokens, *grads)
                tokens, grads = (token_keep, token_send), (grad_own, grad_mate)
                here = here[0], None, None, here[3]
            blocks = ring_step(here)
        else:
            last_s, last_r, *held = tie(here[0], here[3], *tokens, *grads)
            tokens, grads = held[:2], held[2:]
            samplers, readouts = samplers + [last_s], readouts + [last_r]
        if step >= steps - 2:
            sums = tp_terms(partial_sums(patches, back, samplers, readouts))
            tokens = add_products(facts, sums, readouts, tokens, unit, False)
            grads = add_products(facts, sums, samplers, grads, unit, True)
            samplers, readouts = [], []
    lead, grad_even = return_patches(facts, grads[0], swap_cores(grads[1]), chans)
    token_keep, token_send, lead = tie(*tokens, lead)
    grad_odd = shifted(lead, "ctx", -1)
    tokens = (token_keep + swap_cores(token_send)).astype(jnp.bfloat16)
    tokens, grad_even = tie(tokens, grad_even)
    llm_tokens = chips_exchange(tokens)
    grad_relaxed = sum_tp(excite_grad(grad_even, grad_odd, active, excite, squeeze_out))
    grad_features = conv_backward(
        grad_even, grad_odd, slope, excite, squeezed, grad_relaxed, squeeze_in, dense, width
    )
    return (llm_tokens, grad_features)


def solution(mesh):
    placed = (
        P("ctx", None, "tp"),
        P(None, "tp", None),
        P("tp", None),
        P(None, "tp"),
        P("ctx", None, "tp"),
        P("ctx", "tp"),
        P(),
        P(),
        P("ctx", "tp"),
    )
    return jax.shard_map(
        per_device,
        mesh=mesh,
        in_specs=placed,
        out_specs=(P("ctx", "tp"), P("ctx", None, "tp")),
        check_vma=False,
    )
```

```python
import functools

import jax
import jax.numpy as jnp
from jax import lax
from jax.experimental import pallas as pl
from jax.experimental.pallas import tpu as pltpu
from jax.sharding import PartitionSpec as P

SIDE = 14
OUT_SIDE = 8
WIDE = 16
FRAME_ROWS = WIDE * WIDE
EDGE = 8
LANES = 128
VMEM_BYTES = 20 * 2**20
FREE = pl.CostEstimate(flops=0, bytes_accessed=0, transcendentals=0)


def whole_call(kernel, outs, scratch, cost=FREE):
    return pl.pallas_call(
        kernel,
        out_shape=outs,
        scratch_shapes=scratch,
        compiler_params=pltpu.CompilerParams(vmem_limit_bytes=VMEM_BYTES),
        cost_estimate=cost,
    )


def contract_last(left, right):
    return lax.dot_general(
        left, right, (((1,), (1,)), ((), ())), preferred_element_type=jnp.float32
    )


def contract_exact(left, right):
    return lax.dot_general(
        left,
        right,
        (((1,), (1,)), ((), ())),
        precision=lax.Precision.HIGHEST,
        preferred_element_type=jnp.float32,
    )


def silu_slope(values):
    sigma = jax.nn.sigmoid(values)
    return sigma * (1.0 + values * (1.0 - sigma))


def inside(rows):
    row = lax.broadcasted_iota(jnp.int32, (rows, 1), 0)
    across, down = row & (WIDE - 1), (row // WIDE) & (WIDE - 1)
    good = (across >= 1) & (across <= SIDE) & (down >= 1) & (down <= SIDE)
    return good.astype(jnp.float32)


def channel_blocks(chans, width):
    span = 4 * width
    blocks = []
    for low in range(0, chans, span):
        high = min(chans, low + span)
        blocks.append((low, high, low // LANES * LANES, min(chans, -(-high // LANES) * LANES)))
    return blocks


def block_tools(block, width):
    low, high, start, end = block
    size = end - start
    out_row = lax.broadcasted_iota(jnp.int32, (size, width), 0) + start
    within = lax.broadcasted_iota(jnp.int32, (size, width), 1)
    lane = lax.broadcasted_iota(jnp.int32, (size, size), 1) + start
    row = lax.broadcasted_iota(jnp.int32, (size, size), 0) + start
    spread = jnp.zeros((size, width), jnp.float32)
    same = jnp.zeros((size, size), jnp.float32)
    for first in range(low, high, width):
        spread += (out_row == within + first).astype(jnp.float32)
        in_lane = (lane >= first) & (lane < first + width)
        in_row = (row >= first) & (row < first + width)
        same += (in_lane & in_row).astype(jnp.float32)
    return spread.astype(jnp.bfloat16), same


def dense_tap(group_ref, tap, block, spread, same):
    _, _, start, end = block
    full = jnp.dot(spread, group_ref[tap, :, start:end], preferred_element_type=jnp.float32)
    return (full * same).astype(jnp.bfloat16)


def store_shifts(wide_ref, shift_ref, sign):
    rows = shift_ref.shape[1]
    for col in range(3):
        at = EDGE + sign * (col - 1)
        shift_ref[col] = wide_ref[at : at + rows, :].astype(jnp.bfloat16)


def conv_kernel(feat_ref, group_ref, squeeze_ref, *refs):
    conv_ref, pad_ref, sq_ref, flat_ref, wide_ref, shift_ref = refs
    frames, _, chans = feat_ref.shape
    width = group_ref.shape[1]
    rows = frames * FRAME_ROWS
    wide_ref[...] = jnp.zeros_like(wide_ref)
    for frame in range(frames):
        flat_ref[...] = feat_ref[frame].astype(jnp.float32)
        for y in range(SIDE):
            at = EDGE + frame * FRAME_ROWS + (y + 1) * WIDE + 1
            wide_ref[at : at + SIDE, :] = flat_ref[y * SIDE : (y + 1) * SIDE, :]
    store_shifts(wide_ref, shift_ref, 1)
    pad_ref[...] = shift_ref[1]
    conv_ref[...] = jnp.zeros_like(conv_ref)
    body = rows - 2 * WIDE
    for block in channel_blocks(chans, width):
        _, _, start, end = block
        spread, same = block_tools(block, width)
        total = jnp.zeros((body, end - start), jnp.float32)
        for tap in range(9):
            down, across = divmod(tap, 3)
            weights = dense_tap(group_ref, tap, block, spread, same)
            source = shift_ref[across, down * WIDE : down * WIDE + body, start:end]
            total += contract_last(source, weights)
        conv_ref[WIDE : WIDE + body, start:end] += total
    conv = conv_ref[...] * inside(rows)
    conv_ref[...] = conv
    active = conv * jax.nn.sigmoid(conv)
    pooled = jnp.concatenate(
        [
            jnp.sum(active[f * FRAME_ROWS : (f + 1) * FRAME_ROWS], axis=0, keepdims=True)
            for f in range(frames)
        ],
        axis=0,
    ) * (1.0 / (SIDE * SIDE))
    sq_ref[...] = contract_exact(pooled, squeeze_ref[...].astype(jnp.float32))


def hidden_kernel(
    conv_ref, pad_ref, sq_ref, expand_ref, even_ref, odd_ref, excite_ref, active_ref, slope_ref
):
    squeezed = sq_ref[...]
    relaxed = squeezed * jax.nn.sigmoid(squeezed)
    excite = jax.nn.sigmoid(
        jnp.dot(relaxed, expand_ref[...].astype(jnp.float32), precision=lax.Precision.HIGHEST)
    )
    excite_ref[...] = excite
    good = inside(FRAME_ROWS)
    for frame, out_ref in enumerate((even_ref, odd_ref)):
        rows = slice(frame * FRAME_ROWS, (frame + 1) * FRAME_ROWS)
        conv = conv_ref[rows, :]
        sigma = jax.nn.sigmoid(conv)
        active = conv * sigma
        active_ref[rows, :] = active
        slope_ref[rows, :] = sigma * (1.0 + conv * (1.0 - sigma)) * good
        hidden = pad_ref[rows, :].astype(jnp.float32) + active * excite[frame : frame + 1]
        out_ref[...] = hidden.astype(jnp.bfloat16)


def select_rows(to_patches):
    shape = (FRAME_ROWS, FRAME_ROWS)
    out_row = lax.broadcasted_iota(jnp.int32, shape, 0)
    in_row = lax.broadcasted_iota(jnp.int32, shape, 1)
    patch_row, frame_row = (out_row, in_row) if to_patches else (in_row, out_row)
    down, across = patch_row >> 7, (patch_row >> 6) & 1
    a, b = (patch_row >> 3) & 7, patch_row & 7
    return ((2 * a + down) * WIDE + 2 * b + across == frame_row).astype(jnp.float32)


def facts_kernel(clip_ref, keep_ref, out_ref):
    shard = lax.axis_index("ctx")
    frames = clip_ref.shape[0]
    out_ref[0] = shard % 2
    for block in range(2):
        pair = shard // 2 * 2 + block
        clip = clip_ref[2 * pair]
        start = jnp.int32(0)
        for other in range(0, frames, 2):
            start += jnp.where(clip_ref[other] < clip, 1, 0)
        out_ref[1 + block] = keep_ref[clip] - (pair - start) * (OUT_SIDE * OUT_SIDE)
    before = clip_ref[jnp.maximum(2 * shard - 1, 0)]
    out_ref[3] = jnp.where((shard > 0) & (before == clip_ref[2 * shard]), 1, 0)


def token_place(row, core, unit):
    per_block = OUT_SIDE * OUT_SIDE
    within = row % per_block
    block = (within // unit) % 2
    target_core = jnp.where(row < per_block, core, 1 - core)
    return block, unit * (2 * (within // (2 * unit)) + target_core) + within % unit


def reorder_matrix(core, unit, to_sent):
    shape = (2 * OUT_SIDE * OUT_SIDE,) * 2
    out_row = lax.broadcasted_iota(jnp.int32, shape, 0)
    in_row = lax.broadcasted_iota(jnp.int32, shape, 1)
    sent, natural = (out_row, in_row) if to_sent else (in_row, out_row)
    block, token = token_place(sent, core, unit)
    source = jnp.where(block == core, 0, OUT_SIDE * OUT_SIDE) + token
    return (source == natural).astype(jnp.bfloat16)


def order_kernel(unit, facts_ref, own_ref, mate_ref, out_ref):
    rows = jnp.concatenate([own_ref[...], mate_ref[...]], axis=0)
    matrix = reorder_matrix(facts_ref[0], unit, True)
    out_ref[...] = jnp.dot(matrix, rows, preferred_element_type=jnp.float32).astype(jnp.bfloat16)


def patch_kernel(facts_ref, halo_ref, even_ref, out_ref):
    chans = halo_ref.shape[1]
    per_frame = OUT_SIDE * OUT_SIDE
    select = select_rows(True).astype(jnp.bfloat16)
    for frame, source in enumerate((halo_ref, even_ref)):
        rows = jnp.dot(select, source[...], preferred_element_type=jnp.float32)
        if frame == 0:
            rows = rows * facts_ref[3].astype(jnp.float32)
        rows = rows.astype(jnp.bfloat16)
        for tap in range(4):
            at = (frame * 4 + tap) * chans
            out_ref[:, at : at + chans] = rows[tap * per_frame : (tap + 1) * per_frame]


def unpatch_kernel(facts_ref, own_ref, mate_ref, out_ref):
    chans = out_ref.shape[1]
    rows = own_ref[...] + mate_ref[...].astype(jnp.float32)
    pieces = [rows[:, tap * chans : (tap + 1) * chans] for tap in range(4)]
    frame = jnp.dot(
        select_rows(False), jnp.concatenate(pieces, axis=0), precision=lax.Precision.HIGHEST
    ) * inside(FRAME_ROWS)
    if out_ref.dtype == jnp.bfloat16:
        frame = frame * facts_ref[3].astype(jnp.float32)
    out_ref[...] = frame.astype(out_ref.dtype)


def excite_grad_kernel(even_ref, odd_ref, active_ref, excite_ref, expand_ref, out_ref):
    sums = []
    for frame, grad_ref in enumerate((even_ref, odd_ref)):
        active = active_ref[frame * FRAME_ROWS : (frame + 1) * FRAME_ROWS, :]
        sums.append(jnp.sum(grad_ref[...].astype(jnp.float32) * active, axis=0, keepdims=True))
    excite = excite_ref[...]
    inner = jnp.concatenate(sums, axis=0) * excite * (1.0 - excite)
    out_ref[...] = contract_exact(inner, expand_ref[...].astype(jnp.float32))


def conv_grad_kernel(
    width, even_ref, odd_ref, slope_ref, excite_ref, sq_ref, relaxed_ref, squeeze_ref, *refs
):
    *dense_refs, out_ref, flat_ref, wide_ref, shift_ref, grad_ref = refs
    frames, _, chans = out_ref.shape
    rows = frames * FRAME_ROWS
    grad_squeezed = relaxed_ref[...] * silu_slope(sq_ref[...])
    pooled = jnp.dot(
        grad_squeezed, squeeze_ref[...].astype(jnp.float32), precision=lax.Precision.HIGHEST
    ) * (1.0 / (SIDE * SIDE))
    wide_ref[0:EDGE, :] = jnp.zeros((EDGE, chans), jnp.float32)
    wide_ref[EDGE + rows :, :] = jnp.zeros((EDGE, chans), jnp.float32)
    for frame, source in enumerate((even_ref, odd_ref)):
        at = frame * FRAME_ROWS
        grad = source[...].astype(jnp.float32)
        grad_ref[at : at + FRAME_ROWS, :] = grad
        active = grad * excite_ref[frame : frame + 1, :] + pooled[frame : frame + 1]
        slope = slope_ref[at : at + FRAME_ROWS, :]
        wide_ref[EDGE + at : EDGE + at + FRAME_ROWS, :] = active * slope
    store_shifts(wide_ref, shift_ref, -1)
    body = rows - 2 * WIDE
    for block, dense_ref in zip(channel_blocks(chans, width), dense_refs):
        _, _, start, end = block
        total = jnp.zeros((body, end - start), jnp.float32)
        for tap in range(9):
            down, across = divmod(tap, 3)
            at = (2 - down) * WIDE
            source = shift_ref[across, at : at + body, start:end]
            total += jnp.dot(source, dense_ref[tap], preferred_element_type=jnp.float32)
        grad_ref[WIDE : WIDE + body, start:end] += total
    for frame in range(frames):
        for y in range(SIDE):
            at = frame * FRAME_ROWS + (y + 1) * WIDE + 1
            flat_ref[y * SIDE : (y + 1) * SIDE, :] = grad_ref[at : at + SIDE, :]
        out_ref[frame] = flat_ref[...].astype(jnp.bfloat16)


def dense_kernel(group_ref, *dense_refs):
    width, chans = group_ref.shape[1:]
    for block, dense_ref in zip(channel_blocks(chans, width), dense_refs):
        spread, same = block_tools(block, width)
        for tap in range(9):
            dense_ref[tap] = dense_tap(group_ref, tap, block, spread, same)


def dense_weights(group_kernel):
    _, width, chans = group_kernel.shape
    sizes = [end - start for _, _, start, end in channel_blocks(chans, width)]
    return whole_call(dense_kernel, tuple(bf16(9, size, size) for size in sizes), [])(group_kernel)


def f32(*shape):
    return jax.ShapeDtypeStruct(shape, jnp.float32)


def bf16(*shape):
    return jax.ShapeDtypeStruct(shape, jnp.bfloat16)


def conv_forward(features, group_kernel, squeeze_in):
    frames, cells, chans = features.shape
    rows = frames * FRAME_ROWS
    return whole_call(
        conv_kernel,
        (f32(rows, chans), bf16(rows, chans), f32(frames, squeeze_in.shape[0])),
        [
            pltpu.VMEM((cells, chans), jnp.float32),
            pltpu.VMEM((rows + 2 * EDGE, chans), jnp.float32),
            pltpu.VMEM((3, rows, chans), jnp.bfloat16),
        ],
    )(features, group_kernel, squeeze_in)


def hidden_frames(conv, padded, squeezed, squeeze_out):
    rows, chans = conv.shape
    return whole_call(
        hidden_kernel,
        (bf16(FRAME_ROWS, chans),) * 2
        + (f32(rows // FRAME_ROWS, chans), f32(rows, chans), f32(rows, chans)),
        [],
    )(conv, padded, squeezed, squeeze_out)


def vmem_specs(count):
    return [pl.BlockSpec(memory_space=pltpu.SMEM)] + [pl.BlockSpec(memory_space=pltpu.VMEM)] * count


def facts_of(frame_clip, clip_keep):
    smem = pl.BlockSpec(memory_space=pltpu.SMEM)
    return pl.pallas_call(
        facts_kernel,
        out_shape=jax.ShapeDtypeStruct((4,), jnp.int32),
        in_specs=[smem, smem],
        out_specs=smem,
        cost_estimate=FREE,
    )(frame_clip, clip_keep)


def order_rows(facts, own, mate, unit):
    rows, columns = own.shape
    return pl.pallas_call(
        functools.partial(order_kernel, unit),
        out_shape=bf16(2 * rows, columns),
        in_specs=vmem_specs(2),
        compiler_params=pltpu.CompilerParams(vmem_limit_bytes=VMEM_BYTES),
        cost_estimate=FREE,
    )(facts, own, mate)


def take_patches(facts, halo, even):
    chans = even.shape[1]
    return pl.pallas_call(
        patch_kernel,
        out_shape=bf16(OUT_SIDE * OUT_SIDE, 8 * chans),
        in_specs=vmem_specs(2),
        compiler_params=pltpu.CompilerParams(vmem_limit_bytes=VMEM_BYTES),
        cost_estimate=FREE,
    )(facts, halo, even)


def return_patches(facts, own, mate, chans, dtype):
    return pl.pallas_call(
        unpatch_kernel,
        out_shape=jax.ShapeDtypeStruct((FRAME_ROWS, chans), dtype),
        in_specs=vmem_specs(2),
        compiler_params=pltpu.CompilerParams(vmem_limit_bytes=VMEM_BYTES),
        cost_estimate=FREE,
    )(facts, own, mate)


def excite_grad(even, odd, active, excite, squeeze_out):
    rows, chans = active.shape
    return whole_call(
        excite_grad_kernel,
        f32(rows // FRAME_ROWS, squeeze_out.shape[0]),
        [],
    )(even, odd, active, excite, squeeze_out)


def conv_backward(even, odd, slope, excite, squeezed, grad_relaxed, squeeze_in, dense, width):
    rows, chans = slope.shape
    frames = rows // FRAME_ROWS
    return whole_call(
        functools.partial(conv_grad_kernel, width),
        bf16(frames, SIDE * SIDE, chans),
        [
            pltpu.VMEM((SIDE * SIDE, chans), jnp.float32),
            pltpu.VMEM((rows + 2 * EDGE, chans), jnp.float32),
            pltpu.VMEM((3, rows, chans), jnp.bfloat16),
            pltpu.VMEM((rows, chans), jnp.float32),
        ],
        pl.CostEstimate(flops=rows * chans * 9216, bytes_accessed=16 * rows * chans, transcendentals=0),
    )(even, odd, slope, excite, squeezed, grad_relaxed, squeeze_in, *dense)


def shifted(value, axis, by):
    count = lax.axis_size(axis)
    pairs = [(i, i + by) for i in range(count) if 0 <= i + by < count]
    return lax.ppermute(value, axis, pairs)


def ring_order(chips):
    return list(range(0, chips, 2)) + list(range(1, chips, 2))[::-1]


def ring_pairs(count, by):
    order = ring_order(count // 2)
    pairs = []
    for place, chip in enumerate(order):
        target = order[(place + by) % len(order)]
        pairs += [(2 * chip, 2 * target), (2 * chip + 1, 2 * target + 1)]
    return pairs


def swap_cores(value):
    return lax.ppermute(value, "ctx", [(i, i ^ 1) for i in range(lax.axis_size("ctx"))])


def tp_terms(value):
    size = lax.axis_size("tp")
    reach, other = 1, None
    while reach < size:
        value = value if other is None else value + other
        other = lax.ppermute(value, "tp", [(i, i ^ reach) for i in range(size)])
        reach *= 2
    return value, jnp.zeros_like(value) if other is None else other


def sum_tp(value):
    value, other = tp_terms(value)
    return value + other


def ring_step(blocks):
    count = lax.axis_size("ctx")
    onward, backward = ring_pairs(count, 1), ring_pairs(count, -1)
    up_s, up_r, down_s, down_r = blocks
    send = lambda value, pairs: None if value is None else lax.ppermute(value, "ctx", pairs)
    up_r, down_r = send(up_r, onward), send(down_r, backward)
    up_s, down_s = send(up_s, onward), send(down_s, backward)
    return up_s, up_r, down_s, down_r


def tie(*values):
    return lax.optimization_barrier(values)


def sums_kernel(count, patch_ref, keep_ref, send_ref, *refs):
    *blocks, out_ref = refs
    products = [contract_last(patch_ref[...], ref[...]) for ref in blocks[:count]]
    back = jnp.concatenate([keep_ref[...], send_ref[...]], axis=0)
    products += [contract_last(back, ref[...]) for ref in blocks[count:]]
    out_ref[...] = jnp.concatenate(products, axis=1)


def totals_kernel(count, unit, lanes, backward, first, facts_ref, *refs):
    sums = refs[0][...] + refs[1][...]
    blocks, refs = refs[2 : 2 + count], refs[2 + count :]
    before, after = refs[:-2], refs[-2:]
    rows, depth = sums.shape[0], sums.shape[1] // 2
    pre, grad_act = sums[:, :depth], sums[:, depth:]
    core = facts_ref[0]
    block, token = token_place(lax.broadcasted_iota(jnp.int32, (rows, 1), 0), core, unit)
    live = (token < jnp.where(block == 0, facts_ref[1], facts_ref[2])).astype(jnp.float32)
    factor = grad_act * silu_slope(pre) if backward else pre * jax.nn.sigmoid(pre)
    factor = (factor * live).astype(jnp.bfloat16)
    if backward:
        matrix = reorder_matrix(core, unit, False)
        factor = jnp.dot(matrix, factor, preferred_element_type=jnp.float32).astype(jnp.bfloat16)
    width = depth // count
    total = 0.0
    for place, ref in enumerate(blocks):
        piece = factor[:, place * width : (place + 1) * width]
        total += jnp.dot(piece, ref[:, lanes], preferred_element_type=jnp.float32)
    for half, ref in enumerate(after):
        value = total[half * rows // 2 : (half + 1) * rows // 2]
        value = value if first else before[half][...] + value
        ref[...] = value.astype(ref.dtype)


def partial_sums(patches, back, samplers, readouts):
    count, width = len(samplers), samplers[0].shape[0]
    return whole_call(
        functools.partial(sums_kernel, count), f32(patches.shape[0], 2 * count * width), []
    )(patches, *back, *samplers, *readouts)


def add_products(facts, sums, blocks, before, unit, lanes, backward, last):
    rows, columns = sums[0].shape[0] // 2, lanes.stop - lanes.start
    kernel = functools.partial(totals_kernel, len(blocks), unit, lanes, backward, not before)
    operands = (*sums, *blocks, *before)
    return pl.pallas_call(
        kernel,
        out_shape=(f32(rows, columns), (bf16 if last else f32)(rows, columns)),
        in_specs=vmem_specs(len(operands)),
        compiler_params=pltpu.CompilerParams(vmem_limit_bytes=VMEM_BYTES),
        cost_estimate=FREE,
    )(facts, *operands)


def chips_exchange(value):
    count = lax.axis_size("ctx")
    groups = [list(range(core, count, 2)) for core in range(2)]
    return lax.all_to_all(
        value, "ctx", split_axis=0, concat_axis=0, tiled=True, axis_index_groups=groups
    )


def per_device(
    features,
    group_kernel,
    squeeze_in,
    squeeze_out,
    sampler_kernel,
    readout_kernel,
    frame_clip,
    clip_keep,
    token_cotangent,
):
    chans, width = features.shape[2], group_kernel.shape[2]
    count = lax.axis_size("ctx")
    steps, unit = count // 4, OUT_SIDE * OUT_SIDE // count
    flat_sampler = sampler_kernel.reshape(sampler_kernel.shape[0], 8 * chans)
    blocks = ring_step((flat_sampler, readout_kernel) * 2)
    group_kernel = jnp.swapaxes(group_kernel, 1, 2)
    squeeze_in = squeeze_in.T
    facts = facts_of(frame_clip, clip_keep)

    conv, padded, squeezed = conv_forward(features, group_kernel, squeeze_in)
    token_cotangent, squeezed = tie(token_cotangent, squeezed)
    back = chips_exchange(token_cotangent)
    squeezed = sum_tp(squeezed)
    even, odd, excite, active, slope = hidden_frames(conv, padded, squeezed, squeeze_out)
    halo = shifted(odd, "ctx", 1)

    every = slice(0, readout_kernel.shape[1])
    halo_lanes, even_lanes = slice(0, 4 * chans), slice(4 * chans, 8 * chans)
    samplers, readouts = [flat_sampler], [readout_kernel]
    tokens = halo_grads = even_grads = ()
    for step in range(1, steps + 1):
        if step == 1:
            *blocks, halo, even = tie(*blocks, halo, even)
        if step == 2:
            up_s, up_r, down_s, down_r = blocks
            halo, up_s, down_s = tie(halo, up_s, down_s)
            blocks = up_s, up_r, down_s, down_r
            patches = take_patches(facts, halo, even)
            patches = order_rows(facts, patches, swap_cores(patches), unit)
            back = (back, swap_cores(back))
        here = blocks
        if step < steps:
            if step == steps - 1:
                held = *tokens, *halo_grads, *even_grads
                *held, up_s, up_r, down_s, down_r, group_kernel = tie(*held, *here, group_kernel)
                tokens, halo_grads, even_grads = held[:2], held[2:4], held[4:]
                dense = dense_weights(group_kernel)
                here = up_s, up_r, down_s, down_r
            samplers, readouts = samplers + [here[0], here[2]], readouts + [here[1], here[3]]
            if step == steps - 1:
                here = up_s, None, None, down_r
            blocks = ring_step(here)
        else:
            held = *tokens, *halo_grads, *even_grads, *dense
            last_s, last_r, *held = tie(here[0], here[3], *held)
            tokens, halo_grads, even_grads, dense = held[:2], held[2:4], held[4:6], held[6:]
            samplers, readouts = samplers + [last_s], readouts + [last_r]
        if step >= steps - 2:
            last = step == steps
            sums = tp_terms(partial_sums(patches, back, samplers, readouts))
            halo_grads = add_products(
                facts, sums, samplers, halo_grads, unit, halo_lanes, True, last
            )
            if last:
                sums, halo_grads = list(sums), list(halo_grads)
                sums[0], halo_grads[1] = tie(sums[0], halo_grads[1])
            even_grads = add_products(
                facts, sums, samplers, even_grads, unit, even_lanes, True, last
            )
            tokens = add_products(facts, sums, readouts, tokens, unit, every, False, last)
            samplers, readouts = [], []
    halo_mate = swap_cores(halo_grads[1])
    halo_own, even_own, token_keep = tie(halo_grads[0], even_grads[0], tokens[0])
    lead = return_patches(facts, halo_own, halo_mate, chans, jnp.bfloat16)
    grad_odd = shifted(lead, "ctx", -1)
    grad_even = return_patches(
        facts, even_own, swap_cores(even_grads[1]), chans, jnp.float32
    )
    tokens = (token_keep + swap_cores(tokens[1]).astype(jnp.float32)).astype(jnp.bfloat16)
    tokens, grad_odd = tie(tokens, grad_odd)
    llm_tokens = chips_exchange(tokens)
    grad_relaxed = sum_tp(excite_grad(grad_even, grad_odd, active, excite, squeeze_out))
    grad_features = conv_backward(
        grad_even, grad_odd, slope, excite, squeezed, grad_relaxed, squeeze_in, dense, width
    )
    return (llm_tokens, grad_features)


def solution(mesh):
    placed = (
        P("ctx", None, "tp"),
        P(None, "tp", None),
        P("tp", None),
        P(None, "tp"),
        P("ctx", None, "tp"),
        P("ctx", "tp"),
        P(),
        P(),
        P("ctx", "tp"),
    )
    return jax.shard_map(
        per_device,
        mesh=mesh,
        in_specs=placed,
        out_specs=(P("ctx", "tp"), P("ctx", None, "tp")),
        check_vma=False,
    )
```

```python
import functools

import jax
import jax.numpy as jnp
from jax import lax
from jax.experimental import pallas as pl
from jax.experimental.pallas import tpu as pltpu
from jax.sharding import PartitionSpec as P

SIDE = 14
OUT_SIDE = 8
WIDE = 16
FRAME_ROWS = WIDE * WIDE
EDGE = 8
LANES = 128
VMEM_BYTES = 16 * 2**20
FREE = pl.CostEstimate(flops=0, bytes_accessed=0, transcendentals=0)


def whole_call(kernel, outs, scratch, cost=FREE):
    return pl.pallas_call(
        kernel,
        out_shape=outs,
        scratch_shapes=scratch,
        compiler_params=pltpu.CompilerParams(vmem_limit_bytes=VMEM_BYTES),
        cost_estimate=cost,
    )


def contract_last(left, right):
    return lax.dot_general(
        left, right, (((1,), (1,)), ((), ())), preferred_element_type=jnp.float32
    )


def contract_exact(left, right):
    return lax.dot_general(
        left,
        right,
        (((1,), (1,)), ((), ())),
        precision=lax.Precision.HIGHEST,
        preferred_element_type=jnp.float32,
    )


def silu_slope(values):
    sigma = jax.nn.sigmoid(values)
    return sigma * (1.0 + values * (1.0 - sigma))


def inside(rows):
    row = lax.broadcasted_iota(jnp.int32, (rows, 1), 0)
    across, down = row & (WIDE - 1), (row // WIDE) & (WIDE - 1)
    good = (across >= 1) & (across <= SIDE) & (down >= 1) & (down <= SIDE)
    return good.astype(jnp.float32)


def channel_blocks(chans, width):
    span = 4 * width
    blocks = []
    for low in range(0, chans, span):
        high = min(chans, low + span)
        blocks.append((low, high, low // LANES * LANES, min(chans, -(-high // LANES) * LANES)))
    return blocks


def block_tools(block, width):
    low, high, start, end = block
    size = end - start
    out_row = lax.broadcasted_iota(jnp.int32, (size, width), 0) + start
    within = lax.broadcasted_iota(jnp.int32, (size, width), 1)
    lane = lax.broadcasted_iota(jnp.int32, (size, size), 1) + start
    row = lax.broadcasted_iota(jnp.int32, (size, size), 0) + start
    spread = jnp.zeros((size, width), jnp.float32)
    same = jnp.zeros((size, size), jnp.float32)
    for first in range(low, high, width):
        spread += (out_row == within + first).astype(jnp.float32)
        in_lane = (lane >= first) & (lane < first + width)
        in_row = (row >= first) & (row < first + width)
        same += (in_lane & in_row).astype(jnp.float32)
    return spread.astype(jnp.bfloat16), same


def dense_tap(group_ref, tap, block, spread, same):
    _, _, start, end = block
    full = jnp.dot(spread, group_ref[tap, :, start:end], preferred_element_type=jnp.float32)
    return (full * same).astype(jnp.bfloat16)


def store_shifts(wide_ref, shift_ref, sign):
    rows = shift_ref.shape[1]
    for col in range(3):
        at = EDGE + sign * (col - 1)
        shift_ref[col] = wide_ref[at : at + rows, :].astype(jnp.bfloat16)


def conv_kernel(feat_ref, group_ref, squeeze_ref, *refs):
    conv_ref, pad_ref, sq_ref, flat_ref, wide_ref, shift_ref = refs
    frames, _, chans = feat_ref.shape
    width = group_ref.shape[1]
    rows = frames * FRAME_ROWS
    wide_ref[...] = jnp.zeros_like(wide_ref)
    for frame in range(frames):
        flat_ref[...] = feat_ref[frame].astype(jnp.float32)
        for y in range(SIDE):
            at = EDGE + frame * FRAME_ROWS + (y + 1) * WIDE + 1
            wide_ref[at : at + SIDE, :] = flat_ref[y * SIDE : (y + 1) * SIDE, :]
    store_shifts(wide_ref, shift_ref, 1)
    pad_ref[...] = shift_ref[1]
    conv_ref[...] = jnp.zeros_like(conv_ref)
    body = rows - 2 * WIDE
    for block in channel_blocks(chans, width):
        _, _, start, end = block
        spread, same = block_tools(block, width)
        total = jnp.zeros((body, end - start), jnp.float32)
        for tap in range(9):
            down, across = divmod(tap, 3)
            weights = dense_tap(group_ref, tap, block, spread, same)
            source = shift_ref[across, down * WIDE : down * WIDE + body, start:end]
            total += contract_last(source, weights)
        conv_ref[WIDE : WIDE + body, start:end] += total
    conv = conv_ref[...] * inside(rows)
    conv_ref[...] = conv
    active = conv * jax.nn.sigmoid(conv)
    pooled = jnp.concatenate(
        [
            jnp.sum(active[f * FRAME_ROWS : (f + 1) * FRAME_ROWS], axis=0, keepdims=True)
            for f in range(frames)
        ],
        axis=0,
    ) * (1.0 / (SIDE * SIDE))
    sq_ref[...] = contract_exact(pooled, squeeze_ref[...].astype(jnp.float32))


def hidden_kernel(
    conv_ref, pad_ref, sq_ref, expand_ref, even_ref, odd_ref, excite_ref, active_ref, slope_ref
):
    squeezed = sq_ref[...]
    relaxed = squeezed * jax.nn.sigmoid(squeezed)
    excite = jax.nn.sigmoid(
        jnp.dot(relaxed, expand_ref[...].astype(jnp.float32), precision=lax.Precision.HIGHEST)
    )
    excite_ref[...] = excite
    good = inside(FRAME_ROWS)
    for frame, out_ref in enumerate((even_ref, odd_ref)):
        rows = slice(frame * FRAME_ROWS, (frame + 1) * FRAME_ROWS)
        conv = conv_ref[rows, :]
        sigma = jax.nn.sigmoid(conv)
        active = conv * sigma
        active_ref[rows, :] = active
        slope_ref[rows, :] = sigma * (1.0 + conv * (1.0 - sigma)) * good
        hidden = pad_ref[rows, :].astype(jnp.float32) + active * excite[frame : frame + 1]
        out_ref[...] = hidden.astype(jnp.bfloat16)


def select_rows(to_patches):
    shape = (FRAME_ROWS, FRAME_ROWS)
    out_row = lax.broadcasted_iota(jnp.int32, shape, 0)
    in_row = lax.broadcasted_iota(jnp.int32, shape, 1)
    patch_row, frame_row = (out_row, in_row) if to_patches else (in_row, out_row)
    down, across = patch_row >> 7, (patch_row >> 6) & 1
    a, b = (patch_row >> 3) & 7, patch_row & 7
    return ((2 * a + down) * WIDE + 2 * b + across == frame_row).astype(jnp.float32)


def facts_kernel(clip_ref, keep_ref, out_ref):
    shard = lax.axis_index("ctx")
    frames = clip_ref.shape[0]
    out_ref[0] = shard % 2
    for block in range(2):
        pair = shard // 2 * 2 + block
        clip = clip_ref[2 * pair]
        start = jnp.int32(0)
        for other in range(0, frames, 2):
            start += jnp.where(clip_ref[other] < clip, 1, 0)
        out_ref[1 + block] = keep_ref[clip] - (pair - start) * (OUT_SIDE * OUT_SIDE)
    before = clip_ref[jnp.maximum(2 * shard - 1, 0)]
    chip, chips = shard // 2, lax.axis_size("ctx") // 2
    out_ref[4] = jnp.where(chip % 2 == 0, chip // 2, chips - 1 - chip // 2)
    out_ref[3] = jnp.where((shard > 0) & (before == clip_ref[2 * shard]), 1, 0)


def token_place(row, core, unit):
    per_block = OUT_SIDE * OUT_SIDE
    within = row % per_block
    block = (within // unit) % 2
    target_core = jnp.where(row < per_block, core, 1 - core)
    return block, unit * (2 * (within // (2 * unit)) + target_core) + within % unit


def reorder_matrix(core, unit, to_sent):
    shape = (2 * OUT_SIDE * OUT_SIDE,) * 2
    out_row = lax.broadcasted_iota(jnp.int32, shape, 0)
    in_row = lax.broadcasted_iota(jnp.int32, shape, 1)
    sent, natural = (out_row, in_row) if to_sent else (in_row, out_row)
    block, token = token_place(sent, core, unit)
    source = jnp.where(block == core, 0, OUT_SIDE * OUT_SIDE) + token
    return (source == natural).astype(jnp.bfloat16)


def order_kernel(unit, facts_ref, own_ref, mate_ref, out_ref):
    rows = jnp.concatenate([own_ref[...], mate_ref[...]], axis=0)
    matrix = reorder_matrix(facts_ref[0], unit, True)
    out_ref[...] = jnp.dot(matrix, rows, preferred_element_type=jnp.float32).astype(jnp.bfloat16)


def patch_kernel(facts_ref, halo_ref, even_ref, out_ref):
    chans = halo_ref.shape[1]
    per_frame = OUT_SIDE * OUT_SIDE
    select = select_rows(True).astype(jnp.bfloat16)
    for frame, source in enumerate((halo_ref, even_ref)):
        rows = jnp.dot(select, source[...], preferred_element_type=jnp.float32)
        if frame == 0:
            rows = rows * facts_ref[3].astype(jnp.float32)
        rows = rows.astype(jnp.bfloat16)
        for tap in range(4):
            at = (frame * 4 + tap) * chans
            out_ref[:, at : at + chans] = rows[tap * per_frame : (tap + 1) * per_frame]


def unpatch_kernel(facts_ref, own_ref, mate_ref, out_ref, facts_out_ref):
    for place in range(facts_ref.shape[0]):
        facts_out_ref[place] = facts_ref[place]
    chans = out_ref.shape[1]
    rows = own_ref[...] + mate_ref[...].astype(jnp.float32)
    pieces = [rows[:, tap * chans : (tap + 1) * chans] for tap in range(4)]
    frame = jnp.dot(
        select_rows(False), jnp.concatenate(pieces, axis=0), precision=lax.Precision.HIGHEST
    ) * inside(FRAME_ROWS)
    if out_ref.dtype == jnp.bfloat16:
        frame = frame * facts_ref[3].astype(jnp.float32)
    out_ref[...] = frame.astype(out_ref.dtype)


def excite_grad_kernel(even_ref, odd_ref, active_ref, excite_ref, expand_ref, out_ref):
    sums = []
    for frame, grad_ref in enumerate((even_ref, odd_ref)):
        active = active_ref[frame * FRAME_ROWS : (frame + 1) * FRAME_ROWS, :]
        sums.append(jnp.sum(grad_ref[...].astype(jnp.float32) * active, axis=0, keepdims=True))
    excite = excite_ref[...]
    inner = jnp.concatenate(sums, axis=0) * excite * (1.0 - excite)
    out_ref[...] = contract_exact(inner, expand_ref[...].astype(jnp.float32))


def conv_grad_kernel(
    width, even_ref, odd_ref, slope_ref, excite_ref, sq_ref, relaxed_ref, squeeze_ref, *refs
):
    *dense_refs, out_ref, flat_ref, wide_ref, shift_ref, grad_ref = refs
    frames, _, chans = out_ref.shape
    rows = frames * FRAME_ROWS
    grad_squeezed = relaxed_ref[...] * silu_slope(sq_ref[...])
    pooled = jnp.dot(
        grad_squeezed, squeeze_ref[...].astype(jnp.float32), precision=lax.Precision.HIGHEST
    ) * (1.0 / (SIDE * SIDE))
    wide_ref[0:EDGE, :] = jnp.zeros((EDGE, chans), jnp.float32)
    wide_ref[EDGE + rows :, :] = jnp.zeros((EDGE, chans), jnp.float32)
    for frame, source in enumerate((even_ref, odd_ref)):
        at = frame * FRAME_ROWS
        grad = source[...].astype(jnp.float32)
        grad_ref[at : at + FRAME_ROWS, :] = grad
        active = grad * excite_ref[frame : frame + 1, :] + pooled[frame : frame + 1]
        slope = slope_ref[at : at + FRAME_ROWS, :]
        wide_ref[EDGE + at : EDGE + at + FRAME_ROWS, :] = active * slope
    store_shifts(wide_ref, shift_ref, -1)
    body = rows - 2 * WIDE
    for block, dense_ref in zip(channel_blocks(chans, width), dense_refs):
        _, _, start, end = block
        total = jnp.zeros((body, end - start), jnp.float32)
        for tap in range(9):
            down, across = divmod(tap, 3)
            at = (2 - down) * WIDE
            source = shift_ref[across, at : at + body, start:end]
            total += jnp.dot(source, dense_ref[tap], preferred_element_type=jnp.float32)
        grad_ref[WIDE : WIDE + body, start:end] += total
    for frame in range(frames):
        for y in range(SIDE):
            at = frame * FRAME_ROWS + (y + 1) * WIDE + 1
            flat_ref[y * SIDE : (y + 1) * SIDE, :] = grad_ref[at : at + SIDE, :]
        out_ref[frame] = flat_ref[...].astype(jnp.bfloat16)


def dense_kernel(group_ref, *dense_refs):
    width, chans = group_ref.shape[1:]
    for block, dense_ref in zip(channel_blocks(chans, width), dense_refs):
        spread, same = block_tools(block, width)
        for tap in range(9):
            dense_ref[tap] = dense_tap(group_ref, tap, block, spread, same)


def dense_weights(group_kernel):
    _, width, chans = group_kernel.shape
    sizes = [end - start for _, _, start, end in channel_blocks(chans, width)]
    return whole_call(dense_kernel, tuple(bf16(9, size, size) for size in sizes), [])(group_kernel)


def f32(*shape):
    return jax.ShapeDtypeStruct(shape, jnp.float32)


def bf16(*shape):
    return jax.ShapeDtypeStruct(shape, jnp.bfloat16)


def conv_forward(features, group_kernel, squeeze_in):
    frames, cells, chans = features.shape
    rows = frames * FRAME_ROWS
    return whole_call(
        conv_kernel,
        (f32(rows, chans), bf16(rows, chans), f32(frames, squeeze_in.shape[0])),
        [
            pltpu.VMEM((cells, chans), jnp.float32),
            pltpu.VMEM((rows + 2 * EDGE, chans), jnp.float32),
            pltpu.VMEM((3, rows, chans), jnp.bfloat16),
        ],
    )(features, group_kernel, squeeze_in)


def hidden_frames(conv, padded, squeezed, squeeze_out):
    rows, chans = conv.shape
    return whole_call(
        hidden_kernel,
        (bf16(FRAME_ROWS, chans),) * 2
        + (f32(rows // FRAME_ROWS, chans), f32(rows, chans), f32(rows, chans)),
        [],
    )(conv, padded, squeezed, squeeze_out)


def vmem_specs(count):
    return [pl.BlockSpec(memory_space=pltpu.SMEM)] + [pl.BlockSpec(memory_space=pltpu.VMEM)] * count


def facts_of(frame_clip, clip_keep):
    smem = pl.BlockSpec(memory_space=pltpu.SMEM)
    return pl.pallas_call(
        facts_kernel,
        out_shape=jax.ShapeDtypeStruct((5,), jnp.int32),
        in_specs=[smem, smem],
        out_specs=smem,
        cost_estimate=FREE,
    )(frame_clip, clip_keep)


def order_rows(facts, own, mate, unit):
    rows, columns = own.shape
    return pl.pallas_call(
        functools.partial(order_kernel, unit),
        out_shape=bf16(2 * rows, columns),
        in_specs=vmem_specs(2),
        compiler_params=pltpu.CompilerParams(vmem_limit_bytes=VMEM_BYTES),
        cost_estimate=FREE,
    )(facts, own, mate)


def take_patches(facts, halo, even):
    chans = even.shape[1]
    return pl.pallas_call(
        patch_kernel,
        out_shape=bf16(OUT_SIDE * OUT_SIDE, 8 * chans),
        in_specs=vmem_specs(2),
        compiler_params=pltpu.CompilerParams(vmem_limit_bytes=VMEM_BYTES),
        cost_estimate=FREE,
    )(facts, halo, even)


def return_patches(facts, own, mate, chans, dtype):
    return pl.pallas_call(
        unpatch_kernel,
        out_shape=(
            jax.ShapeDtypeStruct((FRAME_ROWS, chans), dtype),
            jax.ShapeDtypeStruct(facts.shape, jnp.int32),
        ),
        in_specs=vmem_specs(2),
        out_specs=vmem_specs(1)[::-1],
        compiler_params=pltpu.CompilerParams(vmem_limit_bytes=VMEM_BYTES),
        cost_estimate=FREE,
    )(facts, own, mate)


def excite_grad(even, odd, active, excite, squeeze_out):
    rows, chans = active.shape
    return whole_call(
        excite_grad_kernel,
        f32(rows // FRAME_ROWS, squeeze_out.shape[0]),
        [],
    )(even, odd, active, excite, squeeze_out)


def conv_backward(even, odd, slope, excite, squeezed, grad_relaxed, squeeze_in, dense, width):
    rows, chans = slope.shape
    frames = rows // FRAME_ROWS
    return whole_call(
        functools.partial(conv_grad_kernel, width),
        bf16(frames, SIDE * SIDE, chans),
        [
            pltpu.VMEM((SIDE * SIDE, chans), jnp.float32),
            pltpu.VMEM((rows + 2 * EDGE, chans), jnp.float32),
            pltpu.VMEM((3, rows, chans), jnp.bfloat16),
            pltpu.VMEM((rows, chans), jnp.float32),
        ],
        pl.CostEstimate(flops=rows * chans * 9216, bytes_accessed=16 * rows * chans, transcendentals=0),
    )(even, odd, slope, excite, squeezed, grad_relaxed, squeeze_in, *dense)


def shifted(value, axis, by):
    count = lax.axis_size(axis)
    pairs = [(i, i + by) for i in range(count) if 0 <= i + by < count]
    return lax.ppermute(value, axis, pairs)


def ring_order(chips):
    return list(range(0, chips, 2)) + list(range(1, chips, 2))[::-1]


def ring_pairs(count, by):
    order = ring_order(count // 2)
    pairs = []
    for place, chip in enumerate(order):
        target = order[(place + by) % len(order)]
        pairs += [(2 * chip, 2 * target), (2 * chip + 1, 2 * target + 1)]
    return pairs


def swap_cores(value):
    return lax.ppermute(value, "ctx", [(i, i ^ 1) for i in range(lax.axis_size("ctx"))])


def tp_terms(value):
    size = lax.axis_size("tp")
    reach, other = 1, None
    while reach < size:
        value = value if other is None else value + other
        other = lax.ppermute(value, "tp", [(i, i ^ reach) for i in range(size)])
        reach *= 2
    return value, jnp.zeros_like(value) if other is None else other


def sum_tp(value):
    value, other = tp_terms(value)
    return value + other


def ring_step(blocks):
    count = lax.axis_size("ctx")
    onward, backward = ring_pairs(count, 1), ring_pairs(count, -1)
    up_s, up_r, down_s, down_r = blocks
    send = lambda value, pairs: None if value is None else lax.ppermute(value, "ctx", pairs)
    up_r, down_r = send(up_r, onward), send(down_r, backward)
    up_s, down_s = send(up_s, onward), send(down_s, backward)
    return up_s, up_r, down_s, down_r


def tie(*values):
    return lax.optimization_barrier(values)


def sums_kernel(count, patch_ref, keep_ref, send_ref, *refs):
    *blocks, out_ref = refs
    products = [contract_last(patch_ref[...], ref[...]) for ref in blocks[:count]]
    back = jnp.concatenate([keep_ref[...], send_ref[...]], axis=0)
    products += [contract_last(back, ref[...]) for ref in blocks[count:]]
    out_ref[...] = jnp.concatenate(products, axis=1)


def live_rows(facts_ref, rows, unit):
    block, token = token_place(
        lax.broadcasted_iota(jnp.int32, (rows, 1), 0), facts_ref[0], unit
    )
    return (token < jnp.where(block == 0, facts_ref[1], facts_ref[2])).astype(jnp.float32)


def totals_kernel(count, unit, lanes, first, facts_ref, *refs):
    sums = refs[0][...] + refs[1][...]
    blocks, refs = refs[2 : 2 + count], refs[2 + count :]
    before, after = refs[:-2], refs[-2:]
    rows, depth = sums.shape[0], sums.shape[1] // 2
    factor = sums[:, depth:] * silu_slope(sums[:, :depth]) * live_rows(facts_ref, rows, unit)
    matrix = reorder_matrix(facts_ref[0], unit, False)
    factor = jnp.dot(
        matrix, factor.astype(jnp.bfloat16), preferred_element_type=jnp.float32
    ).astype(jnp.bfloat16)
    width = depth // count
    total = 0.0
    for place, ref in enumerate(blocks):
        piece = factor[:, place * width : (place + 1) * width]
        total += jnp.dot(piece, ref[:, lanes], preferred_element_type=jnp.float32)
    for half, ref in enumerate(after):
        value = total[half * rows // 2 : (half + 1) * rows // 2]
        value = value if first else before[half][...] + value
        ref[...] = value.astype(ref.dtype)


def ring_offsets(chips):
    offsets = [0]
    for step in range(1, chips // 2):
        offsets += [-step, step]
    return offsets + [chips // 2]


def block_columns(facts_ref, offset, chips, width):
    shape = (width, chips * width)
    place = (facts_ref[4] + offset + chips) % chips
    column = lax.broadcasted_iota(jnp.int32, shape, 1)
    return (column == lax.broadcasted_iota(jnp.int32, shape, 0) + place * width).astype(jnp.bfloat16)


def exchange_matrix(core, unit, to_sent):
    per_block = OUT_SIDE * OUT_SIDE
    shape = (2 * per_block,) * 2
    out_row = lax.broadcasted_iota(jnp.int32, shape, 0)
    in_row = lax.broadcasted_iota(jnp.int32, shape, 1)
    sent, kept = (out_row, in_row) if to_sent else (in_row, out_row)
    target_core = (sent // (2 * unit)) % 2
    within = sent // (4 * unit) * (2 * unit) + sent % (2 * unit)
    return (within + jnp.where(target_core == core, 0, per_block) == kept).astype(jnp.bfloat16)


def act_kernel(counts, unit, facts_ref, *refs):
    *terms, out_ref = refs
    rows = terms[0].shape[0]
    live = live_rows(facts_ref, rows, unit)
    chips = sum(counts)
    offsets = iter(ring_offsets(chips))
    total = 0.0
    for group, count in enumerate(counts):
        depth = terms[2 * group].shape[1] // 2
        pre = terms[2 * group][:, :depth] + terms[2 * group + 1][:, :depth]
        act = (pre * jax.nn.sigmoid(pre) * live).astype(jnp.bfloat16)
        width = depth // count
        for place in range(count):
            columns = block_columns(facts_ref, next(offsets), chips, width)
            piece = act[:, place * width : (place + 1) * width]
            total += jnp.dot(piece, columns, preferred_element_type=jnp.float32)
    matrix = exchange_matrix(facts_ref[0], unit, True)
    out_ref[...] = jnp.dot(
        matrix, total.astype(jnp.bfloat16), preferred_element_type=jnp.float32
    ).astype(jnp.bfloat16)


def token_kernel(unit, facts_ref, act_ref, *refs):
    *blocks, keep_ref, send_ref = refs
    chips, width = len(blocks), blocks[0].shape[0]
    matrix = exchange_matrix(facts_ref[0], unit, False)
    act = jnp.dot(matrix, act_ref[...], preferred_element_type=jnp.float32).astype(jnp.bfloat16)
    total = 0.0
    for offset, ref in zip(ring_offsets(chips), blocks):
        columns = block_columns(facts_ref, offset, chips, width)
        piece = contract_last(act, columns).astype(jnp.bfloat16)
        total += jnp.dot(piece, ref[...], preferred_element_type=jnp.float32)
    rows = keep_ref.shape[0]
    keep_ref[...] = total[:rows]
    send_ref[...] = total[rows:].astype(jnp.bfloat16)


def partial_sums(patches, back, samplers, readouts):
    count, width = len(samplers), samplers[0].shape[0]
    return whole_call(
        functools.partial(sums_kernel, count), f32(patches.shape[0], 2 * count * width), []
    )(patches, *back, *samplers, *readouts)


def facts_call(kernel, outs, facts, operands, cost=FREE):
    return pl.pallas_call(
        kernel,
        out_shape=outs,
        in_specs=vmem_specs(len(operands)),
        compiler_params=pltpu.CompilerParams(vmem_limit_bytes=VMEM_BYTES),
        cost_estimate=cost,
    )(facts, *operands)


def add_products(facts, sums, blocks, before, unit, lanes, last):
    rows, columns = sums[0].shape[0] // 2, lanes.stop - lanes.start
    kernel = functools.partial(totals_kernel, len(blocks), unit, lanes, not before)
    outs = f32(rows, columns), (bf16 if last else f32)(rows, columns)
    return facts_call(kernel, outs, facts, (*sums, *blocks, *before))


def act_to_send(facts, groups, counts, unit):
    rows, columns = groups[0][0].shape[0], sum(terms[0].shape[1] // 2 for terms in groups)
    kernel = functools.partial(act_kernel, counts, unit)
    operands = [term for terms in groups for term in terms]
    return facts_call(kernel, bf16(rows, columns), facts, operands)


def token_products(facts, act, readouts, unit):
    rows, columns = act.shape[0] // 2, readouts[0].shape[1]
    kernel = functools.partial(token_kernel, unit)
    outs = f32(rows, columns), bf16(rows, columns)
    cost = pl.CostEstimate(
        flops=40 * act.size * columns, bytes_accessed=2 * act.shape[1] * columns, transcendentals=0
    )
    return facts_call(kernel, outs, facts, (act, *readouts), cost)


def chips_exchange(value):
    count = lax.axis_size("ctx")
    groups = [list(range(core, count, 2)) for core in range(2)]
    return lax.all_to_all(
        value, "ctx", split_axis=0, concat_axis=0, tiled=True, axis_index_groups=groups
    )


def per_device(
    features,
    group_kernel,
    squeeze_in,
    squeeze_out,
    sampler_kernel,
    readout_kernel,
    frame_clip,
    clip_keep,
    token_cotangent,
):
    chans, width = features.shape[2], group_kernel.shape[2]
    count = lax.axis_size("ctx")
    steps, unit = count // 4, OUT_SIDE * OUT_SIDE // count
    flat_sampler = sampler_kernel.reshape(sampler_kernel.shape[0], 8 * chans)
    blocks = ring_step((flat_sampler, readout_kernel) * 2)
    group_kernel = jnp.swapaxes(group_kernel, 1, 2)
    squeeze_in = squeeze_in.T
    facts = facts_of(frame_clip, clip_keep)

    conv, padded, squeezed = conv_forward(features, group_kernel, squeeze_in)
    token_cotangent, squeezed = tie(token_cotangent, squeezed)
    back = chips_exchange(token_cotangent)
    squeezed = sum_tp(squeezed)
    even, odd, excite, active, slope = hidden_frames(conv, padded, squeezed, squeeze_out)
    halo = shifted(odd, "ctx", 1)

    halo_lanes, even_lanes = slice(0, 4 * chans), slice(4 * chans, 8 * chans)
    samplers, readouts = [flat_sampler], [readout_kernel]
    halo_grads = even_grads = ()
    all_readouts, groups, counts = [], [], []
    for step in range(1, steps + 1):
        if step == 1:
            *blocks, halo, even = tie(*blocks, halo, even)
        if step == 2:
            up_s, up_r, down_s, down_r = blocks
            halo, up_s, down_s = tie(halo, up_s, down_s)
            blocks = up_s, up_r, down_s, down_r
            patches = take_patches(facts, halo, even)
            patches = order_rows(facts, patches, swap_cores(patches), unit)
            back = (back, swap_cores(back))
        here, last = blocks, step == steps
        if not last:
            if step == steps - 1:
                held = *halo_grads, *even_grads
                *held, up_s, up_r, down_s, down_r, group_kernel = tie(*held, *here, group_kernel)
                halo_grads, even_grads = held[:2], held[2:]
                dense = dense_weights(group_kernel)
                here = up_s, up_r, down_s, down_r
            samplers, readouts = samplers + [here[0], here[2]], readouts + [here[1], here[3]]
            if step == steps - 1:
                here = up_s, None, None, down_r
            blocks = ring_step(here)
        else:
            held = *halo_grads, *even_grads, *dense
            last_s, last_r, *held = tie(here[0], here[3], *held)
            halo_grads, even_grads, dense = held[:2], held[2:4], held[4:]
            samplers, readouts = samplers + [last_s], readouts + [last_r]
        if step >= steps - 2:
            sums = tp_terms(partial_sums(patches, back, samplers, readouts))
            halo_grads = add_products(facts, sums, samplers, halo_grads, unit, halo_lanes, last)
            if last:
                halo_own, halo_mate = halo_grads
                halo_mate, first_sums = tie(halo_mate, sums[0])
                sums = first_sums, sums[1]
                halo_mate = swap_cores(halo_mate)
                lead, facts_late = return_patches(facts, halo_own, halo_mate, chans, jnp.bfloat16)
                grad_odd = shifted(lead, "ctx", -1)
            even_grads = add_products(facts, sums, samplers, even_grads, unit, even_lanes, last)
            groups, counts = groups + [sums], counts + [len(samplers)]
            all_readouts += readouts
            samplers, readouts = [], []
    act = chips_exchange(act_to_send(facts, groups, counts, unit))
    grad_even, facts_late = return_patches(
        facts_late, even_grads[0], swap_cores(even_grads[1]), chans, jnp.float32
    )
    grad_relaxed = sum_tp(excite_grad(grad_even, grad_odd, active, excite, squeeze_out))
    tokens, send = token_products(facts_late, act, all_readouts, unit)
    llm_tokens = (tokens + swap_cores(send).astype(jnp.float32)).astype(jnp.bfloat16)
    grad_features = conv_backward(
        grad_even, grad_odd, slope, excite, squeezed, grad_relaxed, squeeze_in, dense, width
    )
    return (llm_tokens, grad_features)


def solution(mesh):
    placed = (
        P("ctx", None, "tp"),
        P(None, "tp", None),
        P("tp", None),
        P(None, "tp"),
        P("ctx", None, "tp"),
        P("ctx", "tp"),
        P(),
        P(),
        P("ctx", "tp"),
    )
    return jax.shard_map(
        per_device,
        mesh=mesh,
        in_specs=placed,
        out_specs=(P("ctx", "tp"), P("ctx", None, "tp")),
        check_vma=False,
    )
```

```python
import functools

import jax
import jax.numpy as jnp
from jax import lax
from jax.experimental import pallas as pl
from jax.experimental.pallas import tpu as pltpu
from jax.sharding import PartitionSpec as P

SIDE = 14
OUT_SIDE = 8
WIDE = 16
FRAME_ROWS = WIDE * WIDE
EDGE = 8
LANES = 128
VMEM_BYTES = 16 * 2**20
FREE = pl.CostEstimate(flops=0, bytes_accessed=0, transcendentals=0)


def whole_call(kernel, outs, scratch, cost=FREE):
    return pl.pallas_call(
        kernel,
        out_shape=outs,
        scratch_shapes=scratch,
        compiler_params=pltpu.CompilerParams(vmem_limit_bytes=VMEM_BYTES),
        cost_estimate=cost,
    )


def contract_last(left, right):
    return lax.dot_general(
        left, right, (((1,), (1,)), ((), ())), preferred_element_type=jnp.float32
    )


def contract_exact(left, right):
    return lax.dot_general(
        left,
        right,
        (((1,), (1,)), ((), ())),
        precision=lax.Precision.HIGHEST,
        preferred_element_type=jnp.float32,
    )


def silu_slope(values):
    sigma = jax.nn.sigmoid(values)
    return sigma * (1.0 + values * (1.0 - sigma))


def inside(rows):
    row = lax.broadcasted_iota(jnp.int32, (rows, 1), 0)
    across, down = row & (WIDE - 1), (row // WIDE) & (WIDE - 1)
    good = (across >= 1) & (across <= SIDE) & (down >= 1) & (down <= SIDE)
    return good.astype(jnp.float32)


def channel_blocks(chans, width):
    span = 4 * width
    blocks = []
    for low in range(0, chans, span):
        high = min(chans, low + span)
        blocks.append((low, high, low // LANES * LANES, min(chans, -(-high // LANES) * LANES)))
    return blocks


def block_tools(block, width):
    low, high, start, end = block
    size = end - start
    out_row = lax.broadcasted_iota(jnp.int32, (size, width), 0) + start
    within = lax.broadcasted_iota(jnp.int32, (size, width), 1)
    lane = lax.broadcasted_iota(jnp.int32, (size, size), 1) + start
    row = lax.broadcasted_iota(jnp.int32, (size, size), 0) + start
    spread = jnp.zeros((size, width), jnp.float32)
    same = jnp.zeros((size, size), jnp.float32)
    for first in range(low, high, width):
        spread += (out_row == within + first).astype(jnp.float32)
        in_lane = (lane >= first) & (lane < first + width)
        in_row = (row >= first) & (row < first + width)
        same += (in_lane & in_row).astype(jnp.float32)
    return spread.astype(jnp.bfloat16), same


def dense_tap(group_ref, tap, block, spread, same):
    _, _, start, end = block
    full = jnp.dot(spread, group_ref[tap, :, start:end], preferred_element_type=jnp.float32)
    return (full * same).astype(jnp.bfloat16)


def store_shifts(wide_ref, shift_ref, sign):
    rows = shift_ref.shape[1]
    for col in range(3):
        at = EDGE + sign * (col - 1)
        shift_ref[col] = wide_ref[at : at + rows, :].astype(jnp.bfloat16)


def conv_kernel(feat_ref, group_ref, squeeze_ref, *refs):
    conv_ref, pad_ref, sq_ref, flat_ref, wide_ref, shift_ref = refs
    frames, _, chans = feat_ref.shape
    width = group_ref.shape[1]
    rows = frames * FRAME_ROWS
    wide_ref[...] = jnp.zeros_like(wide_ref)
    for frame in range(frames):
        flat_ref[...] = feat_ref[frame].astype(jnp.float32)
        for y in range(SIDE):
            at = EDGE + frame * FRAME_ROWS + (y + 1) * WIDE + 1
            wide_ref[at : at + SIDE, :] = flat_ref[y * SIDE : (y + 1) * SIDE, :]
    store_shifts(wide_ref, shift_ref, 1)
    pad_ref[...] = shift_ref[1]
    conv_ref[...] = jnp.zeros_like(conv_ref)
    body = rows - 2 * WIDE
    for block in channel_blocks(chans, width):
        _, _, start, end = block
        spread, same = block_tools(block, width)
        total = jnp.zeros((body, end - start), jnp.float32)
        for tap in range(9):
            down, across = divmod(tap, 3)
            weights = dense_tap(group_ref, tap, block, spread, same)
            source = shift_ref[across, down * WIDE : down * WIDE + body, start:end]
            total += contract_last(source, weights)
        conv_ref[WIDE : WIDE + body, start:end] += total
    conv = conv_ref[...] * inside(rows)
    conv_ref[...] = conv
    active = conv * jax.nn.sigmoid(conv)
    pooled = jnp.concatenate(
        [
            jnp.sum(active[f * FRAME_ROWS : (f + 1) * FRAME_ROWS], axis=0, keepdims=True)
            for f in range(frames)
        ],
        axis=0,
    ) * (1.0 / (SIDE * SIDE))
    sq_ref[...] = contract_exact(pooled, squeeze_ref[...].astype(jnp.float32))


def hidden_kernel(
    conv_ref, pad_ref, sq_ref, expand_ref, even_ref, odd_ref, excite_ref, active_ref, slope_ref
):
    squeezed = sq_ref[...]
    relaxed = squeezed * jax.nn.sigmoid(squeezed)
    excite = jax.nn.sigmoid(
        jnp.dot(relaxed, expand_ref[...].astype(jnp.float32), precision=lax.Precision.HIGHEST)
    )
    excite_ref[...] = excite
    good = inside(FRAME_ROWS)
    for frame, out_ref in enumerate((even_ref, odd_ref)):
        rows = slice(frame * FRAME_ROWS, (frame + 1) * FRAME_ROWS)
        conv = conv_ref[rows, :]
        sigma = jax.nn.sigmoid(conv)
        active = conv * sigma
        active_ref[rows, :] = active
        slope_ref[rows, :] = sigma * (1.0 + conv * (1.0 - sigma)) * good
        hidden = pad_ref[rows, :].astype(jnp.float32) + active * excite[frame : frame + 1]
        out_ref[...] = hidden.astype(jnp.bfloat16)


def select_rows(to_patches):
    shape = (FRAME_ROWS, FRAME_ROWS)
    out_row = lax.broadcasted_iota(jnp.int32, shape, 0)
    in_row = lax.broadcasted_iota(jnp.int32, shape, 1)
    patch_row, frame_row = (out_row, in_row) if to_patches else (in_row, out_row)
    down, across = patch_row >> 7, (patch_row >> 6) & 1
    a, b = (patch_row >> 3) & 7, patch_row & 7
    return ((2 * a + down) * WIDE + 2 * b + across == frame_row).astype(jnp.float32)


def facts_kernel(clip_ref, keep_ref, out_ref):
    shard = lax.axis_index("ctx")
    frames = clip_ref.shape[0]
    out_ref[0] = shard % 2
    for block in range(2):
        pair = shard // 2 * 2 + block
        clip = clip_ref[2 * pair]
        start = jnp.int32(0)
        for other in range(0, frames, 2):
            start += jnp.where(clip_ref[other] < clip, 1, 0)
        out_ref[1 + block] = keep_ref[clip] - (pair - start) * (OUT_SIDE * OUT_SIDE)
    before = clip_ref[jnp.maximum(2 * shard - 1, 0)]
    chip, chips = shard // 2, lax.axis_size("ctx") // 2
    out_ref[4] = jnp.where(chip % 2 == 0, chip // 2, chips - 1 - chip // 2)
    out_ref[3] = jnp.where((shard > 0) & (before == clip_ref[2 * shard]), 1, 0)


def token_place(row, core, unit):
    per_block = OUT_SIDE * OUT_SIDE
    within = row % per_block
    block = (within // unit) % 2
    target_core = jnp.where(row < per_block, core, 1 - core)
    return block, unit * (2 * (within // (2 * unit)) + target_core) + within % unit


def reorder_matrix(core, unit, to_sent):
    shape = (2 * OUT_SIDE * OUT_SIDE,) * 2
    out_row = lax.broadcasted_iota(jnp.int32, shape, 0)
    in_row = lax.broadcasted_iota(jnp.int32, shape, 1)
    sent, natural = (out_row, in_row) if to_sent else (in_row, out_row)
    block, token = token_place(sent, core, unit)
    source = jnp.where(block == core, 0, OUT_SIDE * OUT_SIDE) + token
    return (source == natural).astype(jnp.bfloat16)


def order_kernel(unit, facts_ref, own_ref, mate_ref, out_ref):
    rows = jnp.concatenate([own_ref[...], mate_ref[...]], axis=0)
    matrix = reorder_matrix(facts_ref[0], unit, True)
    out_ref[...] = jnp.dot(matrix, rows, preferred_element_type=jnp.float32).astype(jnp.bfloat16)


def patch_kernel(facts_ref, halo_ref, even_ref, out_ref):
    chans = halo_ref.shape[1]
    per_frame = OUT_SIDE * OUT_SIDE
    select = select_rows(True).astype(jnp.bfloat16)
    for frame, source in enumerate((halo_ref, even_ref)):
        rows = jnp.dot(select, source[...], preferred_element_type=jnp.float32)
        if frame == 0:
            rows = rows * facts_ref[3].astype(jnp.float32)
        rows = rows.astype(jnp.bfloat16)
        for tap in range(4):
            at = (frame * 4 + tap) * chans
            out_ref[:, at : at + chans] = rows[tap * per_frame : (tap + 1) * per_frame]


def unpatch_kernel(facts_ref, own_ref, mate_ref, out_ref, facts_out_ref):
    for place in range(facts_ref.shape[0]):
        facts_out_ref[place] = facts_ref[place]
    chans = out_ref.shape[1]
    rows = own_ref[...] + mate_ref[...].astype(jnp.float32)
    pieces = [rows[:, tap * chans : (tap + 1) * chans] for tap in range(4)]
    frame = jnp.dot(
        select_rows(False), jnp.concatenate(pieces, axis=0), precision=lax.Precision.HIGHEST
    ) * inside(FRAME_ROWS)
    if out_ref.dtype == jnp.bfloat16:
        frame = frame * facts_ref[3].astype(jnp.float32)
    out_ref[...] = frame.astype(out_ref.dtype)


def excite_grad_kernel(even_ref, odd_ref, active_ref, excite_ref, expand_ref, out_ref):
    sums = []
    for frame, grad_ref in enumerate((even_ref, odd_ref)):
        active = active_ref[frame * FRAME_ROWS : (frame + 1) * FRAME_ROWS, :]
        sums.append(jnp.sum(grad_ref[...].astype(jnp.float32) * active, axis=0, keepdims=True))
    excite = excite_ref[...]
    inner = jnp.concatenate(sums, axis=0) * excite * (1.0 - excite)
    out_ref[...] = contract_exact(inner, expand_ref[...].astype(jnp.float32))


def conv_grad_kernel(
    width, even_ref, odd_ref, slope_ref, excite_ref, sq_ref, relaxed_ref, squeeze_ref, *refs
):
    *dense_refs, out_ref, flat_ref, wide_ref, shift_ref, grad_ref = refs
    frames, _, chans = out_ref.shape
    rows = frames * FRAME_ROWS
    grad_squeezed = relaxed_ref[...] * silu_slope(sq_ref[...])
    pooled = jnp.dot(
        grad_squeezed, squeeze_ref[...].astype(jnp.float32), precision=lax.Precision.HIGHEST
    ) * (1.0 / (SIDE * SIDE))
    wide_ref[0:EDGE, :] = jnp.zeros((EDGE, chans), jnp.float32)
    wide_ref[EDGE + rows :, :] = jnp.zeros((EDGE, chans), jnp.float32)
    for frame, source in enumerate((even_ref, odd_ref)):
        at = frame * FRAME_ROWS
        grad = source[...].astype(jnp.float32)
        grad_ref[at : at + FRAME_ROWS, :] = grad
        active = grad * excite_ref[frame : frame + 1, :] + pooled[frame : frame + 1]
        slope = slope_ref[at : at + FRAME_ROWS, :]
        wide_ref[EDGE + at : EDGE + at + FRAME_ROWS, :] = active * slope
    store_shifts(wide_ref, shift_ref, -1)
    body = rows - 2 * WIDE
    for block, dense_ref in zip(channel_blocks(chans, width), dense_refs):
        _, _, start, end = block
        total = jnp.zeros((body, end - start), jnp.float32)
        for tap in range(9):
            down, across = divmod(tap, 3)
            at = (2 - down) * WIDE
            source = shift_ref[across, at : at + body, start:end]
            total += jnp.dot(source, dense_ref[tap], preferred_element_type=jnp.float32)
        grad_ref[WIDE : WIDE + body, start:end] += total
    for frame in range(frames):
        for y in range(SIDE):
            at = frame * FRAME_ROWS + (y + 1) * WIDE + 1
            flat_ref[y * SIDE : (y + 1) * SIDE, :] = grad_ref[at : at + SIDE, :]
        out_ref[frame] = flat_ref[...].astype(jnp.bfloat16)


def dense_kernel(group_ref, *dense_refs):
    width, chans = group_ref.shape[1:]
    for block, dense_ref in zip(channel_blocks(chans, width), dense_refs):
        spread, same = block_tools(block, width)
        for tap in range(9):
            dense_ref[tap] = dense_tap(group_ref, tap, block, spread, same)


def dense_weights(group_kernel):
    _, width, chans = group_kernel.shape
    sizes = [end - start for _, _, start, end in channel_blocks(chans, width)]
    return whole_call(dense_kernel, tuple(bf16(9, size, size) for size in sizes), [])(group_kernel)


def f32(*shape):
    return jax.ShapeDtypeStruct(shape, jnp.float32)


def bf16(*shape):
    return jax.ShapeDtypeStruct(shape, jnp.bfloat16)


def conv_forward(features, group_kernel, squeeze_in):
    frames, cells, chans = features.shape
    rows = frames * FRAME_ROWS
    return whole_call(
        conv_kernel,
        (f32(rows, chans), bf16(rows, chans), f32(frames, squeeze_in.shape[0])),
        [
            pltpu.VMEM((cells, chans), jnp.float32),
            pltpu.VMEM((rows + 2 * EDGE, chans), jnp.float32),
            pltpu.VMEM((3, rows, chans), jnp.bfloat16),
        ],
    )(features, group_kernel, squeeze_in)


def hidden_frames(conv, padded, squeezed, squeeze_out):
    rows, chans = conv.shape
    return whole_call(
        hidden_kernel,
        (bf16(FRAME_ROWS, chans),) * 2
        + (f32(rows // FRAME_ROWS, chans), f32(rows, chans), f32(rows, chans)),
        [],
    )(conv, padded, squeezed, squeeze_out)


def vmem_specs(count):
    return [pl.BlockSpec(memory_space=pltpu.SMEM)] + [pl.BlockSpec(memory_space=pltpu.VMEM)] * count


def facts_of(frame_clip, clip_keep):
    smem = pl.BlockSpec(memory_space=pltpu.SMEM)
    return pl.pallas_call(
        facts_kernel,
        out_shape=jax.ShapeDtypeStruct((5,), jnp.int32),
        in_specs=[smem, smem],
        out_specs=smem,
        cost_estimate=FREE,
    )(frame_clip, clip_keep)


def order_rows(facts, own, mate, unit):
    rows, columns = own.shape
    return pl.pallas_call(
        functools.partial(order_kernel, unit),
        out_shape=bf16(2 * rows, columns),
        in_specs=vmem_specs(2),
        compiler_params=pltpu.CompilerParams(vmem_limit_bytes=VMEM_BYTES),
        cost_estimate=FREE,
    )(facts, own, mate)


def take_patches(facts, halo, even):
    chans = even.shape[1]
    return pl.pallas_call(
        patch_kernel,
        out_shape=bf16(OUT_SIDE * OUT_SIDE, 8 * chans),
        in_specs=vmem_specs(2),
        compiler_params=pltpu.CompilerParams(vmem_limit_bytes=VMEM_BYTES),
        cost_estimate=FREE,
    )(facts, halo, even)


def return_patches(facts, own, mate, chans, dtype):
    return pl.pallas_call(
        unpatch_kernel,
        out_shape=(
            jax.ShapeDtypeStruct((FRAME_ROWS, chans), dtype),
            jax.ShapeDtypeStruct(facts.shape, jnp.int32),
        ),
        in_specs=vmem_specs(2),
        out_specs=vmem_specs(1)[::-1],
        compiler_params=pltpu.CompilerParams(vmem_limit_bytes=VMEM_BYTES),
        cost_estimate=FREE,
    )(facts, own, mate)


def excite_grad(even, odd, active, excite, squeeze_out):
    rows, chans = active.shape
    return whole_call(
        excite_grad_kernel,
        f32(rows // FRAME_ROWS, squeeze_out.shape[0]),
        [],
    )(even, odd, active, excite, squeeze_out)


def conv_backward(even, odd, slope, excite, squeezed, grad_relaxed, squeeze_in, dense, width):
    rows, chans = slope.shape
    frames = rows // FRAME_ROWS
    return whole_call(
        functools.partial(conv_grad_kernel, width),
        bf16(frames, SIDE * SIDE, chans),
        [
            pltpu.VMEM((SIDE * SIDE, chans), jnp.float32),
            pltpu.VMEM((rows + 2 * EDGE, chans), jnp.float32),
            pltpu.VMEM((3, rows, chans), jnp.bfloat16),
            pltpu.VMEM((rows, chans), jnp.float32),
        ],
        pl.CostEstimate(flops=rows * chans * 9216, bytes_accessed=16 * rows * chans, transcendentals=0),
    )(even, odd, slope, excite, squeezed, grad_relaxed, squeeze_in, *dense)


def shifted(value, axis, by):
    count = lax.axis_size(axis)
    pairs = [(i, i + by) for i in range(count) if 0 <= i + by < count]
    return lax.ppermute(value, axis, pairs)


def ring_order(chips):
    return list(range(0, chips, 2)) + list(range(1, chips, 2))[::-1]


def ring_pairs(count, by):
    order = ring_order(count // 2)
    pairs = []
    for place, chip in enumerate(order):
        target = order[(place + by) % len(order)]
        pairs += [(2 * chip, 2 * target), (2 * chip + 1, 2 * target + 1)]
    return pairs


def swap_cores(value):
    return lax.ppermute(value, "ctx", [(i, i ^ 1) for i in range(lax.axis_size("ctx"))])


def tp_terms(value):
    size = lax.axis_size("tp")
    reach, other = 1, None
    while reach < size:
        value = value if other is None else value + other
        other = lax.ppermute(value, "tp", [(i, i ^ reach) for i in range(size)])
        reach *= 2
    return value, jnp.zeros_like(value) if other is None else other


def sum_tp(value):
    value, other = tp_terms(value)
    return value + other


def ring_send(value, by):
    return lax.ppermute(value, "ctx", ring_pairs(lax.axis_size("ctx"), by))


def tie(*values):
    return lax.optimization_barrier(values)


def pre_kernel(patch_ref, *refs):
    *blocks, out_ref = refs
    products = [contract_last(patch_ref[...], ref[...]) for ref in blocks]
    out_ref[...] = jnp.concatenate(products, axis=1)


def back_kernel(keep_ref, send_ref, *refs):
    *blocks, out_ref = refs
    back = jnp.concatenate([keep_ref[...], send_ref[...]], axis=0)
    out_ref[...] = jnp.concatenate([contract_last(back, ref[...]) for ref in blocks], axis=1)


def live_rows(facts_ref, rows, unit):
    block, token = token_place(
        lax.broadcasted_iota(jnp.int32, (rows, 1), 0), facts_ref[0], unit
    )
    return (token < jnp.where(block == 0, facts_ref[1], facts_ref[2])).astype(jnp.float32)


def totals_kernel(pieces, unit, lanes, first, facts_ref, *refs):
    grad_act = refs[0][...] + refs[1][...]
    count = len(pieces)
    slopes, blocks = refs[2:4], refs[4 : 4 + count]
    before, after = refs[4 + count : -2], refs[-2:]
    rows, width = grad_act.shape[0], blocks[0].shape[0]
    matrix = reorder_matrix(facts_ref[0], unit, False)
    total = 0.0
    for place, ((source, index), ref) in enumerate(zip(pieces, blocks)):
        piece = grad_act[:, place * width : (place + 1) * width]
        piece = piece * slopes[source][:, index * width : (index + 1) * width]
        piece = jnp.dot(
            matrix, piece.astype(jnp.bfloat16), preferred_element_type=jnp.float32
        ).astype(jnp.bfloat16)
        total += jnp.dot(piece, ref[:, lanes], preferred_element_type=jnp.float32)
    for half, ref in enumerate(after):
        value = total[half * rows // 2 : (half + 1) * rows // 2]
        value = value if first else before[half][...] + value
        ref[...] = value.astype(ref.dtype)


def ring_offsets(chips):
    offsets = [0]
    for step in range(1, chips // 2):
        offsets += [-step, step]
    return offsets + [chips // 2]


def block_columns(facts_ref, offset, chips, width):
    shape = (width, chips * width)
    place = (facts_ref[4] + offset + chips) % chips
    column = lax.broadcasted_iota(jnp.int32, shape, 1)
    return (column == lax.broadcasted_iota(jnp.int32, shape, 0) + place * width).astype(jnp.bfloat16)


def exchange_matrix(core, unit, to_sent):
    per_block = OUT_SIDE * OUT_SIDE
    shape = (2 * per_block,) * 2
    out_row = lax.broadcasted_iota(jnp.int32, shape, 0)
    in_row = lax.broadcasted_iota(jnp.int32, shape, 1)
    sent, kept = (out_row, in_row) if to_sent else (in_row, out_row)
    target_core = (sent // (2 * unit)) % 2
    within = sent // (4 * unit) * (2 * unit) + sent % (2 * unit)
    return (within + jnp.where(target_core == core, 0, per_block) == kept).astype(jnp.bfloat16)


def act_kernel(offsets, chips, unit, last, facts_ref, own_ref, other_ref, *refs):
    *before, slope_ref, out_ref = refs
    pre = own_ref[...] + other_ref[...]
    width = pre.shape[1] // len(offsets)
    live = live_rows(facts_ref, pre.shape[0], unit)
    sigma = jax.nn.sigmoid(pre)
    slope_ref[...] = sigma * (1.0 + pre * (1.0 - sigma)) * live
    act = (pre * sigma * live).astype(jnp.bfloat16)
    total = before[0][...].astype(jnp.float32) if last else 0.0
    for place, offset in enumerate(offsets):
        columns = block_columns(facts_ref, offset, chips, width)
        piece = act[:, place * width : (place + 1) * width]
        total += jnp.dot(piece, columns, preferred_element_type=jnp.float32)
    total = total.astype(jnp.bfloat16)
    if last:
        matrix = exchange_matrix(facts_ref[0], unit, True)
        total = jnp.dot(matrix, total, preferred_element_type=jnp.float32).astype(jnp.bfloat16)
    out_ref[...] = total


def token_kernel(offsets, chips, unit, first, facts_ref, act_ref, *refs):
    count = len(offsets)
    blocks, before, after = refs[:count], refs[count:-2], refs[-2:]
    width = blocks[0].shape[0]
    matrix = exchange_matrix(facts_ref[0], unit, False)
    act = jnp.dot(matrix, act_ref[...], preferred_element_type=jnp.float32).astype(jnp.bfloat16)
    total = 0.0
    for offset, ref in zip(offsets, blocks):
        columns = block_columns(facts_ref, offset, chips, width)
        piece = contract_last(act, columns).astype(jnp.bfloat16)
        total += jnp.dot(piece, ref[...], preferred_element_type=jnp.float32)
    rows = after[0].shape[0]
    for half, ref in enumerate(after):
        value = total[half * rows : (half + 1) * rows]
        value = value if first else before[half][...] + value
        ref[...] = value.astype(ref.dtype)


def block_products(kernel, left, blocks):
    rows = 2 * OUT_SIDE * OUT_SIDE
    return whole_call(kernel, f32(rows, len(blocks) * blocks[0].shape[0]), [])(*left, *blocks)


def facts_call(kernel, outs, facts, operands, cost=FREE):
    return pl.pallas_call(
        kernel,
        out_shape=outs,
        in_specs=vmem_specs(len(operands)),
        compiler_params=pltpu.CompilerParams(vmem_limit_bytes=VMEM_BYTES),
        cost_estimate=cost,
    )(facts, *operands)


def add_gradients(facts, terms, slopes, pieces, blocks, before, unit, lanes, last):
    rows, columns = terms[0].shape[0] // 2, lanes.stop - lanes.start
    kernel = functools.partial(totals_kernel, pieces, unit, lanes, not before)
    outs = f32(rows, columns), (bf16 if last else f32)(rows, columns)
    return facts_call(kernel, outs, facts, (*terms, *slopes, *blocks, *before))


def act_and_slope(facts, terms, offsets, chips, before, unit):
    rows, columns = terms[0].shape
    kernel = functools.partial(act_kernel, offsets, chips, unit, bool(before))
    outs = f32(rows, columns), bf16(rows, columns // len(offsets) * chips)
    return facts_call(kernel, outs, facts, (*terms, *before))


def add_tokens(facts, act, offsets, chips, blocks, before, unit):
    rows, columns = act.shape[0] // 2, blocks[0].shape[1]
    kernel = functools.partial(token_kernel, offsets, chips, unit, not before)
    outs = f32(rows, columns), (bf16 if before else f32)(rows, columns)
    cost = pl.CostEstimate(
        flops=5 * len(blocks) * act.shape[1] * act.shape[0] * columns // chips * 8,
        bytes_accessed=0,
        transcendentals=0,
    )
    return facts_call(kernel, outs, facts, (act, *blocks, *before), cost if before else FREE)


def chips_exchange(value):
    count = lax.axis_size("ctx")
    groups = [list(range(core, count, 2)) for core in range(2)]
    return lax.all_to_all(
        value, "ctx", split_axis=0, concat_axis=0, tiled=True, axis_index_groups=groups
    )


def per_device(
    features,
    group_kernel,
    squeeze_in,
    squeeze_out,
    sampler_kernel,
    readout_kernel,
    frame_clip,
    clip_keep,
    token_cotangent,
):
    chans, width = features.shape[2], group_kernel.shape[2]
    count = lax.axis_size("ctx")
    steps, unit = count // 4, OUT_SIDE * OUT_SIDE // count
    flat_sampler = sampler_kernel.reshape(sampler_kernel.shape[0], 8 * chans)
    chips = count // 2
    s_up, s_down = [ring_send(flat_sampler, 1)], [ring_send(flat_sampler, -1)]
    group_kernel = jnp.swapaxes(group_kernel, 1, 2)
    squeeze_in = squeeze_in.T
    facts = facts_of(frame_clip, clip_keep)

    conv, padded, squeezed = conv_forward(features, group_kernel, squeeze_in)
    token_cotangent, squeezed = tie(token_cotangent, squeezed)
    back = chips_exchange(token_cotangent)
    squeezed = sum_tp(squeezed)
    even, odd, excite, active, slope = hidden_frames(conv, padded, squeezed, squeeze_out)
    halo = shifted(odd, "ctx", 1)

    s_up[0], s_down[0], even = tie(s_up[0], s_down[0], even)
    for step in range(1, steps - 1):
        s_up.append(ring_send(s_up[-1], 1))
        s_down.append(ring_send(s_down[-1], -1))
        if step == 1:
            halo, s_up[1], s_down[1] = tie(halo, s_up[1], s_down[1])
            patches = take_patches(facts, halo, even)
            patches = order_rows(facts, patches, swap_cores(patches), unit)
            back = (back, swap_cores(back))
    s_up[-1], s_down[-1], readout_kernel = tie(s_up[-1], s_down[-1], readout_kernel)
    s_last = ring_send(s_up[-1], 1)
    r_up, r_down = [ring_send(readout_kernel, 1)], [ring_send(readout_kernel, -1)]
    samplers = [flat_sampler] + [block for pair in zip(s_up, s_down) for block in pair]
    offsets = ring_offsets(chips)
    first_pre = block_products(pre_kernel, (patches,), samplers)
    r_up[0], r_down[0], first_pre = tie(r_up[0], r_down[0], first_pre)
    for step in range(1, steps - 2):
        r_up.append(ring_send(r_up[-1], 1))
        r_down.append(ring_send(r_down[-1], -1))
    first_slope, first_act = act_and_slope(
        facts, tp_terms(first_pre), offsets[:-1], chips, (), unit
    )
    last_pre = tp_terms(block_products(pre_kernel, (patches,), [s_last]))
    last_slope, act = act_and_slope(facts, last_pre, offsets[-1:], chips, (first_act,), unit)
    slopes = first_slope, last_slope

    early = [readout_kernel]
    for step in range(steps - 3):
        early += [r_up[step], r_down[step]]
    early_sums = block_products(back_kernel, back, early)
    r_up[-1], early_sums = tie(r_up[-1], early_sums)
    r_up.append(ring_send(r_up[-1], 1))
    r_down.append(ring_send(r_down[-1], -1))
    halo_lanes, even_lanes = slice(0, 4 * chans), slice(4 * chans, 8 * chans)
    index = len(early)
    *middle, act = tie(r_up[steps - 3], r_down[steps - 3], r_down[steps - 2], act)
    act = chips_exchange(act)
    pieces = [(0, place) for place in range(index)]
    terms = tp_terms(early_sums)
    halo_grads = add_gradients(
        facts, terms, slopes, pieces, samplers[:index], (), unit, halo_lanes, False
    )
    even_grads = add_gradients(
        facts, terms, slopes, pieces, samplers[:index], (), unit, even_lanes, False
    )
    r_last = ring_send(r_down[-1], -1)
    held = tie(group_kernel, *middle, *halo_grads, *even_grads)
    group_kernel, middle, halo_grads, even_grads = held[0], held[1:4], held[4:6], held[6:]
    dense = dense_weights(group_kernel)
    pieces = [(0, index), (0, index + 1), (0, index + 3)]
    blocks = [samplers[index], samplers[index + 1], samplers[index + 3]]
    terms = tp_terms(block_products(back_kernel, back, middle))
    halo_grads = add_gradients(
        facts, terms, slopes, pieces, blocks, halo_grads, unit, halo_lanes, False
    )
    even_grads = add_gradients(
        facts, terms, slopes, pieces, blocks, even_grads, unit, even_lanes, False
    )
    places = offsets[: index + 2] + [offsets[index + 3]]
    tokens = add_tokens(facts, act, places, chips, early + list(middle), (), unit)

    held = tie(r_up[-1], r_last, *halo_grads, *even_grads, *dense, *tokens)
    late, halo_grads, even_grads = held[:2], held[2:4], held[4:6]
    dense, tokens = held[6:-2], held[-2:]
    pieces, blocks = [(0, index + 2), (1, 0)], [samplers[index + 2], s_last]
    terms = tp_terms(block_products(back_kernel, back, late))
    halo_own, halo_mate = add_gradients(
        facts, terms, slopes, pieces, blocks, halo_grads, unit, halo_lanes, True
    )
    halo_mate, first_term = tie(halo_mate, terms[0])
    even_own, even_mate = add_gradients(
        facts, (first_term, terms[1]), slopes, pieces, blocks, even_grads, unit, even_lanes, True
    )
    lead, facts_late = return_patches(facts, halo_own, swap_cores(halo_mate), chans, jnp.bfloat16)
    grad_odd = shifted(lead, "ctx", -1)
    grad_even, facts_late = return_patches(
        facts_late, even_own, swap_cores(even_mate), chans, jnp.float32
    )
    grad_relaxed = sum_tp(excite_grad(grad_even, grad_odd, active, excite, squeeze_out))
    places = [offsets[index + 2], offsets[-1]]
    tokens, send = add_tokens(facts_late, act, places, chips, late, tokens, unit)
    llm_tokens = (tokens + swap_cores(send).astype(jnp.float32)).astype(jnp.bfloat16)
    grad_features = conv_backward(
        grad_even, grad_odd, slope, excite, squeezed, grad_relaxed, squeeze_in, dense, width
    )
    return (llm_tokens, grad_features)


def solution(mesh):
    placed = (
        P("ctx", None, "tp"),
        P(None, "tp", None),
        P("tp", None),
        P(None, "tp"),
        P("ctx", None, "tp"),
        P("ctx", "tp"),
        P(),
        P(),
        P("ctx", "tp"),
    )
    return jax.shard_map(
        per_device,
        mesh=mesh,
        in_specs=placed,
        out_specs=(P("ctx", "tp"), P("ctx", None, "tp")),
        check_vma=False,
    )
```

```python
import functools

import jax
import jax.numpy as jnp
from jax import lax
from jax.experimental import pallas as pl
from jax.experimental.pallas import tpu as pltpu
from jax.sharding import PartitionSpec as P

SIDE = 14
OUT_SIDE = 8
WIDE = 16
FRAME_ROWS = WIDE * WIDE
EDGE = 8
LANES = 128
VMEM_BYTES = 16 * 2**20
FREE = pl.CostEstimate(flops=0, bytes_accessed=0, transcendentals=0)


def whole_call(kernel, outs, scratch, cost=FREE):
    return pl.pallas_call(
        kernel,
        out_shape=outs,
        scratch_shapes=scratch,
        compiler_params=pltpu.CompilerParams(vmem_limit_bytes=VMEM_BYTES),
        cost_estimate=cost,
    )


def contract_last(left, right):
    return lax.dot_general(
        left, right, (((1,), (1,)), ((), ())), preferred_element_type=jnp.float32
    )


def contract_exact(left, right):
    return lax.dot_general(
        left,
        right,
        (((1,), (1,)), ((), ())),
        precision=lax.Precision.HIGHEST,
        preferred_element_type=jnp.float32,
    )


def silu_slope(values):
    sigma = jax.nn.sigmoid(values)
    return sigma * (1.0 + values * (1.0 - sigma))


def inside(rows):
    row = lax.broadcasted_iota(jnp.int32, (rows, 1), 0)
    across, down = row & (WIDE - 1), (row // WIDE) & (WIDE - 1)
    good = (across >= 1) & (across <= SIDE) & (down >= 1) & (down <= SIDE)
    return good.astype(jnp.float32)


def channel_blocks(chans, width):
    span = 4 * width
    blocks = []
    for low in range(0, chans, span):
        high = min(chans, low + span)
        blocks.append((low, high, low // LANES * LANES, min(chans, -(-high // LANES) * LANES)))
    return blocks


def block_tools(block, width):
    low, high, start, end = block
    size = end - start
    out_row = lax.broadcasted_iota(jnp.int32, (size, width), 0) + start
    within = lax.broadcasted_iota(jnp.int32, (size, width), 1)
    lane = lax.broadcasted_iota(jnp.int32, (size, size), 1) + start
    row = lax.broadcasted_iota(jnp.int32, (size, size), 0) + start
    spread = jnp.zeros((size, width), jnp.float32)
    same = jnp.zeros((size, size), jnp.float32)
    for first in range(low, high, width):
        spread += (out_row == within + first).astype(jnp.float32)
        in_lane = (lane >= first) & (lane < first + width)
        in_row = (row >= first) & (row < first + width)
        same += (in_lane & in_row).astype(jnp.float32)
    return spread.astype(jnp.bfloat16), same


def dense_tap(group_ref, tap, block, spread, same):
    _, _, start, end = block
    full = jnp.dot(spread, group_ref[tap, :, start:end], preferred_element_type=jnp.float32)
    return (full * same).astype(jnp.bfloat16)


def store_shifts(wide_ref, shift_ref, sign):
    rows = shift_ref.shape[1]
    for col in range(3):
        at = EDGE + sign * (col - 1)
        shift_ref[col] = wide_ref[at : at + rows, :].astype(jnp.bfloat16)


def conv_kernel(feat_ref, group_ref, squeeze_ref, *refs):
    conv_ref, pad_ref, sq_ref, flat_ref, wide_ref, shift_ref = refs
    frames, _, chans = feat_ref.shape
    width = group_ref.shape[1]
    rows = frames * FRAME_ROWS
    wide_ref[...] = jnp.zeros_like(wide_ref)
    for frame in range(frames):
        flat_ref[...] = feat_ref[frame].astype(jnp.float32)
        for y in range(SIDE):
            at = EDGE + frame * FRAME_ROWS + (y + 1) * WIDE + 1
            wide_ref[at : at + SIDE, :] = flat_ref[y * SIDE : (y + 1) * SIDE, :]
    store_shifts(wide_ref, shift_ref, 1)
    pad_ref[...] = shift_ref[1]
    conv_ref[...] = jnp.zeros_like(conv_ref)
    body = rows - 2 * WIDE
    for block in channel_blocks(chans, width):
        _, _, start, end = block
        spread, same = block_tools(block, width)
        total = jnp.zeros((body, end - start), jnp.float32)
        for tap in range(9):
            down, across = divmod(tap, 3)
            weights = dense_tap(group_ref, tap, block, spread, same)
            source = shift_ref[across, down * WIDE : down * WIDE + body, start:end]
            total += contract_last(source, weights)
        conv_ref[WIDE : WIDE + body, start:end] += total
    conv = conv_ref[...] * inside(rows)
    conv_ref[...] = conv
    active = conv * jax.nn.sigmoid(conv)
    pooled = jnp.concatenate(
        [
            jnp.sum(active[f * FRAME_ROWS : (f + 1) * FRAME_ROWS], axis=0, keepdims=True)
            for f in range(frames)
        ],
        axis=0,
    ) * (1.0 / (SIDE * SIDE))
    sq_ref[...] = contract_exact(pooled, squeeze_ref[...].astype(jnp.float32))


def hidden_kernel(conv_ref, pad_ref, sq_ref, expand_ref, even_ref, odd_ref, excite_ref):
    squeezed = sq_ref[...]
    relaxed = squeezed * jax.nn.sigmoid(squeezed)
    excite = jax.nn.sigmoid(
        jnp.dot(relaxed, expand_ref[...].astype(jnp.float32), precision=lax.Precision.HIGHEST)
    )
    excite_ref[...] = excite
    for frame, out_ref in enumerate((even_ref, odd_ref)):
        rows = slice(frame * FRAME_ROWS, (frame + 1) * FRAME_ROWS)
        conv = conv_ref[rows, :]
        active = conv * jax.nn.sigmoid(conv)
        hidden = pad_ref[rows, :].astype(jnp.float32) + active * excite[frame : frame + 1]
        out_ref[...] = hidden.astype(jnp.bfloat16)


def select_rows(to_patches):
    shape = (FRAME_ROWS, FRAME_ROWS)
    out_row = lax.broadcasted_iota(jnp.int32, shape, 0)
    in_row = lax.broadcasted_iota(jnp.int32, shape, 1)
    patch_row, frame_row = (out_row, in_row) if to_patches else (in_row, out_row)
    down, across = patch_row >> 7, (patch_row >> 6) & 1
    a, b = (patch_row >> 3) & 7, patch_row & 7
    return ((2 * a + down) * WIDE + 2 * b + across == frame_row).astype(jnp.float32)


def facts_kernel(clip_ref, keep_ref, out_ref):
    shard = lax.axis_index("ctx")
    frames = clip_ref.shape[0]
    out_ref[0] = shard % 2
    for block in range(2):
        pair = shard // 2 * 2 + block
        clip = clip_ref[2 * pair]
        start = jnp.int32(0)
        for other in range(0, frames, 2):
            start += jnp.where(clip_ref[other] < clip, 1, 0)
        out_ref[1 + block] = keep_ref[clip] - (pair - start) * (OUT_SIDE * OUT_SIDE)
    before = clip_ref[jnp.maximum(2 * shard - 1, 0)]
    chip, chips = shard // 2, lax.axis_size("ctx") // 2
    out_ref[4] = jnp.where(chip % 2 == 0, chip // 2, chips - 1 - chip // 2)
    out_ref[3] = jnp.where((shard > 0) & (before == clip_ref[2 * shard]), 1, 0)


def token_place(row, core, unit):
    per_block = OUT_SIDE * OUT_SIDE
    within = row % per_block
    block = (within // unit) % 2
    target_core = jnp.where(row < per_block, core, 1 - core)
    return block, unit * (2 * (within // (2 * unit)) + target_core) + within % unit


def reorder_matrix(core, unit, to_sent):
    shape = (2 * OUT_SIDE * OUT_SIDE,) * 2
    out_row = lax.broadcasted_iota(jnp.int32, shape, 0)
    in_row = lax.broadcasted_iota(jnp.int32, shape, 1)
    sent, natural = (out_row, in_row) if to_sent else (in_row, out_row)
    block, token = token_place(sent, core, unit)
    source = jnp.where(block == core, 0, OUT_SIDE * OUT_SIDE) + token
    return (source == natural).astype(jnp.bfloat16)


def order_kernel(unit, facts_ref, own_ref, mate_ref, out_ref):
    rows = jnp.concatenate([own_ref[...], mate_ref[...]], axis=0)
    matrix = reorder_matrix(facts_ref[0], unit, True)
    out_ref[...] = jnp.dot(matrix, rows, preferred_element_type=jnp.float32).astype(jnp.bfloat16)


def patch_kernel(facts_ref, halo_ref, even_ref, out_ref):
    chans = halo_ref.shape[1]
    per_frame = OUT_SIDE * OUT_SIDE
    select = select_rows(True).astype(jnp.bfloat16)
    for frame, source in enumerate((halo_ref, even_ref)):
        rows = jnp.dot(select, source[...], preferred_element_type=jnp.float32)
        if frame == 0:
            rows = rows * facts_ref[3].astype(jnp.float32)
        rows = rows.astype(jnp.bfloat16)
        for tap in range(4):
            at = (frame * 4 + tap) * chans
            out_ref[:, at : at + chans] = rows[tap * per_frame : (tap + 1) * per_frame]


def unpatch_kernel(facts_ref, own_ref, mate_ref, out_ref, facts_out_ref):
    for place in range(facts_ref.shape[0]):
        facts_out_ref[place] = facts_ref[place]
    chans = out_ref.shape[1]
    rows = own_ref[...] + mate_ref[...].astype(jnp.float32)
    pieces = [rows[:, tap * chans : (tap + 1) * chans] for tap in range(4)]
    frame = jnp.dot(
        select_rows(False), jnp.concatenate(pieces, axis=0), precision=lax.Precision.HIGHEST
    ) * inside(FRAME_ROWS)
    if out_ref.dtype == jnp.bfloat16:
        frame = frame * facts_ref[3].astype(jnp.float32)
    out_ref[...] = frame.astype(out_ref.dtype)


def excite_grad_kernel(even_ref, odd_ref, conv_ref, excite_ref, expand_ref, out_ref):
    sums = []
    for frame, grad_ref in enumerate((even_ref, odd_ref)):
        conv = conv_ref[frame * FRAME_ROWS : (frame + 1) * FRAME_ROWS, :]
        active = conv * jax.nn.sigmoid(conv)
        sums.append(jnp.sum(grad_ref[...].astype(jnp.float32) * active, axis=0, keepdims=True))
    excite = excite_ref[...]
    inner = jnp.concatenate(sums, axis=0) * excite * (1.0 - excite)
    out_ref[...] = contract_exact(inner, expand_ref[...].astype(jnp.float32))


def conv_grad_kernel(
    even_ref, odd_ref, conv_ref, excite_ref, sq_ref, relaxed_ref, squeeze_ref, group_ref,
    out_ref, flat_ref, wide_ref, shift_ref, grad_ref,
):
    frames, _, chans = out_ref.shape
    width = group_ref.shape[1]
    rows = frames * FRAME_ROWS
    grad_squeezed = relaxed_ref[...] * silu_slope(sq_ref[...])
    pooled = jnp.dot(
        grad_squeezed, squeeze_ref[...].astype(jnp.float32), precision=lax.Precision.HIGHEST
    ) * (1.0 / (SIDE * SIDE))
    wide_ref[0:EDGE, :] = jnp.zeros((EDGE, chans), jnp.float32)
    wide_ref[EDGE + rows :, :] = jnp.zeros((EDGE, chans), jnp.float32)
    good = inside(FRAME_ROWS)
    for frame, source in enumerate((even_ref, odd_ref)):
        at = frame * FRAME_ROWS
        grad = source[...].astype(jnp.float32)
        grad_ref[at : at + FRAME_ROWS, :] = grad
        active = grad * excite_ref[frame : frame + 1, :] + pooled[frame : frame + 1]
        slope = silu_slope(conv_ref[at : at + FRAME_ROWS, :])
        wide_ref[EDGE + at : EDGE + at + FRAME_ROWS, :] = active * slope * good
    store_shifts(wide_ref, shift_ref, -1)
    body = rows - 2 * WIDE
    for block in channel_blocks(chans, width):
        _, _, start, end = block
        spread, same = block_tools(block, width)
        total = jnp.zeros((body, end - start), jnp.float32)
        for tap in range(9):
            down, across = divmod(tap, 3)
            weights = dense_tap(group_ref, tap, block, spread, same)
            at = (2 - down) * WIDE
            source = shift_ref[across, at : at + body, start:end]
            total += jnp.dot(source, weights, preferred_element_type=jnp.float32)
        grad_ref[WIDE : WIDE + body, start:end] += total
    for frame in range(frames):
        for y in range(SIDE):
            at = frame * FRAME_ROWS + (y + 1) * WIDE + 1
            flat_ref[y * SIDE : (y + 1) * SIDE, :] = grad_ref[at : at + SIDE, :]
        out_ref[frame] = flat_ref[...].astype(jnp.bfloat16)


def f32(*shape):
    return jax.ShapeDtypeStruct(shape, jnp.float32)


def bf16(*shape):
    return jax.ShapeDtypeStruct(shape, jnp.bfloat16)


def conv_forward(features, group_kernel, squeeze_in):
    frames, cells, chans = features.shape
    rows = frames * FRAME_ROWS
    return whole_call(
        conv_kernel,
        (f32(rows, chans), bf16(rows, chans), f32(frames, squeeze_in.shape[0])),
        [
            pltpu.VMEM((cells, chans), jnp.float32),
            pltpu.VMEM((rows + 2 * EDGE, chans), jnp.float32),
            pltpu.VMEM((3, rows, chans), jnp.bfloat16),
        ],
    )(features, group_kernel, squeeze_in)


def hidden_frames(conv, padded, squeezed, squeeze_out):
    rows, chans = conv.shape
    return whole_call(
        hidden_kernel,
        (bf16(FRAME_ROWS, chans), bf16(FRAME_ROWS, chans), f32(rows // FRAME_ROWS, chans)),
        [],
    )(conv, padded, squeezed, squeeze_out)


def vmem_specs(count):
    return [pl.BlockSpec(memory_space=pltpu.SMEM)] + [pl.BlockSpec(memory_space=pltpu.VMEM)] * count


def facts_of(frame_clip, clip_keep):
    smem = pl.BlockSpec(memory_space=pltpu.SMEM)
    return pl.pallas_call(
        facts_kernel,
        out_shape=jax.ShapeDtypeStruct((5,), jnp.int32),
        in_specs=[smem, smem],
        out_specs=smem,
        cost_estimate=FREE,
    )(frame_clip, clip_keep)


def order_rows(facts, own, mate, unit):
    rows, columns = own.shape
    return pl.pallas_call(
        functools.partial(order_kernel, unit),
        out_shape=bf16(2 * rows, columns),
        in_specs=vmem_specs(2),
        compiler_params=pltpu.CompilerParams(vmem_limit_bytes=VMEM_BYTES),
        cost_estimate=FREE,
    )(facts, own, mate)


def take_patches(facts, halo, even):
    chans = even.shape[1]
    return pl.pallas_call(
        patch_kernel,
        out_shape=bf16(OUT_SIDE * OUT_SIDE, 8 * chans),
        in_specs=vmem_specs(2),
        compiler_params=pltpu.CompilerParams(vmem_limit_bytes=VMEM_BYTES),
        cost_estimate=FREE,
    )(facts, halo, even)


def return_patches(facts, own, mate, chans, dtype):
    return pl.pallas_call(
        unpatch_kernel,
        out_shape=(
            jax.ShapeDtypeStruct((FRAME_ROWS, chans), dtype),
            jax.ShapeDtypeStruct(facts.shape, jnp.int32),
        ),
        in_specs=vmem_specs(2),
        out_specs=vmem_specs(1)[::-1],
        compiler_params=pltpu.CompilerParams(vmem_limit_bytes=VMEM_BYTES),
        cost_estimate=FREE,
    )(facts, own, mate)


def excite_grad(even, odd, conv, excite, squeeze_out):
    rows, chans = conv.shape
    return whole_call(
        excite_grad_kernel,
        f32(rows // FRAME_ROWS, squeeze_out.shape[0]),
        [],
    )(even, odd, conv, excite, squeeze_out)


def conv_backward(even, odd, conv, excite, squeezed, grad_relaxed, squeeze_in, group_kernel):
    rows, chans = conv.shape
    frames = rows // FRAME_ROWS
    return whole_call(
        conv_grad_kernel,
        bf16(frames, SIDE * SIDE, chans),
        [
            pltpu.VMEM((SIDE * SIDE, chans), jnp.float32),
            pltpu.VMEM((rows + 2 * EDGE, chans), jnp.float32),
            pltpu.VMEM((3, rows, chans), jnp.bfloat16),
            pltpu.VMEM((rows, chans), jnp.float32),
        ],
        pl.CostEstimate(flops=rows * chans * 9216, bytes_accessed=16 * rows * chans, transcendentals=0),
    )(even, odd, conv, excite, squeezed, grad_relaxed, squeeze_in, group_kernel)


def shifted(value, axis, by):
    count = lax.axis_size(axis)
    pairs = [(i, i + by) for i in range(count) if 0 <= i + by < count]
    return lax.ppermute(value, axis, pairs)


def ring_order(chips):
    return list(range(0, chips, 2)) + list(range(1, chips, 2))[::-1]


def ring_pairs(count, by):
    order = ring_order(count // 2)
    pairs = []
    for place, chip in enumerate(order):
        target = order[(place + by) % len(order)]
        pairs += [(2 * chip, 2 * target), (2 * chip + 1, 2 * target + 1)]
    return pairs


def swap_cores(value):
    return lax.ppermute(value, "ctx", [(i, i ^ 1) for i in range(lax.axis_size("ctx"))])


def tp_terms(value):
    size = lax.axis_size("tp")
    reach, other = 1, None
    while reach < size:
        value = value if other is None else value + other
        other = lax.ppermute(value, "tp", [(i, i ^ reach) for i in range(size)])
        reach *= 2
    return value, jnp.zeros_like(value) if other is None else other


def sum_tp(value):
    value, other = tp_terms(value)
    return value + other


def ring_send(value, by):
    return lax.ppermute(value, "ctx", ring_pairs(lax.axis_size("ctx"), by))


def tie(*values):
    return lax.optimization_barrier(values)


def pre_kernel(patch_ref, *refs):
    *blocks, out_ref = refs
    products = [contract_last(patch_ref[...], ref[...]) for ref in blocks]
    out_ref[...] = jnp.concatenate(products, axis=1)


def back_kernel(keep_ref, send_ref, *refs):
    *blocks, out_ref = refs
    back = jnp.concatenate([keep_ref[...], send_ref[...]], axis=0)
    out_ref[...] = jnp.concatenate([contract_last(back, ref[...]) for ref in blocks], axis=1)


def live_rows(facts_ref, rows, unit):
    block, token = token_place(
        lax.broadcasted_iota(jnp.int32, (rows, 1), 0), facts_ref[0], unit
    )
    return (token < jnp.where(block == 0, facts_ref[1], facts_ref[2])).astype(jnp.float32)


def totals_kernel(pieces, unit, parts, first, facts_ref, *refs):
    grad_act = refs[0][...] + refs[1][...]
    count = len(pieces)
    slopes, blocks = refs[2:4], refs[4 : 4 + count]
    before, after = refs[4 + count : -2 * len(parts)], refs[-2 * len(parts) :]
    rows, width = grad_act.shape[0], blocks[0].shape[0]
    matrix = reorder_matrix(facts_ref[0], unit, False)
    factors = []
    for place, (source, index) in enumerate(pieces):
        piece = grad_act[:, place * width : (place + 1) * width]
        piece = piece * slopes[source][:, index * width : (index + 1) * width]
        piece = jnp.dot(matrix, piece.astype(jnp.bfloat16), preferred_element_type=jnp.float32)
        factors.append(piece.astype(jnp.bfloat16))
    for part, lanes in enumerate(parts):
        total = 0.0
        for factor, ref in zip(factors, blocks):
            total += jnp.dot(factor, ref[:, lanes], preferred_element_type=jnp.float32)
        for half in range(2):
            value = total[half * rows // 2 : (half + 1) * rows // 2]
            value = value if first else before[2 * part + half][...] + value
            ref = after[2 * part + half]
            ref[...] = value.astype(ref.dtype)


def ring_offsets(chips):
    offsets = [0]
    for step in range(1, chips // 2):
        offsets += [-step, step]
    return offsets + [chips // 2]


def block_columns(facts_ref, offset, chips, width):
    shape = (width, chips * width)
    place = (facts_ref[4] + offset + chips) % chips
    column = lax.broadcasted_iota(jnp.int32, shape, 1)
    return (column == lax.broadcasted_iota(jnp.int32, shape, 0) + place * width).astype(jnp.bfloat16)


def exchange_matrix(core, unit, to_sent):
    per_block = OUT_SIDE * OUT_SIDE
    shape = (2 * per_block,) * 2
    out_row = lax.broadcasted_iota(jnp.int32, shape, 0)
    in_row = lax.broadcasted_iota(jnp.int32, shape, 1)
    sent, kept = (out_row, in_row) if to_sent else (in_row, out_row)
    target_core = (sent // (2 * unit)) % 2
    within = sent // (4 * unit) * (2 * unit) + sent % (2 * unit)
    return (within + jnp.where(target_core == core, 0, per_block) == kept).astype(jnp.bfloat16)


def act_kernel(offsets, chips, unit, last, facts_ref, own_ref, other_ref, *refs):
    *before, slope_ref, out_ref = refs
    pre = own_ref[...] + other_ref[...]
    width = pre.shape[1] // len(offsets)
    live = live_rows(facts_ref, pre.shape[0], unit)
    sigma = jax.nn.sigmoid(pre)
    slope_ref[...] = sigma * (1.0 + pre * (1.0 - sigma)) * live
    act = (pre * sigma * live).astype(jnp.bfloat16)
    total = before[0][...].astype(jnp.float32) if last else 0.0
    for place, offset in enumerate(offsets):
        columns = block_columns(facts_ref, offset, chips, width)
        piece = act[:, place * width : (place + 1) * width]
        total += jnp.dot(piece, columns, preferred_element_type=jnp.float32)
    total = total.astype(jnp.bfloat16)
    if last:
        matrix = exchange_matrix(facts_ref[0], unit, True)
        total = jnp.dot(matrix, total, preferred_element_type=jnp.float32).astype(jnp.bfloat16)
    out_ref[...] = total


def token_kernel(offsets, chips, unit, first, facts_ref, act_ref, *refs):
    count = len(offsets)
    blocks, before, after = refs[:count], refs[count:-2], refs[-2:]
    width = blocks[0].shape[0]
    matrix = exchange_matrix(facts_ref[0], unit, False)
    act = jnp.dot(matrix, act_ref[...], preferred_element_type=jnp.float32).astype(jnp.bfloat16)
    total = 0.0
    for offset, ref in zip(offsets, blocks):
        columns = block_columns(facts_ref, offset, chips, width)
        piece = contract_last(act, columns).astype(jnp.bfloat16)
        total += jnp.dot(piece, ref[...], preferred_element_type=jnp.float32)
    rows = after[0].shape[0]
    for half, ref in enumerate(after):
        value = total[half * rows : (half + 1) * rows]
        value = value if first else before[half][...] + value
        ref[...] = value.astype(ref.dtype)


def block_products(kernel, left, blocks):
    rows = 2 * OUT_SIDE * OUT_SIDE
    return whole_call(kernel, f32(rows, len(blocks) * blocks[0].shape[0]), [])(*left, *blocks)


def facts_call(kernel, outs, facts, operands, cost=FREE):
    return pl.pallas_call(
        kernel,
        out_shape=outs,
        in_specs=vmem_specs(len(operands)),
        compiler_params=pltpu.CompilerParams(vmem_limit_bytes=VMEM_BYTES),
        cost_estimate=cost,
    )(facts, *operands)


def add_gradients(facts, terms, slopes, pieces, blocks, before, unit, parts, last):
    rows = terms[0].shape[0] // 2
    kernel = functools.partial(totals_kernel, pieces, unit, parts, not before)
    outs = ()
    for lanes in parts:
        shape = rows, lanes.stop - lanes.start
        outs += f32(*shape), (bf16 if last else f32)(*shape)
    return tuple(facts_call(kernel, outs, facts, (*terms, *slopes, *blocks, *before)))


def act_and_slope(facts, terms, offsets, chips, before, unit):
    rows, columns = terms[0].shape
    kernel = functools.partial(act_kernel, offsets, chips, unit, bool(before))
    outs = f32(rows, columns), bf16(rows, columns // len(offsets) * chips)
    return facts_call(kernel, outs, facts, (*terms, *before))


def add_tokens(facts, act, offsets, chips, blocks, before, unit):
    rows, columns = act.shape[0] // 2, blocks[0].shape[1]
    kernel = functools.partial(token_kernel, offsets, chips, unit, not before)
    outs = f32(rows, columns), (bf16 if before else f32)(rows, columns)
    cost = pl.CostEstimate(
        flops=5 * len(blocks) * act.shape[1] * act.shape[0] * columns // chips * 8,
        bytes_accessed=0,
        transcendentals=0,
    )
    return facts_call(kernel, outs, facts, (act, *blocks, *before), cost if before else FREE)


def chips_exchange(value):
    count = lax.axis_size("ctx")
    groups = [list(range(core, count, 2)) for core in range(2)]
    return lax.all_to_all(
        value, "ctx", split_axis=0, concat_axis=0, tiled=True, axis_index_groups=groups
    )


def per_device(
    features,
    group_kernel,
    squeeze_in,
    squeeze_out,
    sampler_kernel,
    readout_kernel,
    frame_clip,
    clip_keep,
    token_cotangent,
):
    chans = features.shape[2]
    count = lax.axis_size("ctx")
    steps, unit = count // 4, OUT_SIDE * OUT_SIDE // count
    flat_sampler = sampler_kernel.reshape(sampler_kernel.shape[0], 8 * chans)
    chips = count // 2
    s_up, s_down = ring_send(flat_sampler, 1), ring_send(flat_sampler, -1)
    group_kernel = jnp.swapaxes(group_kernel, 1, 2)
    squeeze_in = squeeze_in.T
    facts = facts_of(frame_clip, clip_keep)

    conv, padded, squeezed = conv_forward(features, group_kernel, squeeze_in)
    token_cotangent, squeezed = tie(token_cotangent, squeezed)
    back = chips_exchange(token_cotangent)
    squeezed = sum_tp(squeezed)
    even, odd, excite = hidden_frames(conv, padded, squeezed, squeeze_out)
    halo = shifted(odd, "ctx", 1)

    s_up, s_down = [flat_sampler, s_up], [flat_sampler, s_down]
    s_up[1], s_down[1], even = tie(s_up[1], s_down[1], even)
    for step in range(2, steps):
        s_up.append(ring_send(s_up[-1], 1))
        s_down.append(ring_send(s_down[-1], -1))
        if step == 2:
            halo, s_up[2], s_down[2] = tie(halo, s_up[2], s_down[2])
            patches = take_patches(facts, halo, even)
            patches = order_rows(facts, patches, swap_cores(patches), unit)
    s_up[-1], s_down[-1], readout_kernel, back = tie(s_up[-1], s_down[-1], readout_kernel, back)
    back = (back, swap_cores(back))
    s_last = ring_send(s_up[-1], 1)
    samplers = [flat_sampler] + [block for pair in zip(s_up[1:], s_down[1:]) for block in pair]
    offsets = ring_offsets(chips)
    first_pre = block_products(pre_kernel, (patches,), samplers)
    r_down = [readout_kernel, ring_send(readout_kernel, -1)]
    readout_kernel, first_pre = tie(readout_kernel, first_pre)
    r_up = [readout_kernel, ring_send(readout_kernel, 1)]
    first_pre = tp_terms(first_pre)
    r_down[1], s_last, *first_pre = tie(r_down[1], s_last, *first_pre)
    r_down.append(ring_send(r_down[1], -1))
    sums = block_products(back_kernel, back, [r_up[0], r_down[1]])
    first_slope, first_act = act_and_slope(facts, first_pre, offsets[:-1], chips, (), unit)
    last_pre = tp_terms(block_products(pre_kernel, (patches,), [s_last]))
    last_slope, act = act_and_slope(facts, last_pre, offsets[-1:], chips, (first_act,), unit)
    slopes = first_slope, last_slope
    r_up[1], sums, act = tie(r_up[1], sums, act)
    r_up.append(ring_send(r_up[1], 1))
    act = chips_exchange(act)
    halo_lanes, even_lanes = slice(0, 4 * chans), slice(4 * chans, 8 * chans)
    grads = ()
    terms = tp_terms(sums)
    pieces, blocks = [(0, 0), (0, 2)], [samplers[0], samplers[2]]
    for step in range(2, steps):
        r_down[step], *terms = tie(r_down[step], *terms)
        r_down.append(ring_send(r_down[step], -1))
        sums = block_products(back_kernel, back, [r_up[step - 1], r_down[step]])
        grads = add_gradients(
            facts, terms, slopes, pieces, blocks, grads, unit, (halo_lanes, even_lanes), False
        )
        if step < steps - 1:
            r_up[step], sums, *grads = tie(r_up[step], sums, *grads)
            r_up.append(ring_send(r_up[step], 1))
        terms = tp_terms(sums)
        pieces = [(0, 2 * step - 3), (0, 2 * step)]
        blocks = [samplers[2 * step - 3], samplers[2 * step]]
    grads = add_gradients(
        facts, terms, slopes, pieces, blocks, grads, unit, (halo_lanes, even_lanes), False
    )
    places, blocks = [0], [r_up[0]]
    for step in range(1, steps):
        places, blocks = places + [step], blocks + [r_down[step]]
        if step < steps - 1:
            places, blocks = places + [-step], blocks + [r_up[step]]
    tokens = add_tokens(facts, act, places, chips, blocks, (), unit)

    held = tie(r_up[-1], r_down[-1], *grads, *tokens)
    late, grads, tokens = held[:2], held[2:6], held[6:]
    terms = tp_terms(block_products(back_kernel, back, late))
    pieces, blocks = [(0, 2 * steps - 3), (1, 0)], [samplers[2 * steps - 3], s_last]
    halo_own, halo_mate = add_gradients(
        facts, terms, slopes, pieces, blocks, grads[:2], unit, (halo_lanes,), True
    )
    halo_mate, first_term = tie(halo_mate, terms[0])
    even_own, even_mate = add_gradients(
        facts, (first_term, terms[1]), slopes, pieces, blocks, grads[2:], unit, (even_lanes,), True
    )
    lead, facts_late = return_patches(facts, halo_own, swap_cores(halo_mate), chans, jnp.bfloat16)
    grad_odd = shifted(lead, "ctx", -1)
    grad_even, facts_late = return_patches(
        facts_late, even_own, swap_cores(even_mate), chans, jnp.float32
    )
    grad_relaxed = sum_tp(excite_grad(grad_even, grad_odd, conv, excite, squeeze_out))
    tokens, send = add_tokens(
        facts_late, act, [1 - steps, steps], chips, late, tokens, unit
    )
    llm_tokens = (tokens + swap_cores(send).astype(jnp.float32)).astype(jnp.bfloat16)
    grad_features = conv_backward(
        grad_even, grad_odd, conv, excite, squeezed, grad_relaxed, squeeze_in, group_kernel
    )
    return (llm_tokens, grad_features)


def solution(mesh):
    placed = (
        P("ctx", None, "tp"),
        P(None, "tp", None),
        P("tp", None),
        P(None, "tp"),
        P("ctx", None, "tp"),
        P("ctx", "tp"),
        P(),
        P(),
        P("ctx", "tp"),
    )
    return jax.shard_map(
        per_device,
        mesh=mesh,
        in_specs=placed,
        out_specs=(P("ctx", "tp"), P("ctx", None, "tp")),
        check_vma=False,
    )
```

```python
import functools

import jax
import jax.numpy as jnp
from jax import lax
from jax.experimental import pallas as pl
from jax.experimental.pallas import tpu as pltpu
from jax.sharding import PartitionSpec as P

SIDE = 14
OUT_SIDE = 8
WIDE = 16
FRAME_ROWS = WIDE * WIDE
EDGE = 8
LANES = 128
VMEM_BYTES = 16 * 2**20
FREE = pl.CostEstimate(flops=0, bytes_accessed=0, transcendentals=0)


def whole_call(kernel, outs, scratch, cost=FREE):
    return pl.pallas_call(
        kernel,
        out_shape=outs,
        scratch_shapes=scratch,
        compiler_params=pltpu.CompilerParams(vmem_limit_bytes=VMEM_BYTES),
        cost_estimate=cost,
    )


def contract_last(left, right):
    return lax.dot_general(
        left, right, (((1,), (1,)), ((), ())), preferred_element_type=jnp.float32
    )


def contract_exact(left, right):
    return lax.dot_general(
        left,
        right,
        (((1,), (1,)), ((), ())),
        precision=lax.Precision.HIGHEST,
        preferred_element_type=jnp.float32,
    )


def silu_slope(values):
    sigma = jax.nn.sigmoid(values)
    return sigma * (1.0 + values * (1.0 - sigma))


def inside(rows):
    row = lax.broadcasted_iota(jnp.int32, (rows, 1), 0)
    across, down = row & (WIDE - 1), (row // WIDE) & (WIDE - 1)
    good = (across >= 1) & (across <= SIDE) & (down >= 1) & (down <= SIDE)
    return good.astype(jnp.float32)


def channel_blocks(chans, width):
    span = 4 * width
    blocks = []
    for low in range(0, chans, span):
        high = min(chans, low + span)
        blocks.append((low, high, low // LANES * LANES, min(chans, -(-high // LANES) * LANES)))
    return blocks


def block_tools(block, width):
    low, high, start, end = block
    size = end - start
    out_row = lax.broadcasted_iota(jnp.int32, (size, width), 0) + start
    within = lax.broadcasted_iota(jnp.int32, (size, width), 1)
    lane = lax.broadcasted_iota(jnp.int32, (size, size), 1) + start
    row = lax.broadcasted_iota(jnp.int32, (size, size), 0) + start
    spread = jnp.zeros((size, width), jnp.float32)
    same = jnp.zeros((size, size), jnp.float32)
    for first in range(low, high, width):
        spread += (out_row == within + first).astype(jnp.float32)
        in_lane = (lane >= first) & (lane < first + width)
        in_row = (row >= first) & (row < first + width)
        same += (in_lane & in_row).astype(jnp.float32)
    return spread.astype(jnp.bfloat16), same


def dense_tap(group_ref, tap, block, spread, same):
    _, _, start, end = block
    full = jnp.dot(spread, group_ref[tap, :, start:end], preferred_element_type=jnp.float32)
    return (full * same).astype(jnp.bfloat16)


def store_shifts(wide_ref, shift_ref, sign):
    rows = shift_ref.shape[1]
    for col in range(3):
        at = EDGE + sign * (col - 1)
        shift_ref[col] = wide_ref[at : at + rows, :].astype(jnp.bfloat16)


def conv_kernel(feat_ref, group_ref, squeeze_ref, *refs):
    conv_ref, pad_ref, sq_ref, flat_ref, wide_ref, shift_ref = refs
    frames, _, chans = feat_ref.shape
    width = group_ref.shape[1]
    rows = frames * FRAME_ROWS
    wide_ref[...] = jnp.zeros_like(wide_ref)
    for frame in range(frames):
        flat_ref[...] = feat_ref[frame].astype(jnp.float32)
        for y in range(SIDE):
            at = EDGE + frame * FRAME_ROWS + (y + 1) * WIDE + 1
            wide_ref[at : at + SIDE, :] = flat_ref[y * SIDE : (y + 1) * SIDE, :]
    store_shifts(wide_ref, shift_ref, 1)
    pad_ref[...] = shift_ref[1]
    conv_ref[...] = jnp.zeros_like(conv_ref)
    body = rows - 2 * WIDE
    for block in channel_blocks(chans, width):
        _, _, start, end = block
        spread, same = block_tools(block, width)
        total = jnp.zeros((body, end - start), jnp.float32)
        for tap in range(9):
            down, across = divmod(tap, 3)
            weights = dense_tap(group_ref, tap, block, spread, same)
            source = shift_ref[across, down * WIDE : down * WIDE + body, start:end]
            total += contract_last(source, weights)
        conv_ref[WIDE : WIDE + body, start:end] += total
    conv = conv_ref[...] * inside(rows)
    conv_ref[...] = conv
    active = conv * jax.nn.sigmoid(conv)
    pooled = jnp.concatenate(
        [
            jnp.sum(active[f * FRAME_ROWS : (f + 1) * FRAME_ROWS], axis=0, keepdims=True)
            for f in range(frames)
        ],
        axis=0,
    ) * (1.0 / (SIDE * SIDE))
    sq_ref[...] = contract_exact(pooled, squeeze_ref[...].astype(jnp.float32))


def hidden_kernel(conv_ref, pad_ref, sq_ref, expand_ref, even_ref, odd_ref, excite_ref):
    squeezed = sq_ref[...]
    relaxed = squeezed * jax.nn.sigmoid(squeezed)
    excite = jax.nn.sigmoid(
        jnp.dot(relaxed, expand_ref[...].astype(jnp.float32), precision=lax.Precision.HIGHEST)
    )
    excite_ref[...] = excite
    for frame, out_ref in enumerate((even_ref, odd_ref)):
        rows = slice(frame * FRAME_ROWS, (frame + 1) * FRAME_ROWS)
        conv = conv_ref[rows, :]
        active = conv * jax.nn.sigmoid(conv)
        hidden = pad_ref[rows, :].astype(jnp.float32) + active * excite[frame : frame + 1]
        out_ref[...] = hidden.astype(jnp.bfloat16)


def select_rows(to_patches):
    shape = (FRAME_ROWS, FRAME_ROWS)
    out_row = lax.broadcasted_iota(jnp.int32, shape, 0)
    in_row = lax.broadcasted_iota(jnp.int32, shape, 1)
    patch_row, frame_row = (out_row, in_row) if to_patches else (in_row, out_row)
    down, across = patch_row >> 7, (patch_row >> 6) & 1
    a, b = (patch_row >> 3) & 7, patch_row & 7
    return ((2 * a + down) * WIDE + 2 * b + across == frame_row).astype(jnp.float32)


def facts_kernel(clip_ref, keep_ref, out_ref):
    shard = lax.axis_index("ctx")
    frames = clip_ref.shape[0]
    out_ref[0] = shard % 2
    for block in range(2):
        pair = shard // 2 * 2 + block
        clip = clip_ref[2 * pair]
        start = jnp.int32(0)
        for other in range(0, frames, 2):
            start += jnp.where(clip_ref[other] < clip, 1, 0)
        out_ref[1 + block] = keep_ref[clip] - (pair - start) * (OUT_SIDE * OUT_SIDE)
    before = clip_ref[jnp.maximum(2 * shard - 1, 0)]
    chip, chips = shard // 2, lax.axis_size("ctx") // 2
    out_ref[4] = jnp.where(chip % 2 == 0, chip // 2, chips - 1 - chip // 2)
    out_ref[3] = jnp.where((shard > 0) & (before == clip_ref[2 * shard]), 1, 0)


def token_place(row, core, unit):
    per_block = OUT_SIDE * OUT_SIDE
    within = row % per_block
    block = (within // unit) % 2
    target_core = jnp.where(row < per_block, core, 1 - core)
    return block, unit * (2 * (within // (2 * unit)) + target_core) + within % unit


def reorder_matrix(core, unit, to_sent):
    shape = (2 * OUT_SIDE * OUT_SIDE,) * 2
    out_row = lax.broadcasted_iota(jnp.int32, shape, 0)
    in_row = lax.broadcasted_iota(jnp.int32, shape, 1)
    sent, natural = (out_row, in_row) if to_sent else (in_row, out_row)
    block, token = token_place(sent, core, unit)
    source = jnp.where(block == core, 0, OUT_SIDE * OUT_SIDE) + token
    return (source == natural).astype(jnp.bfloat16)


def order_kernel(unit, facts_ref, own_ref, mate_ref, out_ref):
    rows = jnp.concatenate([own_ref[...], mate_ref[...]], axis=0)
    matrix = reorder_matrix(facts_ref[0], unit, True)
    out_ref[...] = jnp.dot(matrix, rows, preferred_element_type=jnp.float32).astype(jnp.bfloat16)


def patch_kernel(facts_ref, halo_ref, even_ref, out_ref):
    chans = halo_ref.shape[1]
    per_frame = OUT_SIDE * OUT_SIDE
    select = select_rows(True).astype(jnp.bfloat16)
    for frame, source in enumerate((halo_ref, even_ref)):
        rows = jnp.dot(select, source[...], preferred_element_type=jnp.float32)
        if frame == 0:
            rows = rows * facts_ref[3].astype(jnp.float32)
        rows = rows.astype(jnp.bfloat16)
        for tap in range(4):
            at = (frame * 4 + tap) * chans
            out_ref[:, at : at + chans] = rows[tap * per_frame : (tap + 1) * per_frame]


def unpatch_kernel(facts_ref, own_ref, mate_ref, out_ref, facts_out_ref):
    for place in range(facts_ref.shape[0]):
        facts_out_ref[place] = facts_ref[place]
    chans = out_ref.shape[1]
    rows = own_ref[...] + mate_ref[...].astype(jnp.float32)
    pieces = [rows[:, tap * chans : (tap + 1) * chans] for tap in range(4)]
    frame = jnp.dot(
        select_rows(False), jnp.concatenate(pieces, axis=0), precision=lax.Precision.HIGHEST
    ) * inside(FRAME_ROWS)
    if out_ref.dtype == jnp.bfloat16:
        frame = frame * facts_ref[3].astype(jnp.float32)
    out_ref[...] = frame.astype(out_ref.dtype)


def excite_grad_kernel(even_ref, odd_ref, conv_ref, excite_ref, expand_ref, out_ref):
    sums = []
    for frame, grad_ref in enumerate((even_ref, odd_ref)):
        conv = conv_ref[frame * FRAME_ROWS : (frame + 1) * FRAME_ROWS, :]
        active = conv * jax.nn.sigmoid(conv)
        sums.append(jnp.sum(grad_ref[...].astype(jnp.float32) * active, axis=0, keepdims=True))
    excite = excite_ref[...]
    inner = jnp.concatenate(sums, axis=0) * excite * (1.0 - excite)
    out_ref[...] = contract_exact(inner, expand_ref[...].astype(jnp.float32))


def conv_grad_kernel(
    even_ref, odd_ref, conv_ref, excite_ref, sq_ref, relaxed_ref, squeeze_ref, group_ref,
    out_ref, flat_ref, wide_ref, shift_ref, grad_ref,
):
    frames, _, chans = out_ref.shape
    width = group_ref.shape[1]
    rows = frames * FRAME_ROWS
    grad_squeezed = relaxed_ref[...] * silu_slope(sq_ref[...])
    pooled = jnp.dot(
        grad_squeezed, squeeze_ref[...].astype(jnp.float32), precision=lax.Precision.HIGHEST
    ) * (1.0 / (SIDE * SIDE))
    wide_ref[0:EDGE, :] = jnp.zeros((EDGE, chans), jnp.float32)
    wide_ref[EDGE + rows :, :] = jnp.zeros((EDGE, chans), jnp.float32)
    good = inside(FRAME_ROWS)
    for frame, source in enumerate((even_ref, odd_ref)):
        at = frame * FRAME_ROWS
        grad = source[...].astype(jnp.float32)
        grad_ref[at : at + FRAME_ROWS, :] = grad
        active = grad * excite_ref[frame : frame + 1, :] + pooled[frame : frame + 1]
        slope = silu_slope(conv_ref[at : at + FRAME_ROWS, :])
        wide_ref[EDGE + at : EDGE + at + FRAME_ROWS, :] = active * slope * good
    store_shifts(wide_ref, shift_ref, -1)
    body = rows - 2 * WIDE
    for block in channel_blocks(chans, width):
        _, _, start, end = block
        spread, same = block_tools(block, width)
        total = jnp.zeros((body, end - start), jnp.float32)
        for tap in range(9):
            down, across = divmod(tap, 3)
            weights = dense_tap(group_ref, tap, block, spread, same)
            at = (2 - down) * WIDE
            source = shift_ref[across, at : at + body, start:end]
            total += jnp.dot(source, weights, preferred_element_type=jnp.float32)
        grad_ref[WIDE : WIDE + body, start:end] += total
    for frame in range(frames):
        for y in range(SIDE):
            at = frame * FRAME_ROWS + (y + 1) * WIDE + 1
            flat_ref[y * SIDE : (y + 1) * SIDE, :] = grad_ref[at : at + SIDE, :]
        out_ref[frame] = flat_ref[...].astype(jnp.bfloat16)


def f32(*shape):
    return jax.ShapeDtypeStruct(shape, jnp.float32)


def bf16(*shape):
    return jax.ShapeDtypeStruct(shape, jnp.bfloat16)


def conv_forward(features, group_kernel, squeeze_in):
    frames, cells, chans = features.shape
    rows = frames * FRAME_ROWS
    return whole_call(
        conv_kernel,
        (f32(rows, chans), bf16(rows, chans), f32(frames, squeeze_in.shape[0])),
        [
            pltpu.VMEM((cells, chans), jnp.float32),
            pltpu.VMEM((rows + 2 * EDGE, chans), jnp.float32),
            pltpu.VMEM((3, rows, chans), jnp.bfloat16),
        ],
    )(features, group_kernel, squeeze_in)


def hidden_frames(conv, padded, squeezed, squeeze_out):
    rows, chans = conv.shape
    return whole_call(
        hidden_kernel,
        (bf16(FRAME_ROWS, chans), bf16(FRAME_ROWS, chans), f32(rows // FRAME_ROWS, chans)),
        [],
    )(conv, padded, squeezed, squeeze_out)


def vmem_specs(count):
    return [pl.BlockSpec(memory_space=pltpu.SMEM)] + [pl.BlockSpec(memory_space=pltpu.VMEM)] * count


def facts_of(frame_clip, clip_keep):
    smem = pl.BlockSpec(memory_space=pltpu.SMEM)
    return pl.pallas_call(
        facts_kernel,
        out_shape=jax.ShapeDtypeStruct((5,), jnp.int32),
        in_specs=[smem, smem],
        out_specs=smem,
        cost_estimate=FREE,
    )(frame_clip, clip_keep)


def order_rows(facts, own, mate, unit):
    rows, columns = own.shape
    return pl.pallas_call(
        functools.partial(order_kernel, unit),
        out_shape=bf16(2 * rows, columns),
        in_specs=vmem_specs(2),
        compiler_params=pltpu.CompilerParams(vmem_limit_bytes=VMEM_BYTES),
        cost_estimate=FREE,
    )(facts, own, mate)


def take_patches(facts, halo, even):
    chans = even.shape[1]
    return pl.pallas_call(
        patch_kernel,
        out_shape=bf16(OUT_SIDE * OUT_SIDE, 8 * chans),
        in_specs=vmem_specs(2),
        compiler_params=pltpu.CompilerParams(vmem_limit_bytes=VMEM_BYTES),
        cost_estimate=FREE,
    )(facts, halo, even)


def return_patches(facts, own, mate, chans, dtype):
    return pl.pallas_call(
        unpatch_kernel,
        out_shape=(
            jax.ShapeDtypeStruct((FRAME_ROWS, chans), dtype),
            jax.ShapeDtypeStruct(facts.shape, jnp.int32),
        ),
        in_specs=vmem_specs(2),
        out_specs=vmem_specs(1)[::-1],
        compiler_params=pltpu.CompilerParams(vmem_limit_bytes=VMEM_BYTES),
        cost_estimate=FREE,
    )(facts, own, mate)


def excite_grad(even, odd, conv, excite, squeeze_out):
    rows, chans = conv.shape
    return whole_call(
        excite_grad_kernel,
        f32(rows // FRAME_ROWS, squeeze_out.shape[0]),
        [],
    )(even, odd, conv, excite, squeeze_out)


def conv_backward(even, odd, conv, excite, squeezed, grad_relaxed, squeeze_in, group_kernel):
    rows, chans = conv.shape
    frames = rows // FRAME_ROWS
    return whole_call(
        conv_grad_kernel,
        bf16(frames, SIDE * SIDE, chans),
        [
            pltpu.VMEM((SIDE * SIDE, chans), jnp.float32),
            pltpu.VMEM((rows + 2 * EDGE, chans), jnp.float32),
            pltpu.VMEM((3, rows, chans), jnp.bfloat16),
            pltpu.VMEM((rows, chans), jnp.float32),
        ],
        pl.CostEstimate(flops=rows * chans * 9216, bytes_accessed=16 * rows * chans, transcendentals=0),
    )(even, odd, conv, excite, squeezed, grad_relaxed, squeeze_in, group_kernel)


def shifted(value, axis, by):
    count = lax.axis_size(axis)
    pairs = [(i, i + by) for i in range(count) if 0 <= i + by < count]
    return lax.ppermute(value, axis, pairs)


def ring_order(chips):
    return list(range(0, chips, 2)) + list(range(1, chips, 2))[::-1]


def ring_pairs(count, by):
    order = ring_order(count // 2)
    pairs = []
    for place, chip in enumerate(order):
        target = order[(place + by) % len(order)]
        pairs += [(2 * chip, 2 * target), (2 * chip + 1, 2 * target + 1)]
    return pairs


def swap_cores(value):
    return lax.ppermute(value, "ctx", [(i, i ^ 1) for i in range(lax.axis_size("ctx"))])


def tp_terms(value):
    size = lax.axis_size("tp")
    reach, other = 1, None
    while reach < size:
        value = value if other is None else value + other
        other = lax.ppermute(value, "tp", [(i, i ^ reach) for i in range(size)])
        reach *= 2
    return value, jnp.zeros_like(value) if other is None else other


def sum_tp(value):
    value, other = tp_terms(value)
    return value + other


def ring_send(value, by):
    return lax.ppermute(value, "ctx", ring_pairs(lax.axis_size("ctx"), by))


def tie(*values):
    return lax.optimization_barrier(values)


def pre_kernel(patch_ref, *refs):
    *blocks, out_ref = refs
    products = [contract_last(patch_ref[...], ref[...]) for ref in blocks]
    out_ref[...] = jnp.concatenate(products, axis=1)


def back_kernel(keep_ref, send_ref, *refs):
    *blocks, out_ref = refs
    back = jnp.concatenate([keep_ref[...], send_ref[...]], axis=0)
    out_ref[...] = jnp.concatenate([contract_last(back, ref[...]) for ref in blocks], axis=1)


def live_rows(facts_ref, rows, unit):
    block, token = token_place(
        lax.broadcasted_iota(jnp.int32, (rows, 1), 0), facts_ref[0], unit
    )
    return (token < jnp.where(block == 0, facts_ref[1], facts_ref[2])).astype(jnp.float32)


def totals_kernel(pieces, unit, parts, first, facts_ref, *refs):
    grad_act = refs[0][...] + refs[1][...]
    count = len(pieces)
    slopes, blocks = refs[2:4], refs[4 : 4 + count]
    before, after = refs[4 + count : -2 * len(parts)], refs[-2 * len(parts) :]
    rows, width = grad_act.shape[0], blocks[0].shape[0]
    matrix = reorder_matrix(facts_ref[0], unit, False)
    factors = []
    for place, (source, index) in enumerate(pieces):
        piece = grad_act[:, place * width : (place + 1) * width]
        piece = piece * slopes[source][:, index * width : (index + 1) * width]
        piece = jnp.dot(matrix, piece.astype(jnp.bfloat16), preferred_element_type=jnp.float32)
        factors.append(piece.astype(jnp.bfloat16))
    for part, lanes in enumerate(parts):
        total = 0.0
        for factor, ref in zip(factors, blocks):
            total += jnp.dot(factor, ref[:, lanes], preferred_element_type=jnp.float32)
        for half in range(2):
            value = total[half * rows // 2 : (half + 1) * rows // 2]
            value = value if first else before[2 * part + half][...] + value
            ref = after[2 * part + half]
            ref[...] = value.astype(ref.dtype)


def ring_offsets(chips):
    offsets = [0]
    for step in range(1, chips // 2):
        offsets += [-step, step]
    return offsets + [chips // 2]


def block_columns(facts_ref, offset, chips, width):
    shape = (width, chips * width)
    place = (facts_ref[4] + offset + chips) % chips
    column = lax.broadcasted_iota(jnp.int32, shape, 1)
    return (column == lax.broadcasted_iota(jnp.int32, shape, 0) + place * width).astype(jnp.bfloat16)


def exchange_matrix(core, unit, to_sent):
    per_block = OUT_SIDE * OUT_SIDE
    shape = (2 * per_block,) * 2
    out_row = lax.broadcasted_iota(jnp.int32, shape, 0)
    in_row = lax.broadcasted_iota(jnp.int32, shape, 1)
    sent, kept = (out_row, in_row) if to_sent else (in_row, out_row)
    target_core = (sent // (2 * unit)) % 2
    within = sent // (4 * unit) * (2 * unit) + sent % (2 * unit)
    return (within + jnp.where(target_core == core, 0, per_block) == kept).astype(jnp.bfloat16)


def act_kernel(offsets, chips, unit, last, facts_ref, own_ref, other_ref, *refs):
    *before, slope_ref, out_ref = refs
    pre = own_ref[...] + other_ref[...]
    width = pre.shape[1] // len(offsets)
    live = live_rows(facts_ref, pre.shape[0], unit)
    sigma = jax.nn.sigmoid(pre)
    slope_ref[...] = sigma * (1.0 + pre * (1.0 - sigma)) * live
    act = (pre * sigma * live).astype(jnp.bfloat16)
    total = before[0][...].astype(jnp.float32) if last else 0.0
    for place, offset in enumerate(offsets):
        columns = block_columns(facts_ref, offset, chips, width)
        piece = act[:, place * width : (place + 1) * width]
        total += jnp.dot(piece, columns, preferred_element_type=jnp.float32)
    total = total.astype(jnp.bfloat16)
    if last:
        matrix = exchange_matrix(facts_ref[0], unit, True)
        total = jnp.dot(matrix, total, preferred_element_type=jnp.float32).astype(jnp.bfloat16)
    out_ref[...] = total


def token_kernel(offsets, chips, unit, first, facts_ref, act_ref, *refs):
    count, held = len(offsets), 2 if first else 4
    blocks, refs = refs[:count], refs[count:]
    before, after = refs[: held - 2], refs[held - 2 : held]
    buffers, sems = refs[held:-1], refs[-1]
    copies = [
        pltpu.make_async_copy(ref, buffer, sems.at[place])
        for place, (ref, buffer) in enumerate(zip(blocks, buffers))
    ]
    for copy in copies:
        copy.start()
    width = buffers[0].shape[0]
    matrix = exchange_matrix(facts_ref[0], unit, False)
    act = jnp.dot(matrix, act_ref[...], preferred_element_type=jnp.float32).astype(jnp.bfloat16)
    total = 0.0
    for offset, copy, buffer in zip(offsets, copies, buffers):
        columns = block_columns(facts_ref, offset, chips, width)
        piece = contract_last(act, columns).astype(jnp.bfloat16)
        copy.wait()
        total += jnp.dot(piece, buffer[...], preferred_element_type=jnp.float32)
    rows = after[0].shape[0]
    for half, ref in enumerate(after):
        value = total[half * rows : (half + 1) * rows]
        value = value if first else before[half][...] + value
        ref[...] = value.astype(ref.dtype)


def block_products(kernel, left, blocks):
    rows = 2 * OUT_SIDE * OUT_SIDE
    return whole_call(kernel, f32(rows, len(blocks) * blocks[0].shape[0]), [])(*left, *blocks)


def facts_call(kernel, outs, facts, operands, cost=FREE):
    return pl.pallas_call(
        kernel,
        out_shape=outs,
        in_specs=vmem_specs(len(operands)),
        compiler_params=pltpu.CompilerParams(vmem_limit_bytes=VMEM_BYTES),
        cost_estimate=cost,
    )(facts, *operands)


def add_gradients(facts, terms, slopes, pieces, blocks, before, unit, parts, last):
    rows = terms[0].shape[0] // 2
    kernel = functools.partial(totals_kernel, pieces, unit, parts, not before)
    outs = ()
    for lanes in parts:
        shape = rows, lanes.stop - lanes.start
        outs += f32(*shape), (bf16 if last else f32)(*shape)
    return tuple(facts_call(kernel, outs, facts, (*terms, *slopes, *blocks, *before)))


def act_and_slope(facts, terms, offsets, chips, before, unit):
    rows, columns = terms[0].shape
    kernel = functools.partial(act_kernel, offsets, chips, unit, bool(before))
    outs = f32(rows, columns), bf16(rows, columns // len(offsets) * chips)
    return facts_call(kernel, outs, facts, (*terms, *before))


def add_tokens(facts, act, offsets, chips, blocks, before, unit):
    rows, columns = act.shape[0] // 2, blocks[0].shape[1]
    kernel = functools.partial(token_kernel, offsets, chips, unit, not before)
    cost = pl.CostEstimate(
        flops=40 * len(blocks) * act.shape[1] * act.shape[0] * columns // chips,
        bytes_accessed=0,
        transcendentals=0,
    )
    vmem = pl.BlockSpec(memory_space=pltpu.VMEM)
    anywhere = pl.BlockSpec(memory_space=pl.ANY)
    return pl.pallas_call(
        kernel,
        out_shape=(f32(rows, columns), (bf16 if before else f32)(rows, columns)),
        in_specs=vmem_specs(1) + [anywhere] * len(blocks) + [vmem] * len(before),
        scratch_shapes=[pltpu.VMEM(block.shape, block.dtype) for block in blocks]
        + [pltpu.SemaphoreType.DMA((len(blocks),))],
        compiler_params=pltpu.CompilerParams(vmem_limit_bytes=VMEM_BYTES),
        cost_estimate=cost if before else FREE,
    )(facts, act, *blocks, *before)


def chips_exchange(value):
    count = lax.axis_size("ctx")
    groups = [list(range(core, count, 2)) for core in range(2)]
    return lax.all_to_all(
        value, "ctx", split_axis=0, concat_axis=0, tiled=True, axis_index_groups=groups
    )


def per_device(
    features,
    group_kernel,
    squeeze_in,
    squeeze_out,
    sampler_kernel,
    readout_kernel,
    frame_clip,
    clip_keep,
    token_cotangent,
):
    chans = features.shape[2]
    count = lax.axis_size("ctx")
    steps, unit = count // 4, OUT_SIDE * OUT_SIDE // count
    flat_sampler = sampler_kernel.reshape(sampler_kernel.shape[0], 8 * chans)
    chips = count // 2
    s_up, s_down = ring_send(flat_sampler, 1), ring_send(flat_sampler, -1)
    group_kernel = jnp.swapaxes(group_kernel, 1, 2)
    squeeze_in = squeeze_in.T
    facts = facts_of(frame_clip, clip_keep)

    conv, padded, squeezed = conv_forward(features, group_kernel, squeeze_in)
    token_cotangent, squeezed = tie(token_cotangent, squeezed)
    back = chips_exchange(token_cotangent)
    squeezed = sum_tp(squeezed)
    even, odd, excite = hidden_frames(conv, padded, squeezed, squeeze_out)
    halo = shifted(odd, "ctx", 1)

    s_up, s_down = [flat_sampler, s_up], [flat_sampler, s_down]
    s_up[1], s_down[1], even, readout_kernel = tie(s_up[1], s_down[1], even, readout_kernel)
    for step in range(2, steps):
        s_up.append(ring_send(s_up[-1], 1))
        s_down.append(ring_send(s_down[-1], -1))
        if step == 2:
            halo, s_up[2], s_down[2] = tie(halo, s_up[2], s_down[2])
            r_up = [readout_kernel, ring_send(readout_kernel, 1)]
            r_down = [readout_kernel, ring_send(readout_kernel, -1)]
            patches = take_patches(facts, halo, even)
            mate_patches, r_up[1], r_down[1] = tie(swap_cores(patches), r_up[1], r_down[1])
            patches = order_rows(facts, patches, mate_patches, unit)
            r_down.append(ring_send(r_down[1], -1))
    held = tie(s_up[-1], s_down[-1], r_up[1], back, patches)
    s_up[-1], s_down[-1], r_up[1], back, patches = held
    back = (back, swap_cores(back))
    s_last = ring_send(s_up[-1], 1)
    samplers = [flat_sampler] + [block for pair in zip(s_up[1:], s_down[1:]) for block in pair]
    offsets = ring_offsets(chips)
    first_pre = block_products(pre_kernel, (patches,), samplers)
    r_up.append(ring_send(r_up[1], 1))
    sums = block_products(back_kernel, back, [r_up[0], r_down[1]])
    held = tie(*tp_terms(first_pre), sums, s_last, r_down[2])
    first_pre, sums, s_last, r_down[2] = held[:2], *held[2:]
    first_slope, first_act = act_and_slope(facts, first_pre, offsets[:-1], chips, (), unit)
    last_pre = tp_terms(block_products(pre_kernel, (patches,), [s_last]))
    last_slope, act = act_and_slope(facts, last_pre, offsets[-1:], chips, (first_act,), unit)
    slopes = first_slope, last_slope
    r_up[2], act, *terms = tie(r_up[2], act, *tp_terms(sums))
    act = chips_exchange(act)
    halo_lanes, even_lanes = slice(0, 4 * chans), slice(4 * chans, 8 * chans)
    grads = ()
    pieces, blocks = [(0, 0), (0, 2)], [samplers[0], samplers[2]]
    for step in range(2, steps):
        r_down.append(ring_send(r_down[step], -1))
        group = r_up[step - 1], r_down[step]
        if step == steps - 1:
            *group, act = tie(*group, act)
        sums = block_products(back_kernel, back, group)
        grads = add_gradients(
            facts, terms, slopes, pieces, blocks, grads, unit, (halo_lanes, even_lanes), False
        )
        if step < steps - 1:
            if step > 2:
                r_up[step], sums, *grads = tie(r_up[step], sums, *grads)
            r_up.append(ring_send(r_up[step], 1))
        terms = tp_terms(sums)
        pieces = [(0, 2 * step - 3), (0, 2 * step)]
        blocks = [samplers[2 * step - 3], samplers[2 * step]]
    grads = add_gradients(
        facts, terms, slopes, pieces, blocks, grads, unit, (halo_lanes, even_lanes), False
    )
    places, blocks = [0], [r_up[0]]
    for step in range(1, steps):
        places, blocks = places + [step], blocks + [r_down[step]]
        if step < steps - 1:
            places, blocks = places + [-step], blocks + [r_up[step]]
    tokens = add_tokens(facts, act, places, chips, blocks, (), unit)

    held = tie(r_up[-1], r_down[-1], *grads, *tokens)
    late, grads, tokens = held[:2], held[2:6], held[6:]
    terms = tp_terms(block_products(back_kernel, back, late))
    pieces, blocks = [(0, 2 * steps - 3), (1, 0)], [samplers[2 * steps - 3], s_last]
    halo_own, halo_mate = add_gradients(
        facts, terms, slopes, pieces, blocks, grads[:2], unit, (halo_lanes,), True
    )
    halo_mate, first_term = tie(halo_mate, terms[0])
    even_own, even_mate = add_gradients(
        facts, (first_term, terms[1]), slopes, pieces, blocks, grads[2:], unit, (even_lanes,), True
    )
    lead, facts_late = return_patches(facts, halo_own, swap_cores(halo_mate), chans, jnp.bfloat16)
    grad_odd = shifted(lead, "ctx", -1)
    grad_even, facts_late = return_patches(
        facts_late, even_own, swap_cores(even_mate), chans, jnp.float32
    )
    grad_relaxed = sum_tp(excite_grad(grad_even, grad_odd, conv, excite, squeeze_out))
    tokens, send = add_tokens(
        facts_late, act, [1 - steps, steps], chips, late, tokens, unit
    )
    llm_tokens = (tokens + swap_cores(send).astype(jnp.float32)).astype(jnp.bfloat16)
    grad_features = conv_backward(
        grad_even, grad_odd, conv, excite, squeezed, grad_relaxed, squeeze_in, group_kernel
    )
    return (llm_tokens, grad_features)


def solution(mesh):
    placed = (
        P("ctx", None, "tp"),
        P(None, "tp", None),
        P("tp", None),
        P(None, "tp"),
        P("ctx", None, "tp"),
        P("ctx", "tp"),
        P(),
        P(),
        P("ctx", "tp"),
    )
    return jax.shard_map(
        per_device,
        mesh=mesh,
        in_specs=placed,
        out_specs=(P("ctx", "tp"), P("ctx", None, "tp")),
        check_vma=False,
    )
```

```python
import functools

import jax
import jax.numpy as jnp
from jax import lax
from jax.experimental import pallas as pl
from jax.experimental.pallas import tpu as pltpu
from jax.sharding import PartitionSpec as P

SIDE = 14
OUT_SIDE = 8
WIDE = 16
FRAME_ROWS = WIDE * WIDE
EDGE = 8
LANES = 128
VMEM_BYTES = 16 * 2**20
FREE = pl.CostEstimate(flops=0, bytes_accessed=0, transcendentals=0)


def whole_call(kernel, outs, scratch, cost=FREE):
    return pl.pallas_call(
        kernel,
        out_shape=outs,
        scratch_shapes=scratch,
        compiler_params=pltpu.CompilerParams(vmem_limit_bytes=VMEM_BYTES),
        cost_estimate=cost,
    )


def contract_last(left, right):
    return lax.dot_general(
        left, right, (((1,), (1,)), ((), ())), preferred_element_type=jnp.float32
    )


def contract_exact(left, right):
    return lax.dot_general(
        left,
        right,
        (((1,), (1,)), ((), ())),
        precision=lax.Precision.HIGHEST,
        preferred_element_type=jnp.float32,
    )


def silu_slope(values):
    sigma = jax.nn.sigmoid(values)
    return sigma * (1.0 + values * (1.0 - sigma))


def inside(rows):
    row = lax.broadcasted_iota(jnp.int32, (rows, 1), 0)
    across, down = row & (WIDE - 1), (row // WIDE) & (WIDE - 1)
    good = (across >= 1) & (across <= SIDE) & (down >= 1) & (down <= SIDE)
    return good.astype(jnp.float32)


def channel_blocks(chans, width):
    span = 4 * width
    blocks = []
    for low in range(0, chans, span):
        high = min(chans, low + span)
        blocks.append((low, high, low // LANES * LANES, min(chans, -(-high // LANES) * LANES)))
    return blocks


def block_tools(block, width):
    low, high, start, end = block
    size = end - start
    out_row = lax.broadcasted_iota(jnp.int32, (size, width), 0) + start
    within = lax.broadcasted_iota(jnp.int32, (size, width), 1)
    lane = lax.broadcasted_iota(jnp.int32, (size, size), 1) + start
    row = lax.broadcasted_iota(jnp.int32, (size, size), 0) + start
    spread = jnp.zeros((size, width), jnp.float32)
    same = jnp.zeros((size, size), jnp.float32)
    for first in range(low, high, width):
        spread += (out_row == within + first).astype(jnp.float32)
        in_lane = (lane >= first) & (lane < first + width)
        in_row = (row >= first) & (row < first + width)
        same += (in_lane & in_row).astype(jnp.float32)
    return spread.astype(jnp.bfloat16), same


def dense_tap(group_ref, tap, block, spread, same):
    _, _, start, end = block
    full = jnp.dot(spread, group_ref[tap, :, start:end], preferred_element_type=jnp.float32)
    return (full * same).astype(jnp.bfloat16)


def store_shifts(wide_ref, shift_ref, sign):
    rows = shift_ref.shape[1]
    for col in range(3):
        at = EDGE + sign * (col - 1)
        shift_ref[col] = wide_ref[at : at + rows, :].astype(jnp.bfloat16)


def conv_kernel(feat_ref, group_ref, squeeze_ref, *refs):
    conv_ref, pad_ref, sq_ref, flat_ref, wide_ref, shift_ref = refs
    frames, _, chans = feat_ref.shape
    width = group_ref.shape[1]
    rows = frames * FRAME_ROWS
    wide_ref[...] = jnp.zeros_like(wide_ref)
    for frame in range(frames):
        flat_ref[...] = feat_ref[frame].astype(jnp.float32)
        for y in range(SIDE):
            at = EDGE + frame * FRAME_ROWS + (y + 1) * WIDE + 1
            wide_ref[at : at + SIDE, :] = flat_ref[y * SIDE : (y + 1) * SIDE, :]
    store_shifts(wide_ref, shift_ref, 1)
    pad_ref[...] = shift_ref[1]
    conv_ref[...] = jnp.zeros_like(conv_ref)
    body = rows - 2 * WIDE
    for block in channel_blocks(chans, width):
        _, _, start, end = block
        spread, same = block_tools(block, width)
        total = jnp.zeros((body, end - start), jnp.float32)
        for tap in range(9):
            down, across = divmod(tap, 3)
            weights = dense_tap(group_ref, tap, block, spread, same)
            source = shift_ref[across, down * WIDE : down * WIDE + body, start:end]
            total += contract_last(source, weights)
        conv_ref[WIDE : WIDE + body, start:end] += total
    conv = conv_ref[...] * inside(rows)
    conv_ref[...] = conv
    active = conv * jax.nn.sigmoid(conv)
    pooled = jnp.concatenate(
        [
            jnp.sum(active[f * FRAME_ROWS : (f + 1) * FRAME_ROWS], axis=0, keepdims=True)
            for f in range(frames)
        ],
        axis=0,
    ) * (1.0 / (SIDE * SIDE))
    sq_ref[...] = contract_exact(pooled, squeeze_ref[...].astype(jnp.float32))


def hidden_kernel(conv_ref, pad_ref, sq_ref, expand_ref, even_ref, odd_ref, excite_ref):
    squeezed = sq_ref[...]
    relaxed = squeezed * jax.nn.sigmoid(squeezed)
    excite = jax.nn.sigmoid(
        jnp.dot(relaxed, expand_ref[...].astype(jnp.float32), precision=lax.Precision.HIGHEST)
    )
    excite_ref[...] = excite
    for frame, out_ref in enumerate((even_ref, odd_ref)):
        rows = slice(frame * FRAME_ROWS, (frame + 1) * FRAME_ROWS)
        conv = conv_ref[rows, :]
        active = conv * jax.nn.sigmoid(conv)
        hidden = pad_ref[rows, :].astype(jnp.float32) + active * excite[frame : frame + 1]
        out_ref[...] = hidden.astype(jnp.bfloat16)


def select_rows(to_patches):
    shape = (FRAME_ROWS, FRAME_ROWS)
    out_row = lax.broadcasted_iota(jnp.int32, shape, 0)
    in_row = lax.broadcasted_iota(jnp.int32, shape, 1)
    patch_row, frame_row = (out_row, in_row) if to_patches else (in_row, out_row)
    down, across = patch_row >> 7, (patch_row >> 6) & 1
    a, b = (patch_row >> 3) & 7, patch_row & 7
    return ((2 * a + down) * WIDE + 2 * b + across == frame_row).astype(jnp.float32)


def facts_kernel(clip_ref, keep_ref, out_ref):
    shard = lax.axis_index("ctx")
    frames = clip_ref.shape[0]
    out_ref[0] = shard % 2
    for block in range(2):
        pair = shard // 2 * 2 + block
        clip = clip_ref[2 * pair]
        start = jnp.int32(0)
        for other in range(0, frames, 2):
            start += jnp.where(clip_ref[other] < clip, 1, 0)
        out_ref[1 + block] = keep_ref[clip] - (pair - start) * (OUT_SIDE * OUT_SIDE)
    before = clip_ref[jnp.maximum(2 * shard - 1, 0)]
    chip, chips = shard // 2, lax.axis_size("ctx") // 2
    out_ref[4] = jnp.where(chip % 2 == 0, chip // 2, chips - 1 - chip // 2)
    out_ref[3] = jnp.where((shard > 0) & (before == clip_ref[2 * shard]), 1, 0)


def token_place(row, core, unit):
    per_block = OUT_SIDE * OUT_SIDE
    within = row % per_block
    block = (within // unit) % 2
    target_core = jnp.where(row < per_block, core, 1 - core)
    return block, unit * (2 * (within // (2 * unit)) + target_core) + within % unit


def reorder_matrix(core, unit, to_sent):
    shape = (2 * OUT_SIDE * OUT_SIDE,) * 2
    out_row = lax.broadcasted_iota(jnp.int32, shape, 0)
    in_row = lax.broadcasted_iota(jnp.int32, shape, 1)
    sent, natural = (out_row, in_row) if to_sent else (in_row, out_row)
    block, token = token_place(sent, core, unit)
    source = jnp.where(block == core, 0, OUT_SIDE * OUT_SIDE) + token
    return (source == natural).astype(jnp.bfloat16)


def order_kernel(unit, facts_ref, own_ref, mate_ref, out_ref):
    rows = jnp.concatenate([own_ref[...], mate_ref[...]], axis=0)
    matrix = reorder_matrix(facts_ref[0], unit, True)
    out_ref[...] = jnp.dot(matrix, rows, preferred_element_type=jnp.float32).astype(jnp.bfloat16)


def patch_kernel(facts_ref, halo_ref, even_ref, out_ref):
    chans = halo_ref.shape[1]
    per_frame = OUT_SIDE * OUT_SIDE
    select = select_rows(True).astype(jnp.bfloat16)
    for frame, source in enumerate((halo_ref, even_ref)):
        rows = jnp.dot(select, source[...], preferred_element_type=jnp.float32)
        if frame == 0:
            rows = rows * facts_ref[3].astype(jnp.float32)
        rows = rows.astype(jnp.bfloat16)
        for tap in range(4):
            at = (frame * 4 + tap) * chans
            out_ref[:, at : at + chans] = rows[tap * per_frame : (tap + 1) * per_frame]


def unpatch_kernel(facts_ref, own_ref, mate_ref, out_ref, facts_out_ref):
    for place in range(facts_ref.shape[0]):
        facts_out_ref[place] = facts_ref[place]
    chans = out_ref.shape[1]
    rows = own_ref[...] + mate_ref[...].astype(jnp.float32)
    pieces = [rows[:, tap * chans : (tap + 1) * chans] for tap in range(4)]
    frame = jnp.dot(
        select_rows(False), jnp.concatenate(pieces, axis=0), precision=lax.Precision.HIGHEST
    ) * inside(FRAME_ROWS)
    if out_ref.dtype == jnp.bfloat16:
        frame = frame * facts_ref[3].astype(jnp.float32)
    out_ref[...] = frame.astype(out_ref.dtype)


def excite_grad_kernel(even_ref, odd_ref, conv_ref, excite_ref, expand_ref, out_ref):
    sums = []
    for frame, grad_ref in enumerate((even_ref, odd_ref)):
        conv = conv_ref[frame * FRAME_ROWS : (frame + 1) * FRAME_ROWS, :]
        active = conv * jax.nn.sigmoid(conv)
        sums.append(jnp.sum(grad_ref[...].astype(jnp.float32) * active, axis=0, keepdims=True))
    excite = excite_ref[...]
    inner = jnp.concatenate(sums, axis=0) * excite * (1.0 - excite)
    out_ref[...] = contract_exact(inner, expand_ref[...].astype(jnp.float32))


def conv_grad_kernel(
    even_ref, odd_ref, conv_ref, excite_ref, sq_ref, relaxed_ref, squeeze_ref, group_ref,
    out_ref, flat_ref, wide_ref, shift_ref, grad_ref,
):
    frames, _, chans = out_ref.shape
    width = group_ref.shape[1]
    rows = frames * FRAME_ROWS
    grad_squeezed = relaxed_ref[...] * silu_slope(sq_ref[...])
    pooled = jnp.dot(
        grad_squeezed, squeeze_ref[...].astype(jnp.float32), precision=lax.Precision.HIGHEST
    ) * (1.0 / (SIDE * SIDE))
    wide_ref[0:EDGE, :] = jnp.zeros((EDGE, chans), jnp.float32)
    wide_ref[EDGE + rows :, :] = jnp.zeros((EDGE, chans), jnp.float32)
    good = inside(FRAME_ROWS)
    for frame, source in enumerate((even_ref, odd_ref)):
        at = frame * FRAME_ROWS
        grad = source[...].astype(jnp.float32)
        grad_ref[at : at + FRAME_ROWS, :] = grad
        active = grad * excite_ref[frame : frame + 1, :] + pooled[frame : frame + 1]
        slope = silu_slope(conv_ref[at : at + FRAME_ROWS, :])
        wide_ref[EDGE + at : EDGE + at + FRAME_ROWS, :] = active * slope * good
    store_shifts(wide_ref, shift_ref, -1)
    body = rows - 2 * WIDE
    for block in channel_blocks(chans, width):
        _, _, start, end = block
        spread, same = block_tools(block, width)
        total = jnp.zeros((body, end - start), jnp.float32)
        for tap in range(9):
            down, across = divmod(tap, 3)
            weights = dense_tap(group_ref, tap, block, spread, same)
            at = (2 - down) * WIDE
            source = shift_ref[across, at : at + body, start:end]
            total += jnp.dot(source, weights, preferred_element_type=jnp.float32)
        grad_ref[WIDE : WIDE + body, start:end] += total
    for frame in range(frames):
        for y in range(SIDE):
            at = frame * FRAME_ROWS + (y + 1) * WIDE + 1
            flat_ref[y * SIDE : (y + 1) * SIDE, :] = grad_ref[at : at + SIDE, :]
        out_ref[frame] = flat_ref[...].astype(jnp.bfloat16)


def f32(*shape):
    return jax.ShapeDtypeStruct(shape, jnp.float32)


def bf16(*shape):
    return jax.ShapeDtypeStruct(shape, jnp.bfloat16)


def conv_forward(features, group_kernel, squeeze_in):
    frames, cells, chans = features.shape
    rows = frames * FRAME_ROWS
    return whole_call(
        conv_kernel,
        (f32(rows, chans), bf16(rows, chans), f32(frames, squeeze_in.shape[0])),
        [
            pltpu.VMEM((cells, chans), jnp.float32),
            pltpu.VMEM((rows + 2 * EDGE, chans), jnp.float32),
            pltpu.VMEM((3, rows, chans), jnp.bfloat16),
        ],
    )(features, group_kernel, squeeze_in)


def hidden_frames(conv, padded, squeezed, squeeze_out):
    rows, chans = conv.shape
    return whole_call(
        hidden_kernel,
        (bf16(FRAME_ROWS, chans), bf16(FRAME_ROWS, chans), f32(rows // FRAME_ROWS, chans)),
        [],
    )(conv, padded, squeezed, squeeze_out)


def vmem_specs(count):
    return [pl.BlockSpec(memory_space=pltpu.SMEM)] + [pl.BlockSpec(memory_space=pltpu.VMEM)] * count


def facts_of(frame_clip, clip_keep):
    smem = pl.BlockSpec(memory_space=pltpu.SMEM)
    return pl.pallas_call(
        facts_kernel,
        out_shape=jax.ShapeDtypeStruct((5,), jnp.int32),
        in_specs=[smem, smem],
        out_specs=smem,
        cost_estimate=FREE,
    )(frame_clip, clip_keep)


def order_rows(facts, own, mate, unit):
    rows, columns = own.shape
    return pl.pallas_call(
        functools.partial(order_kernel, unit),
        out_shape=bf16(2 * rows, columns),
        in_specs=vmem_specs(2),
        compiler_params=pltpu.CompilerParams(vmem_limit_bytes=VMEM_BYTES),
        cost_estimate=FREE,
    )(facts, own, mate)


def take_patches(facts, halo, even):
    chans = even.shape[1]
    return pl.pallas_call(
        patch_kernel,
        out_shape=bf16(OUT_SIDE * OUT_SIDE, 8 * chans),
        in_specs=vmem_specs(2),
        compiler_params=pltpu.CompilerParams(vmem_limit_bytes=VMEM_BYTES),
        cost_estimate=FREE,
    )(facts, halo, even)


def return_patches(facts, own, mate, chans, dtype):
    return pl.pallas_call(
        unpatch_kernel,
        out_shape=(
            jax.ShapeDtypeStruct((FRAME_ROWS, chans), dtype),
            jax.ShapeDtypeStruct(facts.shape, jnp.int32),
        ),
        in_specs=vmem_specs(2),
        out_specs=vmem_specs(1)[::-1],
        compiler_params=pltpu.CompilerParams(vmem_limit_bytes=VMEM_BYTES),
        cost_estimate=FREE,
    )(facts, own, mate)


def excite_grad(even, odd, conv, excite, squeeze_out):
    rows, chans = conv.shape
    return whole_call(
        excite_grad_kernel,
        f32(rows // FRAME_ROWS, squeeze_out.shape[0]),
        [],
    )(even, odd, conv, excite, squeeze_out)


def conv_backward(even, odd, conv, excite, squeezed, grad_relaxed, squeeze_in, group_kernel):
    rows, chans = conv.shape
    frames = rows // FRAME_ROWS
    return whole_call(
        conv_grad_kernel,
        bf16(frames, SIDE * SIDE, chans),
        [
            pltpu.VMEM((SIDE * SIDE, chans), jnp.float32),
            pltpu.VMEM((rows + 2 * EDGE, chans), jnp.float32),
            pltpu.VMEM((3, rows, chans), jnp.bfloat16),
            pltpu.VMEM((rows, chans), jnp.float32),
        ],
        pl.CostEstimate(flops=rows * chans * 9216, bytes_accessed=16 * rows * chans, transcendentals=0),
    )(even, odd, conv, excite, squeezed, grad_relaxed, squeeze_in, group_kernel)


def shifted(value, axis, by):
    count = lax.axis_size(axis)
    pairs = [(i, i + by) for i in range(count) if 0 <= i + by < count]
    return lax.ppermute(value, axis, pairs)


def ring_order(chips):
    return list(range(0, chips, 2)) + list(range(1, chips, 2))[::-1]


def ring_pairs(count, by):
    order = ring_order(count // 2)
    pairs = []
    for place, chip in enumerate(order):
        target = order[(place + by) % len(order)]
        pairs += [(2 * chip, 2 * target), (2 * chip + 1, 2 * target + 1)]
    return pairs


def swap_cores(value):
    return lax.ppermute(value, "ctx", [(i, i ^ 1) for i in range(lax.axis_size("ctx"))])


def tp_terms(value):
    size = lax.axis_size("tp")
    reach, other = 1, None
    while reach < size:
        value = value if other is None else value + other
        other = lax.ppermute(value, "tp", [(i, i ^ reach) for i in range(size)])
        reach *= 2
    return value, jnp.zeros_like(value) if other is None else other


def sum_tp(value):
    value, other = tp_terms(value)
    return value + other


def ring_send(value, by):
    return lax.ppermute(value, "ctx", ring_pairs(lax.axis_size("ctx"), by))


def tie(*values):
    return lax.optimization_barrier(values)


def pre_kernel(patch_ref, *refs):
    *blocks, out_ref = refs
    products = [contract_last(patch_ref[...], ref[...]) for ref in blocks]
    out_ref[...] = jnp.concatenate(products, axis=1)


def back_kernel(keep_ref, send_ref, *refs):
    *blocks, out_ref = refs
    back = jnp.concatenate([keep_ref[...], send_ref[...]], axis=0)
    out_ref[...] = jnp.concatenate([contract_last(back, ref[...]) for ref in blocks], axis=1)


def late_kernel(facts_ref, keep_ref, send_ref, *refs):
    *refs, out_ref, facts_out_ref = refs
    for place in range(facts_ref.shape[0]):
        facts_out_ref[place] = facts_ref[place]
    back_kernel(keep_ref, send_ref, *refs, out_ref)


def live_rows(facts_ref, rows, unit):
    block, token = token_place(
        lax.broadcasted_iota(jnp.int32, (rows, 1), 0), facts_ref[0], unit
    )
    return (token < jnp.where(block == 0, facts_ref[1], facts_ref[2])).astype(jnp.float32)


def totals_kernel(pieces, unit, parts, first, facts_ref, *refs):
    grad_act = refs[0][...] + refs[1][...]
    count = len(pieces)
    slopes, blocks = refs[2:4], refs[4 : 4 + count]
    before, after = refs[4 + count : -2 * len(parts)], refs[-2 * len(parts) :]
    rows, width = grad_act.shape[0], blocks[0].shape[0]
    matrix = reorder_matrix(facts_ref[0], unit, False)
    factors = []
    for place, (source, index) in enumerate(pieces):
        piece = grad_act[:, place * width : (place + 1) * width]
        piece = piece * slopes[source][:, index * width : (index + 1) * width]
        piece = jnp.dot(matrix, piece.astype(jnp.bfloat16), preferred_element_type=jnp.float32)
        factors.append(piece.astype(jnp.bfloat16))
    for part, lanes in enumerate(parts):
        total = 0.0
        for factor, ref in zip(factors, blocks):
            total += jnp.dot(factor, ref[:, lanes], preferred_element_type=jnp.float32)
        for half in range(2):
            value = total[half * rows // 2 : (half + 1) * rows // 2]
            value = value if first else before[2 * part + half][...] + value
            ref = after[2 * part + half]
            ref[...] = value.astype(ref.dtype)


def ring_offsets(chips):
    offsets = [0]
    for step in range(1, chips // 2):
        offsets += [-step, step]
    return offsets + [chips // 2]


def block_columns(facts_ref, offset, chips, width):
    shape = (width, chips * width)
    place = (facts_ref[4] + offset + chips) % chips
    column = lax.broadcasted_iota(jnp.int32, shape, 1)
    return (column == lax.broadcasted_iota(jnp.int32, shape, 0) + place * width).astype(jnp.bfloat16)


def exchange_matrix(core, unit, to_sent):
    per_block = OUT_SIDE * OUT_SIDE
    shape = (2 * per_block,) * 2
    out_row = lax.broadcasted_iota(jnp.int32, shape, 0)
    in_row = lax.broadcasted_iota(jnp.int32, shape, 1)
    sent, kept = (out_row, in_row) if to_sent else (in_row, out_row)
    target_core = (sent // (2 * unit)) % 2
    within = sent // (4 * unit) * (2 * unit) + sent % (2 * unit)
    return (within + jnp.where(target_core == core, 0, per_block) == kept).astype(jnp.bfloat16)


def act_kernel(offsets, chips, unit, last, facts_ref, own_ref, other_ref, *refs):
    *before, slope_ref, out_ref = refs
    pre = own_ref[...] + other_ref[...]
    width = pre.shape[1] // len(offsets)
    live = live_rows(facts_ref, pre.shape[0], unit)
    sigma = jax.nn.sigmoid(pre)
    slope_ref[...] = sigma * (1.0 + pre * (1.0 - sigma)) * live
    act = (pre * sigma * live).astype(jnp.bfloat16)
    total = before[0][...].astype(jnp.float32) if last else 0.0
    for place, offset in enumerate(offsets):
        columns = block_columns(facts_ref, offset, chips, width)
        piece = act[:, place * width : (place + 1) * width]
        total += jnp.dot(piece, columns, preferred_element_type=jnp.float32)
    total = total.astype(jnp.bfloat16)
    if last:
        matrix = exchange_matrix(facts_ref[0], unit, True)
        total = jnp.dot(matrix, total, preferred_element_type=jnp.float32).astype(jnp.bfloat16)
    out_ref[...] = total


def token_kernel(offsets, chips, unit, facts_ref, act_ref, *refs):
    count = len(offsets)
    blocks, refs = refs[:count], refs[count:]
    keep_ref, send_ref, *buffers, sems = refs
    copies = [
        pltpu.make_async_copy(ref, buffer, sems.at[place])
        for place, (ref, buffer) in enumerate(zip(blocks, buffers))
    ]
    for copy in copies:
        copy.start()
    width = buffers[0].shape[0]
    matrix = exchange_matrix(facts_ref[0], unit, False)
    act = jnp.dot(matrix, act_ref[...], preferred_element_type=jnp.float32).astype(jnp.bfloat16)
    total = 0.0
    for offset, copy, buffer in zip(offsets, copies, buffers):
        columns = block_columns(facts_ref, offset, chips, width)
        piece = contract_last(act, columns).astype(jnp.bfloat16)
        copy.wait()
        total += jnp.dot(piece, buffer[...], preferred_element_type=jnp.float32)
    rows = keep_ref.shape[0]
    keep_ref[...] = total[:rows]
    send_ref[...] = total[rows:].astype(jnp.bfloat16)


def block_products(kernel, left, blocks):
    rows = 2 * OUT_SIDE * OUT_SIDE
    return whole_call(kernel, f32(rows, len(blocks) * blocks[0].shape[0]), [])(*left, *blocks)


def late_products(facts, back, blocks):
    rows = 2 * OUT_SIDE * OUT_SIDE
    return pl.pallas_call(
        late_kernel,
        out_shape=(
            f32(rows, len(blocks) * blocks[0].shape[0]),
            jax.ShapeDtypeStruct(facts.shape, jnp.int32),
        ),
        in_specs=vmem_specs(2 + len(blocks)),
        out_specs=vmem_specs(1)[::-1],
        compiler_params=pltpu.CompilerParams(vmem_limit_bytes=VMEM_BYTES),
        cost_estimate=FREE,
    )(facts, *back, *blocks)


def facts_call(kernel, outs, facts, operands, cost=FREE):
    return pl.pallas_call(
        kernel,
        out_shape=outs,
        in_specs=vmem_specs(len(operands)),
        compiler_params=pltpu.CompilerParams(vmem_limit_bytes=VMEM_BYTES),
        cost_estimate=cost,
    )(facts, *operands)


def add_gradients(facts, terms, slopes, pieces, blocks, before, unit, parts, last):
    rows = terms[0].shape[0] // 2
    kernel = functools.partial(totals_kernel, pieces, unit, parts, not before)
    outs = ()
    for lanes in parts:
        shape = rows, lanes.stop - lanes.start
        outs += f32(*shape), (bf16 if last else f32)(*shape)
    return tuple(facts_call(kernel, outs, facts, (*terms, *slopes, *blocks, *before)))


def act_and_slope(facts, terms, offsets, chips, before, unit):
    rows, columns = terms[0].shape
    kernel = functools.partial(act_kernel, offsets, chips, unit, bool(before))
    outs = f32(rows, columns), bf16(rows, columns // len(offsets) * chips)
    return facts_call(kernel, outs, facts, (*terms, *before))


def token_products(facts, act, offsets, chips, blocks, unit):
    rows, columns = act.shape[0] // 2, blocks[0].shape[1]
    return pl.pallas_call(
        functools.partial(token_kernel, offsets, chips, unit),
        out_shape=(f32(rows, columns), bf16(rows, columns)),
        in_specs=vmem_specs(1) + [pl.BlockSpec(memory_space=pl.ANY)] * len(blocks),
        scratch_shapes=[pltpu.VMEM(block.shape, block.dtype) for block in blocks]
        + [pltpu.SemaphoreType.DMA((len(blocks),))],
        compiler_params=pltpu.CompilerParams(vmem_limit_bytes=VMEM_BYTES),
        cost_estimate=FREE,
    )(facts, act, *blocks)


def chips_exchange(value):
    count = lax.axis_size("ctx")
    groups = [list(range(core, count, 2)) for core in range(2)]
    return lax.all_to_all(
        value, "ctx", split_axis=0, concat_axis=0, tiled=True, axis_index_groups=groups
    )


def per_device(
    features,
    group_kernel,
    squeeze_in,
    squeeze_out,
    sampler_kernel,
    readout_kernel,
    frame_clip,
    clip_keep,
    token_cotangent,
):
    chans = features.shape[2]
    count = lax.axis_size("ctx")
    steps, unit = count // 4, OUT_SIDE * OUT_SIDE // count
    flat_sampler = sampler_kernel.reshape(sampler_kernel.shape[0], 8 * chans)
    chips = count // 2
    s_up, s_down = ring_send(flat_sampler, 1), ring_send(flat_sampler, -1)
    group_kernel = jnp.swapaxes(group_kernel, 1, 2)
    squeeze_in = squeeze_in.T
    facts = facts_of(frame_clip, clip_keep)

    conv, padded, squeezed = conv_forward(features, group_kernel, squeeze_in)
    token_cotangent, squeezed = tie(token_cotangent, squeezed)
    back = chips_exchange(token_cotangent)
    squeezed = sum_tp(squeezed)
    even, odd, excite = hidden_frames(conv, padded, squeezed, squeeze_out)
    halo = shifted(odd, "ctx", 1)

    s_up, s_down = [flat_sampler, s_up], [flat_sampler, s_down]
    s_up[1], s_down[1], even, readout_kernel = tie(s_up[1], s_down[1], even, readout_kernel)
    for step in range(2, steps):
        s_up.append(ring_send(s_up[-1], 1))
        s_down.append(ring_send(s_down[-1], -1))
        if step == 2:
            halo, s_up[2], s_down[2] = tie(halo, s_up[2], s_down[2])
            r_down = [readout_kernel, ring_send(readout_kernel, -1)]
            patches = take_patches(facts, halo, even)
            patches = order_rows(facts, patches, swap_cores(patches), unit)
    s_up[-1], s_down[-1], back, readout_kernel = tie(s_up[-1], s_down[-1], back, readout_kernel)
    back = (back, swap_cores(back))
    s_last = ring_send(s_up[-1], 1)
    r_up = [readout_kernel, ring_send(readout_kernel, 1)]
    samplers = [flat_sampler] + [block for pair in zip(s_up[1:], s_down[1:]) for block in pair]
    offsets = ring_offsets(chips)
    count = 2 * steps - 3
    first_pre = tp_terms(block_products(pre_kernel, (patches,), samplers[:count]))
    r_down[1], s_last, *first_pre = tie(r_down[1], s_last, *first_pre)
    for step in range(1, steps - 2):
        r_down.append(ring_send(r_down[-1], -1))
        r_up.append(ring_send(r_up[-1], 1))
    first_slope, first_act = act_and_slope(facts, first_pre, offsets[:count], chips, (), unit)
    last_pre = block_products(pre_kernel, (patches,), [*samplers[count:], s_last])
    last_slope, act = act_and_slope(
        facts, tp_terms(last_pre), offsets[count:], chips, (first_act,), unit
    )
    slopes = first_slope, last_slope
    r_down[-1], act = tie(r_down[-1], act)
    r_down.append(ring_send(r_down[-1], -1))
    early = r_down[: steps - 1]
    sums = block_products(back_kernel, back, early)
    r_up[-1], act, sums = tie(r_up[-1], act, sums)
    r_up.append(ring_send(r_up[-1], 1))
    act = chips_exchange(act)
    halo_lanes, even_lanes = slice(0, 4 * chans), slice(4 * chans, 8 * chans)
    both = halo_lanes, even_lanes
    terms = tp_terms(sums)
    pieces = [(0, 2 * step) for step in range(steps - 1)]
    blocks = [flat_sampler] + s_down[1 : steps - 1]
    grads = add_gradients(facts, terms, slopes, pieces, blocks, (), unit, both, False)
    middle = r_up[1 : steps - 1] + [r_down[steps - 1]]
    *middle, act = tie(*middle, act)
    r_down.append(ring_send(r_down[-1], -1))
    terms = tp_terms(block_products(back_kernel, back, middle))
    pieces = [(0, 2 * step - 1) for step in range(1, steps - 1)] + [(1, 1)]
    blocks = s_up[1 : steps - 1] + [s_down[steps - 1]]
    grads = add_gradients(facts, terms, slopes, pieces, blocks, grads, unit, both, False)

    late_up, late_down, *grads = tie(r_up[-1], r_down[-1], *grads)
    sums, facts_late = late_products(facts, back, [late_up, late_down])
    terms = tp_terms(sums)
    places = [*range(steps - 1), *range(-1, 1 - steps, -1), steps - 1, 1 - steps, steps]
    tokens = token_products(
        facts_late, act, places, chips, [*early, *middle, late_up, late_down], unit
    )
    other_term, *tokens = tie(terms[1], *tokens)
    terms = terms[0], other_term
    pieces, blocks = [(1, 0), (1, 2)], [s_up[-1], s_last]
    halo_own, halo_mate = add_gradients(
        facts, terms, slopes, pieces, blocks, grads[:2], unit, (halo_lanes,), True
    )
    halo_mate, first_term = tie(halo_mate, terms[0])
    even_own, even_mate = add_gradients(
        facts, (first_term, terms[1]), slopes, pieces, blocks, grads[2:], unit, (even_lanes,), True
    )
    lead, facts_late = return_patches(facts, halo_own, swap_cores(halo_mate), chans, jnp.bfloat16)
    grad_odd = shifted(lead, "ctx", -1)
    grad_even, _ = return_patches(
        facts_late, even_own, swap_cores(even_mate), chans, jnp.float32
    )
    grad_relaxed = sum_tp(excite_grad(grad_even, grad_odd, conv, excite, squeeze_out))
    llm_tokens = (tokens[0] + swap_cores(tokens[1]).astype(jnp.float32)).astype(jnp.bfloat16)
    grad_features = conv_backward(
        grad_even, grad_odd, conv, excite, squeezed, grad_relaxed, squeeze_in, group_kernel
    )
    return (llm_tokens, grad_features)


def solution(mesh):
    placed = (
        P("ctx", None, "tp"),
        P(None, "tp", None),
        P("tp", None),
        P(None, "tp"),
        P("ctx", None, "tp"),
        P("ctx", "tp"),
        P(),
        P(),
        P("ctx", "tp"),
    )
    return jax.shard_map(
        per_device,
        mesh=mesh,
        in_specs=placed,
        out_specs=(P("ctx", "tp"), P("ctx", None, "tp")),
        check_vma=False,
    )
```

```python
import functools

import jax
import jax.numpy as jnp
from jax import lax
from jax.experimental import pallas as pl
from jax.experimental.pallas import tpu as pltpu
from jax.sharding import PartitionSpec as P

SIDE = 14
OUT_SIDE = 8
WIDE = 16
FRAME_ROWS = WIDE * WIDE
EDGE = 8
LANES = 128
VMEM_BYTES = 16 * 2**20
FREE = pl.CostEstimate(flops=0, bytes_accessed=0, transcendentals=0)


def whole_call(kernel, outs, scratch, cost=FREE):
    return pl.pallas_call(
        kernel,
        out_shape=outs,
        scratch_shapes=scratch,
        compiler_params=pltpu.CompilerParams(vmem_limit_bytes=VMEM_BYTES),
        cost_estimate=cost,
    )


def contract_last(left, right):
    return lax.dot_general(
        left, right, (((1,), (1,)), ((), ())), preferred_element_type=jnp.float32
    )


def contract_exact(left, right):
    return lax.dot_general(
        left,
        right,
        (((1,), (1,)), ((), ())),
        precision=lax.Precision.HIGHEST,
        preferred_element_type=jnp.float32,
    )


def silu_slope(values):
    sigma = jax.nn.sigmoid(values)
    return sigma * (1.0 + values * (1.0 - sigma))


def inside(rows):
    row = lax.broadcasted_iota(jnp.int32, (rows, 1), 0)
    across, down = row & (WIDE - 1), (row // WIDE) & (WIDE - 1)
    good = (across >= 1) & (across <= SIDE) & (down >= 1) & (down <= SIDE)
    return good.astype(jnp.float32)


def channel_blocks(chans, width):
    span = 4 * width
    blocks = []
    for low in range(0, chans, span):
        high = min(chans, low + span)
        blocks.append((low, high, low // LANES * LANES, min(chans, -(-high // LANES) * LANES)))
    return blocks


def block_tools(block, width):
    low, high, start, end = block
    size = end - start
    out_row = lax.broadcasted_iota(jnp.int32, (size, width), 0) + start
    within = lax.broadcasted_iota(jnp.int32, (size, width), 1)
    lane = lax.broadcasted_iota(jnp.int32, (size, size), 1) + start
    row = lax.broadcasted_iota(jnp.int32, (size, size), 0) + start
    spread = jnp.zeros((size, width), jnp.float32)
    same = jnp.zeros((size, size), jnp.float32)
    for first in range(low, high, width):
        spread += (out_row == within + first).astype(jnp.float32)
        in_lane = (lane >= first) & (lane < first + width)
        in_row = (row >= first) & (row < first + width)
        same += (in_lane & in_row).astype(jnp.float32)
    return spread.astype(jnp.bfloat16), same


def dense_tap(group_ref, tap, block, spread, same):
    _, _, start, end = block
    full = jnp.dot(spread, group_ref[tap, :, start:end], preferred_element_type=jnp.float32)
    return (full * same).astype(jnp.bfloat16)


def store_shifts(wide_ref, shift_ref, sign):
    rows = shift_ref.shape[1]
    for col in range(3):
        at = EDGE + sign * (col - 1)
        shift_ref[col] = wide_ref[at : at + rows, :].astype(jnp.bfloat16)


def conv_kernel(feat_ref, group_ref, squeeze_ref, *refs):
    conv_ref, pad_ref, sq_ref, flat_ref, wide_ref, shift_ref = refs
    frames, _, chans = feat_ref.shape
    width = group_ref.shape[1]
    rows = frames * FRAME_ROWS
    wide_ref[...] = jnp.zeros_like(wide_ref)
    for frame in range(frames):
        flat_ref[...] = feat_ref[frame].astype(jnp.float32)
        for y in range(SIDE):
            at = EDGE + frame * FRAME_ROWS + (y + 1) * WIDE + 1
            wide_ref[at : at + SIDE, :] = flat_ref[y * SIDE : (y + 1) * SIDE, :]
    store_shifts(wide_ref, shift_ref, 1)
    pad_ref[...] = shift_ref[1]
    conv_ref[...] = jnp.zeros_like(conv_ref)
    body = rows - 2 * WIDE
    for block in channel_blocks(chans, width):
        _, _, start, end = block
        spread, same = block_tools(block, width)
        total = jnp.zeros((body, end - start), jnp.float32)
        for tap in range(9):
            down, across = divmod(tap, 3)
            weights = dense_tap(group_ref, tap, block, spread, same)
            source = shift_ref[across, down * WIDE : down * WIDE + body, start:end]
            total += contract_last(source, weights)
        conv_ref[WIDE : WIDE + body, start:end] += total
    conv = conv_ref[...] * inside(rows)
    conv_ref[...] = conv
    active = conv * jax.nn.sigmoid(conv)
    pooled = jnp.concatenate(
        [
            jnp.sum(active[f * FRAME_ROWS : (f + 1) * FRAME_ROWS], axis=0, keepdims=True)
            for f in range(frames)
        ],
        axis=0,
    ) * (1.0 / (SIDE * SIDE))
    sq_ref[...] = contract_exact(pooled, squeeze_ref[...].astype(jnp.float32))


def hidden_kernel(conv_ref, pad_ref, sq_ref, expand_ref, even_ref, odd_ref, excite_ref):
    squeezed = sq_ref[...]
    relaxed = squeezed * jax.nn.sigmoid(squeezed)
    excite = jax.nn.sigmoid(
        jnp.dot(relaxed, expand_ref[...].astype(jnp.float32), precision=lax.Precision.HIGHEST)
    )
    excite_ref[...] = excite
    for frame, out_ref in enumerate((even_ref, odd_ref)):
        rows = slice(frame * FRAME_ROWS, (frame + 1) * FRAME_ROWS)
        conv = conv_ref[rows, :]
        active = conv * jax.nn.sigmoid(conv)
        hidden = pad_ref[rows, :].astype(jnp.float32) + active * excite[frame : frame + 1]
        out_ref[...] = hidden.astype(jnp.bfloat16)


def select_rows(to_patches):
    shape = (FRAME_ROWS, FRAME_ROWS)
    out_row = lax.broadcasted_iota(jnp.int32, shape, 0)
    in_row = lax.broadcasted_iota(jnp.int32, shape, 1)
    patch_row, frame_row = (out_row, in_row) if to_patches else (in_row, out_row)
    down, across = patch_row >> 7, (patch_row >> 6) & 1
    a, b = (patch_row >> 3) & 7, patch_row & 7
    return ((2 * a + down) * WIDE + 2 * b + across == frame_row).astype(jnp.float32)


def facts_kernel(clip_ref, keep_ref, out_ref):
    shard = lax.axis_index("ctx")
    frames = clip_ref.shape[0]
    out_ref[0] = shard % 2
    for block in range(2):
        pair = shard // 2 * 2 + block
        clip = clip_ref[2 * pair]
        start = jnp.int32(0)
        for other in range(0, frames, 2):
            start += jnp.where(clip_ref[other] < clip, 1, 0)
        out_ref[1 + block] = keep_ref[clip] - (pair - start) * (OUT_SIDE * OUT_SIDE)
    before = clip_ref[jnp.maximum(2 * shard - 1, 0)]
    chip, chips = shard // 2, lax.axis_size("ctx") // 2
    out_ref[4] = jnp.where(chip % 2 == 0, chip // 2, chips - 1 - chip // 2)
    out_ref[3] = jnp.where((shard > 0) & (before == clip_ref[2 * shard]), 1, 0)


def token_place(row, core, unit):
    per_block = OUT_SIDE * OUT_SIDE
    within = row % per_block
    block = (within // unit) % 2
    target_core = jnp.where(row < per_block, core, 1 - core)
    return block, unit * (2 * (within // (2 * unit)) + target_core) + within % unit


def reorder_matrix(core, unit, to_sent):
    shape = (2 * OUT_SIDE * OUT_SIDE,) * 2
    out_row = lax.broadcasted_iota(jnp.int32, shape, 0)
    in_row = lax.broadcasted_iota(jnp.int32, shape, 1)
    sent, natural = (out_row, in_row) if to_sent else (in_row, out_row)
    block, token = token_place(sent, core, unit)
    source = jnp.where(block == core, 0, OUT_SIDE * OUT_SIDE) + token
    return (source == natural).astype(jnp.bfloat16)


def order_kernel(unit, facts_ref, own_ref, mate_ref, out_ref):
    rows = jnp.concatenate([own_ref[...], mate_ref[...]], axis=0)
    matrix = reorder_matrix(facts_ref[0], unit, True)
    out_ref[...] = jnp.dot(matrix, rows, preferred_element_type=jnp.float32).astype(jnp.bfloat16)


def patch_kernel(facts_ref, halo_ref, even_ref, out_ref):
    chans = halo_ref.shape[1]
    per_frame = OUT_SIDE * OUT_SIDE
    select = select_rows(True).astype(jnp.bfloat16)
    for frame, source in enumerate((halo_ref, even_ref)):
        rows = jnp.dot(select, source[...], preferred_element_type=jnp.float32)
        if frame == 0:
            rows = rows * facts_ref[3].astype(jnp.float32)
        rows = rows.astype(jnp.bfloat16)
        for tap in range(4):
            at = (frame * 4 + tap) * chans
            out_ref[:, at : at + chans] = rows[tap * per_frame : (tap + 1) * per_frame]


def unpatch_kernel(facts_ref, own_ref, mate_ref, out_ref, facts_out_ref):
    for place in range(facts_ref.shape[0]):
        facts_out_ref[place] = facts_ref[place]
    chans = out_ref.shape[1]
    rows = own_ref[...] + mate_ref[...].astype(jnp.float32)
    pieces = [rows[:, tap * chans : (tap + 1) * chans] for tap in range(4)]
    frame = jnp.dot(
        select_rows(False), jnp.concatenate(pieces, axis=0), precision=lax.Precision.HIGHEST
    ) * inside(FRAME_ROWS)
    if out_ref.dtype == jnp.bfloat16:
        frame = frame * facts_ref[3].astype(jnp.float32)
    out_ref[...] = frame.astype(out_ref.dtype)


def excite_grad_kernel(even_ref, odd_ref, conv_ref, excite_ref, expand_ref, out_ref):
    sums = []
    for frame, grad_ref in enumerate((even_ref, odd_ref)):
        conv = conv_ref[frame * FRAME_ROWS : (frame + 1) * FRAME_ROWS, :]
        active = conv * jax.nn.sigmoid(conv)
        sums.append(jnp.sum(grad_ref[...].astype(jnp.float32) * active, axis=0, keepdims=True))
    excite = excite_ref[...]
    inner = jnp.concatenate(sums, axis=0) * excite * (1.0 - excite)
    out_ref[...] = contract_exact(inner, expand_ref[...].astype(jnp.float32))


def conv_grad_kernel(
    even_ref, odd_ref, conv_ref, excite_ref, sq_ref, relaxed_ref, squeeze_ref, group_ref,
    out_ref, flat_ref, wide_ref, shift_ref, grad_ref,
):
    frames, _, chans = out_ref.shape
    width = group_ref.shape[1]
    rows = frames * FRAME_ROWS
    grad_squeezed = relaxed_ref[...] * silu_slope(sq_ref[...])
    pooled = jnp.dot(
        grad_squeezed, squeeze_ref[...].astype(jnp.float32), precision=lax.Precision.HIGHEST
    ) * (1.0 / (SIDE * SIDE))
    wide_ref[0:EDGE, :] = jnp.zeros((EDGE, chans), jnp.float32)
    wide_ref[EDGE + rows :, :] = jnp.zeros((EDGE, chans), jnp.float32)
    good = inside(FRAME_ROWS)
    for frame, source in enumerate((even_ref, odd_ref)):
        at = frame * FRAME_ROWS
        grad = source[...].astype(jnp.float32)
        grad_ref[at : at + FRAME_ROWS, :] = grad
        active = grad * excite_ref[frame : frame + 1, :] + pooled[frame : frame + 1]
        slope = silu_slope(conv_ref[at : at + FRAME_ROWS, :])
        wide_ref[EDGE + at : EDGE + at + FRAME_ROWS, :] = active * slope * good
    store_shifts(wide_ref, shift_ref, -1)
    body = rows - 2 * WIDE
    for block in channel_blocks(chans, width):
        _, _, start, end = block
        spread, same = block_tools(block, width)
        total = jnp.zeros((body, end - start), jnp.float32)
        for tap in range(9):
            down, across = divmod(tap, 3)
            weights = dense_tap(group_ref, tap, block, spread, same)
            at = (2 - down) * WIDE
            source = shift_ref[across, at : at + body, start:end]
            total += jnp.dot(source, weights, preferred_element_type=jnp.float32)
        grad_ref[WIDE : WIDE + body, start:end] += total
    for frame in range(frames):
        for y in range(SIDE):
            at = frame * FRAME_ROWS + (y + 1) * WIDE + 1
            flat_ref[y * SIDE : (y + 1) * SIDE, :] = grad_ref[at : at + SIDE, :]
        out_ref[frame] = flat_ref[...].astype(jnp.bfloat16)


def f32(*shape):
    return jax.ShapeDtypeStruct(shape, jnp.float32)


def bf16(*shape):
    return jax.ShapeDtypeStruct(shape, jnp.bfloat16)


def conv_forward(features, group_kernel, squeeze_in):
    frames, cells, chans = features.shape
    rows = frames * FRAME_ROWS
    return whole_call(
        conv_kernel,
        (f32(rows, chans), bf16(rows, chans), f32(frames, squeeze_in.shape[0])),
        [
            pltpu.VMEM((cells, chans), jnp.float32),
            pltpu.VMEM((rows + 2 * EDGE, chans), jnp.float32),
            pltpu.VMEM((3, rows, chans), jnp.bfloat16),
        ],
    )(features, group_kernel, squeeze_in)


def hidden_frames(conv, padded, squeezed, squeeze_out):
    rows, chans = conv.shape
    return whole_call(
        hidden_kernel,
        (bf16(FRAME_ROWS, chans), bf16(FRAME_ROWS, chans), f32(rows // FRAME_ROWS, chans)),
        [],
    )(conv, padded, squeezed, squeeze_out)


def vmem_specs(count):
    return [pl.BlockSpec(memory_space=pltpu.SMEM)] + [pl.BlockSpec(memory_space=pltpu.VMEM)] * count


def facts_of(frame_clip, clip_keep):
    smem = pl.BlockSpec(memory_space=pltpu.SMEM)
    return pl.pallas_call(
        facts_kernel,
        out_shape=jax.ShapeDtypeStruct((5,), jnp.int32),
        in_specs=[smem, smem],
        out_specs=smem,
        cost_estimate=FREE,
    )(frame_clip, clip_keep)


def order_rows(facts, own, mate, unit):
    rows, columns = own.shape
    return pl.pallas_call(
        functools.partial(order_kernel, unit),
        out_shape=bf16(2 * rows, columns),
        in_specs=vmem_specs(2),
        compiler_params=pltpu.CompilerParams(vmem_limit_bytes=VMEM_BYTES),
        cost_estimate=FREE,
    )(facts, own, mate)


def take_patches(facts, halo, even):
    chans = even.shape[1]
    return pl.pallas_call(
        patch_kernel,
        out_shape=bf16(OUT_SIDE * OUT_SIDE, 8 * chans),
        in_specs=vmem_specs(2),
        compiler_params=pltpu.CompilerParams(vmem_limit_bytes=VMEM_BYTES),
        cost_estimate=FREE,
    )(facts, halo, even)


def return_patches(facts, own, mate, chans, dtype):
    return pl.pallas_call(
        unpatch_kernel,
        out_shape=(
            jax.ShapeDtypeStruct((FRAME_ROWS, chans), dtype),
            jax.ShapeDtypeStruct(facts.shape, jnp.int32),
        ),
        in_specs=vmem_specs(2),
        out_specs=vmem_specs(1)[::-1],
        compiler_params=pltpu.CompilerParams(vmem_limit_bytes=VMEM_BYTES),
        cost_estimate=FREE,
    )(facts, own, mate)


def excite_grad(even, odd, conv, excite, squeeze_out):
    rows, chans = conv.shape
    return whole_call(
        excite_grad_kernel,
        f32(rows // FRAME_ROWS, squeeze_out.shape[0]),
        [],
    )(even, odd, conv, excite, squeeze_out)


def conv_backward(even, odd, conv, excite, squeezed, grad_relaxed, squeeze_in, group_kernel):
    rows, chans = conv.shape
    frames = rows // FRAME_ROWS
    return whole_call(
        conv_grad_kernel,
        bf16(frames, SIDE * SIDE, chans),
        [
            pltpu.VMEM((SIDE * SIDE, chans), jnp.float32),
            pltpu.VMEM((rows + 2 * EDGE, chans), jnp.float32),
            pltpu.VMEM((3, rows, chans), jnp.bfloat16),
            pltpu.VMEM((rows, chans), jnp.float32),
        ],
        pl.CostEstimate(flops=rows * chans * 9216, bytes_accessed=16 * rows * chans, transcendentals=0),
    )(even, odd, conv, excite, squeezed, grad_relaxed, squeeze_in, group_kernel)


def shifted(value, axis, by):
    count = lax.axis_size(axis)
    pairs = [(i, i + by) for i in range(count) if 0 <= i + by < count]
    return lax.ppermute(value, axis, pairs)


def ring_order(chips):
    return list(range(0, chips, 2)) + list(range(1, chips, 2))[::-1]


def ring_pairs(count, by):
    order = ring_order(count // 2)
    pairs = []
    for place, chip in enumerate(order):
        target = order[(place + by) % len(order)]
        pairs += [(2 * chip, 2 * target), (2 * chip + 1, 2 * target + 1)]
    return pairs


def swap_cores(value):
    return lax.ppermute(value, "ctx", [(i, i ^ 1) for i in range(lax.axis_size("ctx"))])


def tp_terms(value):
    size = lax.axis_size("tp")
    reach, other = 1, None
    while reach < size:
        value = value if other is None else value + other
        other = lax.ppermute(value, "tp", [(i, i ^ reach) for i in range(size)])
        reach *= 2
    return value, jnp.zeros_like(value) if other is None else other


def sum_tp(value):
    value, other = tp_terms(value)
    return value + other


def ring_send(value, by):
    return lax.ppermute(value, "ctx", ring_pairs(lax.axis_size("ctx"), by))


def tie(*values):
    return lax.optimization_barrier(values)


def pre_kernel(patch_ref, *refs):
    *blocks, out_ref = refs
    products = [contract_last(patch_ref[...], ref[...]) for ref in blocks]
    out_ref[...] = jnp.concatenate(products, axis=1)


def back_kernel(keep_ref, send_ref, *refs):
    *blocks, out_ref = refs
    back = jnp.concatenate([keep_ref[...], send_ref[...]], axis=0)
    out_ref[...] = jnp.concatenate([contract_last(back, ref[...]) for ref in blocks], axis=1)


def late_kernel(facts_ref, keep_ref, send_ref, *refs):
    *refs, out_ref, facts_out_ref = refs
    for place in range(facts_ref.shape[0]):
        facts_out_ref[place] = facts_ref[place]
    back_kernel(keep_ref, send_ref, *refs, out_ref)


def live_rows(facts_ref, rows, unit):
    block, token = token_place(
        lax.broadcasted_iota(jnp.int32, (rows, 1), 0), facts_ref[0], unit
    )
    return (token < jnp.where(block == 0, facts_ref[1], facts_ref[2])).astype(jnp.float32)


def totals_kernel(pieces, unit, parts, first, facts_ref, *refs):
    grad_act = refs[0][...] + refs[1][...]
    count = len(pieces)
    slopes, blocks = refs[2:4], refs[4 : 4 + count]
    before, after = refs[4 + count : -2 * len(parts)], refs[-2 * len(parts) :]
    rows, width = grad_act.shape[0], blocks[0].shape[0]
    matrix = reorder_matrix(facts_ref[0], unit, False)
    factors = []
    for place, (source, index) in enumerate(pieces):
        piece = grad_act[:, place * width : (place + 1) * width]
        piece = piece * slopes[source][:, index * width : (index + 1) * width]
        piece = jnp.dot(matrix, piece.astype(jnp.bfloat16), preferred_element_type=jnp.float32)
        factors.append(piece.astype(jnp.bfloat16))
    for part, lanes in enumerate(parts):
        total = 0.0
        for factor, ref in zip(factors, blocks):
            total += jnp.dot(factor, ref[:, lanes], preferred_element_type=jnp.float32)
        for half in range(2):
            value = total[half * rows // 2 : (half + 1) * rows // 2]
            value = value if first else before[2 * part + half][...] + value
            ref = after[2 * part + half]
            ref[...] = value.astype(ref.dtype)


def ring_offsets(chips):
    offsets = [0]
    for step in range(1, chips // 2):
        offsets += [-step, step]
    return offsets + [chips // 2]


def block_columns(facts_ref, offset, chips, width):
    shape = (width, chips * width)
    place = (facts_ref[4] + offset + chips) % chips
    column = lax.broadcasted_iota(jnp.int32, shape, 1)
    return (column == lax.broadcasted_iota(jnp.int32, shape, 0) + place * width).astype(jnp.bfloat16)


def exchange_matrix(core, unit, to_sent):
    per_block = OUT_SIDE * OUT_SIDE
    shape = (2 * per_block,) * 2
    out_row = lax.broadcasted_iota(jnp.int32, shape, 0)
    in_row = lax.broadcasted_iota(jnp.int32, shape, 1)
    sent, kept = (out_row, in_row) if to_sent else (in_row, out_row)
    target_core = (sent // (2 * unit)) % 2
    within = sent // (4 * unit) * (2 * unit) + sent % (2 * unit)
    return (within + jnp.where(target_core == core, 0, per_block) == kept).astype(jnp.bfloat16)


def act_kernel(offsets, chips, unit, last, facts_ref, own_ref, other_ref, *refs):
    *before, slope_ref, out_ref = refs
    pre = own_ref[...] + other_ref[...]
    width = pre.shape[1] // len(offsets)
    live = live_rows(facts_ref, pre.shape[0], unit)
    sigma = jax.nn.sigmoid(pre)
    slope_ref[...] = sigma * (1.0 + pre * (1.0 - sigma)) * live
    act = (pre * sigma * live).astype(jnp.bfloat16)
    total = before[0][...].astype(jnp.float32) if last else 0.0
    for place, offset in enumerate(offsets):
        columns = block_columns(facts_ref, offset, chips, width)
        piece = act[:, place * width : (place + 1) * width]
        total += jnp.dot(piece, columns, preferred_element_type=jnp.float32)
    total = total.astype(jnp.bfloat16)
    if last:
        matrix = exchange_matrix(facts_ref[0], unit, True)
        total = jnp.dot(matrix, total, preferred_element_type=jnp.float32).astype(jnp.bfloat16)
    out_ref[...] = total


def token_kernel(offsets, chips, unit, facts_ref, act_ref, *refs):
    count = len(offsets)
    blocks, refs = refs[:count], refs[count:]
    keep_ref, send_ref, *buffers, sems = refs
    copies = [
        pltpu.make_async_copy(ref, buffer, sems.at[place])
        for place, (ref, buffer) in enumerate(zip(blocks, buffers))
    ]
    for copy in copies:
        copy.start()
    width = buffers[0].shape[0]
    matrix = exchange_matrix(facts_ref[0], unit, False)
    act = jnp.dot(matrix, act_ref[...], preferred_element_type=jnp.float32).astype(jnp.bfloat16)
    total = 0.0
    for offset, copy, buffer in zip(offsets, copies, buffers):
        columns = block_columns(facts_ref, offset, chips, width)
        piece = contract_last(act, columns).astype(jnp.bfloat16)
        copy.wait()
        total += jnp.dot(piece, buffer[...], preferred_element_type=jnp.float32)
    rows = keep_ref.shape[0]
    keep_ref[...] = total[:rows]
    send_ref[...] = total[rows:].astype(jnp.bfloat16)


def block_products(kernel, left, blocks):
    rows = 2 * OUT_SIDE * OUT_SIDE
    return whole_call(kernel, f32(rows, len(blocks) * blocks[0].shape[0]), [])(*left, *blocks)


def late_products(facts, back, blocks):
    rows = 2 * OUT_SIDE * OUT_SIDE
    return pl.pallas_call(
        late_kernel,
        out_shape=(
            f32(rows, len(blocks) * blocks[0].shape[0]),
            jax.ShapeDtypeStruct(facts.shape, jnp.int32),
        ),
        in_specs=vmem_specs(2 + len(blocks)),
        out_specs=vmem_specs(1)[::-1],
        compiler_params=pltpu.CompilerParams(vmem_limit_bytes=VMEM_BYTES),
        cost_estimate=FREE,
    )(facts, *back, *blocks)


def facts_call(kernel, outs, facts, operands, cost=FREE):
    return pl.pallas_call(
        kernel,
        out_shape=outs,
        in_specs=vmem_specs(len(operands)),
        compiler_params=pltpu.CompilerParams(vmem_limit_bytes=VMEM_BYTES),
        cost_estimate=cost,
    )(facts, *operands)


def add_gradients(facts, terms, slopes, pieces, blocks, before, unit, parts, last):
    rows = terms[0].shape[0] // 2
    kernel = functools.partial(totals_kernel, pieces, unit, parts, not before)
    outs = ()
    for lanes in parts:
        shape = rows, lanes.stop - lanes.start
        outs += f32(*shape), (bf16 if last else f32)(*shape)
    return tuple(facts_call(kernel, outs, facts, (*terms, *slopes, *blocks, *before)))


def act_and_slope(facts, terms, offsets, chips, before, unit):
    rows, columns = terms[0].shape
    kernel = functools.partial(act_kernel, offsets, chips, unit, bool(before))
    outs = f32(rows, columns), bf16(rows, columns // len(offsets) * chips)
    return facts_call(kernel, outs, facts, (*terms, *before))


def token_products(facts, act, offsets, chips, blocks, unit):
    rows, columns = act.shape[0] // 2, blocks[0].shape[1]
    return pl.pallas_call(
        functools.partial(token_kernel, offsets, chips, unit),
        out_shape=(f32(rows, columns), bf16(rows, columns)),
        in_specs=vmem_specs(1) + [pl.BlockSpec(memory_space=pl.ANY)] * len(blocks),
        scratch_shapes=[pltpu.VMEM(block.shape, block.dtype) for block in blocks]
        + [pltpu.SemaphoreType.DMA((len(blocks),))],
        compiler_params=pltpu.CompilerParams(vmem_limit_bytes=VMEM_BYTES),
        cost_estimate=FREE,
    )(facts, act, *blocks)


def chips_exchange(value):
    count = lax.axis_size("ctx")
    groups = [list(range(core, count, 2)) for core in range(2)]
    return lax.all_to_all(
        value, "ctx", split_axis=0, concat_axis=0, tiled=True, axis_index_groups=groups
    )


def per_device(
    features,
    group_kernel,
    squeeze_in,
    squeeze_out,
    sampler_kernel,
    readout_kernel,
    frame_clip,
    clip_keep,
    token_cotangent,
):
    chans = features.shape[2]
    count = lax.axis_size("ctx")
    steps, unit = count // 4, OUT_SIDE * OUT_SIDE // count
    flat_sampler = sampler_kernel.reshape(sampler_kernel.shape[0], 8 * chans)
    chips = count // 2
    s_up, s_down = ring_send(flat_sampler, 1), ring_send(flat_sampler, -1)
    group_kernel = jnp.swapaxes(group_kernel, 1, 2)
    squeeze_in = squeeze_in.T
    facts = facts_of(frame_clip, clip_keep)

    conv, padded, squeezed = conv_forward(features, group_kernel, squeeze_in)
    token_cotangent, squeezed = tie(token_cotangent, squeezed)
    back = chips_exchange(token_cotangent)
    squeezed = sum_tp(squeezed)
    even, odd, excite = hidden_frames(conv, padded, squeezed, squeeze_out)
    halo = shifted(odd, "ctx", 1)

    s_up, s_down = [flat_sampler, s_up], [flat_sampler, s_down]
    s_up[1], s_down[1], even, readout_kernel = tie(s_up[1], s_down[1], even, readout_kernel)
    for step in range(2, steps):
        s_up.append(ring_send(s_up[-1], 1))
        s_down.append(ring_send(s_down[-1], -1))
        if step == 2:
            halo, s_up[2], s_down[2] = tie(halo, s_up[2], s_down[2])
            r_down = [readout_kernel, ring_send(readout_kernel, -1)]
            patches = take_patches(facts, halo, even)
            patches = order_rows(facts, patches, swap_cores(patches), unit)
    s_up[-1], s_down[-1], back, readout_kernel = tie(s_up[-1], s_down[-1], back, readout_kernel)
    back = (back, swap_cores(back))
    s_last = ring_send(s_up[-1], 1)
    r_up = [readout_kernel, ring_send(readout_kernel, 1)]
    samplers = [flat_sampler] + [block for pair in zip(s_up[1:], s_down[1:]) for block in pair]
    offsets = ring_offsets(chips)
    count = 2 * steps - 3
    first_pre = tp_terms(block_products(pre_kernel, (patches,), samplers[:count]))
    r_down[1], s_last, *first_pre = tie(r_down[1], s_last, *first_pre)
    for step in range(1, steps - 2):
        r_down.append(ring_send(r_down[-1], -1))
        r_up.append(ring_send(r_up[-1], 1))
    first_slope, first_act = act_and_slope(facts, first_pre, offsets[:count], chips, (), unit)
    last_pre = block_products(pre_kernel, (patches,), [*samplers[count:], s_last])
    last_slope, act = act_and_slope(
        facts, tp_terms(last_pre), offsets[count:], chips, (first_act,), unit
    )
    slopes = first_slope, last_slope
    r_down[-1], act = tie(r_down[-1], act)
    r_down.append(ring_send(r_down[-1], -1))
    early = r_down[: steps - 1]
    sums = block_products(back_kernel, back, early)
    r_up[-1], act, *terms = tie(r_up[-1], chips_exchange(act), *tp_terms(sums))
    r_up.append(ring_send(r_up[-1], 1))
    halo_lanes, even_lanes = slice(0, 4 * chans), slice(4 * chans, 8 * chans)
    both = halo_lanes, even_lanes
    pieces = [(0, 2 * step) for step in range(steps - 1)]
    blocks = [flat_sampler] + s_down[1 : steps - 1]
    grads = add_gradients(facts, terms, slopes, pieces, blocks, (), unit, both, False)
    middle = r_up[1 : steps - 1] + [r_down[steps - 1]]
    r_down.append(ring_send(r_down[-1], -1))
    terms = tp_terms(block_products(back_kernel, back, middle))
    pieces = [(0, 2 * step - 1) for step in range(1, steps - 1)] + [(1, 1)]
    blocks = s_up[1 : steps - 1] + [s_down[steps - 1]]
    grads = add_gradients(facts, terms, slopes, pieces, blocks, grads, unit, both, False)

    late_up, late_down, *grads = tie(r_up[-1], r_down[-1], *grads)
    sums, facts_late = late_products(facts, back, [late_up, late_down])
    terms = tp_terms(sums)
    places = [*range(steps - 1), *range(-1, 1 - steps, -1), steps - 1, 1 - steps, steps]
    tokens = token_products(
        facts_late, act, places, chips, [*early, *middle, late_up, late_down], unit
    )
    other_term, *tokens = tie(terms[1], *tokens)
    terms = terms[0], other_term
    pieces, blocks = [(1, 0), (1, 2)], [s_up[-1], s_last]
    halo_own, halo_mate = add_gradients(
        facts, terms, slopes, pieces, blocks, grads[:2], unit, (halo_lanes,), True
    )
    halo_mate, first_term = tie(halo_mate, terms[0])
    even_own, even_mate = add_gradients(
        facts, (first_term, terms[1]), slopes, pieces, blocks, grads[2:], unit, (even_lanes,), True
    )
    lead, facts_late = return_patches(facts, halo_own, swap_cores(halo_mate), chans, jnp.bfloat16)
    grad_odd = shifted(lead, "ctx", -1)
    grad_even, _ = return_patches(
        facts_late, even_own, swap_cores(even_mate), chans, jnp.float32
    )
    grad_relaxed = sum_tp(excite_grad(grad_even, grad_odd, conv, excite, squeeze_out))
    llm_tokens = (tokens[0] + swap_cores(tokens[1]).astype(jnp.float32)).astype(jnp.bfloat16)
    grad_features = conv_backward(
        grad_even, grad_odd, conv, excite, squeezed, grad_relaxed, squeeze_in, group_kernel
    )
    return (llm_tokens, grad_features)


def solution(mesh):
    placed = (
        P("ctx", None, "tp"),
        P(None, "tp", None),
        P("tp", None),
        P(None, "tp"),
        P("ctx", None, "tp"),
        P("ctx", "tp"),
        P(),
        P(),
        P("ctx", "tp"),
    )
    return jax.shard_map(
        per_device,
        mesh=mesh,
        in_specs=placed,
        out_specs=(P("ctx", "tp"), P("ctx", None, "tp")),
        check_vma=False,
    )
```

```python
import functools

import jax
import jax.numpy as jnp
from jax import lax
from jax.experimental import pallas as pl
from jax.experimental.pallas import tpu as pltpu
from jax.sharding import PartitionSpec as P

SIDE = 14
OUT_SIDE = 8
WIDE = 16
FRAME_ROWS = WIDE * WIDE
EDGE = 8
LANES = 128
WINDOW = 256
VMEM_BYTES = 16 * 2**20
FREE = pl.CostEstimate(flops=0, bytes_accessed=0, transcendentals=0)


def whole_call(kernel, outs, scratch, cost=FREE):
    return pl.pallas_call(
        kernel,
        out_shape=outs,
        scratch_shapes=scratch,
        compiler_params=pltpu.CompilerParams(vmem_limit_bytes=VMEM_BYTES),
        cost_estimate=cost,
    )


def contract_last(left, right):
    return lax.dot_general(
        left, right, (((1,), (1,)), ((), ())), preferred_element_type=jnp.float32
    )


def contract_exact(left, right):
    return lax.dot_general(
        left,
        right,
        (((1,), (1,)), ((), ())),
        precision=lax.Precision.HIGHEST,
        preferred_element_type=jnp.float32,
    )


def silu_slope(values):
    sigma = jax.nn.sigmoid(values)
    return sigma * (1.0 + values * (1.0 - sigma))


def inside(rows):
    row = lax.broadcasted_iota(jnp.int32, (rows, 1), 0)
    across, down = row & (WIDE - 1), (row // WIDE) & (WIDE - 1)
    good = (across >= 1) & (across <= SIDE) & (down >= 1) & (down <= SIDE)
    return good.astype(jnp.float32)


def channel_blocks(chans, width):
    span = 4 * width
    blocks = []
    for low in range(0, chans, span):
        high = min(chans, low + span)
        blocks.append((low, high, low // LANES * LANES, min(chans, -(-high // LANES) * LANES)))
    return blocks


def block_tools(block, width):
    low, high, start, end = block
    size = end - start
    out_row = lax.broadcasted_iota(jnp.int32, (size, width), 0) + start
    within = lax.broadcasted_iota(jnp.int32, (size, width), 1)
    lane = lax.broadcasted_iota(jnp.int32, (size, size), 1) + start
    row = lax.broadcasted_iota(jnp.int32, (size, size), 0) + start
    spread = jnp.zeros((size, width), jnp.float32)
    same = jnp.zeros((size, size), jnp.float32)
    for first in range(low, high, width):
        spread += (out_row == within + first).astype(jnp.float32)
        in_lane = (lane >= first) & (lane < first + width)
        in_row = (row >= first) & (row < first + width)
        same += (in_lane & in_row).astype(jnp.float32)
    return spread.astype(jnp.bfloat16), same


def dense_tap(group_ref, tap, block, spread, same):
    _, _, start, end = block
    full = jnp.dot(spread, group_ref[tap, :, start:end], preferred_element_type=jnp.float32)
    return (full * same).astype(jnp.bfloat16)


def store_shifts(wide_ref, shift_ref, sign):
    rows = shift_ref.shape[1]
    for col in range(3):
        at = EDGE + sign * (col - 1)
        chans = wide_ref.shape[1]
        shift_ref[col, :, 0:chans] = wide_ref[at : at + rows, :].astype(jnp.bfloat16)
        if shift_ref.shape[2] > chans:
            blank = jnp.zeros((rows, shift_ref.shape[2] - chans), jnp.bfloat16)
            shift_ref[col, :, chans:] = blank


def conv_kernel(feat_ref, group_ref, squeeze_ref, *refs):
    conv_ref, pad_ref, sq_ref, flat_ref, wide_ref, shift_ref = refs
    frames, _, chans = feat_ref.shape
    width = group_ref.shape[1]
    rows = frames * FRAME_ROWS
    wide_ref[...] = jnp.zeros_like(wide_ref)
    for frame in range(frames):
        flat_ref[...] = feat_ref[frame].astype(jnp.float32)
        for y in range(SIDE):
            at = EDGE + frame * FRAME_ROWS + (y + 1) * WIDE + 1
            wide_ref[at : at + SIDE, :] = flat_ref[y * SIDE : (y + 1) * SIDE, :]
    store_shifts(wide_ref, shift_ref, 1)
    pad_ref[...] = shift_ref[1]
    conv_ref[...] = jnp.zeros_like(conv_ref)
    body = rows - 2 * WIDE
    for block in channel_blocks(chans, width):
        _, _, start, end = block
        spread, same = block_tools(block, width)
        total = jnp.zeros((body, end - start), jnp.float32)
        for tap in range(9):
            down, across = divmod(tap, 3)
            weights = dense_tap(group_ref, tap, block, spread, same)
            source = shift_ref[across, down * WIDE : down * WIDE + body, start:end]
            total += contract_last(source, weights)
        conv_ref[WIDE : WIDE + body, start:end] += total
    conv = conv_ref[...] * inside(rows)
    conv_ref[...] = conv
    active = conv * jax.nn.sigmoid(conv)
    pooled = jnp.concatenate(
        [
            jnp.sum(active[f * FRAME_ROWS : (f + 1) * FRAME_ROWS], axis=0, keepdims=True)
            for f in range(frames)
        ],
        axis=0,
    ) * (1.0 / (SIDE * SIDE))
    sq_ref[...] = contract_exact(pooled, squeeze_ref[...].astype(jnp.float32))


def hidden_kernel(conv_ref, pad_ref, sq_ref, expand_ref, even_ref, odd_ref, excite_ref):
    squeezed = sq_ref[...]
    relaxed = squeezed * jax.nn.sigmoid(squeezed)
    excite = jax.nn.sigmoid(
        jnp.dot(relaxed, expand_ref[...].astype(jnp.float32), precision=lax.Precision.HIGHEST)
    )
    excite_ref[...] = excite
    for frame, out_ref in enumerate((even_ref, odd_ref)):
        rows = slice(frame * FRAME_ROWS, (frame + 1) * FRAME_ROWS)
        conv = conv_ref[rows, :]
        active = conv * jax.nn.sigmoid(conv)
        hidden = pad_ref[rows, :].astype(jnp.float32) + active * excite[frame : frame + 1]
        out_ref[...] = hidden.astype(jnp.bfloat16)


def select_rows(to_patches):
    shape = (FRAME_ROWS, FRAME_ROWS)
    out_row = lax.broadcasted_iota(jnp.int32, shape, 0)
    in_row = lax.broadcasted_iota(jnp.int32, shape, 1)
    patch_row, frame_row = (out_row, in_row) if to_patches else (in_row, out_row)
    down, across = patch_row >> 7, (patch_row >> 6) & 1
    a, b = (patch_row >> 3) & 7, patch_row & 7
    return ((2 * a + down) * WIDE + 2 * b + across == frame_row).astype(jnp.float32)


def facts_kernel(clip_ref, keep_ref, out_ref):
    shard = lax.axis_index("ctx")
    frames = clip_ref.shape[0]
    out_ref[0] = shard % 2
    for block in range(2):
        pair = shard // 2 * 2 + block
        clip = clip_ref[2 * pair]
        start = jnp.int32(0)
        for other in range(0, frames, 2):
            start += jnp.where(clip_ref[other] < clip, 1, 0)
        out_ref[1 + block] = keep_ref[clip] - (pair - start) * (OUT_SIDE * OUT_SIDE)
    before = clip_ref[jnp.maximum(2 * shard - 1, 0)]
    chip, chips = shard // 2, lax.axis_size("ctx") // 2
    out_ref[4] = jnp.where(chip % 2 == 0, chip // 2, chips - 1 - chip // 2)
    out_ref[3] = jnp.where((shard > 0) & (before == clip_ref[2 * shard]), 1, 0)


def token_place(row, core, unit):
    per_block = OUT_SIDE * OUT_SIDE
    within = row % per_block
    block = (within // unit) % 2
    target_core = jnp.where(row < per_block, core, 1 - core)
    return block, unit * (2 * (within // (2 * unit)) + target_core) + within % unit


def reorder_matrix(core, unit, to_sent):
    shape = (2 * OUT_SIDE * OUT_SIDE,) * 2
    out_row = lax.broadcasted_iota(jnp.int32, shape, 0)
    in_row = lax.broadcasted_iota(jnp.int32, shape, 1)
    sent, natural = (out_row, in_row) if to_sent else (in_row, out_row)
    block, token = token_place(sent, core, unit)
    source = jnp.where(block == core, 0, OUT_SIDE * OUT_SIDE) + token
    return (source == natural).astype(jnp.bfloat16)


def order_kernel(unit, facts_ref, own_ref, mate_ref, out_ref):
    rows = jnp.concatenate([own_ref[...], mate_ref[...]], axis=0)
    matrix = reorder_matrix(facts_ref[0], unit, True)
    out_ref[...] = jnp.dot(matrix, rows, preferred_element_type=jnp.float32).astype(jnp.bfloat16)


def patch_kernel(facts_ref, halo_ref, even_ref, out_ref):
    chans = halo_ref.shape[1]
    per_frame = OUT_SIDE * OUT_SIDE
    select = select_rows(True).astype(jnp.bfloat16)
    for frame, source in enumerate((halo_ref, even_ref)):
        rows = jnp.dot(select, source[...], preferred_element_type=jnp.float32)
        if frame == 0:
            rows = rows * facts_ref[3].astype(jnp.float32)
        rows = rows.astype(jnp.bfloat16)
        for tap in range(4):
            at = (frame * 4 + tap) * chans
            out_ref[:, at : at + chans] = rows[tap * per_frame : (tap + 1) * per_frame]


def unpatch_kernel(facts_ref, own_ref, mate_ref, out_ref, facts_out_ref):
    for place in range(facts_ref.shape[0]):
        facts_out_ref[place] = facts_ref[place]
    chans = out_ref.shape[1]
    rows = own_ref[...] + mate_ref[...].astype(jnp.float32)
    pieces = [rows[:, tap * chans : (tap + 1) * chans] for tap in range(4)]
    rows = jnp.concatenate(pieces, axis=0)
    select = select_rows(False).astype(jnp.bfloat16)
    coarse = rows.astype(jnp.bfloat16)
    frame = jnp.dot(select, coarse, preferred_element_type=jnp.float32)
    if out_ref.dtype == jnp.bfloat16:
        frame = frame * facts_ref[3].astype(jnp.float32)
    else:
        rest = (rows - coarse.astype(jnp.float32)).astype(jnp.bfloat16)
        frame += jnp.dot(select, rest, preferred_element_type=jnp.float32)
    out_ref[...] = (frame * inside(FRAME_ROWS)).astype(out_ref.dtype)


def excite_grad_kernel(even_ref, odd_ref, conv_ref, excite_ref, expand_ref, out_ref):
    sums = []
    for frame, grad_ref in enumerate((even_ref, odd_ref)):
        conv = conv_ref[frame * FRAME_ROWS : (frame + 1) * FRAME_ROWS, :]
        active = conv * jax.nn.sigmoid(conv)
        sums.append(jnp.sum(grad_ref[...].astype(jnp.float32) * active, axis=0, keepdims=True))
    excite = excite_ref[...]
    inner = jnp.concatenate(sums, axis=0) * excite * (1.0 - excite)
    out_ref[...] = contract_exact(inner, expand_ref[...].astype(jnp.float32))


def conv_grad_kernel(
    width, even_ref, odd_ref, conv_ref, excite_ref, sq_ref, relaxed_ref, squeeze_ref, *refs
):
    *dense_refs, out_ref, flat_ref, wide_ref, shift_ref, grad_ref = refs
    frames, _, chans = out_ref.shape
    rows = frames * FRAME_ROWS
    grad_squeezed = relaxed_ref[...] * silu_slope(sq_ref[...])
    pooled = jnp.dot(
        grad_squeezed, squeeze_ref[...].astype(jnp.float32), precision=lax.Precision.HIGHEST
    ) * (1.0 / (SIDE * SIDE))
    wide_ref[0:EDGE, :] = jnp.zeros((EDGE, chans), jnp.float32)
    wide_ref[EDGE + rows :, :] = jnp.zeros((EDGE, chans), jnp.float32)
    good = inside(FRAME_ROWS)
    for frame, source in enumerate((even_ref, odd_ref)):
        at = frame * FRAME_ROWS
        grad = source[...].astype(jnp.float32)
        grad_ref[at : at + FRAME_ROWS, :] = grad
        active = grad * excite_ref[frame : frame + 1, :] + pooled[frame : frame + 1]
        slope = silu_slope(conv_ref[at : at + FRAME_ROWS, :])
        wide_ref[EDGE + at : EDGE + at + FRAME_ROWS, :] = active * slope * good
    store_shifts(wide_ref, shift_ref, -1)
    body = rows - 2 * WIDE
    for block, dense_ref in zip(channel_blocks(chans, width), dense_refs):
        start = block[2]
        sources = []
        for tap in range(9):
            down, across = divmod(tap, 3)
            at = (2 - down) * WIDE
            sources.append(shift_ref[across, at : at + body, start : start + WINDOW])
        total = jnp.dot(
            jnp.concatenate(sources, axis=1), dense_ref[...], preferred_element_type=jnp.float32
        )
        end = min(chans, start + WINDOW)
        grad_ref[WIDE : WIDE + body, start:end] += total[:, : end - start]
    for frame in range(frames):
        for y in range(SIDE):
            at = frame * FRAME_ROWS + (y + 1) * WIDE + 1
            flat_ref[y * SIDE : (y + 1) * SIDE, :] = grad_ref[at : at + SIDE, :]
        out_ref[frame] = flat_ref[...].astype(jnp.bfloat16)


def f32(*shape):
    return jax.ShapeDtypeStruct(shape, jnp.float32)


def bf16(*shape):
    return jax.ShapeDtypeStruct(shape, jnp.bfloat16)


def conv_forward(features, group_kernel, squeeze_in):
    frames, cells, chans = features.shape
    rows = frames * FRAME_ROWS
    return whole_call(
        conv_kernel,
        (f32(rows, chans), bf16(rows, chans), f32(frames, squeeze_in.shape[0])),
        [
            pltpu.VMEM((cells, chans), jnp.float32),
            pltpu.VMEM((rows + 2 * EDGE, chans), jnp.float32),
            pltpu.VMEM((3, rows, chans), jnp.bfloat16),
        ],
    )(features, group_kernel, squeeze_in)


def hidden_frames(conv, padded, squeezed, squeeze_out):
    rows, chans = conv.shape
    return whole_call(
        hidden_kernel,
        (bf16(FRAME_ROWS, chans), bf16(FRAME_ROWS, chans), f32(rows // FRAME_ROWS, chans)),
        [],
    )(conv, padded, squeezed, squeeze_out)


def vmem_specs(count):
    return [pl.BlockSpec(memory_space=pltpu.SMEM)] + [pl.BlockSpec(memory_space=pltpu.VMEM)] * count


def facts_of(frame_clip, clip_keep):
    smem = pl.BlockSpec(memory_space=pltpu.SMEM)
    return pl.pallas_call(
        facts_kernel,
        out_shape=jax.ShapeDtypeStruct((5,), jnp.int32),
        in_specs=[smem, smem],
        out_specs=smem,
        cost_estimate=FREE,
    )(frame_clip, clip_keep)


def order_rows(facts, own, mate, unit):
    rows, columns = own.shape
    return pl.pallas_call(
        functools.partial(order_kernel, unit),
        out_shape=bf16(2 * rows, columns),
        in_specs=vmem_specs(2),
        compiler_params=pltpu.CompilerParams(vmem_limit_bytes=VMEM_BYTES),
        cost_estimate=FREE,
    )(facts, own, mate)


def take_patches(facts, halo, even):
    chans = even.shape[1]
    return pl.pallas_call(
        patch_kernel,
        out_shape=bf16(OUT_SIDE * OUT_SIDE, 8 * chans),
        in_specs=vmem_specs(2),
        compiler_params=pltpu.CompilerParams(vmem_limit_bytes=VMEM_BYTES),
        cost_estimate=FREE,
    )(facts, halo, even)


def return_patches(facts, own, mate, chans, dtype):
    return pl.pallas_call(
        unpatch_kernel,
        out_shape=(
            jax.ShapeDtypeStruct((FRAME_ROWS, chans), dtype),
            jax.ShapeDtypeStruct(facts.shape, jnp.int32),
        ),
        in_specs=vmem_specs(2),
        out_specs=vmem_specs(1)[::-1],
        compiler_params=pltpu.CompilerParams(vmem_limit_bytes=VMEM_BYTES),
        cost_estimate=FREE,
    )(facts, own, mate)


def excite_grad(even, odd, conv, excite, squeeze_out):
    rows, chans = conv.shape
    return whole_call(
        excite_grad_kernel,
        f32(rows // FRAME_ROWS, squeeze_out.shape[0]),
        [],
    )(even, odd, conv, excite, squeeze_out)


def conv_backward(even, odd, conv, excite, squeezed, grad_relaxed, squeeze_in, dense, width):
    rows, chans = conv.shape
    frames = rows // FRAME_ROWS
    lanes = channel_blocks(chans, width)[-1][2] + WINDOW
    return whole_call(
        functools.partial(conv_grad_kernel, width),
        bf16(frames, SIDE * SIDE, chans),
        [
            pltpu.VMEM((SIDE * SIDE, chans), jnp.float32),
            pltpu.VMEM((rows + 2 * EDGE, chans), jnp.float32),
            pltpu.VMEM((3, rows, lanes), jnp.bfloat16),
            pltpu.VMEM((rows, chans), jnp.float32),
        ],
        pl.CostEstimate(flops=rows * chans * 9216, bytes_accessed=16 * rows * chans, transcendentals=0),
    )(even, odd, conv, excite, squeezed, grad_relaxed, squeeze_in, *dense)


def dense_kernel(facts_ref, group_ref, *dense_refs):
    _, width, chans = group_ref.shape
    for block, dense_ref in zip(channel_blocks(chans, width), dense_refs):
        low, high, start, _ = block
        end = min(chans, start + WINDOW)
        spread, same = block_tools((low, high, start, start + WINDOW), width)
        dense_ref[...] = jnp.zeros_like(dense_ref)
        for tap in range(9):
            full = jnp.dot(spread, group_ref[tap, :, start:end], preferred_element_type=jnp.float32)
            rows = slice(tap * WINDOW, (tap + 1) * WINDOW)
            dense_ref[rows, 0 : end - start] = (full * same[:, : end - start]).astype(jnp.bfloat16)


def dense_weights(facts, group_kernel):
    _, width, chans = group_kernel.shape
    outs = (bf16(9 * WINDOW, WINDOW),) * len(channel_blocks(chans, width))
    return facts_call(dense_kernel, outs, facts, (group_kernel,))


def shifted(value, axis, by):
    count = lax.axis_size(axis)
    pairs = [(i, i + by) for i in range(count) if 0 <= i + by < count]
    return lax.ppermute(value, axis, pairs)


def ring_order(chips):
    return list(range(0, chips, 2)) + list(range(1, chips, 2))[::-1]


def ring_pairs(count, by):
    order = ring_order(count // 2)
    pairs = []
    for place, chip in enumerate(order):
        target = order[(place + by) % len(order)]
        pairs += [(2 * chip, 2 * target), (2 * chip + 1, 2 * target + 1)]
    return pairs


def swap_cores(value):
    return lax.ppermute(value, "ctx", [(i, i ^ 1) for i in range(lax.axis_size("ctx"))])


def tp_terms(value):
    size = lax.axis_size("tp")
    reach, other = 1, None
    while reach < size:
        value = value if other is None else value + other
        other = lax.ppermute(value, "tp", [(i, i ^ reach) for i in range(size)])
        reach *= 2
    return value, jnp.zeros_like(value) if other is None else other


def sum_tp(value):
    value, other = tp_terms(value)
    return value + other


def ring_send(value, by):
    return lax.ppermute(value, "ctx", ring_pairs(lax.axis_size("ctx"), by))


def tie(*values):
    return lax.optimization_barrier(values)


def pre_kernel(patch_ref, *refs):
    *blocks, out_ref = refs
    products = [contract_last(patch_ref[...], ref[...]) for ref in blocks]
    out_ref[...] = jnp.concatenate(products, axis=1)


def back_kernel(keep_ref, send_ref, *refs):
    *blocks, out_ref = refs
    back = jnp.concatenate([keep_ref[...], send_ref[...]], axis=0)
    out_ref[...] = jnp.concatenate([contract_last(back, ref[...]) for ref in blocks], axis=1)


def late_kernel(facts_ref, keep_ref, send_ref, *refs):
    *refs, out_ref, facts_out_ref = refs
    for place in range(facts_ref.shape[0]):
        facts_out_ref[place] = facts_ref[place]
    back_kernel(keep_ref, send_ref, *refs, out_ref)


def live_rows(facts_ref, rows, unit):
    block, token = token_place(
        lax.broadcasted_iota(jnp.int32, (rows, 1), 0), facts_ref[0], unit
    )
    return (token < jnp.where(block == 0, facts_ref[1], facts_ref[2])).astype(jnp.float32)


def stacked_dot(pieces, blocks):
    if blocks[0].shape[0] % 8 == 0:
        pieces = [jnp.concatenate(pieces, axis=1)]
        blocks = [jnp.concatenate(blocks, axis=0)]
    total = 0.0
    for piece, block in zip(pieces, blocks):
        total += jnp.dot(piece, block, preferred_element_type=jnp.float32)
    return total


def totals_kernel(pieces, unit, parts, first, facts_ref, *refs):
    grad_act = refs[0][...] + refs[1][...]
    count = len(pieces)
    slopes, blocks = refs[2:4], refs[4 : 4 + count]
    before, after = refs[4 + count : -2 * len(parts)], refs[-2 * len(parts) :]
    rows, width = grad_act.shape[0], blocks[0].shape[0]
    slope = jnp.concatenate(
        [slopes[source][:, index * width : (index + 1) * width] for source, index in pieces], axis=1
    )
    factor = jnp.dot(
        reorder_matrix(facts_ref[0], unit, False),
        (grad_act * slope).astype(jnp.bfloat16),
        preferred_element_type=jnp.float32,
    ).astype(jnp.bfloat16)
    factors = [factor[:, place * width : (place + 1) * width] for place in range(count)]
    for part, lanes in enumerate(parts):
        total = stacked_dot(factors, [ref[:, lanes] for ref in blocks])
        for half in range(2):
            value = total[half * rows // 2 : (half + 1) * rows // 2]
            value = value if first else before[2 * part + half][...] + value
            ref = after[2 * part + half]
            ref[...] = value.astype(ref.dtype)


def ring_offsets(chips):
    offsets = [0]
    for step in range(1, chips // 2):
        offsets += [-step, step]
    return offsets + [chips // 2]


def block_columns(facts_ref, offset, chips, width):
    shape = (width, chips * width)
    place = (facts_ref[4] + offset + chips) % chips
    column = lax.broadcasted_iota(jnp.int32, shape, 1)
    return (column == lax.broadcasted_iota(jnp.int32, shape, 0) + place * width).astype(jnp.bfloat16)


def exchange_matrix(core, unit, to_sent):
    per_block = OUT_SIDE * OUT_SIDE
    shape = (2 * per_block,) * 2
    out_row = lax.broadcasted_iota(jnp.int32, shape, 0)
    in_row = lax.broadcasted_iota(jnp.int32, shape, 1)
    sent, kept = (out_row, in_row) if to_sent else (in_row, out_row)
    target_core = (sent // (2 * unit)) % 2
    within = sent // (4 * unit) * (2 * unit) + sent % (2 * unit)
    return (within + jnp.where(target_core == core, 0, per_block) == kept).astype(jnp.bfloat16)


def act_kernel(offsets, chips, unit, last, facts_ref, own_ref, other_ref, *refs):
    *before, slope_ref, out_ref = refs
    pre = own_ref[...] + other_ref[...]
    width = pre.shape[1] // len(offsets)
    live = live_rows(facts_ref, pre.shape[0], unit)
    sigma = jax.nn.sigmoid(pre)
    slope_ref[...] = sigma * (1.0 + pre * (1.0 - sigma)) * live
    act = (pre * sigma * live).astype(jnp.bfloat16)
    total = before[0][...].astype(jnp.float32) if last else 0.0
    for place, offset in enumerate(offsets):
        columns = block_columns(facts_ref, offset, chips, width)
        piece = act[:, place * width : (place + 1) * width]
        total += jnp.dot(piece, columns, preferred_element_type=jnp.float32)
    total = total.astype(jnp.bfloat16)
    if last:
        matrix = exchange_matrix(facts_ref[0], unit, True)
        total = jnp.dot(matrix, total, preferred_element_type=jnp.float32).astype(jnp.bfloat16)
    out_ref[...] = total


def token_kernel(offsets, chips, unit, facts_ref, act_ref, *refs):
    count = len(offsets)
    blocks, refs = refs[:count], refs[count:]
    keep_ref, send_ref, *buffers, sems = refs
    copies = [
        pltpu.make_async_copy(ref, buffer, sems.at[place])
        for place, (ref, buffer) in enumerate(zip(blocks, buffers))
    ]
    for copy in copies:
        copy.start()
    width = buffers[0].shape[0]
    matrix = exchange_matrix(facts_ref[0], unit, False)
    act = jnp.dot(matrix, act_ref[...], preferred_element_type=jnp.float32).astype(jnp.bfloat16)
    pieces = [
        contract_last(act, block_columns(facts_ref, offset, chips, width)).astype(jnp.bfloat16)
        for offset in offsets
    ]
    for copy in copies:
        copy.wait()
    total = stacked_dot(pieces, [buffer[...] for buffer in buffers])
    rows = keep_ref.shape[0]
    keep_ref[...] = total[:rows]
    send_ref[...] = total[rows:].astype(jnp.bfloat16)


def block_products(kernel, left, blocks):
    rows = 2 * OUT_SIDE * OUT_SIDE
    return whole_call(kernel, f32(rows, len(blocks) * blocks[0].shape[0]), [])(*left, *blocks)


def late_products(facts, back, blocks):
    rows = 2 * OUT_SIDE * OUT_SIDE
    return pl.pallas_call(
        late_kernel,
        out_shape=(
            f32(rows, len(blocks) * blocks[0].shape[0]),
            jax.ShapeDtypeStruct(facts.shape, jnp.int32),
        ),
        in_specs=vmem_specs(2 + len(blocks)),
        out_specs=vmem_specs(1)[::-1],
        compiler_params=pltpu.CompilerParams(vmem_limit_bytes=VMEM_BYTES),
        cost_estimate=FREE,
    )(facts, *back, *blocks)


def facts_call(kernel, outs, facts, operands, cost=FREE):
    return pl.pallas_call(
        kernel,
        out_shape=outs,
        in_specs=vmem_specs(len(operands)),
        compiler_params=pltpu.CompilerParams(vmem_limit_bytes=VMEM_BYTES),
        cost_estimate=cost,
    )(facts, *operands)


def add_gradients(facts, terms, slopes, pieces, blocks, before, unit, parts, last):
    rows = terms[0].shape[0] // 2
    kernel = functools.partial(totals_kernel, pieces, unit, parts, not before)
    outs = ()
    for lanes in parts:
        shape = rows, lanes.stop - lanes.start
        outs += f32(*shape), (bf16 if last else f32)(*shape)
    return tuple(facts_call(kernel, outs, facts, (*terms, *slopes, *blocks, *before)))


def act_and_slope(facts, terms, offsets, chips, before, unit):
    rows, columns = terms[0].shape
    kernel = functools.partial(act_kernel, offsets, chips, unit, bool(before))
    outs = f32(rows, columns), bf16(rows, columns // len(offsets) * chips)
    return facts_call(kernel, outs, facts, (*terms, *before))


def token_products(facts, act, offsets, chips, blocks, unit):
    rows, columns = act.shape[0] // 2, blocks[0].shape[1]
    return pl.pallas_call(
        functools.partial(token_kernel, offsets, chips, unit),
        out_shape=(f32(rows, columns), bf16(rows, columns)),
        in_specs=vmem_specs(1) + [pl.BlockSpec(memory_space=pl.ANY)] * len(blocks),
        scratch_shapes=[pltpu.VMEM(block.shape, block.dtype) for block in blocks]
        + [pltpu.SemaphoreType.DMA((len(blocks),))],
        compiler_params=pltpu.CompilerParams(vmem_limit_bytes=VMEM_BYTES),
        cost_estimate=FREE,
    )(facts, act, *blocks)


def chips_exchange(value):
    count = lax.axis_size("ctx")
    groups = [list(range(core, count, 2)) for core in range(2)]
    return lax.all_to_all(
        value, "ctx", split_axis=0, concat_axis=0, tiled=True, axis_index_groups=groups
    )


def per_device(
    features,
    group_kernel,
    squeeze_in,
    squeeze_out,
    sampler_kernel,
    readout_kernel,
    frame_clip,
    clip_keep,
    token_cotangent,
):
    chans = features.shape[2]
    count = lax.axis_size("ctx")
    steps, unit = count // 4, OUT_SIDE * OUT_SIDE // count
    flat_sampler = sampler_kernel.reshape(sampler_kernel.shape[0], 8 * chans)
    chips = count // 2
    s_up, s_down = ring_send(flat_sampler, 1), ring_send(flat_sampler, -1)
    group_kernel = jnp.swapaxes(group_kernel, 1, 2)
    squeeze_in = squeeze_in.T
    facts = facts_of(frame_clip, clip_keep)

    conv, padded, squeezed = conv_forward(features, group_kernel, squeeze_in)
    token_cotangent, squeezed = tie(token_cotangent, squeezed)
    back = chips_exchange(token_cotangent)
    squeezed = sum_tp(squeezed)
    even, odd, excite = hidden_frames(conv, padded, squeezed, squeeze_out)
    halo = shifted(odd, "ctx", 1)

    s_up, s_down = [flat_sampler, s_up], [flat_sampler, s_down]
    s_up[1], s_down[1], even, readout_kernel = tie(s_up[1], s_down[1], even, readout_kernel)
    for step in range(2, steps):
        s_up.append(ring_send(s_up[-1], 1))
        s_down.append(ring_send(s_down[-1], -1))
        if step == 2:
            halo, s_up[2], s_down[2] = tie(halo, s_up[2], s_down[2])
            r_down = [readout_kernel, ring_send(readout_kernel, -1)]
            patches = take_patches(facts, halo, even)
            patches = order_rows(facts, patches, swap_cores(patches), unit)
    s_up[-1], s_down[-1], back, readout_kernel = tie(s_up[-1], s_down[-1], back, readout_kernel)
    back = (back, swap_cores(back))
    s_last = ring_send(s_up[-1], 1)
    r_up = [readout_kernel, ring_send(readout_kernel, 1)]
    samplers = [flat_sampler] + [block for pair in zip(s_up[1:], s_down[1:]) for block in pair]
    offsets = ring_offsets(chips)
    count = 2 * steps - 3
    first_pre = tp_terms(block_products(pre_kernel, (patches,), samplers[:count]))
    r_down[1], s_last, *first_pre = tie(r_down[1], s_last, *first_pre)
    for step in range(1, steps - 2):
        r_down.append(ring_send(r_down[-1], -1))
        r_up.append(ring_send(r_up[-1], 1))
    first_slope, first_act = act_and_slope(facts, first_pre, offsets[:count], chips, (), unit)
    last_pre = block_products(pre_kernel, (patches,), [*samplers[count:], s_last])
    last_slope, act = act_and_slope(
        facts, tp_terms(last_pre), offsets[count:], chips, (first_act,), unit
    )
    slopes = first_slope, last_slope
    r_down[-1], act = tie(r_down[-1], act)
    r_down.append(ring_send(r_down[-1], -1))
    early = r_down[: steps - 1]
    sums = block_products(back_kernel, back, early)
    r_up[-1], act, *terms = tie(r_up[-1], chips_exchange(act), *tp_terms(sums))
    r_up.append(ring_send(r_up[-1], 1))
    halo_lanes, even_lanes = slice(0, 4 * chans), slice(4 * chans, 8 * chans)
    both = halo_lanes, even_lanes
    pieces = [(0, 2 * step) for step in range(steps - 1)]
    blocks = [flat_sampler] + s_down[1 : steps - 1]
    grads = add_gradients(facts, terms, slopes, pieces, blocks, (), unit, both, False)
    middle = r_up[1 : steps - 1] + [r_down[steps - 1]]
    r_down.append(ring_send(r_down[-1], -1))
    terms = tp_terms(block_products(back_kernel, back, middle))
    pieces = [(0, 2 * step - 1) for step in range(1, steps - 1)] + [(1, 1)]
    blocks = s_up[1 : steps - 1] + [s_down[steps - 1]]
    grads = add_gradients(facts, terms, slopes, pieces, blocks, grads, unit, both, False)

    late_up, late_down, *grads = tie(r_up[-1], r_down[-1], *grads)
    sums, facts_late = late_products(facts, back, [late_up, late_down])
    terms = tp_terms(sums)
    places = [*range(steps - 1), *range(-1, 1 - steps, -1), steps - 1, 1 - steps, steps]
    tokens = token_products(
        facts_late, act, places, chips, [*early, *middle, late_up, late_down], unit
    )
    other_term, *tokens = tie(terms[1], *tokens)
    terms = terms[0], other_term
    pieces, blocks = [(1, 0), (1, 2)], [s_up[-1], s_last]
    halo_own, halo_mate = add_gradients(
        facts, terms, slopes, pieces, blocks, grads[:2], unit, (halo_lanes,), True
    )
    halo_mate, first_term = tie(halo_mate, terms[0])
    even_own, even_mate = add_gradients(
        facts, (first_term, terms[1]), slopes, pieces, blocks, grads[2:], unit, (even_lanes,), True
    )
    lead, facts_late = return_patches(facts, halo_own, swap_cores(halo_mate), chans, jnp.bfloat16)
    grad_odd = shifted(lead, "ctx", -1)
    grad_even, facts_late = return_patches(
        facts_late, even_own, swap_cores(even_mate), chans, jnp.float32
    )
    grad_relaxed = sum_tp(excite_grad(grad_even, grad_odd, conv, excite, squeeze_out))
    llm_tokens = (tokens[0] + swap_cores(tokens[1]).astype(jnp.float32)).astype(jnp.bfloat16)
    grad_features = conv_backward(
        grad_even, grad_odd, conv, excite, squeezed, grad_relaxed, squeeze_in,
        dense_weights(facts_late, group_kernel), group_kernel.shape[1],
    )
    return (llm_tokens, grad_features)


def solution(mesh):
    placed = (
        P("ctx", None, "tp"),
        P(None, "tp", None),
        P("tp", None),
        P(None, "tp"),
        P("ctx", None, "tp"),
        P("ctx", "tp"),
        P(),
        P(),
        P("ctx", "tp"),
    )
    return jax.shard_map(
        per_device,
        mesh=mesh,
        in_specs=placed,
        out_specs=(P("ctx", "tp"), P("ctx", None, "tp")),
        check_vma=False,
    )
```

```python
import functools

import jax
import jax.numpy as jnp
from jax import lax
from jax.experimental import pallas as pl
from jax.experimental.pallas import tpu as pltpu
from jax.sharding import PartitionSpec as P

SIDE = 14
OUT_SIDE = 8
WIDE = 16
FRAME_ROWS = WIDE * WIDE
EDGE = 8
LANES = 128
WINDOW = 256
VMEM_BYTES = 16 * 2**20
FREE = pl.CostEstimate(flops=0, bytes_accessed=0, transcendentals=0)


def whole_call(kernel, outs, scratch, cost=FREE):
    return pl.pallas_call(
        kernel,
        out_shape=outs,
        scratch_shapes=scratch,
        compiler_params=pltpu.CompilerParams(vmem_limit_bytes=VMEM_BYTES),
        cost_estimate=cost,
    )


def contract_last(left, right):
    return lax.dot_general(
        left, right, (((1,), (1,)), ((), ())), preferred_element_type=jnp.float32
    )


def contract_exact(left, right):
    return lax.dot_general(
        left,
        right,
        (((1,), (1,)), ((), ())),
        precision=lax.Precision.HIGHEST,
        preferred_element_type=jnp.float32,
    )


def silu_slope(values):
    sigma = jax.nn.sigmoid(values)
    return sigma * (1.0 + values * (1.0 - sigma))


def inside(rows):
    row = lax.broadcasted_iota(jnp.int32, (rows, 1), 0)
    across, down = row & (WIDE - 1), (row // WIDE) & (WIDE - 1)
    good = (across >= 1) & (across <= SIDE) & (down >= 1) & (down <= SIDE)
    return good.astype(jnp.float32)


def channel_blocks(chans, width):
    span = 4 * width
    blocks = []
    for low in range(0, chans, span):
        high = min(chans, low + span)
        blocks.append((low, high, low // LANES * LANES, min(chans, -(-high // LANES) * LANES)))
    return blocks


def block_tools(block, width):
    low, high, start, end = block
    size = end - start
    out_row = lax.broadcasted_iota(jnp.int32, (size, width), 0) + start
    within = lax.broadcasted_iota(jnp.int32, (size, width), 1)
    lane = lax.broadcasted_iota(jnp.int32, (size, size), 1) + start
    row = lax.broadcasted_iota(jnp.int32, (size, size), 0) + start
    spread = jnp.zeros((size, width), jnp.float32)
    same = jnp.zeros((size, size), jnp.float32)
    for first in range(low, high, width):
        spread += (out_row == within + first).astype(jnp.float32)
        in_lane = (lane >= first) & (lane < first + width)
        in_row = (row >= first) & (row < first + width)
        same += (in_lane & in_row).astype(jnp.float32)
    return spread.astype(jnp.bfloat16), same


def dense_tap(group_ref, tap, block, spread, same):
    _, _, start, end = block
    full = jnp.dot(spread, group_ref[tap, :, start:end], preferred_element_type=jnp.float32)
    return (full * same).astype(jnp.bfloat16)


def store_shifts(wide_ref, shift_ref, sign):
    rows = shift_ref.shape[1]
    for col in range(3):
        at = EDGE + sign * (col - 1)
        chans = wide_ref.shape[1]
        shift_ref[col, :, 0:chans] = wide_ref[at : at + rows, :].astype(jnp.bfloat16)
        if shift_ref.shape[2] > chans:
            blank = jnp.zeros((rows, shift_ref.shape[2] - chans), jnp.bfloat16)
            shift_ref[col, :, chans:] = blank


def conv_kernel(feat_ref, group_ref, squeeze_ref, *refs):
    conv_ref, pad_ref, sq_ref, flat_ref, wide_ref, shift_ref = refs
    frames, _, chans = feat_ref.shape
    width = group_ref.shape[1]
    rows = frames * FRAME_ROWS
    wide_ref[...] = jnp.zeros_like(wide_ref)
    for frame in range(frames):
        flat_ref[...] = feat_ref[frame].astype(jnp.float32)
        for y in range(SIDE):
            at = EDGE + frame * FRAME_ROWS + (y + 1) * WIDE + 1
            wide_ref[at : at + SIDE, :] = flat_ref[y * SIDE : (y + 1) * SIDE, :]
    store_shifts(wide_ref, shift_ref, 1)
    pad_ref[...] = shift_ref[1]
    conv_ref[...] = jnp.zeros_like(conv_ref)
    body = rows - 2 * WIDE
    for block in channel_blocks(chans, width):
        _, _, start, end = block
        spread, same = block_tools(block, width)
        total = jnp.zeros((body, end - start), jnp.float32)
        for tap in range(9):
            down, across = divmod(tap, 3)
            weights = dense_tap(group_ref, tap, block, spread, same)
            source = shift_ref[across, down * WIDE : down * WIDE + body, start:end]
            total += contract_last(source, weights)
        conv_ref[WIDE : WIDE + body, start:end] += total
    conv = conv_ref[...] * inside(rows)
    conv_ref[...] = conv
    active = conv * jax.nn.sigmoid(conv)
    pooled = jnp.concatenate(
        [
            jnp.sum(active[f * FRAME_ROWS : (f + 1) * FRAME_ROWS], axis=0, keepdims=True)
            for f in range(frames)
        ],
        axis=0,
    ) * (1.0 / (SIDE * SIDE))
    sq_ref[...] = contract_exact(pooled, squeeze_ref[...].astype(jnp.float32))


def hidden_kernel(conv_ref, pad_ref, sq_ref, expand_ref, even_ref, odd_ref, excite_ref):
    squeezed = sq_ref[...]
    relaxed = squeezed * jax.nn.sigmoid(squeezed)
    excite = jax.nn.sigmoid(
        jnp.dot(relaxed, expand_ref[...].astype(jnp.float32), precision=lax.Precision.HIGHEST)
    )
    excite_ref[...] = excite
    for frame, out_ref in enumerate((even_ref, odd_ref)):
        rows = slice(frame * FRAME_ROWS, (frame + 1) * FRAME_ROWS)
        conv = conv_ref[rows, :]
        active = conv * jax.nn.sigmoid(conv)
        hidden = pad_ref[rows, :].astype(jnp.float32) + active * excite[frame : frame + 1]
        out_ref[...] = hidden.astype(jnp.bfloat16)


def select_rows(to_patches):
    shape = (FRAME_ROWS, FRAME_ROWS)
    out_row = lax.broadcasted_iota(jnp.int32, shape, 0)
    in_row = lax.broadcasted_iota(jnp.int32, shape, 1)
    patch_row, frame_row = (out_row, in_row) if to_patches else (in_row, out_row)
    down, across = patch_row >> 7, (patch_row >> 6) & 1
    a, b = (patch_row >> 3) & 7, patch_row & 7
    return ((2 * a + down) * WIDE + 2 * b + across == frame_row).astype(jnp.float32)


def facts_kernel(clip_ref, keep_ref, out_ref):
    shard = lax.axis_index("ctx")
    frames = clip_ref.shape[0]
    out_ref[0] = shard % 2
    for block in range(2):
        pair = shard // 2 * 2 + block
        clip = clip_ref[2 * pair]
        start = jnp.int32(0)
        for other in range(0, frames, 2):
            start += jnp.where(clip_ref[other] < clip, 1, 0)
        out_ref[1 + block] = keep_ref[clip] - (pair - start) * (OUT_SIDE * OUT_SIDE)
    before = clip_ref[jnp.maximum(2 * shard - 1, 0)]
    chip, chips = shard // 2, lax.axis_size("ctx") // 2
    out_ref[4] = jnp.where(chip % 2 == 0, chip // 2, chips - 1 - chip // 2)
    out_ref[3] = jnp.where((shard > 0) & (before == clip_ref[2 * shard]), 1, 0)


def token_place(row, core, unit):
    per_block = OUT_SIDE * OUT_SIDE
    within = row % per_block
    block = (within // unit) % 2
    target_core = jnp.where(row < per_block, core, 1 - core)
    return block, unit * (2 * (within // (2 * unit)) + target_core) + within % unit


def reorder_matrix(core, unit, to_sent):
    shape = (2 * OUT_SIDE * OUT_SIDE,) * 2
    out_row = lax.broadcasted_iota(jnp.int32, shape, 0)
    in_row = lax.broadcasted_iota(jnp.int32, shape, 1)
    sent, natural = (out_row, in_row) if to_sent else (in_row, out_row)
    block, token = token_place(sent, core, unit)
    source = jnp.where(block == core, 0, OUT_SIDE * OUT_SIDE) + token
    return (source == natural).astype(jnp.bfloat16)


def order_kernel(unit, facts_ref, own_ref, mate_ref, out_ref):
    rows = jnp.concatenate([own_ref[...], mate_ref[...]], axis=0)
    matrix = reorder_matrix(facts_ref[0], unit, True)
    out_ref[...] = jnp.dot(matrix, rows, preferred_element_type=jnp.float32).astype(jnp.bfloat16)


def patch_kernel(facts_ref, halo_ref, even_ref, out_ref):
    chans = halo_ref.shape[1]
    per_frame = OUT_SIDE * OUT_SIDE
    select = select_rows(True).astype(jnp.bfloat16)
    for frame, source in enumerate((halo_ref, even_ref)):
        rows = jnp.dot(select, source[...], preferred_element_type=jnp.float32)
        if frame == 0:
            rows = rows * facts_ref[3].astype(jnp.float32)
        rows = rows.astype(jnp.bfloat16)
        for tap in range(4):
            at = (frame * 4 + tap) * chans
            out_ref[:, at : at + chans] = rows[tap * per_frame : (tap + 1) * per_frame]


def unpatch_kernel(facts_ref, own_ref, mate_ref, out_ref, facts_out_ref):
    for place in range(facts_ref.shape[0]):
        facts_out_ref[place] = facts_ref[place]
    chans = out_ref.shape[1]
    rows = own_ref[...] + mate_ref[...].astype(jnp.float32)
    pieces = [rows[:, tap * chans : (tap + 1) * chans] for tap in range(4)]
    rows = jnp.concatenate(pieces, axis=0)
    select = select_rows(False).astype(jnp.bfloat16)
    coarse = rows.astype(jnp.bfloat16)
    frame = jnp.dot(select, coarse, preferred_element_type=jnp.float32)
    if out_ref.dtype == jnp.bfloat16:
        frame = frame * facts_ref[3].astype(jnp.float32)
    else:
        rest = (rows - coarse.astype(jnp.float32)).astype(jnp.bfloat16)
        frame += jnp.dot(select, rest, preferred_element_type=jnp.float32)
    out_ref[...] = (frame * inside(FRAME_ROWS)).astype(out_ref.dtype)


def excite_grad_kernel(even_ref, odd_ref, conv_ref, excite_ref, expand_ref, out_ref):
    sums = []
    for frame, grad_ref in enumerate((even_ref, odd_ref)):
        conv = conv_ref[frame * FRAME_ROWS : (frame + 1) * FRAME_ROWS, :]
        active = conv * jax.nn.sigmoid(conv)
        sums.append(jnp.sum(grad_ref[...].astype(jnp.float32) * active, axis=0, keepdims=True))
    excite = excite_ref[...]
    inner = jnp.concatenate(sums, axis=0) * excite * (1.0 - excite)
    out_ref[...] = contract_exact(inner, expand_ref[...].astype(jnp.float32))


def conv_grad_kernel(
    width, even_ref, odd_ref, conv_ref, excite_ref, sq_ref, relaxed_ref, squeeze_ref, *refs
):
    *dense_refs, out_ref, flat_ref, wide_ref, shift_ref, grad_ref = refs
    frames, _, chans = out_ref.shape
    rows = frames * FRAME_ROWS
    grad_squeezed = relaxed_ref[...] * silu_slope(sq_ref[...])
    pooled = jnp.dot(
        grad_squeezed, squeeze_ref[...].astype(jnp.float32), precision=lax.Precision.HIGHEST
    ) * (1.0 / (SIDE * SIDE))
    wide_ref[0:EDGE, :] = jnp.zeros((EDGE, chans), jnp.float32)
    wide_ref[EDGE + rows :, :] = jnp.zeros((EDGE, chans), jnp.float32)
    good = inside(FRAME_ROWS)
    for frame, source in enumerate((even_ref, odd_ref)):
        at = frame * FRAME_ROWS
        grad = source[...].astype(jnp.float32)
        grad_ref[at : at + FRAME_ROWS, :] = grad
        active = grad * excite_ref[frame : frame + 1, :] + pooled[frame : frame + 1]
        slope = silu_slope(conv_ref[at : at + FRAME_ROWS, :])
        wide_ref[EDGE + at : EDGE + at + FRAME_ROWS, :] = active * slope * good
    store_shifts(wide_ref, shift_ref, -1)
    body = rows - 2 * WIDE
    for block, dense_ref in zip(channel_blocks(chans, width), dense_refs):
        start = block[2]
        sources = []
        for tap in range(9):
            down, across = divmod(tap, 3)
            at = (2 - down) * WIDE
            sources.append(shift_ref[across, at : at + body, start : start + WINDOW])
        total = jnp.dot(
            jnp.concatenate(sources, axis=1), dense_ref[...], preferred_element_type=jnp.float32
        )
        end = min(chans, start + WINDOW)
        grad_ref[WIDE : WIDE + body, start:end] += total[:, : end - start]
    for frame in range(frames):
        for y in range(SIDE):
            at = frame * FRAME_ROWS + (y + 1) * WIDE + 1
            flat_ref[y * SIDE : (y + 1) * SIDE, :] = grad_ref[at : at + SIDE, :]
        out_ref[frame] = flat_ref[...].astype(jnp.bfloat16)


def f32(*shape):
    return jax.ShapeDtypeStruct(shape, jnp.float32)


def bf16(*shape):
    return jax.ShapeDtypeStruct(shape, jnp.bfloat16)


def conv_forward(features, group_kernel, squeeze_in):
    frames, cells, chans = features.shape
    rows = frames * FRAME_ROWS
    return whole_call(
        conv_kernel,
        (f32(rows, chans), bf16(rows, chans), f32(frames, squeeze_in.shape[0])),
        [
            pltpu.VMEM((cells, chans), jnp.float32),
            pltpu.VMEM((rows + 2 * EDGE, chans), jnp.float32),
            pltpu.VMEM((3, rows, chans), jnp.bfloat16),
        ],
    )(features, group_kernel, squeeze_in)


def hidden_frames(conv, padded, squeezed, squeeze_out):
    rows, chans = conv.shape
    return whole_call(
        hidden_kernel,
        (bf16(FRAME_ROWS, chans), bf16(FRAME_ROWS, chans), f32(rows // FRAME_ROWS, chans)),
        [],
    )(conv, padded, squeezed, squeeze_out)


def vmem_specs(count):
    return [pl.BlockSpec(memory_space=pltpu.SMEM)] + [pl.BlockSpec(memory_space=pltpu.VMEM)] * count


def facts_of(frame_clip, clip_keep):
    smem = pl.BlockSpec(memory_space=pltpu.SMEM)
    return pl.pallas_call(
        facts_kernel,
        out_shape=jax.ShapeDtypeStruct((5,), jnp.int32),
        in_specs=[smem, smem],
        out_specs=smem,
        cost_estimate=FREE,
    )(frame_clip, clip_keep)


def order_rows(facts, own, mate, unit):
    rows, columns = own.shape
    return pl.pallas_call(
        functools.partial(order_kernel, unit),
        out_shape=bf16(2 * rows, columns),
        in_specs=vmem_specs(2),
        compiler_params=pltpu.CompilerParams(vmem_limit_bytes=VMEM_BYTES),
        cost_estimate=FREE,
    )(facts, own, mate)


def take_patches(facts, halo, even):
    chans = even.shape[1]
    return pl.pallas_call(
        patch_kernel,
        out_shape=bf16(OUT_SIDE * OUT_SIDE, 8 * chans),
        in_specs=vmem_specs(2),
        compiler_params=pltpu.CompilerParams(vmem_limit_bytes=VMEM_BYTES),
        cost_estimate=FREE,
    )(facts, halo, even)


def return_patches(facts, own, mate, chans, dtype):
    return pl.pallas_call(
        unpatch_kernel,
        out_shape=(
            jax.ShapeDtypeStruct((FRAME_ROWS, chans), dtype),
            jax.ShapeDtypeStruct(facts.shape, jnp.int32),
        ),
        in_specs=vmem_specs(2),
        out_specs=vmem_specs(1)[::-1],
        compiler_params=pltpu.CompilerParams(vmem_limit_bytes=VMEM_BYTES),
        cost_estimate=FREE,
    )(facts, own, mate)


def excite_grad(even, odd, conv, excite, squeeze_out):
    rows, chans = conv.shape
    return whole_call(
        excite_grad_kernel,
        f32(rows // FRAME_ROWS, squeeze_out.shape[0]),
        [],
    )(even, odd, conv, excite, squeeze_out)


def conv_backward(even, odd, conv, excite, squeezed, grad_relaxed, squeeze_in, dense, width):
    rows, chans = conv.shape
    frames = rows // FRAME_ROWS
    lanes = channel_blocks(chans, width)[-1][2] + WINDOW
    return whole_call(
        functools.partial(conv_grad_kernel, width),
        bf16(frames, SIDE * SIDE, chans),
        [
            pltpu.VMEM((SIDE * SIDE, chans), jnp.float32),
            pltpu.VMEM((rows + 2 * EDGE, chans), jnp.float32),
            pltpu.VMEM((3, rows, lanes), jnp.bfloat16),
            pltpu.VMEM((rows, chans), jnp.float32),
        ],
        pl.CostEstimate(flops=rows * chans * 9216, bytes_accessed=16 * rows * chans, transcendentals=0),
    )(even, odd, conv, excite, squeezed, grad_relaxed, squeeze_in, *dense)


def dense_kernel(facts_ref, group_ref, *dense_refs):
    _, width, chans = group_ref.shape
    for block, dense_ref in zip(channel_blocks(chans, width), dense_refs):
        low, high, start, _ = block
        end = min(chans, start + WINDOW)
        spread, same = block_tools((low, high, start, start + WINDOW), width)
        dense_ref[...] = jnp.zeros_like(dense_ref)
        for tap in range(9):
            full = jnp.dot(spread, group_ref[tap, :, start:end], preferred_element_type=jnp.float32)
            rows = slice(tap * WINDOW, (tap + 1) * WINDOW)
            dense_ref[rows, 0 : end - start] = (full * same[:, : end - start]).astype(jnp.bfloat16)


def dense_weights(facts, group_kernel):
    _, width, chans = group_kernel.shape
    outs = (bf16(9 * WINDOW, WINDOW),) * len(channel_blocks(chans, width))
    return facts_call(dense_kernel, outs, facts, (group_kernel,))


def shifted(value, axis, by):
    count = lax.axis_size(axis)
    pairs = [(i, i + by) for i in range(count) if 0 <= i + by < count]
    return lax.ppermute(value, axis, pairs)


def ring_order(chips):
    return list(range(0, chips, 2)) + list(range(1, chips, 2))[::-1]


def ring_pairs(count, by):
    order = ring_order(count // 2)
    pairs = []
    for place, chip in enumerate(order):
        target = order[(place + by) % len(order)]
        pairs += [(2 * chip, 2 * target), (2 * chip + 1, 2 * target + 1)]
    return pairs


def swap_cores(value):
    return lax.ppermute(value, "ctx", [(i, i ^ 1) for i in range(lax.axis_size("ctx"))])


def tp_terms(value):
    size = lax.axis_size("tp")
    reach, other = 1, None
    while reach < size:
        value = value if other is None else value + other
        other = lax.ppermute(value, "tp", [(i, i ^ reach) for i in range(size)])
        reach *= 2
    return value, jnp.zeros_like(value) if other is None else other


def sum_tp(value):
    value, other = tp_terms(value)
    return value + other


def ring_send(value, by):
    return lax.ppermute(value, "ctx", ring_pairs(lax.axis_size("ctx"), by))


def tie(*values):
    return lax.optimization_barrier(values)


def stacked_contract(left, blocks):
    blocks = [ref[...] for ref in blocks]
    if blocks[0].shape[0] % 8 == 0:
        blocks = [jnp.concatenate(blocks, axis=0)]
    return jnp.concatenate([contract_last(left, block) for block in blocks], axis=1)


def pre_kernel(patch_ref, *refs):
    *blocks, out_ref = refs
    out_ref[...] = stacked_contract(patch_ref[...], blocks)


def back_kernel(keep_ref, send_ref, *refs):
    *blocks, out_ref = refs
    back = jnp.concatenate([keep_ref[...], send_ref[...]], axis=0)
    out_ref[...] = stacked_contract(back, blocks)


def live_rows(facts_ref, rows, unit):
    block, token = token_place(
        lax.broadcasted_iota(jnp.int32, (rows, 1), 0), facts_ref[0], unit
    )
    return (token < jnp.where(block == 0, facts_ref[1], facts_ref[2])).astype(jnp.float32)


def stacked_dot(pieces, blocks):
    if blocks[0].shape[0] % 8 == 0:
        pieces = [jnp.concatenate(pieces, axis=1)]
        blocks = [jnp.concatenate(blocks, axis=0)]
    total = 0.0
    for piece, block in zip(pieces, blocks):
        total += jnp.dot(piece, block, preferred_element_type=jnp.float32)
    return total


def totals_kernel(pieces, unit, parts, first, facts_ref, *refs):
    grad_act = refs[0][...] + refs[1][...]
    count = len(pieces)
    slopes, blocks = refs[2:4], refs[4 : 4 + count]
    before, after = refs[4 + count : -2 * len(parts)], refs[-2 * len(parts) :]
    rows, width = grad_act.shape[0], blocks[0].shape[0]
    slope = jnp.concatenate(
        [slopes[source][:, index * width : (index + 1) * width] for source, index in pieces], axis=1
    )
    factor = jnp.dot(
        reorder_matrix(facts_ref[0], unit, False),
        (grad_act * slope).astype(jnp.bfloat16),
        preferred_element_type=jnp.float32,
    ).astype(jnp.bfloat16)
    factors = [factor[:, place * width : (place + 1) * width] for place in range(count)]
    for part, lanes in enumerate(parts):
        total = stacked_dot(factors, [ref[:, lanes] for ref in blocks])
        for half in range(2):
            value = total[half * rows // 2 : (half + 1) * rows // 2]
            value = value if first else before[2 * part + half][...] + value
            ref = after[2 * part + half]
            ref[...] = value.astype(ref.dtype)


def ring_offsets(chips):
    offsets = [0]
    for step in range(1, chips // 2):
        offsets += [-step, step]
    return offsets + [chips // 2]


def block_columns(facts_ref, offset, chips, width):
    shape = (width, chips * width)
    place = (facts_ref[4] + offset + chips) % chips
    column = lax.broadcasted_iota(jnp.int32, shape, 1)
    return (column == lax.broadcasted_iota(jnp.int32, shape, 0) + place * width).astype(jnp.bfloat16)


def exchange_matrix(core, unit, to_sent):
    per_block = OUT_SIDE * OUT_SIDE
    shape = (2 * per_block,) * 2
    out_row = lax.broadcasted_iota(jnp.int32, shape, 0)
    in_row = lax.broadcasted_iota(jnp.int32, shape, 1)
    sent, kept = (out_row, in_row) if to_sent else (in_row, out_row)
    target_core = (sent // (2 * unit)) % 2
    within = sent // (4 * unit) * (2 * unit) + sent % (2 * unit)
    return (within + jnp.where(target_core == core, 0, per_block) == kept).astype(jnp.bfloat16)


def act_kernel(offsets, chips, unit, last, facts_ref, own_ref, other_ref, *refs):
    *before, slope_ref, out_ref = refs
    pre = own_ref[...] + other_ref[...]
    width = pre.shape[1] // len(offsets)
    live = live_rows(facts_ref, pre.shape[0], unit)
    sigma = jax.nn.sigmoid(pre)
    slope_ref[...] = sigma * (1.0 + pre * (1.0 - sigma)) * live
    act = (pre * sigma * live).astype(jnp.bfloat16)
    total = before[0][...].astype(jnp.float32) if last else 0.0
    for place, offset in enumerate(offsets):
        columns = block_columns(facts_ref, offset, chips, width)
        piece = act[:, place * width : (place + 1) * width]
        total += jnp.dot(piece, columns, preferred_element_type=jnp.float32)
    total = total.astype(jnp.bfloat16)
    if last:
        matrix = exchange_matrix(facts_ref[0], unit, True)
        total = jnp.dot(matrix, total, preferred_element_type=jnp.float32).astype(jnp.bfloat16)
    out_ref[...] = total


def token_kernel(offsets, chips, unit, facts_ref, act_ref, *refs):
    count = len(offsets)
    blocks, refs = refs[:count], refs[count:]
    keep_ref, send_ref, *buffers, sems = refs
    copies = [
        pltpu.make_async_copy(ref, buffer, sems.at[place])
        for place, (ref, buffer) in enumerate(zip(blocks, buffers))
    ]
    for copy in copies:
        copy.start()
    width = buffers[0].shape[0]
    matrix = exchange_matrix(facts_ref[0], unit, False)
    act = jnp.dot(matrix, act_ref[...], preferred_element_type=jnp.float32).astype(jnp.bfloat16)
    pieces = [
        contract_last(act, block_columns(facts_ref, offset, chips, width)).astype(jnp.bfloat16)
        for offset in offsets
    ]
    for copy in copies:
        copy.wait()
    total = stacked_dot(pieces, [buffer[...] for buffer in buffers])
    rows = keep_ref.shape[0]
    keep_ref[...] = total[:rows]
    send_ref[...] = total[rows:].astype(jnp.bfloat16)


def block_products(kernel, left, blocks):
    rows = 2 * OUT_SIDE * OUT_SIDE
    return whole_call(kernel, f32(rows, len(blocks) * blocks[0].shape[0]), [])(*left, *blocks)


def facts_call(kernel, outs, facts, operands, cost=FREE):
    return pl.pallas_call(
        kernel,
        out_shape=outs,
        in_specs=vmem_specs(len(operands)),
        compiler_params=pltpu.CompilerParams(vmem_limit_bytes=VMEM_BYTES),
        cost_estimate=cost,
    )(facts, *operands)


def add_gradients(facts, terms, slopes, pieces, blocks, before, unit, parts, last):
    rows = terms[0].shape[0] // 2
    kernel = functools.partial(totals_kernel, pieces, unit, parts, not before)
    outs = ()
    for lanes in parts:
        shape = rows, lanes.stop - lanes.start
        outs += f32(*shape), (bf16 if last else f32)(*shape)
    return tuple(facts_call(kernel, outs, facts, (*terms, *slopes, *blocks, *before)))


def act_and_slope(facts, terms, offsets, chips, before, unit):
    rows, columns = terms[0].shape
    kernel = functools.partial(act_kernel, offsets, chips, unit, bool(before))
    outs = f32(rows, columns), bf16(rows, columns // len(offsets) * chips)
    return facts_call(kernel, outs, facts, (*terms, *before))


def token_products(facts, act, offsets, chips, blocks, unit):
    rows, columns = act.shape[0] // 2, blocks[0].shape[1]
    return pl.pallas_call(
        functools.partial(token_kernel, offsets, chips, unit),
        out_shape=(f32(rows, columns), bf16(rows, columns)),
        in_specs=vmem_specs(1) + [pl.BlockSpec(memory_space=pl.ANY)] * len(blocks),
        scratch_shapes=[pltpu.VMEM(block.shape, block.dtype) for block in blocks]
        + [pltpu.SemaphoreType.DMA((len(blocks),))],
        compiler_params=pltpu.CompilerParams(vmem_limit_bytes=VMEM_BYTES),
        cost_estimate=FREE,
    )(facts, act, *blocks)


def chips_exchange(value):
    count = lax.axis_size("ctx")
    groups = [list(range(core, count, 2)) for core in range(2)]
    return lax.all_to_all(
        value, "ctx", split_axis=0, concat_axis=0, tiled=True, axis_index_groups=groups
    )


def per_device(
    features,
    group_kernel,
    squeeze_in,
    squeeze_out,
    sampler_kernel,
    readout_kernel,
    frame_clip,
    clip_keep,
    token_cotangent,
):
    chans = features.shape[2]
    count = lax.axis_size("ctx")
    steps, unit = count // 4, OUT_SIDE * OUT_SIDE // count
    flat_sampler = sampler_kernel.reshape(sampler_kernel.shape[0], 8 * chans)
    chips = count // 2
    s_up, s_down = ring_send(flat_sampler, 1), ring_send(flat_sampler, -1)
    group_kernel = jnp.swapaxes(group_kernel, 1, 2)
    squeeze_in = squeeze_in.T
    facts = facts_of(frame_clip, clip_keep)

    conv, padded, squeezed = conv_forward(features, group_kernel, squeeze_in)
    token_cotangent, squeezed = tie(token_cotangent, squeezed)
    back = chips_exchange(token_cotangent)
    squeezed = sum_tp(squeezed)
    even, odd, excite = hidden_frames(conv, padded, squeezed, squeeze_out)
    halo = shifted(odd, "ctx", 1)

    s_up, s_down = [flat_sampler, s_up], [flat_sampler, s_down]
    s_up[1], s_down[1], even, readout_kernel = tie(s_up[1], s_down[1], even, readout_kernel)
    for step in range(2, steps):
        s_up.append(ring_send(s_up[-1], 1))
        s_down.append(ring_send(s_down[-1], -1))
        if step == 2:
            halo, s_up[2], s_down[2] = tie(halo, s_up[2], s_down[2])
            r_down = [readout_kernel, ring_send(readout_kernel, -1)]
            patches = take_patches(facts, halo, even)
            patches = order_rows(facts, patches, swap_cores(patches), unit)
    s_up[-1], s_down[-1], back, readout_kernel = tie(s_up[-1], s_down[-1], back, readout_kernel)
    back = (back, swap_cores(back))
    s_last = ring_send(s_up[-1], 1)
    r_up = [readout_kernel, ring_send(readout_kernel, 1)]
    samplers = [flat_sampler] + [block for pair in zip(s_up[1:], s_down[1:]) for block in pair]
    offsets = ring_offsets(chips)
    count = 2 * steps - 3
    first_pre = tp_terms(block_products(pre_kernel, (patches,), samplers[:count]))
    r_down[1], s_last, *first_pre = tie(r_down[1], s_last, *first_pre)
    for step in range(1, steps - 2):
        r_down.append(ring_send(r_down[-1], -1))
        r_up.append(ring_send(r_up[-1], 1))
    first_slope, first_act = act_and_slope(facts, first_pre, offsets[:count], chips, (), unit)
    last_pre = block_products(pre_kernel, (patches,), [*samplers[count:], s_last])
    last_slope, act = act_and_slope(
        facts, tp_terms(last_pre), offsets[count:], chips, (first_act,), unit
    )
    slopes = first_slope, last_slope
    r_down[-1], act = tie(r_down[-1], act)
    r_down.append(ring_send(r_down[-1], -1))
    early = r_down[: steps - 1]
    sums = block_products(back_kernel, back, early)
    r_up[-1], act, *terms = tie(r_up[-1], chips_exchange(act), *tp_terms(sums))
    r_up.append(ring_send(r_up[-1], 1))
    halo_lanes, even_lanes = slice(0, 4 * chans), slice(4 * chans, 8 * chans)
    both = halo_lanes, even_lanes
    pieces = [(0, 2 * step) for step in range(steps - 1)]
    blocks = [flat_sampler] + s_down[1 : steps - 1]
    grads = add_gradients(facts, terms, slopes, pieces, blocks, (), unit, both, False)
    middle = r_up[1 : steps - 1] + [r_down[steps - 1]]
    r_down.append(ring_send(r_down[-1], -1))
    terms = tp_terms(block_products(back_kernel, back, middle))
    pieces = [(0, 2 * step - 1) for step in range(1, steps - 1)] + [(1, 1)]
    blocks = s_up[1 : steps - 1] + [s_down[steps - 1]]
    grads = add_gradients(facts, terms, slopes, pieces, blocks, grads, unit, both, False)

    late_up, late_down, *grads = tie(r_up[-1], r_down[-1], *grads)
    terms = tp_terms(block_products(back_kernel, back, [late_up, late_down]))
    pieces, blocks = [(1, 0), (1, 2)], [s_up[-1], s_last]
    halo_own, halo_mate = add_gradients(
        facts, terms, slopes, pieces, blocks, grads[:2], unit, (halo_lanes,), True
    )
    halo_mate, first_term = tie(halo_mate, terms[0])
    even_own, even_mate = add_gradients(
        facts, (first_term, terms[1]), slopes, pieces, blocks, grads[2:], unit, (even_lanes,), True
    )
    lead, facts_late = return_patches(facts, halo_own, swap_cores(halo_mate), chans, jnp.bfloat16)
    grad_odd = shifted(lead, "ctx", -1)
    grad_even, facts_late = return_patches(
        facts_late, even_own, swap_cores(even_mate), chans, jnp.float32
    )
    places = [*range(steps - 1), *range(-1, 1 - steps, -1), steps - 1, 1 - steps, steps]
    tokens = token_products(
        facts_late, act, places, chips, [*early, *middle, late_up, late_down], unit
    )
    grad_relaxed = sum_tp(excite_grad(grad_even, grad_odd, conv, excite, squeeze_out))
    llm_tokens = (tokens[0] + swap_cores(tokens[1]).astype(jnp.float32)).astype(jnp.bfloat16)
    grad_features = conv_backward(
        grad_even, grad_odd, conv, excite, squeezed, grad_relaxed, squeeze_in,
        dense_weights(facts_late, group_kernel), group_kernel.shape[1],
    )
    return (llm_tokens, grad_features)


def solution(mesh):
    placed = (
        P("ctx", None, "tp"),
        P(None, "tp", None),
        P("tp", None),
        P(None, "tp"),
        P("ctx", None, "tp"),
        P("ctx", "tp"),
        P(),
        P(),
        P("ctx", "tp"),
    )
    return jax.shard_map(
        per_device,
        mesh=mesh,
        in_specs=placed,
        out_specs=(P("ctx", "tp"), P("ctx", None, "tp")),
        check_vma=False,
    )
```

```python
import functools

import jax
import jax.numpy as jnp
from jax import lax
from jax.experimental import pallas as pl
from jax.experimental.pallas import tpu as pltpu
from jax.sharding import PartitionSpec as P

SIDE = 14
OUT_SIDE = 8
WIDE = 16
FRAME_ROWS = WIDE * WIDE
EDGE = 8
LANES = 128
WINDOW = 256
VMEM_BYTES = 16 * 2**20
FREE = pl.CostEstimate(flops=0, bytes_accessed=0, transcendentals=0)


def whole_call(kernel, outs, scratch, cost=FREE):
    return pl.pallas_call(
        kernel,
        out_shape=outs,
        scratch_shapes=scratch,
        compiler_params=pltpu.CompilerParams(vmem_limit_bytes=VMEM_BYTES),
        cost_estimate=cost,
    )


def contract_last(left, right):
    return lax.dot_general(
        left, right, (((1,), (1,)), ((), ())), preferred_element_type=jnp.float32
    )


def contract_exact(left, right):
    return lax.dot_general(
        left,
        right,
        (((1,), (1,)), ((), ())),
        precision=lax.Precision.HIGHEST,
        preferred_element_type=jnp.float32,
    )


def silu_slope(values):
    sigma = jax.nn.sigmoid(values)
    return sigma * (1.0 + values * (1.0 - sigma))


def inside(rows):
    row = lax.broadcasted_iota(jnp.int32, (rows, 1), 0)
    across, down = row & (WIDE - 1), (row // WIDE) & (WIDE - 1)
    good = (across >= 1) & (across <= SIDE) & (down >= 1) & (down <= SIDE)
    return good.astype(jnp.float32)


def channel_blocks(chans, width):
    span = 4 * width
    blocks = []
    for low in range(0, chans, span):
        high = min(chans, low + span)
        blocks.append((low, high, low // LANES * LANES, min(chans, -(-high // LANES) * LANES)))
    return blocks


def block_tools(block, width):
    low, high, start, end = block
    size = end - start
    out_row = lax.broadcasted_iota(jnp.int32, (size, width), 0) + start
    within = lax.broadcasted_iota(jnp.int32, (size, width), 1)
    lane = lax.broadcasted_iota(jnp.int32, (size, size), 1) + start
    row = lax.broadcasted_iota(jnp.int32, (size, size), 0) + start
    spread = jnp.zeros((size, width), jnp.float32)
    same = jnp.zeros((size, size), jnp.float32)
    for first in range(low, high, width):
        spread += (out_row == within + first).astype(jnp.float32)
        in_lane = (lane >= first) & (lane < first + width)
        in_row = (row >= first) & (row < first + width)
        same += (in_lane & in_row).astype(jnp.float32)
    return spread.astype(jnp.bfloat16), same


def dense_tap(group_ref, tap, block, spread, same):
    _, _, start, end = block
    full = jnp.dot(spread, group_ref[tap, :, start:end], preferred_element_type=jnp.float32)
    return (full * same).astype(jnp.bfloat16)


def store_shifts(wide_ref, shift_ref, sign):
    rows = shift_ref.shape[1]
    for col in range(3):
        at = EDGE + sign * (col - 1)
        chans = wide_ref.shape[1]
        shift_ref[col, :, 0:chans] = wide_ref[at : at + rows, :].astype(jnp.bfloat16)
        if shift_ref.shape[2] > chans:
            blank = jnp.zeros((rows, shift_ref.shape[2] - chans), jnp.bfloat16)
            shift_ref[col, :, chans:] = blank


def conv_kernel(feat_ref, group_ref, squeeze_ref, *refs):
    conv_ref, pad_ref, sq_ref, flat_ref, wide_ref, shift_ref = refs
    frames, _, chans = feat_ref.shape
    width = group_ref.shape[1]
    rows = frames * FRAME_ROWS
    wide_ref[...] = jnp.zeros_like(wide_ref)
    for frame in range(frames):
        flat_ref[...] = feat_ref[frame].astype(jnp.float32)
        for y in range(SIDE):
            at = EDGE + frame * FRAME_ROWS + (y + 1) * WIDE + 1
            wide_ref[at : at + SIDE, :] = flat_ref[y * SIDE : (y + 1) * SIDE, :]
    store_shifts(wide_ref, shift_ref, 1)
    pad_ref[...] = shift_ref[1]
    conv_ref[...] = jnp.zeros_like(conv_ref)
    body = rows - 2 * WIDE
    for block in channel_blocks(chans, width):
        _, _, start, end = block
        spread, same = block_tools(block, width)
        total = jnp.zeros((body, end - start), jnp.float32)
        for tap in range(9):
            down, across = divmod(tap, 3)
            weights = dense_tap(group_ref, tap, block, spread, same)
            source = shift_ref[across, down * WIDE : down * WIDE + body, start:end]
            total += contract_last(source, weights)
        conv_ref[WIDE : WIDE + body, start:end] += total
    conv = conv_ref[...] * inside(rows)
    conv_ref[...] = conv
    active = conv * jax.nn.sigmoid(conv)
    pooled = jnp.concatenate(
        [
            jnp.sum(active[f * FRAME_ROWS : (f + 1) * FRAME_ROWS], axis=0, keepdims=True)
            for f in range(frames)
        ],
        axis=0,
    ) * (1.0 / (SIDE * SIDE))
    sq_ref[...] = contract_exact(pooled, squeeze_ref[...].astype(jnp.float32))


def hidden_kernel(conv_ref, pad_ref, sq_ref, expand_ref, even_ref, odd_ref, excite_ref):
    squeezed = sq_ref[...]
    relaxed = squeezed * jax.nn.sigmoid(squeezed)
    excite = jax.nn.sigmoid(
        jnp.dot(relaxed, expand_ref[...].astype(jnp.float32), precision=lax.Precision.HIGHEST)
    )
    excite_ref[...] = excite
    for frame, out_ref in enumerate((even_ref, odd_ref)):
        rows = slice(frame * FRAME_ROWS, (frame + 1) * FRAME_ROWS)
        conv = conv_ref[rows, :]
        active = conv * jax.nn.sigmoid(conv)
        hidden = pad_ref[rows, :].astype(jnp.float32) + active * excite[frame : frame + 1]
        out_ref[...] = hidden.astype(jnp.bfloat16)


def select_rows(to_patches):
    shape = (FRAME_ROWS, FRAME_ROWS)
    out_row = lax.broadcasted_iota(jnp.int32, shape, 0)
    in_row = lax.broadcasted_iota(jnp.int32, shape, 1)
    patch_row, frame_row = (out_row, in_row) if to_patches else (in_row, out_row)
    down, across = patch_row >> 7, (patch_row >> 6) & 1
    a, b = (patch_row >> 3) & 7, patch_row & 7
    return ((2 * a + down) * WIDE + 2 * b + across == frame_row).astype(jnp.float32)


def facts_kernel(clip_ref, keep_ref, out_ref):
    shard = lax.axis_index("ctx")
    frames = clip_ref.shape[0]
    out_ref[0] = shard % 2
    for block in range(2):
        pair = shard // 2 * 2 + block
        clip = clip_ref[2 * pair]
        start = jnp.int32(0)
        for other in range(0, frames, 2):
            start += jnp.where(clip_ref[other] < clip, 1, 0)
        out_ref[1 + block] = keep_ref[clip] - (pair - start) * (OUT_SIDE * OUT_SIDE)
    before = clip_ref[jnp.maximum(2 * shard - 1, 0)]
    chip, chips = shard // 2, lax.axis_size("ctx") // 2
    out_ref[4] = jnp.where(chip % 2 == 0, chip // 2, chips - 1 - chip // 2)
    out_ref[3] = jnp.where((shard > 0) & (before == clip_ref[2 * shard]), 1, 0)


def token_place(row, core, unit):
    per_block = OUT_SIDE * OUT_SIDE
    within = row % per_block
    block = (within // unit) % 2
    target_core = jnp.where(row < per_block, core, 1 - core)
    return block, unit * (2 * (within // (2 * unit)) + target_core) + within % unit


def reorder_matrix(core, unit, to_sent):
    shape = (2 * OUT_SIDE * OUT_SIDE,) * 2
    out_row = lax.broadcasted_iota(jnp.int32, shape, 0)
    in_row = lax.broadcasted_iota(jnp.int32, shape, 1)
    sent, natural = (out_row, in_row) if to_sent else (in_row, out_row)
    block, token = token_place(sent, core, unit)
    source = jnp.where(block == core, 0, OUT_SIDE * OUT_SIDE) + token
    return (source == natural).astype(jnp.bfloat16)


def order_kernel(unit, facts_ref, own_ref, mate_ref, out_ref):
    rows = jnp.concatenate([own_ref[...], mate_ref[...]], axis=0)
    matrix = reorder_matrix(facts_ref[0], unit, True)
    out_ref[...] = jnp.dot(matrix, rows, preferred_element_type=jnp.float32).astype(jnp.bfloat16)


def patch_kernel(facts_ref, halo_ref, even_ref, out_ref):
    chans = halo_ref.shape[1]
    per_frame = OUT_SIDE * OUT_SIDE
    select = select_rows(True).astype(jnp.bfloat16)
    for frame, source in enumerate((halo_ref, even_ref)):
        rows = jnp.dot(select, source[...], preferred_element_type=jnp.float32)
        if frame == 0:
            rows = rows * facts_ref[3].astype(jnp.float32)
        rows = rows.astype(jnp.bfloat16)
        for tap in range(4):
            at = (frame * 4 + tap) * chans
            out_ref[:, at : at + chans] = rows[tap * per_frame : (tap + 1) * per_frame]


def unpatch_kernel(facts_ref, own_ref, mate_ref, out_ref, facts_out_ref):
    for place in range(facts_ref.shape[0]):
        facts_out_ref[place] = facts_ref[place]
    chans = out_ref.shape[1]
    rows = own_ref[...] + mate_ref[...].astype(jnp.float32)
    pieces = [rows[:, tap * chans : (tap + 1) * chans] for tap in range(4)]
    rows = jnp.concatenate(pieces, axis=0)
    select = select_rows(False).astype(jnp.bfloat16)
    coarse = rows.astype(jnp.bfloat16)
    frame = jnp.dot(select, coarse, preferred_element_type=jnp.float32)
    if out_ref.dtype == jnp.bfloat16:
        frame = frame * facts_ref[3].astype(jnp.float32)
    else:
        rest = (rows - coarse.astype(jnp.float32)).astype(jnp.bfloat16)
        frame += jnp.dot(select, rest, preferred_element_type=jnp.float32)
    out_ref[...] = (frame * inside(FRAME_ROWS)).astype(out_ref.dtype)


def excite_grad_kernel(even_ref, odd_ref, conv_ref, excite_ref, expand_ref, out_ref):
    sums = []
    for frame, grad_ref in enumerate((even_ref, odd_ref)):
        conv = conv_ref[frame * FRAME_ROWS : (frame + 1) * FRAME_ROWS, :]
        active = conv * jax.nn.sigmoid(conv)
        sums.append(jnp.sum(grad_ref[...].astype(jnp.float32) * active, axis=0, keepdims=True))
    excite = excite_ref[...]
    inner = jnp.concatenate(sums, axis=0) * excite * (1.0 - excite)
    out_ref[...] = contract_exact(inner, expand_ref[...].astype(jnp.float32))


def conv_grad_kernel(
    width, even_ref, odd_ref, conv_ref, excite_ref, sq_ref, relaxed_ref, squeeze_ref, *refs
):
    *dense_refs, out_ref, flat_ref, wide_ref, shift_ref, grad_ref = refs
    frames, _, chans = out_ref.shape
    rows = frames * FRAME_ROWS
    grad_squeezed = relaxed_ref[...] * silu_slope(sq_ref[...])
    pooled = jnp.dot(
        grad_squeezed, squeeze_ref[...].astype(jnp.float32), precision=lax.Precision.HIGHEST
    ) * (1.0 / (SIDE * SIDE))
    wide_ref[0:EDGE, :] = jnp.zeros((EDGE, chans), jnp.float32)
    wide_ref[EDGE + rows :, :] = jnp.zeros((EDGE, chans), jnp.float32)
    good = inside(FRAME_ROWS)
    for frame, source in enumerate((even_ref, odd_ref)):
        at = frame * FRAME_ROWS
        grad = source[...].astype(jnp.float32)
        grad_ref[at : at + FRAME_ROWS, :] = grad
        active = grad * excite_ref[frame : frame + 1, :] + pooled[frame : frame + 1]
        slope = silu_slope(conv_ref[at : at + FRAME_ROWS, :])
        wide_ref[EDGE + at : EDGE + at + FRAME_ROWS, :] = active * slope * good
    store_shifts(wide_ref, shift_ref, -1)
    body = rows - 2 * WIDE
    for block, dense_ref in zip(channel_blocks(chans, width), dense_refs):
        start = block[2]
        sources = []
        for tap in range(9):
            down, across = divmod(tap, 3)
            at = (2 - down) * WIDE
            sources.append(shift_ref[across, at : at + body, start : start + WINDOW])
        total = jnp.dot(
            jnp.concatenate(sources, axis=1), dense_ref[...], preferred_element_type=jnp.float32
        )
        end = min(chans, start + WINDOW)
        grad_ref[WIDE : WIDE + body, start:end] += total[:, : end - start]
    for frame in range(frames):
        for y in range(SIDE):
            at = frame * FRAME_ROWS + (y + 1) * WIDE + 1
            flat_ref[y * SIDE : (y + 1) * SIDE, :] = grad_ref[at : at + SIDE, :]
        out_ref[frame] = flat_ref[...].astype(jnp.bfloat16)


def f32(*shape):
    return jax.ShapeDtypeStruct(shape, jnp.float32)


def bf16(*shape):
    return jax.ShapeDtypeStruct(shape, jnp.bfloat16)


def conv_forward(features, group_kernel, squeeze_in):
    frames, cells, chans = features.shape
    rows = frames * FRAME_ROWS
    return whole_call(
        conv_kernel,
        (f32(rows, chans), bf16(rows, chans), f32(frames, squeeze_in.shape[0])),
        [
            pltpu.VMEM((cells, chans), jnp.float32),
            pltpu.VMEM((rows + 2 * EDGE, chans), jnp.float32),
            pltpu.VMEM((3, rows, chans), jnp.bfloat16),
        ],
    )(features, group_kernel, squeeze_in)


def hidden_frames(conv, padded, squeezed, squeeze_out):
    rows, chans = conv.shape
    return whole_call(
        hidden_kernel,
        (bf16(FRAME_ROWS, chans), bf16(FRAME_ROWS, chans), f32(rows // FRAME_ROWS, chans)),
        [],
    )(conv, padded, squeezed, squeeze_out)


def vmem_specs(count):
    return [pl.BlockSpec(memory_space=pltpu.SMEM)] + [pl.BlockSpec(memory_space=pltpu.VMEM)] * count


def facts_of(frame_clip, clip_keep):
    smem = pl.BlockSpec(memory_space=pltpu.SMEM)
    return pl.pallas_call(
        facts_kernel,
        out_shape=jax.ShapeDtypeStruct((5,), jnp.int32),
        in_specs=[smem, smem],
        out_specs=smem,
        cost_estimate=FREE,
    )(frame_clip, clip_keep)


def order_rows(facts, own, mate, unit):
    rows, columns = own.shape
    return pl.pallas_call(
        functools.partial(order_kernel, unit),
        out_shape=bf16(2 * rows, columns),
        in_specs=vmem_specs(2),
        compiler_params=pltpu.CompilerParams(vmem_limit_bytes=VMEM_BYTES),
        cost_estimate=FREE,
    )(facts, own, mate)


def take_patches(facts, halo, even):
    chans = even.shape[1]
    return pl.pallas_call(
        patch_kernel,
        out_shape=bf16(OUT_SIDE * OUT_SIDE, 8 * chans),
        in_specs=vmem_specs(2),
        compiler_params=pltpu.CompilerParams(vmem_limit_bytes=VMEM_BYTES),
        cost_estimate=FREE,
    )(facts, halo, even)


def return_patches(facts, own, mate, chans, dtype):
    return pl.pallas_call(
        unpatch_kernel,
        out_shape=(
            jax.ShapeDtypeStruct((FRAME_ROWS, chans), dtype),
            jax.ShapeDtypeStruct(facts.shape, jnp.int32),
        ),
        in_specs=vmem_specs(2),
        out_specs=vmem_specs(1)[::-1],
        compiler_params=pltpu.CompilerParams(vmem_limit_bytes=VMEM_BYTES),
        cost_estimate=FREE,
    )(facts, own, mate)


def excite_grad(even, odd, conv, excite, squeeze_out):
    rows, chans = conv.shape
    return whole_call(
        excite_grad_kernel,
        f32(rows // FRAME_ROWS, squeeze_out.shape[0]),
        [],
    )(even, odd, conv, excite, squeeze_out)


def conv_backward(even, odd, conv, excite, squeezed, grad_relaxed, squeeze_in, dense, width):
    rows, chans = conv.shape
    frames = rows // FRAME_ROWS
    lanes = channel_blocks(chans, width)[-1][2] + WINDOW
    return whole_call(
        functools.partial(conv_grad_kernel, width),
        bf16(frames, SIDE * SIDE, chans),
        [
            pltpu.VMEM((SIDE * SIDE, chans), jnp.float32),
            pltpu.VMEM((rows + 2 * EDGE, chans), jnp.float32),
            pltpu.VMEM((3, rows, lanes), jnp.bfloat16),
            pltpu.VMEM((rows, chans), jnp.float32),
        ],
        pl.CostEstimate(flops=rows * chans * 9216, bytes_accessed=16 * rows * chans, transcendentals=0),
    )(even, odd, conv, excite, squeezed, grad_relaxed, squeeze_in, *dense)


def dense_kernel(facts_ref, group_ref, *dense_refs):
    _, width, chans = group_ref.shape
    for block, dense_ref in zip(channel_blocks(chans, width), dense_refs):
        low, high, start, _ = block
        end = min(chans, start + WINDOW)
        spread, same = block_tools((low, high, start, start + WINDOW), width)
        dense_ref[...] = jnp.zeros_like(dense_ref)
        for tap in range(9):
            full = jnp.dot(spread, group_ref[tap, :, start:end], preferred_element_type=jnp.float32)
            rows = slice(tap * WINDOW, (tap + 1) * WINDOW)
            dense_ref[rows, 0 : end - start] = (full * same[:, : end - start]).astype(jnp.bfloat16)


def dense_weights(facts, group_kernel):
    _, width, chans = group_kernel.shape
    outs = (bf16(9 * WINDOW, WINDOW),) * len(channel_blocks(chans, width))
    return facts_call(dense_kernel, outs, facts, (group_kernel,))


def shifted(value, axis, by):
    count = lax.axis_size(axis)
    pairs = [(i, i + by) for i in range(count) if 0 <= i + by < count]
    return lax.ppermute(value, axis, pairs)


def ring_order(chips):
    return list(range(0, chips, 2)) + list(range(1, chips, 2))[::-1]


def ring_pairs(count, by):
    order = ring_order(count // 2)
    pairs = []
    for place, chip in enumerate(order):
        target = order[(place + by) % len(order)]
        pairs += [(2 * chip, 2 * target), (2 * chip + 1, 2 * target + 1)]
    return pairs


def swap_cores(value):
    return lax.ppermute(value, "ctx", [(i, i ^ 1) for i in range(lax.axis_size("ctx"))])


def tp_terms(value):
    size = lax.axis_size("tp")
    reach, other = 1, None
    while reach < size:
        value = value if other is None else value + other
        other = lax.ppermute(value, "tp", [(i, i ^ reach) for i in range(size)])
        reach *= 2
    return value, jnp.zeros_like(value) if other is None else other


def sum_tp(value):
    value, other = tp_terms(value)
    return value + other


def ring_send(value, by):
    return lax.ppermute(value, "ctx", ring_pairs(lax.axis_size("ctx"), by))


def tie(*values):
    return lax.optimization_barrier(values)


def stacked_contract(left, blocks):
    if blocks[0].shape[0] % 8 == 0:
        blocks = [jnp.concatenate(blocks, axis=0)]
    return jnp.concatenate([contract_last(left, block) for block in blocks], axis=1)


def pre_kernel(patch_ref, *refs):
    *blocks, out_ref = refs
    out_ref[...] = stacked_contract(patch_ref[...], [ref[...] for ref in blocks])


def back_kernel(halves, keep_ref, send_ref, *refs):
    *blocks, out_ref = refs
    blocks = [ref[...] for ref in blocks]
    if halves:
        blocks = blocks[:-2] + [jnp.concatenate(blocks[-2:], axis=1)]
    back = jnp.concatenate([keep_ref[...], send_ref[...]], axis=0)
    out_ref[...] = stacked_contract(back, blocks)


def live_rows(facts_ref, rows, unit):
    block, token = token_place(
        lax.broadcasted_iota(jnp.int32, (rows, 1), 0), facts_ref[0], unit
    )
    return (token < jnp.where(block == 0, facts_ref[1], facts_ref[2])).astype(jnp.float32)


def stacked_dot(pieces, blocks):
    if blocks[0].shape[0] % 8 == 0:
        pieces = [jnp.concatenate(pieces, axis=1)]
        blocks = [jnp.concatenate(blocks, axis=0)]
    total = 0.0
    for piece, block in zip(pieces, blocks):
        total += jnp.dot(piece, block, preferred_element_type=jnp.float32)
    return total


def totals_kernel(pieces, unit, parts, first, facts_ref, *refs):
    grad_act = refs[0][...] + refs[1][...]
    count = len(pieces)
    slopes, blocks = refs[2:4], refs[4 : 4 + count]
    before, after = refs[4 + count : -2 * len(parts)], refs[-2 * len(parts) :]
    rows, width = grad_act.shape[0], blocks[0].shape[0]
    slope = jnp.concatenate(
        [slopes[source][:, index * width : (index + 1) * width] for source, index in pieces], axis=1
    )
    factor = jnp.dot(
        reorder_matrix(facts_ref[0], unit, False),
        (grad_act * slope).astype(jnp.bfloat16),
        preferred_element_type=jnp.float32,
    ).astype(jnp.bfloat16)
    factors = [factor[:, place * width : (place + 1) * width] for place in range(count)]
    for part, lanes in enumerate(parts):
        total = stacked_dot(factors, [ref[:, lanes] for ref in blocks])
        for half in range(2):
            value = total[half * rows // 2 : (half + 1) * rows // 2]
            value = value if first else before[2 * part + half][...] + value
            ref = after[2 * part + half]
            ref[...] = value.astype(ref.dtype)


def ring_offsets(chips):
    offsets = [0]
    for step in range(1, chips // 2):
        offsets += [-step, step]
    return offsets + [chips // 2]


def block_columns(facts_ref, offset, chips, width):
    shape = (width, chips * width)
    place = (facts_ref[4] + offset + chips) % chips
    column = lax.broadcasted_iota(jnp.int32, shape, 1)
    return (column == lax.broadcasted_iota(jnp.int32, shape, 0) + place * width).astype(jnp.bfloat16)


def exchange_matrix(core, unit, to_sent):
    per_block = OUT_SIDE * OUT_SIDE
    shape = (2 * per_block,) * 2
    out_row = lax.broadcasted_iota(jnp.int32, shape, 0)
    in_row = lax.broadcasted_iota(jnp.int32, shape, 1)
    sent, kept = (out_row, in_row) if to_sent else (in_row, out_row)
    target_core = (sent // (2 * unit)) % 2
    within = sent // (4 * unit) * (2 * unit) + sent % (2 * unit)
    return (within + jnp.where(target_core == core, 0, per_block) == kept).astype(jnp.bfloat16)


def act_kernel(offsets, chips, unit, last, facts_ref, own_ref, other_ref, *refs):
    *before, slope_ref, out_ref = refs
    pre = own_ref[...] + other_ref[...]
    width = pre.shape[1] // len(offsets)
    live = live_rows(facts_ref, pre.shape[0], unit)
    sigma = jax.nn.sigmoid(pre)
    slope_ref[...] = sigma * (1.0 + pre * (1.0 - sigma)) * live
    act = (pre * sigma * live).astype(jnp.bfloat16)
    total = before[0][...].astype(jnp.float32) if last else 0.0
    for place, offset in enumerate(offsets):
        columns = block_columns(facts_ref, offset, chips, width)
        piece = act[:, place * width : (place + 1) * width]
        total += jnp.dot(piece, columns, preferred_element_type=jnp.float32)
    total = total.astype(jnp.bfloat16)
    if last:
        matrix = exchange_matrix(facts_ref[0], unit, True)
        total = jnp.dot(matrix, total, preferred_element_type=jnp.float32).astype(jnp.bfloat16)
    out_ref[...] = total


def token_kernel(offsets, chips, unit, facts_ref, act_ref, *refs):
    count = len(offsets) + 1
    blocks, refs = refs[:count], refs[count:]
    keep_ref, send_ref, *buffers, sems = refs
    half = buffers[-1].shape[1] // 2
    targets = [*buffers[:-1], buffers[-1].at[:, :half], buffers[-1].at[:, half:]]
    copies = [
        pltpu.make_async_copy(ref, target, sems.at[place])
        for place, (ref, target) in enumerate(zip(blocks, targets))
    ]
    for copy in copies:
        copy.start()
    width = buffers[0].shape[0]
    matrix = exchange_matrix(facts_ref[0], unit, False)
    act = jnp.dot(matrix, act_ref[...], preferred_element_type=jnp.float32).astype(jnp.bfloat16)
    pieces = [
        contract_last(act, block_columns(facts_ref, offset, chips, width)).astype(jnp.bfloat16)
        for offset in offsets
    ]
    for copy in copies:
        copy.wait()
    total = stacked_dot(pieces, [buffer[...] for buffer in buffers])
    rows = keep_ref.shape[0]
    keep_ref[...] = total[:rows]
    send_ref[...] = total[rows:].astype(jnp.bfloat16)


def block_products(kernel, left, blocks):
    rows = 2 * OUT_SIDE * OUT_SIDE
    return whole_call(kernel, f32(rows, len(blocks) * blocks[0].shape[0]), [])(*left, *blocks)


def back_products(back, blocks, halves=()):
    rows, count = 2 * OUT_SIDE * OUT_SIDE, len(blocks) + (1 if halves else 0)
    kernel = functools.partial(back_kernel, bool(halves))
    operands = *back, *blocks, *halves
    return whole_call(kernel, f32(rows, count * blocks[0].shape[0]), [])(*operands)


def facts_call(kernel, outs, facts, operands, cost=FREE):
    return pl.pallas_call(
        kernel,
        out_shape=outs,
        in_specs=vmem_specs(len(operands)),
        compiler_params=pltpu.CompilerParams(vmem_limit_bytes=VMEM_BYTES),
        cost_estimate=cost,
    )(facts, *operands)


def add_gradients(facts, terms, slopes, pieces, blocks, before, unit, parts, last):
    rows = terms[0].shape[0] // 2
    kernel = functools.partial(totals_kernel, pieces, unit, parts, not before)
    outs = ()
    for lanes in parts:
        shape = rows, lanes.stop - lanes.start
        outs += f32(*shape), (bf16 if last else f32)(*shape)
    return tuple(facts_call(kernel, outs, facts, (*terms, *slopes, *blocks, *before)))


def act_and_slope(facts, terms, offsets, chips, before, unit):
    rows, columns = terms[0].shape
    kernel = functools.partial(act_kernel, offsets, chips, unit, bool(before))
    outs = f32(rows, columns), bf16(rows, columns // len(offsets) * chips)
    return facts_call(kernel, outs, facts, (*terms, *before))


def token_products(facts, act, offsets, chips, blocks, unit):
    rows, columns = act.shape[0] // 2, blocks[0].shape[1]
    return pl.pallas_call(
        functools.partial(token_kernel, offsets, chips, unit),
        out_shape=(f32(rows, columns), bf16(rows, columns)),
        in_specs=vmem_specs(1) + [pl.BlockSpec(memory_space=pl.ANY)] * len(blocks),
        scratch_shapes=[pltpu.VMEM(blocks[0].shape, jnp.bfloat16)] * len(offsets)
        + [pltpu.SemaphoreType.DMA((len(blocks),))],
        compiler_params=pltpu.CompilerParams(vmem_limit_bytes=VMEM_BYTES),
        cost_estimate=FREE,
    )(facts, act, *blocks)


def chips_exchange(value):
    count = lax.axis_size("ctx")
    groups = [list(range(core, count, 2)) for core in range(2)]
    return lax.all_to_all(
        value, "ctx", split_axis=0, concat_axis=0, tiled=True, axis_index_groups=groups
    )


def per_device(
    features,
    group_kernel,
    squeeze_in,
    squeeze_out,
    sampler_kernel,
    readout_kernel,
    frame_clip,
    clip_keep,
    token_cotangent,
):
    chans = features.shape[2]
    count = lax.axis_size("ctx")
    steps, unit = count // 4, OUT_SIDE * OUT_SIDE // count
    flat_sampler = sampler_kernel.reshape(sampler_kernel.shape[0], 8 * chans)
    chips = count // 2
    s_up, s_down = ring_send(flat_sampler, 1), ring_send(flat_sampler, -1)
    group_kernel = jnp.swapaxes(group_kernel, 1, 2)
    squeeze_in = squeeze_in.T
    facts = facts_of(frame_clip, clip_keep)

    conv, padded, squeezed = conv_forward(features, group_kernel, squeeze_in)
    token_cotangent, squeezed = tie(token_cotangent, squeezed)
    back = chips_exchange(token_cotangent)
    squeezed = sum_tp(squeezed)
    even, odd, excite = hidden_frames(conv, padded, squeezed, squeeze_out)
    halo = shifted(odd, "ctx", 1)

    s_up, s_down = [flat_sampler, s_up], [flat_sampler, s_down]
    s_up[1], s_down[1], even, readout_kernel = tie(s_up[1], s_down[1], even, readout_kernel)
    for step in range(2, steps):
        s_up.append(ring_send(s_up[-1], 1))
        s_down.append(ring_send(s_down[-1], -1))
        if step == 2:
            halo, s_up[2], s_down[2] = tie(halo, s_up[2], s_down[2])
            r_down = [readout_kernel, ring_send(readout_kernel, -1)]
            patches = take_patches(facts, halo, even)
            patches = order_rows(facts, patches, swap_cores(patches), unit)
    s_up[-1], s_down[-1], back, readout_kernel = tie(s_up[-1], s_down[-1], back, readout_kernel)
    back = (back, swap_cores(back))
    cut = 4 * chans
    s_last = ring_send(s_up[-1][:, :cut], 1), ring_send(s_down[-1][:, cut:], -1)
    samplers = [flat_sampler] + [block for pair in zip(s_up[1:], s_down[1:]) for block in pair]
    offsets = ring_offsets(chips)
    count = 2 * steps - 3
    r_up, r_down = [ring_send(readout_kernel, 1)], [ring_send(readout_kernel, -1)]
    first_pre = tp_terms(block_products(pre_kernel, (patches,), samplers[:count]))
    held = tie(r_up[0], r_down[0], *s_last, *first_pre)
    r_up[0], r_down[0], s_last, first_pre = held[0], held[1], held[2:4], held[4:]
    for step in range(2, steps - 1):
        r_up.append(ring_send(r_up[-1], 1))
        r_down.append(ring_send(r_down[-1], -1))
    samplers.append(jnp.concatenate(s_last, axis=1))
    first_slope, first_act = act_and_slope(facts, first_pre, offsets[:count], chips, (), unit)
    last_pre = block_products(pre_kernel, (patches,), samplers[count:])
    last_slope, act = act_and_slope(
        facts, tp_terms(last_pre), offsets[count:], chips, (first_act,), unit
    )
    slopes = first_slope, last_slope
    halo_lanes, even_lanes = slice(0, cut), slice(cut, 2 * cut)
    both = halo_lanes, even_lanes
    readouts = [readout_kernel] + [block for pair in zip(r_up, r_down) for block in pair]
    sums = back_products(back, readouts[: count - 2])
    r_up[-1], r_down[-1], act, sums = tie(r_up[-1], r_down[-1], act, sums)
    readouts[count - 2 :] = r_up[-1], r_down[-1]
    r_up.append(ring_send(r_up[-1], 1))
    r_down.append(ring_send(r_down[-1], -1))
    held = tie(r_up[-1], r_down[-1], chips_exchange(act), *tp_terms(sums))
    r_up[-1], r_down[-1], act, terms = *held[:3], held[3:]
    pieces = [(0, place) for place in range(count - 2)]
    grads = add_gradients(
        facts, terms, slopes, pieces, samplers[: count - 2], (), unit, both, False
    )
    terms = tp_terms(back_products(back, readouts[count - 2 :]))
    pieces = [(0, count - 2), (0, count - 1)]
    grads = add_gradients(
        facts, terms, slopes, pieces, samplers[count - 2 : count], grads, unit, both, False
    )
    cut = readout_kernel.shape[1] // 2
    r_last = ring_send(r_up[-1][:, :cut], 1), ring_send(r_down[-1][:, cut:], -1)
    held = tie(r_up[-1], r_down[-1], *r_last, *grads)
    late, r_last, grads = held[:2], held[2:4], held[4:]
    terms = tp_terms(back_products(back, late, r_last))
    pieces, blocks = [(1, 0), (1, 1), (1, 2)], samplers[count:]
    halo_own, halo_mate = add_gradients(
        facts, terms, slopes, pieces, blocks, grads[:2], unit, (halo_lanes,), True
    )
    halo_mate, first_term = tie(halo_mate, terms[0])
    even_own, even_mate = add_gradients(
        facts, (first_term, terms[1]), slopes, pieces, blocks, grads[2:], unit, (even_lanes,), True
    )
    lead, facts_late = return_patches(facts, halo_own, swap_cores(halo_mate), chans, jnp.bfloat16)
    grad_odd = shifted(lead, "ctx", -1)
    grad_even, facts_late = return_patches(
        facts_late, even_own, swap_cores(even_mate), chans, jnp.float32
    )
    tokens = token_products(
        facts_late, act, offsets, chips, [*readouts, *late, *r_last], unit
    )
    grad_relaxed = sum_tp(excite_grad(grad_even, grad_odd, conv, excite, squeeze_out))
    llm_tokens = (tokens[0] + swap_cores(tokens[1]).astype(jnp.float32)).astype(jnp.bfloat16)
    grad_features = conv_backward(
        grad_even, grad_odd, conv, excite, squeezed, grad_relaxed, squeeze_in,
        dense_weights(facts_late, group_kernel), group_kernel.shape[1],
    )
    return (llm_tokens, grad_features)


def solution(mesh):
    placed = (
        P("ctx", None, "tp"),
        P(None, "tp", None),
        P("tp", None),
        P(None, "tp"),
        P("ctx", None, "tp"),
        P("ctx", "tp"),
        P(),
        P(),
        P("ctx", "tp"),
    )
    return jax.shard_map(
        per_device,
        mesh=mesh,
        in_specs=placed,
        out_specs=(P("ctx", "tp"), P("ctx", None, "tp")),
        check_vma=False,
    )
```

```python
import functools

import jax
import jax.numpy as jnp
from jax import lax
from jax.experimental import pallas as pl
from jax.experimental.pallas import tpu as pltpu
from jax.sharding import PartitionSpec as P

SIDE = 14
OUT_SIDE = 8
WIDE = 16
FRAME_ROWS = WIDE * WIDE
EDGE = 8
LANES = 128
WINDOW = 256
VMEM_BYTES = 16 * 2**20
FREE = pl.CostEstimate(flops=0, bytes_accessed=0, transcendentals=0)


def whole_call(kernel, outs, scratch, cost=FREE):
    return pl.pallas_call(
        kernel,
        out_shape=outs,
        scratch_shapes=scratch,
        compiler_params=pltpu.CompilerParams(vmem_limit_bytes=VMEM_BYTES),
        cost_estimate=cost,
    )


def contract_last(left, right):
    return lax.dot_general(
        left, right, (((1,), (1,)), ((), ())), preferred_element_type=jnp.float32
    )


def contract_exact(left, right):
    return lax.dot_general(
        left,
        right,
        (((1,), (1,)), ((), ())),
        precision=lax.Precision.HIGHEST,
        preferred_element_type=jnp.float32,
    )


def silu_slope(values):
    sigma = jax.nn.sigmoid(values)
    return sigma * (1.0 + values * (1.0 - sigma))


def inside(rows):
    row = lax.broadcasted_iota(jnp.int32, (rows, 1), 0)
    across, down = row & (WIDE - 1), (row // WIDE) & (WIDE - 1)
    good = (across >= 1) & (across <= SIDE) & (down >= 1) & (down <= SIDE)
    return good.astype(jnp.float32)


def channel_blocks(chans, width):
    span = 4 * width
    blocks = []
    for low in range(0, chans, span):
        high = min(chans, low + span)
        blocks.append((low, high, low // LANES * LANES, min(chans, -(-high // LANES) * LANES)))
    return blocks


def block_tools(block, width):
    low, high, start, end = block
    size = end - start
    out_row = lax.broadcasted_iota(jnp.int32, (size, width), 0) + start
    within = lax.broadcasted_iota(jnp.int32, (size, width), 1)
    lane = lax.broadcasted_iota(jnp.int32, (size, size), 1) + start
    row = lax.broadcasted_iota(jnp.int32, (size, size), 0) + start
    spread = jnp.zeros((size, width), jnp.float32)
    same = jnp.zeros((size, size), jnp.float32)
    for first in range(low, high, width):
        spread += (out_row == within + first).astype(jnp.float32)
        in_lane = (lane >= first) & (lane < first + width)
        in_row = (row >= first) & (row < first + width)
        same += (in_lane & in_row).astype(jnp.float32)
    return spread.astype(jnp.bfloat16), same


def dense_tap(group_ref, tap, block, spread, same):
    _, _, start, end = block
    full = jnp.dot(spread, group_ref[tap, :, start:end], preferred_element_type=jnp.float32)
    return (full * same).astype(jnp.bfloat16)


def store_shifts(wide_ref, shift_ref, sign):
    rows = shift_ref.shape[1]
    for col in range(3):
        at = EDGE + sign * (col - 1)
        chans = wide_ref.shape[1]
        shift_ref[col, :, 0:chans] = wide_ref[at : at + rows, :].astype(jnp.bfloat16)
        if shift_ref.shape[2] > chans:
            blank = jnp.zeros((rows, shift_ref.shape[2] - chans), jnp.bfloat16)
            shift_ref[col, :, chans:] = blank


def conv_kernel(feat_ref, group_ref, squeeze_ref, *refs):
    conv_ref, pad_ref, sq_ref, flat_ref, wide_ref, shift_ref = refs
    frames, _, chans = feat_ref.shape
    width = group_ref.shape[1]
    rows = frames * FRAME_ROWS
    wide_ref[...] = jnp.zeros_like(wide_ref)
    for frame in range(frames):
        flat_ref[...] = feat_ref[frame].astype(jnp.float32)
        for y in range(SIDE):
            at = EDGE + frame * FRAME_ROWS + (y + 1) * WIDE + 1
            wide_ref[at : at + SIDE, :] = flat_ref[y * SIDE : (y + 1) * SIDE, :]
    store_shifts(wide_ref, shift_ref, 1)
    pad_ref[...] = shift_ref[1]
    conv_ref[...] = jnp.zeros_like(conv_ref)
    body = rows - 2 * WIDE
    for block in channel_blocks(chans, width):
        _, _, start, end = block
        spread, same = block_tools(block, width)
        total = jnp.zeros((body, end - start), jnp.float32)
        for tap in range(9):
            down, across = divmod(tap, 3)
            weights = dense_tap(group_ref, tap, block, spread, same)
            source = shift_ref[across, down * WIDE : down * WIDE + body, start:end]
            total += contract_last(source, weights)
        conv_ref[WIDE : WIDE + body, start:end] += total
    conv = conv_ref[...] * inside(rows)
    conv_ref[...] = conv
    active = conv * jax.nn.sigmoid(conv)
    pooled = jnp.concatenate(
        [
            jnp.sum(active[f * FRAME_ROWS : (f + 1) * FRAME_ROWS], axis=0, keepdims=True)
            for f in range(frames)
        ],
        axis=0,
    ) * (1.0 / (SIDE * SIDE))
    sq_ref[...] = contract_exact(pooled, squeeze_ref[...].astype(jnp.float32))


def hidden_kernel(conv_ref, pad_ref, sq_ref, expand_ref, even_ref, odd_ref, excite_ref):
    squeezed = sq_ref[...]
    relaxed = squeezed * jax.nn.sigmoid(squeezed)
    excite = jax.nn.sigmoid(
        jnp.dot(relaxed, expand_ref[...].astype(jnp.float32), precision=lax.Precision.HIGHEST)
    )
    excite_ref[...] = excite
    for frame, out_ref in enumerate((even_ref, odd_ref)):
        rows = slice(frame * FRAME_ROWS, (frame + 1) * FRAME_ROWS)
        conv = conv_ref[rows, :]
        active = conv * jax.nn.sigmoid(conv)
        hidden = pad_ref[rows, :].astype(jnp.float32) + active * excite[frame : frame + 1]
        out_ref[...] = hidden.astype(jnp.bfloat16)


def select_rows(to_patches):
    shape = (FRAME_ROWS, FRAME_ROWS)
    out_row = lax.broadcasted_iota(jnp.int32, shape, 0)
    in_row = lax.broadcasted_iota(jnp.int32, shape, 1)
    patch_row, frame_row = (out_row, in_row) if to_patches else (in_row, out_row)
    down, across = patch_row >> 7, (patch_row >> 6) & 1
    a, b = (patch_row >> 3) & 7, patch_row & 7
    return ((2 * a + down) * WIDE + 2 * b + across == frame_row).astype(jnp.float32)


def facts_kernel(clip_ref, keep_ref, out_ref):
    shard = lax.axis_index("ctx")
    frames = clip_ref.shape[0]
    out_ref[0] = shard % 2
    for block in range(2):
        pair = shard // 2 * 2 + block
        clip = clip_ref[2 * pair]
        start = jnp.int32(0)
        for other in range(0, frames, 2):
            start += jnp.where(clip_ref[other] < clip, 1, 0)
        out_ref[1 + block] = keep_ref[clip] - (pair - start) * (OUT_SIDE * OUT_SIDE)
    before = clip_ref[jnp.maximum(2 * shard - 1, 0)]
    chip, chips = shard // 2, lax.axis_size("ctx") // 2
    out_ref[4] = jnp.where(chip % 2 == 0, chip // 2, chips - 1 - chip // 2)
    out_ref[3] = jnp.where((shard > 0) & (before == clip_ref[2 * shard]), 1, 0)


def token_place(row, core, unit):
    per_block = OUT_SIDE * OUT_SIDE
    within = row % per_block
    block = (within // unit) % 2
    target_core = jnp.where(row < per_block, core, 1 - core)
    return block, unit * (2 * (within // (2 * unit)) + target_core) + within % unit


def reorder_matrix(core, unit, to_sent):
    shape = (2 * OUT_SIDE * OUT_SIDE,) * 2
    out_row = lax.broadcasted_iota(jnp.int32, shape, 0)
    in_row = lax.broadcasted_iota(jnp.int32, shape, 1)
    sent, natural = (out_row, in_row) if to_sent else (in_row, out_row)
    block, token = token_place(sent, core, unit)
    source = jnp.where(block == core, 0, OUT_SIDE * OUT_SIDE) + token
    return (source == natural).astype(jnp.bfloat16)


def order_kernel(unit, facts_ref, own_ref, mate_ref, out_ref):
    rows = jnp.concatenate([own_ref[...], mate_ref[...]], axis=0)
    matrix = reorder_matrix(facts_ref[0], unit, True)
    out_ref[...] = jnp.dot(matrix, rows, preferred_element_type=jnp.float32).astype(jnp.bfloat16)


def patch_kernel(facts_ref, halo_ref, even_ref, out_ref):
    chans = halo_ref.shape[1]
    per_frame = OUT_SIDE * OUT_SIDE
    select = select_rows(True).astype(jnp.bfloat16)
    for frame, source in enumerate((halo_ref, even_ref)):
        rows = jnp.dot(select, source[...], preferred_element_type=jnp.float32)
        if frame == 0:
            rows = rows * facts_ref[3].astype(jnp.float32)
        rows = rows.astype(jnp.bfloat16)
        for tap in range(4):
            at = (frame * 4 + tap) * chans
            out_ref[:, at : at + chans] = rows[tap * per_frame : (tap + 1) * per_frame]


def unpatch_kernel(facts_ref, own_ref, mate_ref, out_ref, facts_out_ref):
    for place in range(facts_ref.shape[0]):
        facts_out_ref[place] = facts_ref[place]
    chans = out_ref.shape[1]
    rows = own_ref[...] + mate_ref[...].astype(jnp.float32)
    pieces = [rows[:, tap * chans : (tap + 1) * chans] for tap in range(4)]
    rows = jnp.concatenate(pieces, axis=0)
    select = select_rows(False).astype(jnp.bfloat16)
    coarse = rows.astype(jnp.bfloat16)
    frame = jnp.dot(select, coarse, preferred_element_type=jnp.float32)
    if out_ref.dtype == jnp.bfloat16:
        frame = frame * facts_ref[3].astype(jnp.float32)
    else:
        rest = (rows - coarse.astype(jnp.float32)).astype(jnp.bfloat16)
        frame += jnp.dot(select, rest, preferred_element_type=jnp.float32)
    out_ref[...] = (frame * inside(FRAME_ROWS)).astype(out_ref.dtype)


def excite_grad_kernel(even_ref, odd_ref, conv_ref, excite_ref, expand_ref, out_ref):
    sums = []
    for frame, grad_ref in enumerate((even_ref, odd_ref)):
        conv = conv_ref[frame * FRAME_ROWS : (frame + 1) * FRAME_ROWS, :]
        active = conv * jax.nn.sigmoid(conv)
        sums.append(jnp.sum(grad_ref[...].astype(jnp.float32) * active, axis=0, keepdims=True))
    excite = excite_ref[...]
    inner = jnp.concatenate(sums, axis=0) * excite * (1.0 - excite)
    out_ref[...] = contract_exact(inner, expand_ref[...].astype(jnp.float32))


def conv_grad_kernel(
    width, even_ref, odd_ref, conv_ref, excite_ref, sq_ref, relaxed_ref, squeeze_ref, *refs
):
    *dense_refs, out_ref, flat_ref, wide_ref, shift_ref, grad_ref = refs
    frames, _, chans = out_ref.shape
    rows = frames * FRAME_ROWS
    grad_squeezed = relaxed_ref[...] * silu_slope(sq_ref[...])
    pooled = jnp.dot(
        grad_squeezed, squeeze_ref[...].astype(jnp.float32), precision=lax.Precision.HIGHEST
    ) * (1.0 / (SIDE * SIDE))
    wide_ref[0:EDGE, :] = jnp.zeros((EDGE, chans), jnp.float32)
    wide_ref[EDGE + rows :, :] = jnp.zeros((EDGE, chans), jnp.float32)
    good = inside(FRAME_ROWS)
    for frame, source in enumerate((even_ref, odd_ref)):
        at = frame * FRAME_ROWS
        grad = source[...].astype(jnp.float32)
        grad_ref[at : at + FRAME_ROWS, :] = grad
        active = grad * excite_ref[frame : frame + 1, :] + pooled[frame : frame + 1]
        slope = silu_slope(conv_ref[at : at + FRAME_ROWS, :])
        wide_ref[EDGE + at : EDGE + at + FRAME_ROWS, :] = active * slope * good
    store_shifts(wide_ref, shift_ref, -1)
    body = rows - 2 * WIDE
    for block, dense_ref in zip(channel_blocks(chans, width), dense_refs):
        start = block[2]
        sources = []
        for tap in range(9):
            down, across = divmod(tap, 3)
            at = (2 - down) * WIDE
            sources.append(shift_ref[across, at : at + body, start : start + WINDOW])
        total = jnp.dot(
            jnp.concatenate(sources, axis=1), dense_ref[...], preferred_element_type=jnp.float32
        )
        end = min(chans, start + WINDOW)
        grad_ref[WIDE : WIDE + body, start:end] += total[:, : end - start]
    for frame in range(frames):
        for y in range(SIDE):
            at = frame * FRAME_ROWS + (y + 1) * WIDE + 1
            flat_ref[y * SIDE : (y + 1) * SIDE, :] = grad_ref[at : at + SIDE, :]
        out_ref[frame] = flat_ref[...].astype(jnp.bfloat16)


def f32(*shape):
    return jax.ShapeDtypeStruct(shape, jnp.float32)


def bf16(*shape):
    return jax.ShapeDtypeStruct(shape, jnp.bfloat16)


def conv_forward(features, group_kernel, squeeze_in):
    frames, cells, chans = features.shape
    rows = frames * FRAME_ROWS
    return whole_call(
        conv_kernel,
        (f32(rows, chans), bf16(rows, chans), f32(frames, squeeze_in.shape[0])),
        [
            pltpu.VMEM((cells, chans), jnp.float32),
            pltpu.VMEM((rows + 2 * EDGE, chans), jnp.float32),
            pltpu.VMEM((3, rows, chans), jnp.bfloat16),
        ],
    )(features, group_kernel, squeeze_in)


def hidden_frames(conv, padded, squeezed, squeeze_out):
    rows, chans = conv.shape
    return whole_call(
        hidden_kernel,
        (bf16(FRAME_ROWS, chans), bf16(FRAME_ROWS, chans), f32(rows // FRAME_ROWS, chans)),
        [],
    )(conv, padded, squeezed, squeeze_out)


def vmem_specs(count):
    return [pl.BlockSpec(memory_space=pltpu.SMEM)] + [pl.BlockSpec(memory_space=pltpu.VMEM)] * count


def facts_of(frame_clip, clip_keep):
    smem = pl.BlockSpec(memory_space=pltpu.SMEM)
    return pl.pallas_call(
        facts_kernel,
        out_shape=jax.ShapeDtypeStruct((5,), jnp.int32),
        in_specs=[smem, smem],
        out_specs=smem,
        cost_estimate=FREE,
    )(frame_clip, clip_keep)


def order_rows(facts, own, mate, unit):
    rows, columns = own.shape
    return pl.pallas_call(
        functools.partial(order_kernel, unit),
        out_shape=bf16(2 * rows, columns),
        in_specs=vmem_specs(2),
        compiler_params=pltpu.CompilerParams(vmem_limit_bytes=VMEM_BYTES),
        cost_estimate=FREE,
    )(facts, own, mate)


def take_patches(facts, halo, even):
    chans = even.shape[1]
    return pl.pallas_call(
        patch_kernel,
        out_shape=bf16(OUT_SIDE * OUT_SIDE, 8 * chans),
        in_specs=vmem_specs(2),
        compiler_params=pltpu.CompilerParams(vmem_limit_bytes=VMEM_BYTES),
        cost_estimate=FREE,
    )(facts, halo, even)


def return_patches(facts, own, mate, chans, dtype):
    return pl.pallas_call(
        unpatch_kernel,
        out_shape=(
            jax.ShapeDtypeStruct((FRAME_ROWS, chans), dtype),
            jax.ShapeDtypeStruct(facts.shape, jnp.int32),
        ),
        in_specs=vmem_specs(2),
        out_specs=vmem_specs(1)[::-1],
        compiler_params=pltpu.CompilerParams(vmem_limit_bytes=VMEM_BYTES),
        cost_estimate=FREE,
    )(facts, own, mate)


def excite_grad(even, odd, conv, excite, squeeze_out):
    rows, chans = conv.shape
    return whole_call(
        excite_grad_kernel,
        f32(rows // FRAME_ROWS, squeeze_out.shape[0]),
        [],
    )(even, odd, conv, excite, squeeze_out)


def conv_backward(even, odd, conv, excite, squeezed, grad_relaxed, squeeze_in, dense, width):
    rows, chans = conv.shape
    frames = rows // FRAME_ROWS
    lanes = channel_blocks(chans, width)[-1][2] + WINDOW
    return whole_call(
        functools.partial(conv_grad_kernel, width),
        bf16(frames, SIDE * SIDE, chans),
        [
            pltpu.VMEM((SIDE * SIDE, chans), jnp.float32),
            pltpu.VMEM((rows + 2 * EDGE, chans), jnp.float32),
            pltpu.VMEM((3, rows, lanes), jnp.bfloat16),
            pltpu.VMEM((rows, chans), jnp.float32),
        ],
        pl.CostEstimate(flops=rows * chans * 9216, bytes_accessed=16 * rows * chans, transcendentals=0),
    )(even, odd, conv, excite, squeezed, grad_relaxed, squeeze_in, *dense)


def dense_kernel(facts_ref, group_ref, *dense_refs):
    _, width, chans = group_ref.shape
    for block, dense_ref in zip(channel_blocks(chans, width), dense_refs):
        low, high, start, _ = block
        end = min(chans, start + WINDOW)
        spread, same = block_tools((low, high, start, start + WINDOW), width)
        dense_ref[...] = jnp.zeros_like(dense_ref)
        for tap in range(9):
            full = jnp.dot(spread, group_ref[tap, :, start:end], preferred_element_type=jnp.float32)
            rows = slice(tap * WINDOW, (tap + 1) * WINDOW)
            dense_ref[rows, 0 : end - start] = (full * same[:, : end - start]).astype(jnp.bfloat16)


def dense_weights(facts, group_kernel):
    _, width, chans = group_kernel.shape
    outs = (bf16(9 * WINDOW, WINDOW),) * len(channel_blocks(chans, width))
    return facts_call(dense_kernel, outs, facts, (group_kernel,))


def shifted(value, axis, by):
    count = lax.axis_size(axis)
    pairs = [(i, i + by) for i in range(count) if 0 <= i + by < count]
    return lax.ppermute(value, axis, pairs)


def ring_order(chips):
    return list(range(0, chips, 2)) + list(range(1, chips, 2))[::-1]


def ring_pairs(count, by):
    order = ring_order(count // 2)
    pairs = []
    for place, chip in enumerate(order):
        target = order[(place + by) % len(order)]
        pairs += [(2 * chip, 2 * target), (2 * chip + 1, 2 * target + 1)]
    return pairs


def swap_cores(value):
    return lax.ppermute(value, "ctx", [(i, i ^ 1) for i in range(lax.axis_size("ctx"))])


def tp_terms(value):
    size = lax.axis_size("tp")
    reach, other = 1, None
    while reach < size:
        value = value if other is None else value + other
        other = lax.ppermute(value, "tp", [(i, i ^ reach) for i in range(size)])
        reach *= 2
    return value, jnp.zeros_like(value) if other is None else other


def sum_tp(value):
    value, other = tp_terms(value)
    return value + other


def ring_send(value, by):
    return lax.ppermute(value, "ctx", ring_pairs(lax.axis_size("ctx"), by))


def tie(*values):
    return lax.optimization_barrier(values)


def stacked_contract(left, blocks):
    if blocks[0].shape[0] % 8 == 0:
        blocks = [jnp.concatenate(blocks, axis=0)]
    return jnp.concatenate([contract_last(left, block) for block in blocks], axis=1)


def pre_kernel(patch_ref, *refs):
    *blocks, out_ref = refs
    out_ref[...] = stacked_contract(patch_ref[...], [ref[...] for ref in blocks])


def back_kernel(halves, keep_ref, send_ref, *refs):
    *blocks, out_ref = refs
    blocks = [ref[...] for ref in blocks]
    if halves:
        blocks = blocks[:-2] + [jnp.concatenate(blocks[-2:], axis=1)]
    back = jnp.concatenate([keep_ref[...], send_ref[...]], axis=0)
    out_ref[...] = stacked_contract(back, blocks)


def live_rows(facts_ref, rows, unit):
    block, token = token_place(
        lax.broadcasted_iota(jnp.int32, (rows, 1), 0), facts_ref[0], unit
    )
    return (token < jnp.where(block == 0, facts_ref[1], facts_ref[2])).astype(jnp.float32)


def stacked_dot(pieces, blocks):
    if blocks[0].shape[0] % 8 == 0:
        pieces = [jnp.concatenate(pieces, axis=1)]
        blocks = [jnp.concatenate(blocks, axis=0)]
    total = 0.0
    for piece, block in zip(pieces, blocks):
        total += jnp.dot(piece, block, preferred_element_type=jnp.float32)
    return total


def totals_kernel(pieces, unit, parts, first, facts_ref, *refs):
    grad_act = refs[0][...] + refs[1][...]
    count = len(pieces)
    slopes, blocks = refs[2:4], refs[4 : 4 + count]
    before, after = refs[4 + count : -2 * len(parts)], refs[-2 * len(parts) :]
    rows, width = grad_act.shape[0], blocks[0].shape[0]
    slope = jnp.concatenate(
        [slopes[source][:, index * width : (index + 1) * width] for source, index in pieces], axis=1
    )
    factor = jnp.dot(
        reorder_matrix(facts_ref[0], unit, False),
        (grad_act * slope).astype(jnp.bfloat16),
        preferred_element_type=jnp.float32,
    ).astype(jnp.bfloat16)
    factors = [factor[:, place * width : (place + 1) * width] for place in range(count)]
    for part, lanes in enumerate(parts):
        total = stacked_dot(factors, [ref[:, lanes] for ref in blocks])
        for half in range(2):
            value = total[half * rows // 2 : (half + 1) * rows // 2]
            value = value if first else before[2 * part + half][...] + value
            ref = after[2 * part + half]
            ref[...] = value.astype(ref.dtype)


def ring_offsets(chips):
    offsets = [0]
    for step in range(1, chips // 2):
        offsets += [-step, step]
    return offsets + [chips // 2]


def block_columns(facts_ref, offset, chips, width):
    shape = (width, chips * width)
    place = (facts_ref[4] + offset + chips) % chips
    column = lax.broadcasted_iota(jnp.int32, shape, 1)
    return (column == lax.broadcasted_iota(jnp.int32, shape, 0) + place * width).astype(jnp.bfloat16)


def exchange_matrix(core, unit, to_sent):
    per_block = OUT_SIDE * OUT_SIDE
    shape = (2 * per_block,) * 2
    out_row = lax.broadcasted_iota(jnp.int32, shape, 0)
    in_row = lax.broadcasted_iota(jnp.int32, shape, 1)
    sent, kept = (out_row, in_row) if to_sent else (in_row, out_row)
    target_core = (sent // (2 * unit)) % 2
    within = sent // (4 * unit) * (2 * unit) + sent % (2 * unit)
    return (within + jnp.where(target_core == core, 0, per_block) == kept).astype(jnp.bfloat16)


def act_kernel(offsets, chips, unit, last, facts_ref, own_ref, other_ref, *refs):
    *before, slope_ref, out_ref = refs
    pre = own_ref[...] + other_ref[...]
    width = pre.shape[1] // len(offsets)
    live = live_rows(facts_ref, pre.shape[0], unit)
    sigma = jax.nn.sigmoid(pre)
    slope_ref[...] = sigma * (1.0 + pre * (1.0 - sigma)) * live
    act = (pre * sigma * live).astype(jnp.bfloat16)
    total = before[0][...].astype(jnp.float32) if last else 0.0
    for place, offset in enumerate(offsets):
        columns = block_columns(facts_ref, offset, chips, width)
        piece = act[:, place * width : (place + 1) * width]
        total += jnp.dot(piece, columns, preferred_element_type=jnp.float32)
    total = total.astype(jnp.bfloat16)
    if last:
        matrix = exchange_matrix(facts_ref[0], unit, True)
        total = jnp.dot(matrix, total, preferred_element_type=jnp.float32).astype(jnp.bfloat16)
    out_ref[...] = total


def token_kernel(offsets, chips, unit, facts_ref, act_ref, *refs):
    count = len(offsets) + 1
    blocks, refs = refs[:count], refs[count:]
    keep_ref, send_ref, *buffers, sems = refs
    half = buffers[-1].shape[1] // 2
    targets = [*buffers[:-1], buffers[-1].at[:, :half], buffers[-1].at[:, half:]]
    copies = [
        pltpu.make_async_copy(ref, target, sems.at[place])
        for place, (ref, target) in enumerate(zip(blocks, targets))
    ]
    for copy in copies:
        copy.start()
    width = buffers[0].shape[0]
    matrix = exchange_matrix(facts_ref[0], unit, False)
    act = jnp.dot(matrix, act_ref[...], preferred_element_type=jnp.float32).astype(jnp.bfloat16)
    pieces = [
        contract_last(act, block_columns(facts_ref, offset, chips, width)).astype(jnp.bfloat16)
        for offset in offsets
    ]
    for copy in copies:
        copy.wait()
    total = stacked_dot(pieces, [buffer[...] for buffer in buffers])
    rows = keep_ref.shape[0]
    keep_ref[...] = total[:rows]
    send_ref[...] = total[rows:].astype(jnp.bfloat16)


def block_products(kernel, left, blocks):
    rows = 2 * OUT_SIDE * OUT_SIDE
    return whole_call(kernel, f32(rows, len(blocks) * blocks[0].shape[0]), [])(*left, *blocks)


def back_products(back, blocks, halves=()):
    rows, count = 2 * OUT_SIDE * OUT_SIDE, len(blocks) + (1 if halves else 0)
    kernel = functools.partial(back_kernel, bool(halves))
    operands = *back, *blocks, *halves
    return whole_call(kernel, f32(rows, count * blocks[0].shape[0]), [])(*operands)


def facts_call(kernel, outs, facts, operands, cost=FREE):
    return pl.pallas_call(
        kernel,
        out_shape=outs,
        in_specs=vmem_specs(len(operands)),
        compiler_params=pltpu.CompilerParams(vmem_limit_bytes=VMEM_BYTES),
        cost_estimate=cost,
    )(facts, *operands)


def add_gradients(facts, terms, slopes, pieces, blocks, before, unit, parts, last):
    rows = terms[0].shape[0] // 2
    kernel = functools.partial(totals_kernel, pieces, unit, parts, not before)
    outs = ()
    for lanes in parts:
        shape = rows, lanes.stop - lanes.start
        outs += f32(*shape), (bf16 if last else f32)(*shape)
    return tuple(facts_call(kernel, outs, facts, (*terms, *slopes, *blocks, *before)))


def act_and_slope(facts, terms, offsets, chips, before, unit):
    rows, columns = terms[0].shape
    kernel = functools.partial(act_kernel, offsets, chips, unit, bool(before))
    outs = f32(rows, columns), bf16(rows, columns // len(offsets) * chips)
    return facts_call(kernel, outs, facts, (*terms, *before))


def token_products(facts, act, offsets, chips, blocks, unit):
    rows, columns = act.shape[0] // 2, blocks[0].shape[1]
    return pl.pallas_call(
        functools.partial(token_kernel, offsets, chips, unit),
        out_shape=(f32(rows, columns), bf16(rows, columns)),
        in_specs=vmem_specs(1) + [pl.BlockSpec(memory_space=pl.ANY)] * len(blocks),
        scratch_shapes=[pltpu.VMEM(blocks[0].shape, jnp.bfloat16)] * len(offsets)
        + [pltpu.SemaphoreType.DMA((len(blocks),))],
        compiler_params=pltpu.CompilerParams(vmem_limit_bytes=VMEM_BYTES),
        cost_estimate=FREE,
    )(facts, act, *blocks)


def chips_exchange(value):
    count = lax.axis_size("ctx")
    groups = [list(range(core, count, 2)) for core in range(2)]
    return lax.all_to_all(
        value, "ctx", split_axis=0, concat_axis=0, tiled=True, axis_index_groups=groups
    )


def per_device(
    features,
    group_kernel,
    squeeze_in,
    squeeze_out,
    sampler_kernel,
    readout_kernel,
    frame_clip,
    clip_keep,
    token_cotangent,
):
    chans = features.shape[2]
    count = lax.axis_size("ctx")
    steps, unit = count // 4, OUT_SIDE * OUT_SIDE // count
    flat_sampler = sampler_kernel.reshape(sampler_kernel.shape[0], 8 * chans)
    chips = count // 2
    s_up, s_down = ring_send(flat_sampler, 1), ring_send(flat_sampler, -1)
    group_kernel = jnp.swapaxes(group_kernel, 1, 2)
    squeeze_in = squeeze_in.T
    facts = facts_of(frame_clip, clip_keep)

    conv, padded, squeezed = conv_forward(features, group_kernel, squeeze_in)
    token_cotangent, squeezed = tie(token_cotangent, squeezed)
    back = chips_exchange(token_cotangent)
    squeezed = sum_tp(squeezed)
    even, odd, excite = hidden_frames(conv, padded, squeezed, squeeze_out)
    halo = shifted(odd, "ctx", 1)

    s_up, s_down = [flat_sampler, s_up], [flat_sampler, s_down]
    s_up[1], s_down[1], even, readout_kernel = tie(s_up[1], s_down[1], even, readout_kernel)
    for step in range(2, steps):
        s_up.append(ring_send(s_up[-1], 1))
        s_down.append(ring_send(s_down[-1], -1))
        if step == 2:
            halo, s_up[2], s_down[2] = tie(halo, s_up[2], s_down[2])
            r_down = [readout_kernel, ring_send(readout_kernel, -1)]
            patches = take_patches(facts, halo, even)
            patches = order_rows(facts, patches, swap_cores(patches), unit)
    s_up[-1], s_down[-1], back, readout_kernel = tie(s_up[-1], s_down[-1], back, readout_kernel)
    back = (back, swap_cores(back))
    cut = 4 * chans
    s_last = ring_send(s_up[-1][:, :cut], 1), ring_send(s_down[-1][:, cut:], -1)
    samplers = [flat_sampler] + [block for pair in zip(s_up[1:], s_down[1:]) for block in pair]
    offsets = ring_offsets(chips)
    count = 2 * steps - 3
    r_up, r_down = [ring_send(readout_kernel, 1)], [ring_send(readout_kernel, -1)]
    first_pre = tp_terms(block_products(pre_kernel, (patches,), samplers[:count]))
    r_up[0], r_down[0], *first_pre = tie(r_up[0], r_down[0], *first_pre)
    for step in range(2, steps - 1):
        r_up.append(ring_send(r_up[-1], 1))
        r_down.append(ring_send(r_down[-1], -1))
    samplers.append(jnp.concatenate(s_last, axis=1))
    first_slope, first_act = act_and_slope(facts, first_pre, offsets[:count], chips, (), unit)
    last_pre = block_products(pre_kernel, (patches,), samplers[count:])
    last_slope, act = act_and_slope(
        facts, tp_terms(last_pre), offsets[count:], chips, (first_act,), unit
    )
    slopes = first_slope, last_slope
    halo_lanes, even_lanes = slice(0, cut), slice(cut, 2 * cut)
    both = halo_lanes, even_lanes
    readouts = [readout_kernel] + [block for pair in zip(r_up, r_down) for block in pair]
    sums = back_products(back, readouts[: count - 2])
    r_up[-1], r_down[-1], act, sums = tie(r_up[-1], r_down[-1], act, sums)
    readouts[count - 2 :] = r_up[-1], r_down[-1]
    r_up.append(ring_send(r_up[-1], 1))
    r_down.append(ring_send(r_down[-1], -1))
    held = tie(r_up[-1], r_down[-1], chips_exchange(act), *tp_terms(sums))
    r_up[-1], r_down[-1], act, terms = *held[:3], held[3:]
    pieces = [(0, place) for place in range(count - 2)]
    grads = add_gradients(
        facts, terms, slopes, pieces, samplers[: count - 2], (), unit, both, False
    )
    terms = tp_terms(back_products(back, readouts[count - 2 :]))
    pieces = [(0, count - 2), (0, count - 1)]
    grads = add_gradients(
        facts, terms, slopes, pieces, samplers[count - 2 : count], grads, unit, both, False
    )
    cut = readout_kernel.shape[1] // 2
    r_last = ring_send(r_up[-1][:, :cut], 1), ring_send(r_down[-1][:, cut:], -1)
    held = tie(r_up[-1], r_down[-1], *r_last, *grads)
    late, r_last, grads = held[:2], held[2:4], held[4:]
    terms = tp_terms(back_products(back, late, r_last))
    pieces, blocks = [(1, 0), (1, 1), (1, 2)], samplers[count:]
    halo_own, halo_mate = add_gradients(
        facts, terms, slopes, pieces, blocks, grads[:2], unit, (halo_lanes,), True
    )
    halo_mate, first_term = tie(halo_mate, terms[0])
    even_own, even_mate = add_gradients(
        facts, (first_term, terms[1]), slopes, pieces, blocks, grads[2:], unit, (even_lanes,), True
    )
    lead, facts_late = return_patches(facts, halo_own, swap_cores(halo_mate), chans, jnp.bfloat16)
    grad_odd = shifted(lead, "ctx", -1)
    grad_even, facts_late = return_patches(
        facts_late, even_own, swap_cores(even_mate), chans, jnp.float32
    )
    tokens = token_products(
        facts_late, act, offsets, chips, [*readouts, *late, *r_last], unit
    )
    grad_relaxed = sum_tp(excite_grad(grad_even, grad_odd, conv, excite, squeeze_out))
    llm_tokens = (tokens[0] + swap_cores(tokens[1]).astype(jnp.float32)).astype(jnp.bfloat16)
    grad_features = conv_backward(
        grad_even, grad_odd, conv, excite, squeezed, grad_relaxed, squeeze_in,
        dense_weights(facts_late, group_kernel), group_kernel.shape[1],
    )
    return (llm_tokens, grad_features)


def solution(mesh):
    placed = (
        P("ctx", None, "tp"),
        P(None, "tp", None),
        P("tp", None),
        P(None, "tp"),
        P("ctx", None, "tp"),
        P("ctx", "tp"),
        P(),
        P(),
        P("ctx", "tp"),
    )
    return jax.shard_map(
        per_device,
        mesh=mesh,
        in_specs=placed,
        out_specs=(P("ctx", "tp"), P("ctx", None, "tp")),
        check_vma=False,
    )
```

```python
import functools

import jax
import jax.numpy as jnp
from jax import lax
from jax.experimental import pallas as pl
from jax.experimental.pallas import tpu as pltpu
from jax.sharding import PartitionSpec as P

SIDE = 14
OUT_SIDE = 8
WIDE = 16
FRAME_ROWS = WIDE * WIDE
EDGE = 8
LANES = 128
WINDOW = 256
VMEM_BYTES = 16 * 2**20
FREE = pl.CostEstimate(flops=0, bytes_accessed=0, transcendentals=0)


def whole_call(kernel, outs, scratch, cost=FREE):
    return pl.pallas_call(
        kernel,
        out_shape=outs,
        scratch_shapes=scratch,
        compiler_params=pltpu.CompilerParams(vmem_limit_bytes=VMEM_BYTES),
        cost_estimate=cost,
    )


def contract_last(left, right):
    return lax.dot_general(
        left, right, (((1,), (1,)), ((), ())), preferred_element_type=jnp.float32
    )


def contract_exact(left, right):
    return lax.dot_general(
        left,
        right,
        (((1,), (1,)), ((), ())),
        precision=lax.Precision.HIGHEST,
        preferred_element_type=jnp.float32,
    )


def silu_slope(values):
    sigma = jax.nn.sigmoid(values)
    return sigma * (1.0 + values * (1.0 - sigma))


def inside(rows):
    row = lax.broadcasted_iota(jnp.int32, (rows, 1), 0)
    across, down = row & (WIDE - 1), (row // WIDE) & (WIDE - 1)
    good = (across >= 1) & (across <= SIDE) & (down >= 1) & (down <= SIDE)
    return good.astype(jnp.float32)


def channel_blocks(chans, width):
    span = 4 * width
    blocks = []
    for low in range(0, chans, span):
        high = min(chans, low + span)
        blocks.append((low, high, low // LANES * LANES, min(chans, -(-high // LANES) * LANES)))
    return blocks


def block_tools(block, width):
    low, high, start, end = block
    size = end - start
    out_row = lax.broadcasted_iota(jnp.int32, (size, width), 0) + start
    within = lax.broadcasted_iota(jnp.int32, (size, width), 1)
    lane = lax.broadcasted_iota(jnp.int32, (size, size), 1) + start
    row = lax.broadcasted_iota(jnp.int32, (size, size), 0) + start
    spread = jnp.zeros((size, width), jnp.float32)
    same = jnp.zeros((size, size), jnp.float32)
    for first in range(low, high, width):
        spread += (out_row == within + first).astype(jnp.float32)
        in_lane = (lane >= first) & (lane < first + width)
        in_row = (row >= first) & (row < first + width)
        same += (in_lane & in_row).astype(jnp.float32)
    return spread.astype(jnp.bfloat16), same


def dense_tap(group_ref, tap, block, spread, same):
    _, _, start, end = block
    full = jnp.dot(spread, group_ref[tap, :, start:end], preferred_element_type=jnp.float32)
    return (full * same).astype(jnp.bfloat16)


def store_shifts(wide_ref, shift_ref, sign):
    rows = shift_ref.shape[1]
    for col in range(3):
        at = EDGE + sign * (col - 1)
        chans = wide_ref.shape[1]
        shift_ref[col, :, 0:chans] = wide_ref[at : at + rows, :].astype(jnp.bfloat16)
        if shift_ref.shape[2] > chans:
            blank = jnp.zeros((rows, shift_ref.shape[2] - chans), jnp.bfloat16)
            shift_ref[col, :, chans:] = blank


def conv_kernel(feat_ref, group_ref, squeeze_ref, *refs):
    conv_ref, pad_ref, sq_ref, flat_ref, wide_ref, shift_ref = refs
    frames, _, chans = feat_ref.shape
    width = group_ref.shape[1]
    rows = frames * FRAME_ROWS
    wide_ref[...] = jnp.zeros_like(wide_ref)
    for frame in range(frames):
        flat_ref[...] = feat_ref[frame].astype(jnp.float32)
        for y in range(SIDE):
            at = EDGE + frame * FRAME_ROWS + (y + 1) * WIDE + 1
            wide_ref[at : at + SIDE, :] = flat_ref[y * SIDE : (y + 1) * SIDE, :]
    store_shifts(wide_ref, shift_ref, 1)
    pad_ref[...] = shift_ref[1]
    conv_ref[...] = jnp.zeros_like(conv_ref)
    body = rows - 2 * WIDE
    for block in channel_blocks(chans, width):
        _, _, start, end = block
        spread, same = block_tools(block, width)
        total = jnp.zeros((body, end - start), jnp.float32)
        for tap in range(9):
            down, across = divmod(tap, 3)
            weights = dense_tap(group_ref, tap, block, spread, same)
            source = shift_ref[across, down * WIDE : down * WIDE + body, start:end]
            total += contract_last(source, weights)
        conv_ref[WIDE : WIDE + body, start:end] += total
    conv = conv_ref[...] * inside(rows)
    conv_ref[...] = conv
    active = conv * jax.nn.sigmoid(conv)
    pooled = jnp.concatenate(
        [
            jnp.sum(active[f * FRAME_ROWS : (f + 1) * FRAME_ROWS], axis=0, keepdims=True)
            for f in range(frames)
        ],
        axis=0,
    ) * (1.0 / (SIDE * SIDE))
    sq_ref[...] = contract_exact(pooled, squeeze_ref[...].astype(jnp.float32))


def hidden_kernel(conv_ref, pad_ref, sq_ref, expand_ref, even_ref, odd_ref, excite_ref):
    squeezed = sq_ref[...]
    relaxed = squeezed * jax.nn.sigmoid(squeezed)
    excite = jax.nn.sigmoid(
        jnp.dot(relaxed, expand_ref[...].astype(jnp.float32), precision=lax.Precision.HIGHEST)
    )
    excite_ref[...] = excite
    for frame, out_ref in enumerate((even_ref, odd_ref)):
        rows = slice(frame * FRAME_ROWS, (frame + 1) * FRAME_ROWS)
        conv = conv_ref[rows, :]
        active = conv * jax.nn.sigmoid(conv)
        hidden = pad_ref[rows, :].astype(jnp.float32) + active * excite[frame : frame + 1]
        out_ref[...] = hidden.astype(jnp.bfloat16)


def select_rows(to_patches):
    shape = (FRAME_ROWS, FRAME_ROWS)
    out_row = lax.broadcasted_iota(jnp.int32, shape, 0)
    in_row = lax.broadcasted_iota(jnp.int32, shape, 1)
    patch_row, frame_row = (out_row, in_row) if to_patches else (in_row, out_row)
    down, across = patch_row >> 7, (patch_row >> 6) & 1
    a, b = (patch_row >> 3) & 7, patch_row & 7
    return ((2 * a + down) * WIDE + 2 * b + across == frame_row).astype(jnp.float32)


def facts_kernel(clip_ref, keep_ref, out_ref):
    shard = lax.axis_index("ctx")
    frames = clip_ref.shape[0]
    out_ref[0] = shard % 2
    for block in range(2):
        pair = shard // 2 * 2 + block
        clip = clip_ref[2 * pair]
        start = jnp.int32(0)
        for other in range(0, frames, 2):
            start += jnp.where(clip_ref[other] < clip, 1, 0)
        out_ref[1 + block] = keep_ref[clip] - (pair - start) * (OUT_SIDE * OUT_SIDE)
    before = clip_ref[jnp.maximum(2 * shard - 1, 0)]
    chip, chips = shard // 2, lax.axis_size("ctx") // 2
    out_ref[4] = jnp.where(chip % 2 == 0, chip // 2, chips - 1 - chip // 2)
    out_ref[3] = jnp.where((shard > 0) & (before == clip_ref[2 * shard]), 1, 0)


def token_place(row, core, unit):
    per_block = OUT_SIDE * OUT_SIDE
    within = row % per_block
    block = (within // unit) % 2
    target_core = jnp.where(row < per_block, core, 1 - core)
    return block, unit * (2 * (within // (2 * unit)) + target_core) + within % unit


def reorder_matrix(core, unit, to_sent):
    shape = (2 * OUT_SIDE * OUT_SIDE,) * 2
    out_row = lax.broadcasted_iota(jnp.int32, shape, 0)
    in_row = lax.broadcasted_iota(jnp.int32, shape, 1)
    sent, natural = (out_row, in_row) if to_sent else (in_row, out_row)
    block, token = token_place(sent, core, unit)
    source = jnp.where(block == core, 0, OUT_SIDE * OUT_SIDE) + token
    return (source == natural).astype(jnp.bfloat16)


def order_kernel(unit, facts_ref, own_ref, mate_ref, out_ref):
    rows = jnp.concatenate([own_ref[...], mate_ref[...]], axis=0)
    matrix = reorder_matrix(facts_ref[0], unit, True)
    out_ref[...] = jnp.dot(matrix, rows, preferred_element_type=jnp.float32).astype(jnp.bfloat16)


def patch_kernel(facts_ref, halo_ref, even_ref, out_ref):
    chans = halo_ref.shape[1]
    per_frame = OUT_SIDE * OUT_SIDE
    select = select_rows(True).astype(jnp.bfloat16)
    for frame, source in enumerate((halo_ref, even_ref)):
        rows = jnp.dot(select, source[...], preferred_element_type=jnp.float32)
        if frame == 0:
            rows = rows * facts_ref[3].astype(jnp.float32)
        rows = rows.astype(jnp.bfloat16)
        for tap in range(4):
            at = (frame * 4 + tap) * chans
            out_ref[:, at : at + chans] = rows[tap * per_frame : (tap + 1) * per_frame]


def unpatch_kernel(facts_ref, own_ref, mate_ref, out_ref, facts_out_ref):
    for place in range(facts_ref.shape[0]):
        facts_out_ref[place] = facts_ref[place]
    chans = out_ref.shape[1]
    rows = own_ref[...] + mate_ref[...].astype(jnp.float32)
    pieces = [rows[:, tap * chans : (tap + 1) * chans] for tap in range(4)]
    rows = jnp.concatenate(pieces, axis=0)
    select = select_rows(False).astype(jnp.bfloat16)
    coarse = rows.astype(jnp.bfloat16)
    frame = jnp.dot(select, coarse, preferred_element_type=jnp.float32)
    if out_ref.dtype == jnp.bfloat16:
        frame = frame * facts_ref[3].astype(jnp.float32)
    else:
        rest = (rows - coarse.astype(jnp.float32)).astype(jnp.bfloat16)
        frame += jnp.dot(select, rest, preferred_element_type=jnp.float32)
    out_ref[...] = (frame * inside(FRAME_ROWS)).astype(out_ref.dtype)


def excite_grad_kernel(even_ref, odd_ref, conv_ref, excite_ref, expand_ref, out_ref):
    sums = []
    for frame, grad_ref in enumerate((even_ref, odd_ref)):
        conv = conv_ref[frame * FRAME_ROWS : (frame + 1) * FRAME_ROWS, :]
        active = conv * jax.nn.sigmoid(conv)
        sums.append(jnp.sum(grad_ref[...].astype(jnp.float32) * active, axis=0, keepdims=True))
    excite = excite_ref[...]
    inner = jnp.concatenate(sums, axis=0) * excite * (1.0 - excite)
    out_ref[...] = contract_exact(inner, expand_ref[...].astype(jnp.float32))


def conv_grad_kernel(
    width, even_ref, odd_ref, conv_ref, excite_ref, sq_ref, relaxed_ref, squeeze_ref, *refs
):
    *dense_refs, out_ref, flat_ref, wide_ref, shift_ref, grad_ref = refs
    frames, _, chans = out_ref.shape
    rows = frames * FRAME_ROWS
    grad_squeezed = relaxed_ref[...] * silu_slope(sq_ref[...])
    pooled = jnp.dot(
        grad_squeezed, squeeze_ref[...].astype(jnp.float32), precision=lax.Precision.HIGHEST
    ) * (1.0 / (SIDE * SIDE))
    wide_ref[0:EDGE, :] = jnp.zeros((EDGE, chans), jnp.float32)
    wide_ref[EDGE + rows :, :] = jnp.zeros((EDGE, chans), jnp.float32)
    good = inside(FRAME_ROWS)
    for frame, source in enumerate((even_ref, odd_ref)):
        at = frame * FRAME_ROWS
        grad = source[...].astype(jnp.float32)
        grad_ref[at : at + FRAME_ROWS, :] = grad
        active = grad * excite_ref[frame : frame + 1, :] + pooled[frame : frame + 1]
        slope = silu_slope(conv_ref[at : at + FRAME_ROWS, :])
        wide_ref[EDGE + at : EDGE + at + FRAME_ROWS, :] = active * slope * good
    store_shifts(wide_ref, shift_ref, -1)
    body = rows - 2 * WIDE
    for block, dense_ref in zip(channel_blocks(chans, width), dense_refs):
        start = block[2]
        sources = []
        for tap in range(9):
            down, across = divmod(tap, 3)
            at = (2 - down) * WIDE
            sources.append(shift_ref[across, at : at + body, start : start + WINDOW])
        total = jnp.dot(
            jnp.concatenate(sources, axis=1), dense_ref[...], preferred_element_type=jnp.float32
        )
        end = min(chans, start + WINDOW)
        grad_ref[WIDE : WIDE + body, start:end] += total[:, : end - start]
    for frame in range(frames):
        for y in range(SIDE):
            at = frame * FRAME_ROWS + (y + 1) * WIDE + 1
            flat_ref[y * SIDE : (y + 1) * SIDE, :] = grad_ref[at : at + SIDE, :]
        out_ref[frame] = flat_ref[...].astype(jnp.bfloat16)


def f32(*shape):
    return jax.ShapeDtypeStruct(shape, jnp.float32)


def bf16(*shape):
    return jax.ShapeDtypeStruct(shape, jnp.bfloat16)


def conv_forward(features, group_kernel, squeeze_in):
    frames, cells, chans = features.shape
    rows = frames * FRAME_ROWS
    return whole_call(
        conv_kernel,
        (f32(rows, chans), bf16(rows, chans), f32(frames, squeeze_in.shape[0])),
        [
            pltpu.VMEM((cells, chans), jnp.float32),
            pltpu.VMEM((rows + 2 * EDGE, chans), jnp.float32),
            pltpu.VMEM((3, rows, chans), jnp.bfloat16),
        ],
    )(features, group_kernel, squeeze_in)


def hidden_frames(conv, padded, squeezed, squeeze_out):
    rows, chans = conv.shape
    return whole_call(
        hidden_kernel,
        (bf16(FRAME_ROWS, chans), bf16(FRAME_ROWS, chans), f32(rows // FRAME_ROWS, chans)),
        [],
    )(conv, padded, squeezed, squeeze_out)


def vmem_specs(count):
    return [pl.BlockSpec(memory_space=pltpu.SMEM)] + [pl.BlockSpec(memory_space=pltpu.VMEM)] * count


def facts_of(frame_clip, clip_keep):
    smem = pl.BlockSpec(memory_space=pltpu.SMEM)
    return pl.pallas_call(
        facts_kernel,
        out_shape=jax.ShapeDtypeStruct((5,), jnp.int32),
        in_specs=[smem, smem],
        out_specs=smem,
        cost_estimate=FREE,
    )(frame_clip, clip_keep)


def order_rows(facts, own, mate, unit):
    rows, columns = own.shape
    return pl.pallas_call(
        functools.partial(order_kernel, unit),
        out_shape=bf16(2 * rows, columns),
        in_specs=vmem_specs(2),
        compiler_params=pltpu.CompilerParams(vmem_limit_bytes=VMEM_BYTES),
        cost_estimate=FREE,
    )(facts, own, mate)


def take_patches(facts, halo, even):
    chans = even.shape[1]
    return pl.pallas_call(
        patch_kernel,
        out_shape=bf16(OUT_SIDE * OUT_SIDE, 8 * chans),
        in_specs=vmem_specs(2),
        compiler_params=pltpu.CompilerParams(vmem_limit_bytes=VMEM_BYTES),
        cost_estimate=FREE,
    )(facts, halo, even)


def return_patches(facts, own, mate, chans, dtype):
    return pl.pallas_call(
        unpatch_kernel,
        out_shape=(
            jax.ShapeDtypeStruct((FRAME_ROWS, chans), dtype),
            jax.ShapeDtypeStruct(facts.shape, jnp.int32),
        ),
        in_specs=vmem_specs(2),
        out_specs=vmem_specs(1)[::-1],
        compiler_params=pltpu.CompilerParams(vmem_limit_bytes=VMEM_BYTES),
        cost_estimate=FREE,
    )(facts, own, mate)


def excite_grad(even, odd, conv, excite, squeeze_out):
    rows, chans = conv.shape
    return whole_call(
        excite_grad_kernel,
        f32(rows // FRAME_ROWS, squeeze_out.shape[0]),
        [],
    )(even, odd, conv, excite, squeeze_out)


def conv_backward(even, odd, conv, excite, squeezed, grad_relaxed, squeeze_in, dense, width):
    rows, chans = conv.shape
    frames = rows // FRAME_ROWS
    lanes = channel_blocks(chans, width)[-1][2] + WINDOW
    return whole_call(
        functools.partial(conv_grad_kernel, width),
        bf16(frames, SIDE * SIDE, chans),
        [
            pltpu.VMEM((SIDE * SIDE, chans), jnp.float32),
            pltpu.VMEM((rows + 2 * EDGE, chans), jnp.float32),
            pltpu.VMEM((3, rows, lanes), jnp.bfloat16),
            pltpu.VMEM((rows, chans), jnp.float32),
        ],
        pl.CostEstimate(flops=rows * chans * 9216, bytes_accessed=16 * rows * chans, transcendentals=0),
    )(even, odd, conv, excite, squeezed, grad_relaxed, squeeze_in, *dense)


def dense_kernel(facts_ref, group_ref, *dense_refs):
    _, width, chans = group_ref.shape
    for block, dense_ref in zip(channel_blocks(chans, width), dense_refs):
        low, high, start, _ = block
        end = min(chans, start + WINDOW)
        spread, same = block_tools((low, high, start, start + WINDOW), width)
        dense_ref[...] = jnp.zeros_like(dense_ref)
        for tap in range(9):
            full = jnp.dot(spread, group_ref[tap, :, start:end], preferred_element_type=jnp.float32)
            rows = slice(tap * WINDOW, (tap + 1) * WINDOW)
            dense_ref[rows, 0 : end - start] = (full * same[:, : end - start]).astype(jnp.bfloat16)


def dense_weights(facts, group_kernel):
    _, width, chans = group_kernel.shape
    outs = (bf16(9 * WINDOW, WINDOW),) * len(channel_blocks(chans, width))
    return facts_call(dense_kernel, outs, facts, (group_kernel,))


def shifted(value, axis, by):
    count = lax.axis_size(axis)
    pairs = [(i, i + by) for i in range(count) if 0 <= i + by < count]
    return lax.ppermute(value, axis, pairs)


def ring_order(chips):
    return list(range(0, chips, 2)) + list(range(1, chips, 2))[::-1]


def ring_pairs(count, by):
    order = ring_order(count // 2)
    pairs = []
    for place, chip in enumerate(order):
        target = order[(place + by) % len(order)]
        pairs += [(2 * chip, 2 * target), (2 * chip + 1, 2 * target + 1)]
    return pairs


def swap_cores(value):
    return lax.ppermute(value, "ctx", [(i, i ^ 1) for i in range(lax.axis_size("ctx"))])


def tp_terms(value):
    size = lax.axis_size("tp")
    reach, other = 1, None
    while reach < size:
        value = value if other is None else value + other
        other = lax.ppermute(value, "tp", [(i, i ^ reach) for i in range(size)])
        reach *= 2
    return value, jnp.zeros_like(value) if other is None else other


def sum_tp(value):
    value, other = tp_terms(value)
    return value + other


def ring_send(value, by):
    return lax.ppermute(value, "ctx", ring_pairs(lax.axis_size("ctx"), by))


def tie(*values):
    return lax.optimization_barrier(values)


def stacked_contract(left, blocks):
    blocks = [ref[...] for ref in blocks]
    if blocks[0].shape[0] % 8 == 0:
        blocks = [jnp.concatenate(blocks, axis=0)]
    return jnp.concatenate([contract_last(left, block) for block in blocks], axis=1)


def pre_kernel(patch_ref, *refs):
    *blocks, out_ref = refs
    out_ref[...] = stacked_contract(patch_ref[...], blocks)


def back_kernel(keep_ref, send_ref, *refs):
    *blocks, out_ref = refs
    back = jnp.concatenate([keep_ref[...], send_ref[...]], axis=0)
    out_ref[...] = stacked_contract(back, blocks)


def live_rows(facts_ref, rows, unit):
    block, token = token_place(
        lax.broadcasted_iota(jnp.int32, (rows, 1), 0), facts_ref[0], unit
    )
    return (token < jnp.where(block == 0, facts_ref[1], facts_ref[2])).astype(jnp.float32)


def stacked_dot(pieces, blocks):
    if blocks[0].shape[0] % 8 == 0:
        pieces = [jnp.concatenate(pieces, axis=1)]
        blocks = [jnp.concatenate(blocks, axis=0)]
    total = 0.0
    for piece, block in zip(pieces, blocks):
        total += jnp.dot(piece, block, preferred_element_type=jnp.float32)
    return total


def totals_kernel(pieces, unit, parts, first, facts_ref, *refs):
    grad_act = refs[0][...] + refs[1][...]
    count = len(pieces)
    slopes, blocks = refs[2:4], refs[4 : 4 + count]
    before, after = refs[4 + count : -2 * len(parts)], refs[-2 * len(parts) :]
    rows, width = grad_act.shape[0], blocks[0].shape[0]
    slope = jnp.concatenate(
        [slopes[source][:, index * width : (index + 1) * width] for source, index in pieces], axis=1
    )
    factor = jnp.dot(
        reorder_matrix(facts_ref[0], unit, False),
        (grad_act * slope).astype(jnp.bfloat16),
        preferred_element_type=jnp.float32,
    ).astype(jnp.bfloat16)
    factors = [factor[:, place * width : (place + 1) * width] for place in range(count)]
    for part, lanes in enumerate(parts):
        total = stacked_dot(factors, [ref[:, lanes] for ref in blocks])
        for half in range(2):
            value = total[half * rows // 2 : (half + 1) * rows // 2]
            value = value if first else before[2 * part + half][...] + value
            ref = after[2 * part + half]
            ref[...] = value.astype(ref.dtype)


def ring_offsets(chips):
    offsets = [0]
    for step in range(1, chips // 2):
        offsets += [-step, step]
    return offsets + [chips // 2]


def block_columns(facts_ref, offset, chips, width):
    shape = (width, chips * width)
    place = (facts_ref[4] + offset + chips) % chips
    column = lax.broadcasted_iota(jnp.int32, shape, 1)
    return (column == lax.broadcasted_iota(jnp.int32, shape, 0) + place * width).astype(jnp.bfloat16)


def exchange_matrix(core, unit, to_sent):
    per_block = OUT_SIDE * OUT_SIDE
    shape = (2 * per_block,) * 2
    out_row = lax.broadcasted_iota(jnp.int32, shape, 0)
    in_row = lax.broadcasted_iota(jnp.int32, shape, 1)
    sent, kept = (out_row, in_row) if to_sent else (in_row, out_row)
    target_core = (sent // (2 * unit)) % 2
    within = sent // (4 * unit) * (2 * unit) + sent % (2 * unit)
    return (within + jnp.where(target_core == core, 0, per_block) == kept).astype(jnp.bfloat16)


def act_kernel(offsets, chips, unit, last, facts_ref, own_ref, other_ref, *refs):
    *before, slope_ref, out_ref = refs
    pre = own_ref[...] + other_ref[...]
    width = pre.shape[1] // len(offsets)
    live = live_rows(facts_ref, pre.shape[0], unit)
    sigma = jax.nn.sigmoid(pre)
    slope_ref[...] = sigma * (1.0 + pre * (1.0 - sigma)) * live
    act = (pre * sigma * live).astype(jnp.bfloat16)
    total = before[0][...].astype(jnp.float32) if last else 0.0
    for place, offset in enumerate(offsets):
        columns = block_columns(facts_ref, offset, chips, width)
        piece = act[:, place * width : (place + 1) * width]
        total += jnp.dot(piece, columns, preferred_element_type=jnp.float32)
    total = total.astype(jnp.bfloat16)
    if last:
        matrix = exchange_matrix(facts_ref[0], unit, True)
        total = jnp.dot(matrix, total, preferred_element_type=jnp.float32).astype(jnp.bfloat16)
    out_ref[...] = total


def token_kernel(offsets, chips, unit, facts_ref, act_ref, *refs):
    count = len(offsets)
    blocks, refs = refs[:count], refs[count:]
    keep_ref, send_ref, *buffers, sems = refs
    copies = [
        pltpu.make_async_copy(ref, buffer, sems.at[place])
        for place, (ref, buffer) in enumerate(zip(blocks, buffers))
    ]
    for copy in copies:
        copy.start()
    width = buffers[0].shape[0]
    matrix = exchange_matrix(facts_ref[0], unit, False)
    act = jnp.dot(matrix, act_ref[...], preferred_element_type=jnp.float32).astype(jnp.bfloat16)
    pieces = [
        contract_last(act, block_columns(facts_ref, offset, chips, width)).astype(jnp.bfloat16)
        for offset in offsets
    ]
    for copy in copies:
        copy.wait()
    total = stacked_dot(pieces, [buffer[...] for buffer in buffers])
    rows = keep_ref.shape[0]
    keep_ref[...] = total[:rows]
    send_ref[...] = total[rows:].astype(jnp.bfloat16)


def block_products(kernel, left, blocks):
    rows = 2 * OUT_SIDE * OUT_SIDE
    return whole_call(kernel, f32(rows, len(blocks) * blocks[0].shape[0]), [])(*left, *blocks)


def facts_call(kernel, outs, facts, operands, cost=FREE):
    return pl.pallas_call(
        kernel,
        out_shape=outs,
        in_specs=vmem_specs(len(operands)),
        compiler_params=pltpu.CompilerParams(vmem_limit_bytes=VMEM_BYTES),
        cost_estimate=cost,
    )(facts, *operands)


def add_gradients(facts, terms, slopes, pieces, blocks, before, unit, parts, last):
    rows = terms[0].shape[0] // 2
    kernel = functools.partial(totals_kernel, pieces, unit, parts, not before)
    outs = ()
    for lanes in parts:
        shape = rows, lanes.stop - lanes.start
        outs += f32(*shape), (bf16 if last else f32)(*shape)
    return tuple(facts_call(kernel, outs, facts, (*terms, *slopes, *blocks, *before)))


def act_and_slope(facts, terms, offsets, chips, before, unit):
    rows, columns = terms[0].shape
    kernel = functools.partial(act_kernel, offsets, chips, unit, bool(before))
    outs = f32(rows, columns), bf16(rows, columns // len(offsets) * chips)
    return facts_call(kernel, outs, facts, (*terms, *before))


def token_products(facts, act, offsets, chips, blocks, unit):
    rows, columns = act.shape[0] // 2, blocks[0].shape[1]
    return pl.pallas_call(
        functools.partial(token_kernel, offsets, chips, unit),
        out_shape=(f32(rows, columns), bf16(rows, columns)),
        in_specs=vmem_specs(1) + [pl.BlockSpec(memory_space=pl.ANY)] * len(blocks),
        scratch_shapes=[pltpu.VMEM(block.shape, block.dtype) for block in blocks]
        + [pltpu.SemaphoreType.DMA((len(blocks),))],
        compiler_params=pltpu.CompilerParams(vmem_limit_bytes=VMEM_BYTES),
        cost_estimate=FREE,
    )(facts, act, *blocks)


def chips_exchange(value):
    count = lax.axis_size("ctx")
    groups = [list(range(core, count, 2)) for core in range(2)]
    return lax.all_to_all(
        value, "ctx", split_axis=0, concat_axis=0, tiled=True, axis_index_groups=groups
    )


def per_device(
    features,
    group_kernel,
    squeeze_in,
    squeeze_out,
    sampler_kernel,
    readout_kernel,
    frame_clip,
    clip_keep,
    token_cotangent,
):
    chans = features.shape[2]
    count = lax.axis_size("ctx")
    steps, unit = count // 4, OUT_SIDE * OUT_SIDE // count
    flat_sampler = sampler_kernel.reshape(sampler_kernel.shape[0], 8 * chans)
    chips = count // 2
    s_up, s_down = ring_send(flat_sampler, 1), ring_send(flat_sampler, -1)
    group_kernel = jnp.swapaxes(group_kernel, 1, 2)
    squeeze_in = squeeze_in.T
    facts = facts_of(frame_clip, clip_keep)

    conv, padded, squeezed = conv_forward(features, group_kernel, squeeze_in)
    squeezed = sum_tp(squeezed)
    even, odd, excite = hidden_frames(conv, padded, squeezed, squeeze_out)
    halo = shifted(odd, "ctx", 1)

    s_up, s_down = [flat_sampler, s_up], [flat_sampler, s_down]
    s_up[1], s_down[1], even, readout_kernel = tie(s_up[1], s_down[1], even, readout_kernel)
    for step in range(2, steps):
        s_up.append(ring_send(s_up[-1], 1))
        s_down.append(ring_send(s_down[-1], -1))
        if step == 2:
            halo, s_up[2], s_down[2] = tie(halo, s_up[2], s_down[2])
            r_down = [readout_kernel, ring_send(readout_kernel, -1)]
            patches = take_patches(facts, halo, even)
            patches = order_rows(facts, patches, swap_cores(patches), unit)
    held = tie(s_up[-1], s_down[-1], token_cotangent, readout_kernel)
    s_up[-1], s_down[-1], token_cotangent, readout_kernel = held
    back = chips_exchange(token_cotangent)
    back = (back, swap_cores(back))
    s_last = ring_send(s_up[-1], 1)
    r_up = [readout_kernel, ring_send(readout_kernel, 1)]
    samplers = [flat_sampler] + [block for pair in zip(s_up[1:], s_down[1:]) for block in pair]
    offsets = ring_offsets(chips)
    count = 2 * steps - 3
    first_pre = tp_terms(block_products(pre_kernel, (patches,), samplers[:count]))
    r_down[1], s_last, *first_pre = tie(r_down[1], s_last, *first_pre)
    first_slope, first_act = act_and_slope(facts, first_pre, offsets[:count], chips, (), unit)
    last_pre = block_products(pre_kernel, (patches,), [*samplers[count:], s_last])
    last_slope, act = act_and_slope(
        facts, tp_terms(last_pre), offsets[count:], chips, (first_act,), unit
    )
    slopes = first_slope, last_slope
    r_up[1], act = tie(r_up[1], chips_exchange(act))
    for step in range(1, steps - 2):
        r_down.append(ring_send(r_down[-1], -1))
        r_up.append(ring_send(r_up[-1], 1))
    r_down.append(ring_send(r_down[-1], -1))
    early = r_down[: steps - 1]
    sums = block_products(back_kernel, back, early)
    r_up[-1], *terms = tie(r_up[-1], *tp_terms(sums))
    r_up.append(ring_send(r_up[-1], 1))
    halo_lanes, even_lanes = slice(0, 4 * chans), slice(4 * chans, 8 * chans)
    both = halo_lanes, even_lanes
    pieces = [(0, 2 * step) for step in range(steps - 1)]
    blocks = [flat_sampler] + s_down[1 : steps - 1]
    grads = add_gradients(facts, terms, slopes, pieces, blocks, (), unit, both, False)
    middle = r_up[1 : steps - 1] + [r_down[steps - 1]]
    r_down.append(ring_send(r_down[-1], -1))
    terms = tp_terms(block_products(back_kernel, back, middle))
    pieces = [(0, 2 * step - 1) for step in range(1, steps - 1)] + [(1, 1)]
    blocks = s_up[1 : steps - 1] + [s_down[steps - 1]]
    grads = add_gradients(facts, terms, slopes, pieces, blocks, grads, unit, both, False)

    late_up, late_down, *grads = tie(r_up[-1], r_down[-1], *grads)
    terms = tp_terms(block_products(back_kernel, back, [late_up, late_down]))
    pieces, blocks = [(1, 0), (1, 2)], [s_up[-1], s_last]
    halo_own, halo_mate = add_gradients(
        facts, terms, slopes, pieces, blocks, grads[:2], unit, (halo_lanes,), True
    )
    halo_mate, first_term = tie(halo_mate, terms[0])
    even_own, even_mate = add_gradients(
        facts, (first_term, terms[1]), slopes, pieces, blocks, grads[2:], unit, (even_lanes,), True
    )
    lead, facts_late = return_patches(facts, halo_own, swap_cores(halo_mate), chans, jnp.bfloat16)
    grad_odd = shifted(lead, "ctx", -1)
    grad_even, facts_late = return_patches(
        facts_late, even_own, swap_cores(even_mate), chans, jnp.float32
    )
    places = [*range(steps - 1), *range(-1, 1 - steps, -1), steps - 1, 1 - steps, steps]
    tokens = token_products(
        facts_late, act, places, chips, [*early, *middle, late_up, late_down], unit
    )
    grad_relaxed = sum_tp(excite_grad(grad_even, grad_odd, conv, excite, squeeze_out))
    llm_tokens = (tokens[0] + swap_cores(tokens[1]).astype(jnp.float32)).astype(jnp.bfloat16)
    grad_features = conv_backward(
        grad_even, grad_odd, conv, excite, squeezed, grad_relaxed, squeeze_in,
        dense_weights(facts_late, group_kernel), group_kernel.shape[1],
    )
    return (llm_tokens, grad_features)


def solution(mesh):
    placed = (
        P("ctx", None, "tp"),
        P(None, "tp", None),
        P("tp", None),
        P(None, "tp"),
        P("ctx", None, "tp"),
        P("ctx", "tp"),
        P(),
        P(),
        P("ctx", "tp"),
    )
    return jax.shard_map(
        per_device,
        mesh=mesh,
        in_specs=placed,
        out_specs=(P("ctx", "tp"), P("ctx", None, "tp")),
        check_vma=False,
    )
```

```python
import functools

import jax
import jax.numpy as jnp
from jax import lax
from jax.experimental import pallas as pl
from jax.experimental.pallas import tpu as pltpu
from jax.sharding import PartitionSpec as P

SIDE = 14
OUT_SIDE = 8
WIDE = 16
FRAME_ROWS = WIDE * WIDE
EDGE = 8
LANES = 128
WINDOW = 256
VMEM_BYTES = 16 * 2**20
FREE = pl.CostEstimate(flops=0, bytes_accessed=0, transcendentals=0)


def whole_call(kernel, outs, scratch, cost=FREE):
    return pl.pallas_call(
        kernel,
        out_shape=outs,
        scratch_shapes=scratch,
        compiler_params=pltpu.CompilerParams(vmem_limit_bytes=VMEM_BYTES),
        cost_estimate=cost,
    )


def contract_last(left, right):
    return lax.dot_general(
        left, right, (((1,), (1,)), ((), ())), preferred_element_type=jnp.float32
    )


def contract_exact(left, right):
    return lax.dot_general(
        left,
        right,
        (((1,), (1,)), ((), ())),
        precision=lax.Precision.HIGHEST,
        preferred_element_type=jnp.float32,
    )


def silu_slope(values):
    sigma = jax.nn.sigmoid(values)
    return sigma * (1.0 + values * (1.0 - sigma))


def inside(rows):
    row = lax.broadcasted_iota(jnp.int32, (rows, 1), 0)
    across, down = row & (WIDE - 1), (row // WIDE) & (WIDE - 1)
    good = (across >= 1) & (across <= SIDE) & (down >= 1) & (down <= SIDE)
    return good.astype(jnp.float32)


def channel_blocks(chans, width):
    span = 4 * width
    blocks = []
    for low in range(0, chans, span):
        high = min(chans, low + span)
        blocks.append((low, high, low // LANES * LANES, min(chans, -(-high // LANES) * LANES)))
    return blocks


def block_tools(block, width):
    low, high, start, end = block
    size = end - start
    out_row = lax.broadcasted_iota(jnp.int32, (size, width), 0) + start
    within = lax.broadcasted_iota(jnp.int32, (size, width), 1)
    lane = lax.broadcasted_iota(jnp.int32, (size, size), 1) + start
    row = lax.broadcasted_iota(jnp.int32, (size, size), 0) + start
    spread = jnp.zeros((size, width), jnp.float32)
    same = jnp.zeros((size, size), jnp.float32)
    for first in range(low, high, width):
        spread += (out_row == within + first).astype(jnp.float32)
        in_lane = (lane >= first) & (lane < first + width)
        in_row = (row >= first) & (row < first + width)
        same += (in_lane & in_row).astype(jnp.float32)
    return spread.astype(jnp.bfloat16), same


def dense_tap(group_ref, tap, block, spread, same):
    _, _, start, end = block
    full = jnp.dot(spread, group_ref[tap, :, start:end], preferred_element_type=jnp.float32)
    return (full * same).astype(jnp.bfloat16)


def store_shifts(wide_ref, shift_ref, sign):
    rows = shift_ref.shape[1]
    for col in range(3):
        at = EDGE + sign * (col - 1)
        chans = wide_ref.shape[1]
        shift_ref[col, :, 0:chans] = wide_ref[at : at + rows, :].astype(jnp.bfloat16)
        if shift_ref.shape[2] > chans:
            blank = jnp.zeros((rows, shift_ref.shape[2] - chans), jnp.bfloat16)
            shift_ref[col, :, chans:] = blank


def conv_kernel(feat_ref, group_ref, squeeze_ref, *refs):
    conv_ref, pad_ref, sq_ref, flat_ref, wide_ref, shift_ref = refs
    frames, _, chans = feat_ref.shape
    width = group_ref.shape[1]
    rows = frames * FRAME_ROWS
    wide_ref[...] = jnp.zeros_like(wide_ref)
    for frame in range(frames):
        flat_ref[...] = feat_ref[frame].astype(jnp.float32)
        for y in range(SIDE):
            at = EDGE + frame * FRAME_ROWS + (y + 1) * WIDE + 1
            wide_ref[at : at + SIDE, :] = flat_ref[y * SIDE : (y + 1) * SIDE, :]
    store_shifts(wide_ref, shift_ref, 1)
    pad_ref[...] = shift_ref[1]
    conv_ref[...] = jnp.zeros_like(conv_ref)
    body = rows - 2 * WIDE
    for block in channel_blocks(chans, width):
        _, _, start, end = block
        spread, same = block_tools(block, width)
        total = jnp.zeros((body, end - start), jnp.float32)
        for tap in range(9):
            down, across = divmod(tap, 3)
            weights = dense_tap(group_ref, tap, block, spread, same)
            source = shift_ref[across, down * WIDE : down * WIDE + body, start:end]
            total += contract_last(source, weights)
        conv_ref[WIDE : WIDE + body, start:end] += total
    conv = conv_ref[...] * inside(rows)
    conv_ref[...] = conv
    active = conv * jax.nn.sigmoid(conv)
    pooled = jnp.concatenate(
        [
            jnp.sum(active[f * FRAME_ROWS : (f + 1) * FRAME_ROWS], axis=0, keepdims=True)
            for f in range(frames)
        ],
        axis=0,
    ) * (1.0 / (SIDE * SIDE))
    sq_ref[...] = contract_exact(pooled, squeeze_ref[...].astype(jnp.float32))


def hidden_kernel(conv_ref, pad_ref, sq_ref, expand_ref, even_ref, odd_ref, excite_ref):
    squeezed = sq_ref[...]
    relaxed = squeezed * jax.nn.sigmoid(squeezed)
    excite = jax.nn.sigmoid(
        jnp.dot(relaxed, expand_ref[...].astype(jnp.float32), precision=lax.Precision.HIGHEST)
    )
    excite_ref[...] = excite
    for frame, out_ref in enumerate((even_ref, odd_ref)):
        rows = slice(frame * FRAME_ROWS, (frame + 1) * FRAME_ROWS)
        conv = conv_ref[rows, :]
        active = conv * jax.nn.sigmoid(conv)
        hidden = pad_ref[rows, :].astype(jnp.float32) + active * excite[frame : frame + 1]
        out_ref[...] = hidden.astype(jnp.bfloat16)


def select_rows(to_patches):
    shape = (FRAME_ROWS, FRAME_ROWS)
    out_row = lax.broadcasted_iota(jnp.int32, shape, 0)
    in_row = lax.broadcasted_iota(jnp.int32, shape, 1)
    patch_row, frame_row = (out_row, in_row) if to_patches else (in_row, out_row)
    down, across = patch_row >> 7, (patch_row >> 6) & 1
    a, b = (patch_row >> 3) & 7, patch_row & 7
    return ((2 * a + down) * WIDE + 2 * b + across == frame_row).astype(jnp.float32)


def facts_kernel(clip_ref, keep_ref, out_ref):
    shard = lax.axis_index("ctx")
    frames = clip_ref.shape[0]
    out_ref[0] = shard % 2
    for block in range(2):
        pair = shard // 2 * 2 + block
        clip = clip_ref[2 * pair]
        start = jnp.int32(0)
        for other in range(0, frames, 2):
            start += jnp.where(clip_ref[other] < clip, 1, 0)
        out_ref[1 + block] = keep_ref[clip] - (pair - start) * (OUT_SIDE * OUT_SIDE)
    before = clip_ref[jnp.maximum(2 * shard - 1, 0)]
    chip, chips = shard // 2, lax.axis_size("ctx") // 2
    out_ref[4] = jnp.where(chip % 2 == 0, chip // 2, chips - 1 - chip // 2)
    out_ref[3] = jnp.where((shard > 0) & (before == clip_ref[2 * shard]), 1, 0)


def token_place(row, core, unit):
    per_block = OUT_SIDE * OUT_SIDE
    within = row % per_block
    block = (within // unit) % 2
    target_core = jnp.where(row < per_block, core, 1 - core)
    return block, unit * (2 * (within // (2 * unit)) + target_core) + within % unit


def reorder_matrix(core, unit, to_sent):
    shape = (2 * OUT_SIDE * OUT_SIDE,) * 2
    out_row = lax.broadcasted_iota(jnp.int32, shape, 0)
    in_row = lax.broadcasted_iota(jnp.int32, shape, 1)
    sent, natural = (out_row, in_row) if to_sent else (in_row, out_row)
    block, token = token_place(sent, core, unit)
    source = jnp.where(block == core, 0, OUT_SIDE * OUT_SIDE) + token
    return (source == natural).astype(jnp.bfloat16)


def order_kernel(unit, facts_ref, own_ref, mate_ref, out_ref):
    rows = jnp.concatenate([own_ref[...], mate_ref[...]], axis=0)
    matrix = reorder_matrix(facts_ref[0], unit, True)
    out_ref[...] = jnp.dot(matrix, rows, preferred_element_type=jnp.float32).astype(jnp.bfloat16)


def patch_kernel(facts_ref, halo_ref, even_ref, out_ref):
    chans = halo_ref.shape[1]
    per_frame = OUT_SIDE * OUT_SIDE
    select = select_rows(True).astype(jnp.bfloat16)
    for frame, source in enumerate((halo_ref, even_ref)):
        rows = jnp.dot(select, source[...], preferred_element_type=jnp.float32)
        if frame == 0:
            rows = rows * facts_ref[3].astype(jnp.float32)
        rows = rows.astype(jnp.bfloat16)
        for tap in range(4):
            at = (frame * 4 + tap) * chans
            out_ref[:, at : at + chans] = rows[tap * per_frame : (tap + 1) * per_frame]


def unpatch_kernel(facts_ref, own_ref, mate_ref, out_ref, facts_out_ref):
    for place in range(facts_ref.shape[0]):
        facts_out_ref[place] = facts_ref[place]
    chans = out_ref.shape[1]
    rows = own_ref[...] + mate_ref[...].astype(jnp.float32)
    pieces = [rows[:, tap * chans : (tap + 1) * chans] for tap in range(4)]
    rows = jnp.concatenate(pieces, axis=0)
    select = select_rows(False).astype(jnp.bfloat16)
    coarse = rows.astype(jnp.bfloat16)
    frame = jnp.dot(select, coarse, preferred_element_type=jnp.float32)
    if out_ref.dtype == jnp.bfloat16:
        frame = frame * facts_ref[3].astype(jnp.float32)
    else:
        rest = (rows - coarse.astype(jnp.float32)).astype(jnp.bfloat16)
        frame += jnp.dot(select, rest, preferred_element_type=jnp.float32)
    out_ref[...] = (frame * inside(FRAME_ROWS)).astype(out_ref.dtype)


def excite_grad_kernel(even_ref, odd_ref, conv_ref, excite_ref, expand_ref, out_ref):
    sums = []
    for frame, grad_ref in enumerate((even_ref, odd_ref)):
        conv = conv_ref[frame * FRAME_ROWS : (frame + 1) * FRAME_ROWS, :]
        active = conv * jax.nn.sigmoid(conv)
        sums.append(jnp.sum(grad_ref[...].astype(jnp.float32) * active, axis=0, keepdims=True))
    excite = excite_ref[...]
    inner = jnp.concatenate(sums, axis=0) * excite * (1.0 - excite)
    out_ref[...] = contract_exact(inner, expand_ref[...].astype(jnp.float32))


def conv_grad_kernel(
    width, even_ref, odd_ref, conv_ref, excite_ref, sq_ref, relaxed_ref, squeeze_ref, *refs
):
    *dense_refs, out_ref, flat_ref, wide_ref, shift_ref, grad_ref = refs
    frames, _, chans = out_ref.shape
    rows = frames * FRAME_ROWS
    grad_squeezed = relaxed_ref[...] * silu_slope(sq_ref[...])
    pooled = jnp.dot(
        grad_squeezed, squeeze_ref[...].astype(jnp.float32), precision=lax.Precision.HIGHEST
    ) * (1.0 / (SIDE * SIDE))
    wide_ref[0:EDGE, :] = jnp.zeros((EDGE, chans), jnp.float32)
    wide_ref[EDGE + rows :, :] = jnp.zeros((EDGE, chans), jnp.float32)
    good = inside(FRAME_ROWS)
    for frame, source in enumerate((even_ref, odd_ref)):
        at = frame * FRAME_ROWS
        grad = source[...].astype(jnp.float32)
        grad_ref[at : at + FRAME_ROWS, :] = grad
        active = grad * excite_ref[frame : frame + 1, :] + pooled[frame : frame + 1]
        slope = silu_slope(conv_ref[at : at + FRAME_ROWS, :])
        wide_ref[EDGE + at : EDGE + at + FRAME_ROWS, :] = active * slope * good
    store_shifts(wide_ref, shift_ref, -1)
    body = rows - 2 * WIDE
    for block, dense_ref in zip(channel_blocks(chans, width), dense_refs):
        start = block[2]
        sources = []
        for tap in range(9):
            down, across = divmod(tap, 3)
            at = (2 - down) * WIDE
            sources.append(shift_ref[across, at : at + body, start : start + WINDOW])
        total = jnp.dot(
            jnp.concatenate(sources, axis=1), dense_ref[...], preferred_element_type=jnp.float32
        )
        end = min(chans, start + WINDOW)
        grad_ref[WIDE : WIDE + body, start:end] += total[:, : end - start]
    for frame in range(frames):
        for y in range(SIDE):
            at = frame * FRAME_ROWS + (y + 1) * WIDE + 1
            flat_ref[y * SIDE : (y + 1) * SIDE, :] = grad_ref[at : at + SIDE, :]
        out_ref[frame] = flat_ref[...].astype(jnp.bfloat16)


def f32(*shape):
    return jax.ShapeDtypeStruct(shape, jnp.float32)


def bf16(*shape):
    return jax.ShapeDtypeStruct(shape, jnp.bfloat16)


def conv_forward(features, group_kernel, squeeze_in):
    frames, cells, chans = features.shape
    rows = frames * FRAME_ROWS
    return whole_call(
        conv_kernel,
        (f32(rows, chans), bf16(rows, chans), f32(frames, squeeze_in.shape[0])),
        [
            pltpu.VMEM((cells, chans), jnp.float32),
            pltpu.VMEM((rows + 2 * EDGE, chans), jnp.float32),
            pltpu.VMEM((3, rows, chans), jnp.bfloat16),
        ],
    )(features, group_kernel, squeeze_in)


def hidden_frames(conv, padded, squeezed, squeeze_out):
    rows, chans = conv.shape
    return whole_call(
        hidden_kernel,
        (bf16(FRAME_ROWS, chans), bf16(FRAME_ROWS, chans), f32(rows // FRAME_ROWS, chans)),
        [],
    )(conv, padded, squeezed, squeeze_out)


def vmem_specs(count):
    return [pl.BlockSpec(memory_space=pltpu.SMEM)] + [pl.BlockSpec(memory_space=pltpu.VMEM)] * count


def facts_of(frame_clip, clip_keep):
    smem = pl.BlockSpec(memory_space=pltpu.SMEM)
    return pl.pallas_call(
        facts_kernel,
        out_shape=jax.ShapeDtypeStruct((5,), jnp.int32),
        in_specs=[smem, smem],
        out_specs=smem,
        cost_estimate=FREE,
    )(frame_clip, clip_keep)


def order_rows(facts, own, mate, unit):
    rows, columns = own.shape
    return pl.pallas_call(
        functools.partial(order_kernel, unit),
        out_shape=bf16(2 * rows, columns),
        in_specs=vmem_specs(2),
        compiler_params=pltpu.CompilerParams(vmem_limit_bytes=VMEM_BYTES),
        cost_estimate=FREE,
    )(facts, own, mate)


def take_patches(facts, halo, even):
    chans = even.shape[1]
    return pl.pallas_call(
        patch_kernel,
        out_shape=bf16(OUT_SIDE * OUT_SIDE, 8 * chans),
        in_specs=vmem_specs(2),
        compiler_params=pltpu.CompilerParams(vmem_limit_bytes=VMEM_BYTES),
        cost_estimate=FREE,
    )(facts, halo, even)


def return_patches(facts, own, mate, chans, dtype):
    return pl.pallas_call(
        unpatch_kernel,
        out_shape=(
            jax.ShapeDtypeStruct((FRAME_ROWS, chans), dtype),
            jax.ShapeDtypeStruct(facts.shape, jnp.int32),
        ),
        in_specs=vmem_specs(2),
        out_specs=vmem_specs(1)[::-1],
        compiler_params=pltpu.CompilerParams(vmem_limit_bytes=VMEM_BYTES),
        cost_estimate=FREE,
    )(facts, own, mate)


def excite_grad(even, odd, conv, excite, squeeze_out):
    rows, chans = conv.shape
    return whole_call(
        excite_grad_kernel,
        f32(rows // FRAME_ROWS, squeeze_out.shape[0]),
        [],
    )(even, odd, conv, excite, squeeze_out)


def conv_backward(even, odd, conv, excite, squeezed, grad_relaxed, squeeze_in, dense, width):
    rows, chans = conv.shape
    frames = rows // FRAME_ROWS
    lanes = channel_blocks(chans, width)[-1][2] + WINDOW
    return whole_call(
        functools.partial(conv_grad_kernel, width),
        bf16(frames, SIDE * SIDE, chans),
        [
            pltpu.VMEM((SIDE * SIDE, chans), jnp.float32),
            pltpu.VMEM((rows + 2 * EDGE, chans), jnp.float32),
            pltpu.VMEM((3, rows, lanes), jnp.bfloat16),
            pltpu.VMEM((rows, chans), jnp.float32),
        ],
        pl.CostEstimate(flops=rows * chans * 9216, bytes_accessed=16 * rows * chans, transcendentals=0),
    )(even, odd, conv, excite, squeezed, grad_relaxed, squeeze_in, *dense)


def dense_kernel(facts_ref, group_ref, *dense_refs):
    _, width, chans = group_ref.shape
    for block, dense_ref in zip(channel_blocks(chans, width), dense_refs):
        low, high, start, _ = block
        end = min(chans, start + WINDOW)
        spread, same = block_tools((low, high, start, start + WINDOW), width)
        dense_ref[...] = jnp.zeros_like(dense_ref)
        for tap in range(9):
            full = jnp.dot(spread, group_ref[tap, :, start:end], preferred_element_type=jnp.float32)
            rows = slice(tap * WINDOW, (tap + 1) * WINDOW)
            dense_ref[rows, 0 : end - start] = (full * same[:, : end - start]).astype(jnp.bfloat16)


def dense_weights(facts, group_kernel):
    _, width, chans = group_kernel.shape
    outs = (bf16(9 * WINDOW, WINDOW),) * len(channel_blocks(chans, width))
    return facts_call(dense_kernel, outs, facts, (group_kernel,))


def shifted(value, axis, by):
    count = lax.axis_size(axis)
    pairs = [(i, i + by) for i in range(count) if 0 <= i + by < count]
    return lax.ppermute(value, axis, pairs)


def ring_order(chips):
    return list(range(0, chips, 2)) + list(range(1, chips, 2))[::-1]


def ring_pairs(count, by):
    order = ring_order(count // 2)
    pairs = []
    for place, chip in enumerate(order):
        target = order[(place + by) % len(order)]
        pairs += [(2 * chip, 2 * target), (2 * chip + 1, 2 * target + 1)]
    return pairs


def swap_cores(value):
    return lax.ppermute(value, "ctx", [(i, i ^ 1) for i in range(lax.axis_size("ctx"))])


def tp_terms(value):
    size = lax.axis_size("tp")
    reach, other = 1, None
    while reach < size:
        value = value if other is None else value + other
        other = lax.ppermute(value, "tp", [(i, i ^ reach) for i in range(size)])
        reach *= 2
    return value, jnp.zeros_like(value) if other is None else other


def sum_tp(value):
    value, other = tp_terms(value)
    return value + other


def ring_send(value, by):
    return lax.ppermute(value, "ctx", ring_pairs(lax.axis_size("ctx"), by))


def tie(*values):
    return lax.optimization_barrier(values)


def stacked_contract(left, blocks):
    blocks = [ref[...] for ref in blocks]
    if blocks[0].shape[0] % 8 == 0:
        blocks = [jnp.concatenate(blocks, axis=0)]
    return jnp.concatenate([contract_last(left, block) for block in blocks], axis=1)


def pre_kernel(patch_ref, *refs):
    *blocks, out_ref = refs
    out_ref[...] = stacked_contract(patch_ref[...], blocks)


def back_kernel(keep_ref, send_ref, *refs):
    *blocks, out_ref = refs
    back = jnp.concatenate([keep_ref[...], send_ref[...]], axis=0)
    out_ref[...] = stacked_contract(back, blocks)


def live_rows(facts_ref, rows, unit):
    block, token = token_place(
        lax.broadcasted_iota(jnp.int32, (rows, 1), 0), facts_ref[0], unit
    )
    return (token < jnp.where(block == 0, facts_ref[1], facts_ref[2])).astype(jnp.float32)


def stacked_dot(pieces, blocks):
    if blocks[0].shape[0] % 8 == 0:
        pieces = [jnp.concatenate(pieces, axis=1)]
        blocks = [jnp.concatenate(blocks, axis=0)]
    total = 0.0
    for piece, block in zip(pieces, blocks):
        total += jnp.dot(piece, block, preferred_element_type=jnp.float32)
    return total


def totals_kernel(pieces, unit, parts, first, facts_ref, *refs):
    grad_act = refs[0][...] + refs[1][...]
    count = len(pieces)
    slopes, blocks = refs[2:4], refs[4 : 4 + count]
    before, after = refs[4 + count : -2 * len(parts)], refs[-2 * len(parts) :]
    rows, width = grad_act.shape[0], blocks[0].shape[0]
    slope = jnp.concatenate(
        [slopes[source][:, index * width : (index + 1) * width] for source, index in pieces], axis=1
    )
    factor = jnp.dot(
        reorder_matrix(facts_ref[0], unit, False),
        (grad_act * slope).astype(jnp.bfloat16),
        preferred_element_type=jnp.float32,
    ).astype(jnp.bfloat16)
    factors = [factor[:, place * width : (place + 1) * width] for place in range(count)]
    for part, lanes in enumerate(parts):
        total = stacked_dot(factors, [ref[:, lanes] for ref in blocks])
        for half in range(2):
            value = total[half * rows // 2 : (half + 1) * rows // 2]
            value = value if first else before[2 * part + half][...] + value
            ref = after[2 * part + half]
            ref[...] = value.astype(ref.dtype)


def ring_offsets(chips):
    offsets = [0]
    for step in range(1, chips // 2):
        offsets += [-step, step]
    return offsets + [chips // 2]


def block_columns(facts_ref, offset, chips, width):
    shape = (width, chips * width)
    place = (facts_ref[4] + offset + chips) % chips
    column = lax.broadcasted_iota(jnp.int32, shape, 1)
    return (column == lax.broadcasted_iota(jnp.int32, shape, 0) + place * width).astype(jnp.bfloat16)


def exchange_matrix(core, unit, to_sent):
    per_block = OUT_SIDE * OUT_SIDE
    shape = (2 * per_block,) * 2
    out_row = lax.broadcasted_iota(jnp.int32, shape, 0)
    in_row = lax.broadcasted_iota(jnp.int32, shape, 1)
    sent, kept = (out_row, in_row) if to_sent else (in_row, out_row)
    target_core = (sent // (2 * unit)) % 2
    within = sent // (4 * unit) * (2 * unit) + sent % (2 * unit)
    return (within + jnp.where(target_core == core, 0, per_block) == kept).astype(jnp.bfloat16)


def act_kernel(offsets, chips, unit, last, facts_ref, own_ref, other_ref, *refs):
    *before, slope_ref, out_ref = refs
    pre = own_ref[...] + other_ref[...]
    width = pre.shape[1] // len(offsets)
    live = live_rows(facts_ref, pre.shape[0], unit)
    sigma = jax.nn.sigmoid(pre)
    slope_ref[...] = sigma * (1.0 + pre * (1.0 - sigma)) * live
    act = (pre * sigma * live).astype(jnp.bfloat16)
    total = before[0][...].astype(jnp.float32) if last else 0.0
    for place, offset in enumerate(offsets):
        columns = block_columns(facts_ref, offset, chips, width)
        piece = act[:, place * width : (place + 1) * width]
        total += jnp.dot(piece, columns, preferred_element_type=jnp.float32)
    total = total.astype(jnp.bfloat16)
    if last:
        matrix = exchange_matrix(facts_ref[0], unit, True)
        total = jnp.dot(matrix, total, preferred_element_type=jnp.float32).astype(jnp.bfloat16)
    out_ref[...] = total


def token_kernel(offsets, chips, unit, facts_ref, act_ref, *refs):
    count = len(offsets)
    blocks, refs = refs[:count], refs[count:]
    keep_ref, send_ref, *buffers, sems = refs
    copies = [
        pltpu.make_async_copy(ref, buffer, sems.at[place])
        for place, (ref, buffer) in enumerate(zip(blocks, buffers))
    ]
    for copy in copies:
        copy.start()
    width = buffers[0].shape[0]
    matrix = exchange_matrix(facts_ref[0], unit, False)
    act = jnp.dot(matrix, act_ref[...], preferred_element_type=jnp.float32).astype(jnp.bfloat16)
    pieces = [
        contract_last(act, block_columns(facts_ref, offset, chips, width)).astype(jnp.bfloat16)
        for offset in offsets
    ]
    for copy in copies:
        copy.wait()
    total = stacked_dot(pieces, [buffer[...] for buffer in buffers])
    rows = keep_ref.shape[0]
    keep_ref[...] = total[:rows]
    send_ref[...] = total[rows:].astype(jnp.bfloat16)


def block_products(kernel, left, blocks):
    rows = 2 * OUT_SIDE * OUT_SIDE
    return whole_call(kernel, f32(rows, len(blocks) * blocks[0].shape[0]), [])(*left, *blocks)


def facts_call(kernel, outs, facts, operands, cost=FREE):
    return pl.pallas_call(
        kernel,
        out_shape=outs,
        in_specs=vmem_specs(len(operands)),
        compiler_params=pltpu.CompilerParams(vmem_limit_bytes=VMEM_BYTES),
        cost_estimate=cost,
    )(facts, *operands)


def add_gradients(facts, terms, slopes, pieces, blocks, before, unit, parts, last):
    rows = terms[0].shape[0] // 2
    kernel = functools.partial(totals_kernel, pieces, unit, parts, not before)
    outs = ()
    for lanes in parts:
        shape = rows, lanes.stop - lanes.start
        outs += f32(*shape), (bf16 if last else f32)(*shape)
    return tuple(facts_call(kernel, outs, facts, (*terms, *slopes, *blocks, *before)))


def act_and_slope(facts, terms, offsets, chips, before, unit):
    rows, columns = terms[0].shape
    kernel = functools.partial(act_kernel, offsets, chips, unit, bool(before))
    outs = f32(rows, columns), bf16(rows, columns // len(offsets) * chips)
    return facts_call(kernel, outs, facts, (*terms, *before))


def token_products(facts, act, offsets, chips, blocks, unit):
    rows, columns = act.shape[0] // 2, blocks[0].shape[1]
    return pl.pallas_call(
        functools.partial(token_kernel, offsets, chips, unit),
        out_shape=(f32(rows, columns), bf16(rows, columns)),
        in_specs=vmem_specs(1) + [pl.BlockSpec(memory_space=pl.ANY)] * len(blocks),
        scratch_shapes=[pltpu.VMEM(block.shape, block.dtype) for block in blocks]
        + [pltpu.SemaphoreType.DMA((len(blocks),))],
        compiler_params=pltpu.CompilerParams(vmem_limit_bytes=VMEM_BYTES),
        cost_estimate=FREE,
    )(facts, act, *blocks)


def chips_exchange(value):
    count = lax.axis_size("ctx")
    groups = [list(range(core, count, 2)) for core in range(2)]
    return lax.all_to_all(
        value, "ctx", split_axis=0, concat_axis=0, tiled=True, axis_index_groups=groups
    )


def per_device(
    features,
    group_kernel,
    squeeze_in,
    squeeze_out,
    sampler_kernel,
    readout_kernel,
    frame_clip,
    clip_keep,
    token_cotangent,
):
    chans = features.shape[2]
    count = lax.axis_size("ctx")
    steps, unit = count // 4, OUT_SIDE * OUT_SIDE // count
    flat_sampler = sampler_kernel.reshape(sampler_kernel.shape[0], 8 * chans)
    chips = count // 2
    s_up, s_down = ring_send(flat_sampler, 1), ring_send(flat_sampler, -1)
    group_kernel = jnp.swapaxes(group_kernel, 1, 2)
    squeeze_in = squeeze_in.T
    facts = facts_of(frame_clip, clip_keep)

    conv, padded, squeezed = conv_forward(features, group_kernel, squeeze_in)
    squeezed = sum_tp(squeezed)
    even, odd, excite = hidden_frames(conv, padded, squeezed, squeeze_out)
    halo = shifted(odd, "ctx", 1)

    s_up, s_down = [flat_sampler, s_up], [flat_sampler, s_down]
    s_up[1], s_down[1], even, readout_kernel = tie(s_up[1], s_down[1], even, readout_kernel)
    for step in range(2, steps):
        s_up.append(ring_send(s_up[-1], 1))
        s_down.append(ring_send(s_down[-1], -1))
        if step == 2:
            halo, s_up[2], s_down[2] = tie(halo, s_up[2], s_down[2])
            r_down = [readout_kernel, ring_send(readout_kernel, -1)]
            patches = take_patches(facts, halo, even)
            patches = order_rows(facts, patches, swap_cores(patches), unit)
    held = tie(s_up[-1], s_down[-1], token_cotangent, readout_kernel)
    s_up[-1], s_down[-1], token_cotangent, readout_kernel = held
    back = chips_exchange(token_cotangent)
    back = (back, swap_cores(back))
    s_last = ring_send(s_up[-1], 1)
    r_up = [readout_kernel, ring_send(readout_kernel, 1)]
    samplers = [flat_sampler] + [block for pair in zip(s_up[1:], s_down[1:]) for block in pair]
    offsets = ring_offsets(chips)
    count = 2 * steps - 1
    first_pre = tp_terms(block_products(pre_kernel, (patches,), samplers[:count]))
    r_down[1], s_last, *first_pre = tie(r_down[1], s_last, *first_pre)
    first_slope, first_act = act_and_slope(facts, first_pre, offsets[:count], chips, (), unit)
    last_pre = block_products(pre_kernel, (patches,), [*samplers[count:], s_last])
    last_slope, act = act_and_slope(
        facts, tp_terms(last_pre), offsets[count:], chips, (first_act,), unit
    )
    slopes = first_slope, last_slope
    r_up[1], act = tie(r_up[1], chips_exchange(act))
    for step in range(1, steps - 2):
        r_down.append(ring_send(r_down[-1], -1))
        r_up.append(ring_send(r_up[-1], 1))
    r_down.append(ring_send(r_down[-1], -1))
    early = r_down[: steps - 1]
    sums = block_products(back_kernel, back, early)
    r_up[-1], *terms = tie(r_up[-1], *tp_terms(sums))
    r_up.append(ring_send(r_up[-1], 1))
    halo_lanes, even_lanes = slice(0, 4 * chans), slice(4 * chans, 8 * chans)
    both = halo_lanes, even_lanes
    pieces = [(0, 2 * step) for step in range(steps - 1)]
    blocks = [flat_sampler] + s_down[1 : steps - 1]
    grads = add_gradients(facts, terms, slopes, pieces, blocks, (), unit, both, False)
    middle = r_up[1 : steps - 1] + [r_down[steps - 1]]
    r_down.append(ring_send(r_down[-1], -1))
    terms = tp_terms(block_products(back_kernel, back, middle))
    pieces = [(0, 2 * step - 1) for step in range(1, steps - 1)] + [(0, 2 * steps - 2)]
    blocks = s_up[1 : steps - 1] + [s_down[steps - 1]]
    grads = add_gradients(facts, terms, slopes, pieces, blocks, grads, unit, both, False)

    late_up, late_down, *grads = tie(r_up[-1], r_down[-1], *grads)
    terms = tp_terms(block_products(back_kernel, back, [late_up, late_down]))
    pieces, blocks = [(0, 2 * steps - 3), (1, 0)], [s_up[-1], s_last]
    halo_own, halo_mate = add_gradients(
        facts, terms, slopes, pieces, blocks, grads[:2], unit, (halo_lanes,), True
    )
    halo_mate, first_term = tie(halo_mate, terms[0])
    even_own, even_mate = add_gradients(
        facts, (first_term, terms[1]), slopes, pieces, blocks, grads[2:], unit, (even_lanes,), True
    )
    lead, facts_late = return_patches(facts, halo_own, swap_cores(halo_mate), chans, jnp.bfloat16)
    grad_odd = shifted(lead, "ctx", -1)
    grad_even, facts_late = return_patches(
        facts_late, even_own, swap_cores(even_mate), chans, jnp.float32
    )
    places = [*range(steps - 1), *range(-1, 1 - steps, -1), steps - 1, 1 - steps, steps]
    tokens = token_products(
        facts_late, act, places, chips, [*early, *middle, late_up, late_down], unit
    )
    grad_relaxed = sum_tp(excite_grad(grad_even, grad_odd, conv, excite, squeeze_out))
    llm_tokens = (tokens[0] + swap_cores(tokens[1]).astype(jnp.float32)).astype(jnp.bfloat16)
    grad_features = conv_backward(
        grad_even, grad_odd, conv, excite, squeezed, grad_relaxed, squeeze_in,
        dense_weights(facts_late, group_kernel), group_kernel.shape[1],
    )
    return (llm_tokens, grad_features)


def solution(mesh):
    placed = (
        P("ctx", None, "tp"),
        P(None, "tp", None),
        P("tp", None),
        P(None, "tp"),
        P("ctx", None, "tp"),
        P("ctx", "tp"),
        P(),
        P(),
        P("ctx", "tp"),
    )
    return jax.shard_map(
        per_device,
        mesh=mesh,
        in_specs=placed,
        out_specs=(P("ctx", "tp"), P("ctx", None, "tp")),
        check_vma=False,
    )
```

```python
import functools

import jax
import jax.numpy as jnp
from jax import lax
from jax.experimental import pallas as pl
from jax.experimental.pallas import tpu as pltpu
from jax.sharding import PartitionSpec as P

SIDE = 14
OUT_SIDE = 8
WIDE = 16
FRAME_ROWS = WIDE * WIDE
EDGE = 8
LANES = 128
WINDOW = 256
VMEM_BYTES = 16 * 2**20
FREE = pl.CostEstimate(flops=0, bytes_accessed=0, transcendentals=0)


def whole_call(kernel, outs, scratch, cost=FREE):
    return pl.pallas_call(
        kernel,
        out_shape=outs,
        scratch_shapes=scratch,
        compiler_params=pltpu.CompilerParams(vmem_limit_bytes=VMEM_BYTES),
        cost_estimate=cost,
    )


def contract_last(left, right):
    return lax.dot_general(
        left, right, (((1,), (1,)), ((), ())), preferred_element_type=jnp.float32
    )


def contract_exact(left, right):
    return lax.dot_general(
        left,
        right,
        (((1,), (1,)), ((), ())),
        precision=lax.Precision.HIGHEST,
        preferred_element_type=jnp.float32,
    )


def silu_slope(values):
    sigma = jax.nn.sigmoid(values)
    return sigma * (1.0 + values * (1.0 - sigma))


def inside(rows):
    row = lax.broadcasted_iota(jnp.int32, (rows, 1), 0)
    across, down = row & (WIDE - 1), (row // WIDE) & (WIDE - 1)
    good = (across >= 1) & (across <= SIDE) & (down >= 1) & (down <= SIDE)
    return good.astype(jnp.float32)


def channel_blocks(chans, width):
    span = 4 * width
    blocks = []
    for low in range(0, chans, span):
        high = min(chans, low + span)
        blocks.append((low, high, low // LANES * LANES, min(chans, -(-high // LANES) * LANES)))
    return blocks


def block_tools(block, width):
    low, high, start, end = block
    size = end - start
    out_row = lax.broadcasted_iota(jnp.int32, (size, width), 0) + start
    within = lax.broadcasted_iota(jnp.int32, (size, width), 1)
    lane = lax.broadcasted_iota(jnp.int32, (size, size), 1) + start
    row = lax.broadcasted_iota(jnp.int32, (size, size), 0) + start
    spread = jnp.zeros((size, width), jnp.float32)
    same = jnp.zeros((size, size), jnp.float32)
    for first in range(low, high, width):
        spread += (out_row == within + first).astype(jnp.float32)
        in_lane = (lane >= first) & (lane < first + width)
        in_row = (row >= first) & (row < first + width)
        same += (in_lane & in_row).astype(jnp.float32)
    return spread.astype(jnp.bfloat16), same


def dense_tap(group_ref, tap, block, spread, same):
    _, _, start, end = block
    full = jnp.dot(spread, group_ref[tap, :, start:end], preferred_element_type=jnp.float32)
    return (full * same).astype(jnp.bfloat16)


def store_shifts(wide_ref, shift_ref, sign):
    rows = shift_ref.shape[1]
    for col in range(3):
        at = EDGE + sign * (col - 1)
        chans = wide_ref.shape[1]
        shift_ref[col, :, 0:chans] = wide_ref[at : at + rows, :].astype(jnp.bfloat16)
        if shift_ref.shape[2] > chans:
            blank = jnp.zeros((rows, shift_ref.shape[2] - chans), jnp.bfloat16)
            shift_ref[col, :, chans:] = blank


def conv_kernel(feat_ref, group_ref, squeeze_ref, *refs):
    conv_ref, pad_ref, sq_ref, flat_ref, wide_ref, shift_ref = refs
    frames, _, chans = feat_ref.shape
    width = group_ref.shape[1]
    rows = frames * FRAME_ROWS
    wide_ref[...] = jnp.zeros_like(wide_ref)
    for frame in range(frames):
        flat_ref[...] = feat_ref[frame].astype(jnp.float32)
        for y in range(SIDE):
            at = EDGE + frame * FRAME_ROWS + (y + 1) * WIDE + 1
            wide_ref[at : at + SIDE, :] = flat_ref[y * SIDE : (y + 1) * SIDE, :]
    store_shifts(wide_ref, shift_ref, 1)
    pad_ref[...] = shift_ref[1]
    conv_ref[...] = jnp.zeros_like(conv_ref)
    body = rows - 2 * WIDE
    for block in channel_blocks(chans, width):
        _, _, start, end = block
        spread, same = block_tools(block, width)
        total = jnp.zeros((body, end - start), jnp.float32)
        for tap in range(9):
            down, across = divmod(tap, 3)
            weights = dense_tap(group_ref, tap, block, spread, same)
            source = shift_ref[across, down * WIDE : down * WIDE + body, start:end]
            total += contract_last(source, weights)
        conv_ref[WIDE : WIDE + body, start:end] += total
    conv = conv_ref[...] * inside(rows)
    conv_ref[...] = conv
    active = conv * jax.nn.sigmoid(conv)
    pooled = jnp.concatenate(
        [
            jnp.sum(active[f * FRAME_ROWS : (f + 1) * FRAME_ROWS], axis=0, keepdims=True)
            for f in range(frames)
        ],
        axis=0,
    ) * (1.0 / (SIDE * SIDE))
    sq_ref[...] = contract_exact(pooled, squeeze_ref[...].astype(jnp.float32))


def hidden_kernel(conv_ref, pad_ref, sq_ref, expand_ref, even_ref, odd_ref, excite_ref):
    squeezed = sq_ref[...]
    relaxed = squeezed * jax.nn.sigmoid(squeezed)
    excite = jax.nn.sigmoid(
        jnp.dot(relaxed, expand_ref[...].astype(jnp.float32), precision=lax.Precision.HIGHEST)
    )
    excite_ref[...] = excite
    for frame, out_ref in enumerate((even_ref, odd_ref)):
        rows = slice(frame * FRAME_ROWS, (frame + 1) * FRAME_ROWS)
        conv = conv_ref[rows, :]
        active = conv * jax.nn.sigmoid(conv)
        hidden = pad_ref[rows, :].astype(jnp.float32) + active * excite[frame : frame + 1]
        out_ref[...] = hidden.astype(jnp.bfloat16)


def select_rows(to_patches):
    shape = (FRAME_ROWS, FRAME_ROWS)
    out_row = lax.broadcasted_iota(jnp.int32, shape, 0)
    in_row = lax.broadcasted_iota(jnp.int32, shape, 1)
    patch_row, frame_row = (out_row, in_row) if to_patches else (in_row, out_row)
    down, across = patch_row >> 7, (patch_row >> 6) & 1
    a, b = (patch_row >> 3) & 7, patch_row & 7
    return ((2 * a + down) * WIDE + 2 * b + across == frame_row).astype(jnp.float32)


def facts_kernel(clip_ref, keep_ref, out_ref):
    shard = lax.axis_index("ctx")
    frames = clip_ref.shape[0]
    out_ref[0] = shard % 2
    for block in range(2):
        pair = shard // 2 * 2 + block
        clip = clip_ref[2 * pair]
        start = jnp.int32(0)
        for other in range(0, frames, 2):
            start += jnp.where(clip_ref[other] < clip, 1, 0)
        out_ref[1 + block] = keep_ref[clip] - (pair - start) * (OUT_SIDE * OUT_SIDE)
    before = clip_ref[jnp.maximum(2 * shard - 1, 0)]
    chip, chips = shard // 2, lax.axis_size("ctx") // 2
    out_ref[4] = jnp.where(chip % 2 == 0, chip // 2, chips - 1 - chip // 2)
    out_ref[3] = jnp.where((shard > 0) & (before == clip_ref[2 * shard]), 1, 0)


def token_place(row, core, unit):
    per_block = OUT_SIDE * OUT_SIDE
    within = row % per_block
    block = (within // unit) % 2
    target_core = jnp.where(row < per_block, core, 1 - core)
    return block, unit * (2 * (within // (2 * unit)) + target_core) + within % unit


def reorder_matrix(core, unit, to_sent):
    shape = (2 * OUT_SIDE * OUT_SIDE,) * 2
    out_row = lax.broadcasted_iota(jnp.int32, shape, 0)
    in_row = lax.broadcasted_iota(jnp.int32, shape, 1)
    sent, natural = (out_row, in_row) if to_sent else (in_row, out_row)
    block, token = token_place(sent, core, unit)
    source = jnp.where(block == core, 0, OUT_SIDE * OUT_SIDE) + token
    return (source == natural).astype(jnp.bfloat16)


def order_kernel(unit, facts_ref, own_ref, mate_ref, out_ref):
    rows = jnp.concatenate([own_ref[...], mate_ref[...]], axis=0)
    matrix = reorder_matrix(facts_ref[0], unit, True)
    out_ref[...] = jnp.dot(matrix, rows, preferred_element_type=jnp.float32).astype(jnp.bfloat16)


def patch_kernel(facts_ref, halo_ref, even_ref, out_ref):
    chans = halo_ref.shape[1]
    per_frame = OUT_SIDE * OUT_SIDE
    select = select_rows(True).astype(jnp.bfloat16)
    for frame, source in enumerate((halo_ref, even_ref)):
        rows = jnp.dot(select, source[...], preferred_element_type=jnp.float32)
        if frame == 0:
            rows = rows * facts_ref[3].astype(jnp.float32)
        rows = rows.astype(jnp.bfloat16)
        for tap in range(4):
            at = (frame * 4 + tap) * chans
            out_ref[:, at : at + chans] = rows[tap * per_frame : (tap + 1) * per_frame]


def unpatch_kernel(facts_ref, own_ref, mate_ref, out_ref, facts_out_ref):
    for place in range(facts_ref.shape[0]):
        facts_out_ref[place] = facts_ref[place]
    chans = out_ref.shape[1]
    rows = own_ref[...] + mate_ref[...].astype(jnp.float32)
    pieces = [rows[:, tap * chans : (tap + 1) * chans] for tap in range(4)]
    rows = jnp.concatenate(pieces, axis=0)
    select = select_rows(False).astype(jnp.bfloat16)
    coarse = rows.astype(jnp.bfloat16)
    frame = jnp.dot(select, coarse, preferred_element_type=jnp.float32)
    if out_ref.dtype == jnp.bfloat16:
        frame = frame * facts_ref[3].astype(jnp.float32)
    else:
        rest = (rows - coarse.astype(jnp.float32)).astype(jnp.bfloat16)
        frame += jnp.dot(select, rest, preferred_element_type=jnp.float32)
    out_ref[...] = (frame * inside(FRAME_ROWS)).astype(out_ref.dtype)


def excite_grad_kernel(even_ref, odd_ref, conv_ref, excite_ref, expand_ref, out_ref):
    sums = []
    for frame, grad_ref in enumerate((even_ref, odd_ref)):
        conv = conv_ref[frame * FRAME_ROWS : (frame + 1) * FRAME_ROWS, :]
        active = conv * jax.nn.sigmoid(conv)
        sums.append(jnp.sum(grad_ref[...].astype(jnp.float32) * active, axis=0, keepdims=True))
    excite = excite_ref[...]
    inner = jnp.concatenate(sums, axis=0) * excite * (1.0 - excite)
    out_ref[...] = contract_exact(inner, expand_ref[...].astype(jnp.float32))


def conv_grad_kernel(
    width, even_ref, odd_ref, conv_ref, excite_ref, sq_ref, relaxed_ref, squeeze_ref, *refs
):
    *dense_refs, out_ref, flat_ref, wide_ref, shift_ref, grad_ref = refs
    _, frames, chans = out_ref.shape
    rows = frames * FRAME_ROWS
    grad_squeezed = relaxed_ref[...] * silu_slope(sq_ref[...])
    pooled = jnp.dot(
        grad_squeezed, squeeze_ref[...].astype(jnp.float32), precision=lax.Precision.HIGHEST
    ) * (1.0 / (SIDE * SIDE))
    wide_ref[0:EDGE, :] = jnp.zeros((EDGE, chans), jnp.float32)
    wide_ref[EDGE + rows :, :] = jnp.zeros((EDGE, chans), jnp.float32)
    good = inside(FRAME_ROWS)
    for frame, source in enumerate((even_ref, odd_ref)):
        at = frame * FRAME_ROWS
        grad = source[...].astype(jnp.float32)
        grad_ref[at : at + FRAME_ROWS, :] = grad
        active = grad * excite_ref[frame : frame + 1, :] + pooled[frame : frame + 1]
        slope = silu_slope(conv_ref[at : at + FRAME_ROWS, :])
        wide_ref[EDGE + at : EDGE + at + FRAME_ROWS, :] = active * slope * good
    store_shifts(wide_ref, shift_ref, -1)
    body = rows - 2 * WIDE
    for block, dense_ref in zip(channel_blocks(chans, width), dense_refs):
        start = block[2]
        sources = []
        for tap in range(9):
            down, across = divmod(tap, 3)
            at = (2 - down) * WIDE
            sources.append(shift_ref[across, at : at + body, start : start + WINDOW])
        total = jnp.dot(
            jnp.concatenate(sources, axis=1), dense_ref[...], preferred_element_type=jnp.float32
        )
        end = min(chans, start + WINDOW)
        grad_ref[WIDE : WIDE + body, start:end] += total[:, : end - start]
    cells = []
    for frame in range(frames):
        for y in range(SIDE):
            at = frame * FRAME_ROWS + (y + 1) * WIDE + 1
            flat_ref[y * SIDE : (y + 1) * SIDE, :] = grad_ref[at : at + SIDE, :]
        cells.append(flat_ref[...].astype(jnp.bfloat16))
    out_ref[...] = jnp.stack(cells, axis=1)


def f32(*shape):
    return jax.ShapeDtypeStruct(shape, jnp.float32)


def bf16(*shape):
    return jax.ShapeDtypeStruct(shape, jnp.bfloat16)


def conv_forward(features, group_kernel, squeeze_in):
    frames, cells, chans = features.shape
    rows = frames * FRAME_ROWS
    return whole_call(
        conv_kernel,
        (f32(rows, chans), bf16(rows, chans), f32(frames, squeeze_in.shape[0])),
        [
            pltpu.VMEM((cells, chans), jnp.float32),
            pltpu.VMEM((rows + 2 * EDGE, chans), jnp.float32),
            pltpu.VMEM((3, rows, chans), jnp.bfloat16),
        ],
    )(features, group_kernel, squeeze_in)


def hidden_frames(conv, padded, squeezed, squeeze_out):
    rows, chans = conv.shape
    return whole_call(
        hidden_kernel,
        (bf16(FRAME_ROWS, chans), bf16(FRAME_ROWS, chans), f32(rows // FRAME_ROWS, chans)),
        [],
    )(conv, padded, squeezed, squeeze_out)


def vmem_specs(count):
    return [pl.BlockSpec(memory_space=pltpu.SMEM)] + [pl.BlockSpec(memory_space=pltpu.VMEM)] * count


def facts_of(frame_clip, clip_keep):
    smem = pl.BlockSpec(memory_space=pltpu.SMEM)
    return pl.pallas_call(
        facts_kernel,
        out_shape=jax.ShapeDtypeStruct((5,), jnp.int32),
        in_specs=[smem, smem],
        out_specs=smem,
        cost_estimate=FREE,
    )(frame_clip, clip_keep)


def order_rows(facts, own, mate, unit):
    rows, columns = own.shape
    return pl.pallas_call(
        functools.partial(order_kernel, unit),
        out_shape=bf16(2 * rows, columns),
        in_specs=vmem_specs(2),
        compiler_params=pltpu.CompilerParams(vmem_limit_bytes=VMEM_BYTES),
        cost_estimate=FREE,
    )(facts, own, mate)


def take_patches(facts, halo, even):
    chans = even.shape[1]
    return pl.pallas_call(
        patch_kernel,
        out_shape=bf16(OUT_SIDE * OUT_SIDE, 8 * chans),
        in_specs=vmem_specs(2),
        compiler_params=pltpu.CompilerParams(vmem_limit_bytes=VMEM_BYTES),
        cost_estimate=FREE,
    )(facts, halo, even)


def return_patches(facts, own, mate, chans, dtype):
    return pl.pallas_call(
        unpatch_kernel,
        out_shape=(
            jax.ShapeDtypeStruct((FRAME_ROWS, chans), dtype),
            jax.ShapeDtypeStruct(facts.shape, jnp.int32),
        ),
        in_specs=vmem_specs(2),
        out_specs=vmem_specs(1)[::-1],
        compiler_params=pltpu.CompilerParams(vmem_limit_bytes=VMEM_BYTES),
        cost_estimate=FREE,
    )(facts, own, mate)


def excite_grad(even, odd, conv, excite, squeeze_out):
    rows, chans = conv.shape
    return whole_call(
        excite_grad_kernel,
        f32(rows // FRAME_ROWS, squeeze_out.shape[0]),
        [],
    )(even, odd, conv, excite, squeeze_out)


def conv_backward(even, odd, conv, excite, squeezed, grad_relaxed, squeeze_in, dense, width):
    rows, chans = conv.shape
    frames = rows // FRAME_ROWS
    lanes = channel_blocks(chans, width)[-1][2] + WINDOW
    return whole_call(
        functools.partial(conv_grad_kernel, width),
        bf16(SIDE * SIDE, frames, chans),
        [
            pltpu.VMEM((SIDE * SIDE, chans), jnp.float32),
            pltpu.VMEM((rows + 2 * EDGE, chans), jnp.float32),
            pltpu.VMEM((3, rows, lanes), jnp.bfloat16),
            pltpu.VMEM((rows, chans), jnp.float32),
        ],
        pl.CostEstimate(flops=rows * chans * 9216, bytes_accessed=16 * rows * chans, transcendentals=0),
    )(even, odd, conv, excite, squeezed, grad_relaxed, squeeze_in, *dense)


def dense_kernel(facts_ref, group_ref, *dense_refs):
    _, width, chans = group_ref.shape
    for block, dense_ref in zip(channel_blocks(chans, width), dense_refs):
        low, high, start, _ = block
        end = min(chans, start + WINDOW)
        spread, same = block_tools((low, high, start, start + WINDOW), width)
        dense_ref[...] = jnp.zeros_like(dense_ref)
        for tap in range(9):
            full = jnp.dot(spread, group_ref[tap, :, start:end], preferred_element_type=jnp.float32)
            rows = slice(tap * WINDOW, (tap + 1) * WINDOW)
            dense_ref[rows, 0 : end - start] = (full * same[:, : end - start]).astype(jnp.bfloat16)


def dense_weights(facts, group_kernel):
    _, width, chans = group_kernel.shape
    outs = (bf16(9 * WINDOW, WINDOW),) * len(channel_blocks(chans, width))
    return facts_call(dense_kernel, outs, facts, (group_kernel,))


def shifted(value, axis, by):
    count = lax.axis_size(axis)
    pairs = [(i, i + by) for i in range(count) if 0 <= i + by < count]
    return lax.ppermute(value, axis, pairs)


def ring_order(chips):
    return list(range(0, chips, 2)) + list(range(1, chips, 2))[::-1]


def ring_pairs(count, by):
    order = ring_order(count // 2)
    pairs = []
    for place, chip in enumerate(order):
        target = order[(place + by) % len(order)]
        pairs += [(2 * chip, 2 * target), (2 * chip + 1, 2 * target + 1)]
    return pairs


def swap_cores(value):
    return lax.ppermute(value, "ctx", [(i, i ^ 1) for i in range(lax.axis_size("ctx"))])


def tp_terms(value):
    size = lax.axis_size("tp")
    reach, other = 1, None
    while reach < size:
        value = value if other is None else value + other
        other = lax.ppermute(value, "tp", [(i, i ^ reach) for i in range(size)])
        reach *= 2
    return value, jnp.zeros_like(value) if other is None else other


def sum_tp(value):
    value, other = tp_terms(value)
    return value + other


def ring_send(value, by):
    return lax.ppermute(value, "ctx", ring_pairs(lax.axis_size("ctx"), by))


def tie(*values):
    return lax.optimization_barrier(values)


def stacked_contract(left, blocks):
    blocks = [ref[...] for ref in blocks]
    if blocks[0].shape[0] % 8 == 0:
        blocks = [jnp.concatenate(blocks, axis=0)]
    return jnp.concatenate([contract_last(left, block) for block in blocks], axis=1)


def pre_kernel(patch_ref, *refs):
    *blocks, out_ref = refs
    out_ref[...] = stacked_contract(patch_ref[...], blocks)


def back_kernel(keep_ref, send_ref, *refs):
    *blocks, out_ref = refs
    back = jnp.concatenate([keep_ref[...], send_ref[...]], axis=0)
    out_ref[...] = stacked_contract(back, blocks)


def live_rows(facts_ref, rows, unit):
    block, token = token_place(
        lax.broadcasted_iota(jnp.int32, (rows, 1), 0), facts_ref[0], unit
    )
    return (token < jnp.where(block == 0, facts_ref[1], facts_ref[2])).astype(jnp.float32)


def stacked_dot(pieces, blocks):
    if blocks[0].shape[0] % 8 == 0:
        pieces = [jnp.concatenate(pieces, axis=1)]
        blocks = [jnp.concatenate(blocks, axis=0)]
    total = 0.0
    for piece, block in zip(pieces, blocks):
        total += jnp.dot(piece, block, preferred_element_type=jnp.float32)
    return total


def totals_kernel(pieces, unit, parts, first, facts_ref, *refs):
    grad_act = refs[0][...] + refs[1][...]
    count = len(pieces)
    slopes, blocks = refs[2:4], refs[4 : 4 + count]
    before, after = refs[4 + count : -2 * len(parts)], refs[-2 * len(parts) :]
    rows, width = grad_act.shape[0], blocks[0].shape[0]
    slope = jnp.concatenate(
        [slopes[source][:, index * width : (index + 1) * width] for source, index in pieces], axis=1
    )
    factor = jnp.dot(
        reorder_matrix(facts_ref[0], unit, False),
        (grad_act * slope).astype(jnp.bfloat16),
        preferred_element_type=jnp.float32,
    ).astype(jnp.bfloat16)
    factors = [factor[:, place * width : (place + 1) * width] for place in range(count)]
    for part, lanes in enumerate(parts):
        total = stacked_dot(factors, [ref[:, lanes] for ref in blocks])
        for half in range(2):
            value = total[half * rows // 2 : (half + 1) * rows // 2]
            value = value if first else before[2 * part + half][...] + value
            ref = after[2 * part + half]
            ref[...] = value.astype(ref.dtype)


def ring_offsets(chips):
    offsets = [0]
    for step in range(1, chips // 2):
        offsets += [-step, step]
    return offsets + [chips // 2]


def block_columns(facts_ref, offset, chips, width):
    shape = (width, chips * width)
    place = (facts_ref[4] + offset + chips) % chips
    column = lax.broadcasted_iota(jnp.int32, shape, 1)
    return (column == lax.broadcasted_iota(jnp.int32, shape, 0) + place * width).astype(jnp.bfloat16)


def exchange_matrix(core, unit, to_sent):
    per_block = OUT_SIDE * OUT_SIDE
    shape = (2 * per_block,) * 2
    out_row = lax.broadcasted_iota(jnp.int32, shape, 0)
    in_row = lax.broadcasted_iota(jnp.int32, shape, 1)
    sent, kept = (out_row, in_row) if to_sent else (in_row, out_row)
    target_core = (sent // (2 * unit)) % 2
    within = sent // (4 * unit) * (2 * unit) + sent % (2 * unit)
    return (within + jnp.where(target_core == core, 0, per_block) == kept).astype(jnp.bfloat16)


def act_kernel(offsets, chips, unit, last, facts_ref, own_ref, other_ref, *refs):
    *before, slope_ref, out_ref = refs
    pre = own_ref[...] + other_ref[...]
    width = pre.shape[1] // len(offsets)
    live = live_rows(facts_ref, pre.shape[0], unit)
    sigma = jax.nn.sigmoid(pre)
    slope_ref[...] = sigma * (1.0 + pre * (1.0 - sigma)) * live
    act = (pre * sigma * live).astype(jnp.bfloat16)
    total = before[0][...].astype(jnp.float32) if last else 0.0
    for place, offset in enumerate(offsets):
        columns = block_columns(facts_ref, offset, chips, width)
        piece = act[:, place * width : (place + 1) * width]
        total += jnp.dot(piece, columns, preferred_element_type=jnp.float32)
    total = total.astype(jnp.bfloat16)
    if last:
        matrix = exchange_matrix(facts_ref[0], unit, True)
        total = jnp.dot(matrix, total, preferred_element_type=jnp.float32).astype(jnp.bfloat16)
    out_ref[...] = total


def token_kernel(offsets, chips, unit, facts_ref, act_ref, *refs):
    count = len(offsets)
    blocks, refs = refs[:count], refs[count:]
    keep_ref, send_ref, *buffers, sems = refs
    copies = [
        pltpu.make_async_copy(ref, buffer, sems.at[place])
        for place, (ref, buffer) in enumerate(zip(blocks, buffers))
    ]
    for copy in copies:
        copy.start()
    width = buffers[0].shape[0]
    matrix = exchange_matrix(facts_ref[0], unit, False)
    act = jnp.dot(matrix, act_ref[...], preferred_element_type=jnp.float32).astype(jnp.bfloat16)
    pieces = [
        contract_last(act, block_columns(facts_ref, offset, chips, width)).astype(jnp.bfloat16)
        for offset in offsets
    ]
    for copy in copies:
        copy.wait()
    total = stacked_dot(pieces, [buffer[...] for buffer in buffers])
    rows = keep_ref.shape[0]
    keep_ref[...] = total[:rows]
    send_ref[...] = total[rows:].astype(jnp.bfloat16)


def block_products(kernel, left, blocks):
    rows = 2 * OUT_SIDE * OUT_SIDE
    return whole_call(kernel, f32(rows, len(blocks) * blocks[0].shape[0]), [])(*left, *blocks)


def facts_call(kernel, outs, facts, operands, cost=FREE):
    return pl.pallas_call(
        kernel,
        out_shape=outs,
        in_specs=vmem_specs(len(operands)),
        compiler_params=pltpu.CompilerParams(vmem_limit_bytes=VMEM_BYTES),
        cost_estimate=cost,
    )(facts, *operands)


def add_gradients(facts, terms, slopes, pieces, blocks, before, unit, parts, last):
    rows = terms[0].shape[0] // 2
    kernel = functools.partial(totals_kernel, pieces, unit, parts, not before)
    outs = ()
    for lanes in parts:
        shape = rows, lanes.stop - lanes.start
        outs += f32(*shape), (bf16 if last else f32)(*shape)
    return tuple(facts_call(kernel, outs, facts, (*terms, *slopes, *blocks, *before)))


def act_and_slope(facts, terms, offsets, chips, before, unit):
    rows, columns = terms[0].shape
    kernel = functools.partial(act_kernel, offsets, chips, unit, bool(before))
    outs = f32(rows, columns), bf16(rows, columns // len(offsets) * chips)
    return facts_call(kernel, outs, facts, (*terms, *before))


def token_products(facts, act, offsets, chips, blocks, unit):
    rows, columns = act.shape[0] // 2, blocks[0].shape[1]
    return pl.pallas_call(
        functools.partial(token_kernel, offsets, chips, unit),
        out_shape=(f32(rows, columns), bf16(rows, columns)),
        in_specs=vmem_specs(1) + [pl.BlockSpec(memory_space=pl.ANY)] * len(blocks),
        scratch_shapes=[pltpu.VMEM(block.shape, block.dtype) for block in blocks]
        + [pltpu.SemaphoreType.DMA((len(blocks),))],
        compiler_params=pltpu.CompilerParams(vmem_limit_bytes=VMEM_BYTES),
        cost_estimate=FREE,
    )(facts, act, *blocks)


def chips_exchange(value):
    count = lax.axis_size("ctx")
    groups = [list(range(core, count, 2)) for core in range(2)]
    return lax.all_to_all(
        value, "ctx", split_axis=0, concat_axis=0, tiled=True, axis_index_groups=groups
    )


def per_device(
    features,
    group_kernel,
    squeeze_in,
    squeeze_out,
    sampler_kernel,
    readout_kernel,
    frame_clip,
    clip_keep,
    token_cotangent,
):
    chans = features.shape[2]
    count = lax.axis_size("ctx")
    steps, unit = count // 4, OUT_SIDE * OUT_SIDE // count
    flat_sampler = sampler_kernel.reshape(sampler_kernel.shape[0], 8 * chans)
    chips = count // 2
    s_up, s_down = ring_send(flat_sampler, 1), ring_send(flat_sampler, -1)
    group_kernel = jnp.swapaxes(group_kernel, 1, 2)
    squeeze_in = squeeze_in.T
    facts = facts_of(frame_clip, clip_keep)

    conv, padded, squeezed = conv_forward(features, group_kernel, squeeze_in)
    squeezed = sum_tp(squeezed)
    even, odd, excite = hidden_frames(conv, padded, squeezed, squeeze_out)
    halo = shifted(odd, "ctx", 1)

    s_up, s_down = [flat_sampler, s_up], [flat_sampler, s_down]
    s_up[1], s_down[1], even, readout_kernel = tie(s_up[1], s_down[1], even, readout_kernel)
    for step in range(2, steps):
        s_up.append(ring_send(s_up[-1], 1))
        s_down.append(ring_send(s_down[-1], -1))
        if step == 2:
            halo, s_up[2], s_down[2] = tie(halo, s_up[2], s_down[2])
            r_down = [readout_kernel, ring_send(readout_kernel, -1)]
            patches = take_patches(facts, halo, even)
            patches = order_rows(facts, patches, swap_cores(patches), unit)
    held = tie(s_up[-1], s_down[-1], token_cotangent, readout_kernel)
    s_up[-1], s_down[-1], token_cotangent, readout_kernel = held
    back = chips_exchange(token_cotangent)
    back = (back, swap_cores(back))
    s_last = ring_send(s_up[-1], 1)
    r_up = [readout_kernel, ring_send(readout_kernel, 1)]
    samplers = [flat_sampler] + [block for pair in zip(s_up[1:], s_down[1:]) for block in pair]
    offsets = ring_offsets(chips)
    count = 2 * steps - 3
    first_pre = tp_terms(block_products(pre_kernel, (patches,), samplers[:count]))
    r_down[1], s_last, *first_pre = tie(r_down[1], s_last, *first_pre)
    first_slope, first_act = act_and_slope(facts, first_pre, offsets[:count], chips, (), unit)
    last_pre = block_products(pre_kernel, (patches,), [*samplers[count:], s_last])
    last_slope, act = act_and_slope(
        facts, tp_terms(last_pre), offsets[count:], chips, (first_act,), unit
    )
    slopes = first_slope, last_slope
    r_up[1], act = tie(r_up[1], chips_exchange(act))
    for step in range(1, steps - 2):
        r_down.append(ring_send(r_down[-1], -1))
        r_up.append(ring_send(r_up[-1], 1))
    r_down.append(ring_send(r_down[-1], -1))
    early = r_down[: steps - 1]
    sums = block_products(back_kernel, back, early)
    r_up[-1], *terms = tie(r_up[-1], *tp_terms(sums))
    r_up.append(ring_send(r_up[-1], 1))
    halo_lanes, even_lanes = slice(0, 4 * chans), slice(4 * chans, 8 * chans)
    both = halo_lanes, even_lanes
    pieces = [(0, 2 * step) for step in range(steps - 1)]
    blocks = [flat_sampler] + s_down[1 : steps - 1]
    grads = add_gradients(facts, terms, slopes, pieces, blocks, (), unit, both, False)
    middle = r_up[1 : steps - 1] + [r_down[steps - 1]]
    r_down.append(ring_send(r_down[-1], -1))
    terms = tp_terms(block_products(back_kernel, back, middle))
    pieces = [(0, 2 * step - 1) for step in range(1, steps - 1)] + [(1, 1)]
    blocks = s_up[1 : steps - 1] + [s_down[steps - 1]]
    grads = add_gradients(facts, terms, slopes, pieces, blocks, grads, unit, both, False)

    late_up, late_down, *grads = tie(r_up[-1], r_down[-1], *grads)
    terms = tp_terms(block_products(back_kernel, back, [late_up, late_down]))
    pieces, blocks = [(1, 0), (1, 2)], [s_up[-1], s_last]
    halo_own, halo_mate = add_gradients(
        facts, terms, slopes, pieces, blocks, grads[:2], unit, (halo_lanes,), True
    )
    halo_mate, first_term = tie(halo_mate, terms[0])
    even_own, even_mate = add_gradients(
        facts, (first_term, terms[1]), slopes, pieces, blocks, grads[2:], unit, (even_lanes,), True
    )
    lead, facts_late = return_patches(facts, halo_own, swap_cores(halo_mate), chans, jnp.bfloat16)
    grad_odd = shifted(lead, "ctx", -1)
    grad_even, facts_late = return_patches(
        facts_late, even_own, swap_cores(even_mate), chans, jnp.float32
    )
    places = [*range(steps - 1), *range(-1, 1 - steps, -1), steps - 1, 1 - steps, steps]
    tokens = token_products(
        facts_late, act, places, chips, [*early, *middle, late_up, late_down], unit
    )
    grad_relaxed = sum_tp(excite_grad(grad_even, grad_odd, conv, excite, squeeze_out))
    llm_tokens = (tokens[0] + swap_cores(tokens[1]).astype(jnp.float32)).astype(jnp.bfloat16)
    grad_features = conv_backward(
        grad_even, grad_odd, conv, excite, squeezed, grad_relaxed, squeeze_in,
        dense_weights(facts_late, group_kernel), group_kernel.shape[1],
    )
    return (llm_tokens, jnp.swapaxes(grad_features, 0, 1))


def solution(mesh):
    placed = (
        P("ctx", None, "tp"),
        P(None, "tp", None),
        P("tp", None),
        P(None, "tp"),
        P("ctx", None, "tp"),
        P("ctx", "tp"),
        P(),
        P(),
        P("ctx", "tp"),
    )
    return jax.shard_map(
        per_device,
        mesh=mesh,
        in_specs=placed,
        out_specs=(P("ctx", "tp"), P("ctx", None, "tp")),
        check_vma=False,
    )
```

```python
import functools

import jax
import jax.numpy as jnp
from jax import lax
from jax.experimental import pallas as pl
from jax.experimental.pallas import tpu as pltpu
from jax.sharding import PartitionSpec as P

SIDE = 14
OUT_SIDE = 8
WIDE = 16
FRAME_ROWS = WIDE * WIDE
EDGE = 8
LANES = 128
WINDOW = 256
VMEM_BYTES = 16 * 2**20
FREE = pl.CostEstimate(flops=0, bytes_accessed=0, transcendentals=0)


def whole_call(kernel, outs, scratch, cost=FREE):
    return pl.pallas_call(
        kernel,
        out_shape=outs,
        scratch_shapes=scratch,
        compiler_params=pltpu.CompilerParams(vmem_limit_bytes=VMEM_BYTES),
        cost_estimate=cost,
    )


def contract_last(left, right):
    return lax.dot_general(
        left, right, (((1,), (1,)), ((), ())), preferred_element_type=jnp.float32
    )


def contract_exact(left, right):
    return lax.dot_general(
        left,
        right,
        (((1,), (1,)), ((), ())),
        precision=lax.Precision.HIGHEST,
        preferred_element_type=jnp.float32,
    )


def silu_slope(values):
    sigma = jax.nn.sigmoid(values)
    return sigma * (1.0 + values * (1.0 - sigma))


def inside(rows):
    row = lax.broadcasted_iota(jnp.int32, (rows, 1), 0)
    across, down = row & (WIDE - 1), (row // WIDE) & (WIDE - 1)
    good = (across >= 1) & (across <= SIDE) & (down >= 1) & (down <= SIDE)
    return good.astype(jnp.float32)


def channel_blocks(chans, width):
    span = 4 * width
    blocks = []
    for low in range(0, chans, span):
        high = min(chans, low + span)
        blocks.append((low, high, low // LANES * LANES, min(chans, -(-high // LANES) * LANES)))
    return blocks


def block_tools(block, width):
    low, high, start, end = block
    size = end - start
    out_row = lax.broadcasted_iota(jnp.int32, (size, width), 0) + start
    within = lax.broadcasted_iota(jnp.int32, (size, width), 1)
    lane = lax.broadcasted_iota(jnp.int32, (size, size), 1) + start
    row = lax.broadcasted_iota(jnp.int32, (size, size), 0) + start
    spread = jnp.zeros((size, width), jnp.float32)
    same = jnp.zeros((size, size), jnp.float32)
    for first in range(low, high, width):
        spread += (out_row == within + first).astype(jnp.float32)
        in_lane = (lane >= first) & (lane < first + width)
        in_row = (row >= first) & (row < first + width)
        same += (in_lane & in_row).astype(jnp.float32)
    return spread.astype(jnp.bfloat16), same


def dense_tap(group_ref, tap, block, spread, same):
    _, _, start, end = block
    full = jnp.dot(spread, group_ref[tap, :, start:end], preferred_element_type=jnp.float32)
    return (full * same).astype(jnp.bfloat16)


def store_shifts(wide_ref, shift_ref, sign):
    rows = shift_ref.shape[1]
    for col in range(3):
        at = EDGE + sign * (col - 1)
        chans = wide_ref.shape[1]
        shift_ref[col, :, 0:chans] = wide_ref[at : at + rows, :].astype(jnp.bfloat16)
        if shift_ref.shape[2] > chans:
            blank = jnp.zeros((rows, shift_ref.shape[2] - chans), jnp.bfloat16)
            shift_ref[col, :, chans:] = blank


def conv_kernel(feat_ref, group_ref, squeeze_ref, *refs):
    conv_ref, pad_ref, sq_ref, flat_ref, wide_ref, shift_ref = refs
    frames, _, chans = feat_ref.shape
    width = group_ref.shape[1]
    rows = frames * FRAME_ROWS
    wide_ref[...] = jnp.zeros_like(wide_ref)
    for frame in range(frames):
        flat_ref[...] = feat_ref[frame].astype(jnp.float32)
        for y in range(SIDE):
            at = EDGE + frame * FRAME_ROWS + (y + 1) * WIDE + 1
            wide_ref[at : at + SIDE, :] = flat_ref[y * SIDE : (y + 1) * SIDE, :]
    store_shifts(wide_ref, shift_ref, 1)
    pad_ref[...] = shift_ref[1]
    conv_ref[...] = jnp.zeros_like(conv_ref)
    body = rows - 2 * WIDE
    for block in channel_blocks(chans, width):
        _, _, start, end = block
        spread, same = block_tools(block, width)
        total = jnp.zeros((body, end - start), jnp.float32)
        for tap in range(9):
            down, across = divmod(tap, 3)
            weights = dense_tap(group_ref, tap, block, spread, same)
            source = shift_ref[across, down * WIDE : down * WIDE + body, start:end]
            total += contract_last(source, weights)
        conv_ref[WIDE : WIDE + body, start:end] += total
    conv = conv_ref[...] * inside(rows)
    conv_ref[...] = conv
    active = conv * jax.nn.sigmoid(conv)
    pooled = jnp.concatenate(
        [
            jnp.sum(active[f * FRAME_ROWS : (f + 1) * FRAME_ROWS], axis=0, keepdims=True)
            for f in range(frames)
        ],
        axis=0,
    ) * (1.0 / (SIDE * SIDE))
    sq_ref[...] = contract_exact(pooled, squeeze_ref[...].astype(jnp.float32))


def hidden_kernel(conv_ref, pad_ref, sq_ref, expand_ref, even_ref, odd_ref, excite_ref):
    squeezed = sq_ref[...]
    relaxed = squeezed * jax.nn.sigmoid(squeezed)
    excite = jax.nn.sigmoid(
        jnp.dot(relaxed, expand_ref[...].astype(jnp.float32), precision=lax.Precision.HIGHEST)
    )
    excite_ref[...] = excite
    for frame, out_ref in enumerate((even_ref, odd_ref)):
        rows = slice(frame * FRAME_ROWS, (frame + 1) * FRAME_ROWS)
        conv = conv_ref[rows, :]
        active = conv * jax.nn.sigmoid(conv)
        hidden = pad_ref[rows, :].astype(jnp.float32) + active * excite[frame : frame + 1]
        out_ref[...] = hidden.astype(jnp.bfloat16)


def select_rows(to_patches):
    shape = (FRAME_ROWS, FRAME_ROWS)
    out_row = lax.broadcasted_iota(jnp.int32, shape, 0)
    in_row = lax.broadcasted_iota(jnp.int32, shape, 1)
    patch_row, frame_row = (out_row, in_row) if to_patches else (in_row, out_row)
    down, across = patch_row >> 7, (patch_row >> 6) & 1
    a, b = (patch_row >> 3) & 7, patch_row & 7
    return ((2 * a + down) * WIDE + 2 * b + across == frame_row).astype(jnp.float32)


def facts_kernel(clip_ref, keep_ref, out_ref):
    shard = lax.axis_index("ctx")
    frames = clip_ref.shape[0]
    out_ref[0] = shard % 2
    for block in range(2):
        pair = shard // 2 * 2 + block
        clip = clip_ref[2 * pair]
        start = jnp.int32(0)
        for other in range(0, frames, 2):
            start += jnp.where(clip_ref[other] < clip, 1, 0)
        out_ref[1 + block] = keep_ref[clip] - (pair - start) * (OUT_SIDE * OUT_SIDE)
    before = clip_ref[jnp.maximum(2 * shard - 1, 0)]
    chip, chips = shard // 2, lax.axis_size("ctx") // 2
    out_ref[4] = jnp.where(chip % 2 == 0, chip // 2, chips - 1 - chip // 2)
    out_ref[3] = jnp.where((shard > 0) & (before == clip_ref[2 * shard]), 1, 0)


def token_place(row, core, unit):
    per_block = OUT_SIDE * OUT_SIDE
    within = row % per_block
    block = (within // unit) % 2
    target_core = jnp.where(row < per_block, core, 1 - core)
    return block, unit * (2 * (within // (2 * unit)) + target_core) + within % unit


def reorder_matrix(core, unit, to_sent):
    shape = (2 * OUT_SIDE * OUT_SIDE,) * 2
    out_row = lax.broadcasted_iota(jnp.int32, shape, 0)
    in_row = lax.broadcasted_iota(jnp.int32, shape, 1)
    sent, natural = (out_row, in_row) if to_sent else (in_row, out_row)
    block, token = token_place(sent, core, unit)
    source = jnp.where(block == core, 0, OUT_SIDE * OUT_SIDE) + token
    return (source == natural).astype(jnp.bfloat16)


def order_kernel(unit, facts_ref, own_ref, mate_ref, out_ref):
    rows = jnp.concatenate([own_ref[...], mate_ref[...]], axis=0)
    matrix = reorder_matrix(facts_ref[0], unit, True)
    out_ref[...] = jnp.dot(matrix, rows, preferred_element_type=jnp.float32).astype(jnp.bfloat16)


def patch_kernel(facts_ref, halo_ref, even_ref, out_ref):
    chans = halo_ref.shape[1]
    per_frame = OUT_SIDE * OUT_SIDE
    select = select_rows(True).astype(jnp.bfloat16)
    for frame, source in enumerate((halo_ref, even_ref)):
        rows = jnp.dot(select, source[...], preferred_element_type=jnp.float32)
        if frame == 0:
            rows = rows * facts_ref[3].astype(jnp.float32)
        rows = rows.astype(jnp.bfloat16)
        for tap in range(4):
            at = (frame * 4 + tap) * chans
            out_ref[:, at : at + chans] = rows[tap * per_frame : (tap + 1) * per_frame]


def unpatch_kernel(facts_ref, own_ref, mate_ref, out_ref, facts_out_ref):
    for place in range(facts_ref.shape[0]):
        facts_out_ref[place] = facts_ref[place]
    chans = out_ref.shape[1]
    rows = own_ref[...] + mate_ref[...].astype(jnp.float32)
    pieces = [rows[:, tap * chans : (tap + 1) * chans] for tap in range(4)]
    rows = jnp.concatenate(pieces, axis=0)
    select = select_rows(False).astype(jnp.bfloat16)
    coarse = rows.astype(jnp.bfloat16)
    frame = jnp.dot(select, coarse, preferred_element_type=jnp.float32)
    if out_ref.dtype == jnp.bfloat16:
        frame = frame * facts_ref[3].astype(jnp.float32)
    else:
        rest = (rows - coarse.astype(jnp.float32)).astype(jnp.bfloat16)
        frame += jnp.dot(select, rest, preferred_element_type=jnp.float32)
    out_ref[...] = (frame * inside(FRAME_ROWS)).astype(out_ref.dtype)


def excite_grad_kernel(even_ref, odd_ref, conv_ref, excite_ref, expand_ref, out_ref):
    sums = []
    for frame, grad_ref in enumerate((even_ref, odd_ref)):
        conv = conv_ref[frame * FRAME_ROWS : (frame + 1) * FRAME_ROWS, :]
        active = conv * jax.nn.sigmoid(conv)
        sums.append(jnp.sum(grad_ref[...].astype(jnp.float32) * active, axis=0, keepdims=True))
    excite = excite_ref[...]
    inner = jnp.concatenate(sums, axis=0) * excite * (1.0 - excite)
    out_ref[...] = contract_exact(inner, expand_ref[...].astype(jnp.float32))


def conv_grad_kernel(
    width, even_ref, odd_ref, conv_ref, excite_ref, sq_ref, relaxed_ref, squeeze_ref, *refs
):
    *dense_refs, out_ref, flat_ref, wide_ref, shift_ref, grad_ref = refs
    frames, _, chans = out_ref.shape
    rows = frames * FRAME_ROWS
    grad_squeezed = relaxed_ref[...] * silu_slope(sq_ref[...])
    pooled = jnp.dot(
        grad_squeezed, squeeze_ref[...].astype(jnp.float32), precision=lax.Precision.HIGHEST
    ) * (1.0 / (SIDE * SIDE))
    wide_ref[0:EDGE, :] = jnp.zeros((EDGE, chans), jnp.float32)
    wide_ref[EDGE + rows :, :] = jnp.zeros((EDGE, chans), jnp.float32)
    good = inside(FRAME_ROWS)
    for frame, source in enumerate((even_ref, odd_ref)):
        at = frame * FRAME_ROWS
        grad = source[...].astype(jnp.float32)
        grad_ref[at : at + FRAME_ROWS, :] = grad
        active = grad * excite_ref[frame : frame + 1, :] + pooled[frame : frame + 1]
        slope = silu_slope(conv_ref[at : at + FRAME_ROWS, :])
        wide_ref[EDGE + at : EDGE + at + FRAME_ROWS, :] = active * slope * good
    store_shifts(wide_ref, shift_ref, -1)
    body = rows - 2 * WIDE
    for block, dense_ref in zip(channel_blocks(chans, width), dense_refs):
        start = block[2]
        sources = []
        for tap in range(9):
            down, across = divmod(tap, 3)
            at = (2 - down) * WIDE
            sources.append(shift_ref[across, at : at + body, start : start + WINDOW])
        total = jnp.dot(
            jnp.concatenate(sources, axis=1), dense_ref[...], preferred_element_type=jnp.float32
        )
        end = min(chans, start + WINDOW)
        grad_ref[WIDE : WIDE + body, start:end] += total[:, : end - start]
    for frame in range(frames):
        for y in range(SIDE):
            at = frame * FRAME_ROWS + (y + 1) * WIDE + 1
            flat_ref[y * SIDE : (y + 1) * SIDE, :] = grad_ref[at : at + SIDE, :]
        out_ref[frame] = flat_ref[...].astype(jnp.bfloat16)


def f32(*shape):
    return jax.ShapeDtypeStruct(shape, jnp.float32)


def bf16(*shape):
    return jax.ShapeDtypeStruct(shape, jnp.bfloat16)


def conv_forward(features, group_kernel, squeeze_in):
    frames, cells, chans = features.shape
    rows = frames * FRAME_ROWS
    return whole_call(
        conv_kernel,
        (f32(rows, chans), bf16(rows, chans), f32(frames, squeeze_in.shape[0])),
        [
            pltpu.VMEM((cells, chans), jnp.float32),
            pltpu.VMEM((rows + 2 * EDGE, chans), jnp.float32),
            pltpu.VMEM((3, rows, chans), jnp.bfloat16),
        ],
    )(features, group_kernel, squeeze_in)


def hidden_frames(conv, padded, squeezed, squeeze_out):
    rows, chans = conv.shape
    return whole_call(
        hidden_kernel,
        (bf16(FRAME_ROWS, chans), bf16(FRAME_ROWS, chans), f32(rows // FRAME_ROWS, chans)),
        [],
    )(conv, padded, squeezed, squeeze_out)


def vmem_specs(count):
    return [pl.BlockSpec(memory_space=pltpu.SMEM)] + [pl.BlockSpec(memory_space=pltpu.VMEM)] * count


def facts_of(frame_clip, clip_keep):
    smem = pl.BlockSpec(memory_space=pltpu.SMEM)
    return pl.pallas_call(
        facts_kernel,
        out_shape=jax.ShapeDtypeStruct((5,), jnp.int32),
        in_specs=[smem, smem],
        out_specs=smem,
        cost_estimate=FREE,
    )(frame_clip, clip_keep)


def order_rows(facts, own, mate, unit):
    rows, columns = own.shape
    return pl.pallas_call(
        functools.partial(order_kernel, unit),
        out_shape=bf16(2 * rows, columns),
        in_specs=vmem_specs(2),
        compiler_params=pltpu.CompilerParams(vmem_limit_bytes=VMEM_BYTES),
        cost_estimate=FREE,
    )(facts, own, mate)


def take_patches(facts, halo, even):
    chans = even.shape[1]
    return pl.pallas_call(
        patch_kernel,
        out_shape=bf16(OUT_SIDE * OUT_SIDE, 8 * chans),
        in_specs=vmem_specs(2),
        compiler_params=pltpu.CompilerParams(vmem_limit_bytes=VMEM_BYTES),
        cost_estimate=FREE,
    )(facts, halo, even)


def return_patches(facts, own, mate, chans, dtype):
    return pl.pallas_call(
        unpatch_kernel,
        out_shape=(
            jax.ShapeDtypeStruct((FRAME_ROWS, chans), dtype),
            jax.ShapeDtypeStruct(facts.shape, jnp.int32),
        ),
        in_specs=vmem_specs(2),
        out_specs=vmem_specs(1)[::-1],
        compiler_params=pltpu.CompilerParams(vmem_limit_bytes=VMEM_BYTES),
        cost_estimate=FREE,
    )(facts, own, mate)


def excite_grad(even, odd, conv, excite, squeeze_out):
    rows, chans = conv.shape
    return whole_call(
        excite_grad_kernel,
        f32(rows // FRAME_ROWS, squeeze_out.shape[0]),
        [],
    )(even, odd, conv, excite, squeeze_out)


def conv_backward(even, odd, conv, excite, squeezed, grad_relaxed, squeeze_in, dense, width):
    rows, chans = conv.shape
    frames = rows // FRAME_ROWS
    lanes = channel_blocks(chans, width)[-1][2] + WINDOW
    return whole_call(
        functools.partial(conv_grad_kernel, width),
        bf16(frames, SIDE * SIDE, chans),
        [
            pltpu.VMEM((SIDE * SIDE, chans), jnp.float32),
            pltpu.VMEM((rows + 2 * EDGE, chans), jnp.float32),
            pltpu.VMEM((3, rows, lanes), jnp.bfloat16),
            pltpu.VMEM((rows, chans), jnp.float32),
        ],
        pl.CostEstimate(flops=rows * chans * 9216, bytes_accessed=16 * rows * chans, transcendentals=0),
    )(even, odd, conv, excite, squeezed, grad_relaxed, squeeze_in, *dense)


def dense_kernel(facts_ref, group_ref, *dense_refs):
    _, width, chans = group_ref.shape
    for block, dense_ref in zip(channel_blocks(chans, width), dense_refs):
        low, high, start, _ = block
        end = min(chans, start + WINDOW)
        spread, same = block_tools((low, high, start, start + WINDOW), width)
        dense_ref[...] = jnp.zeros_like(dense_ref)
        for tap in range(9):
            full = jnp.dot(spread, group_ref[tap, :, start:end], preferred_element_type=jnp.float32)
            rows = slice(tap * WINDOW, (tap + 1) * WINDOW)
            dense_ref[rows, 0 : end - start] = (full * same[:, : end - start]).astype(jnp.bfloat16)


def dense_weights(facts, group_kernel):
    _, width, chans = group_kernel.shape
    outs = (bf16(9 * WINDOW, WINDOW),) * len(channel_blocks(chans, width))
    return facts_call(dense_kernel, outs, facts, (group_kernel,))


def shifted(value, axis, by):
    count = lax.axis_size(axis)
    pairs = [(i, i + by) for i in range(count) if 0 <= i + by < count]
    return lax.ppermute(value, axis, pairs)


def ring_order(chips):
    return list(range(0, chips, 2)) + list(range(1, chips, 2))[::-1]


def ring_pairs(count, by):
    order = ring_order(count // 2)
    pairs = []
    for place, chip in enumerate(order):
        target = order[(place + by) % len(order)]
        pairs += [(2 * chip, 2 * target), (2 * chip + 1, 2 * target + 1)]
    return pairs


def swap_cores(value):
    return lax.ppermute(value, "ctx", [(i, i ^ 1) for i in range(lax.axis_size("ctx"))])


def tp_terms(value):
    size = lax.axis_size("tp")
    reach, other = 1, None
    while reach < size:
        value = value if other is None else value + other
        other = lax.ppermute(value, "tp", [(i, i ^ reach) for i in range(size)])
        reach *= 2
    return value, jnp.zeros_like(value) if other is None else other


def sum_tp(value):
    value, other = tp_terms(value)
    return value + other


def ring_send(value, by):
    return lax.ppermute(value, "ctx", ring_pairs(lax.axis_size("ctx"), by))


def tie(*values):
    return lax.optimization_barrier(values)


def stacked_contract(left, blocks):
    blocks = [ref[...] for ref in blocks]
    if blocks[0].shape[0] % 8 == 0:
        blocks = [jnp.concatenate(blocks, axis=0)]
    return jnp.concatenate([contract_last(left, block) for block in blocks], axis=1)


def pre_kernel(patch_ref, *refs):
    *blocks, out_ref = refs
    out_ref[...] = stacked_contract(patch_ref[...], blocks)


def back_kernel(keep_ref, send_ref, *refs):
    *blocks, out_ref = refs
    back = jnp.concatenate([keep_ref[...], send_ref[...]], axis=0)
    out_ref[...] = stacked_contract(back, blocks)


def live_rows(facts_ref, rows, unit):
    block, token = token_place(
        lax.broadcasted_iota(jnp.int32, (rows, 1), 0), facts_ref[0], unit
    )
    return (token < jnp.where(block == 0, facts_ref[1], facts_ref[2])).astype(jnp.float32)


def stacked_dot(pieces, blocks):
    if blocks[0].shape[0] % 8 == 0:
        pieces = [jnp.concatenate(pieces, axis=1)]
        blocks = [jnp.concatenate(blocks, axis=0)]
    total = 0.0
    for piece, block in zip(pieces, blocks):
        total += jnp.dot(piece, block, preferred_element_type=jnp.float32)
    return total


def totals_kernel(pieces, unit, parts, first, facts_ref, *refs):
    grad_act = refs[0][...] + refs[1][...]
    count = len(pieces)
    slopes, blocks = refs[2:4], refs[4 : 4 + count]
    before, after = refs[4 + count : -2 * len(parts)], refs[-2 * len(parts) :]
    rows, width = grad_act.shape[0], blocks[0].shape[0]
    slope = jnp.concatenate(
        [slopes[source][:, index * width : (index + 1) * width] for source, index in pieces], axis=1
    )
    factor = jnp.dot(
        reorder_matrix(facts_ref[0], unit, False),
        (grad_act * slope).astype(jnp.bfloat16),
        preferred_element_type=jnp.float32,
    ).astype(jnp.bfloat16)
    factors = [factor[:, place * width : (place + 1) * width] for place in range(count)]
    for part, lanes in enumerate(parts):
        total = stacked_dot(factors, [ref[:, lanes] for ref in blocks])
        for half in range(2):
            value = total[half * rows // 2 : (half + 1) * rows // 2]
            value = value if first else before[2 * part + half][...] + value
            ref = after[2 * part + half]
            ref[...] = value.astype(ref.dtype)


def ring_offsets(chips):
    offsets = [0]
    for step in range(1, chips // 2):
        offsets += [-step, step]
    return offsets + [chips // 2]


def block_columns(facts_ref, offset, chips, width):
    shape = (width, chips * width)
    place = (facts_ref[4] + offset + chips) % chips
    column = lax.broadcasted_iota(jnp.int32, shape, 1)
    return (column == lax.broadcasted_iota(jnp.int32, shape, 0) + place * width).astype(jnp.bfloat16)


def exchange_matrix(core, unit, to_sent):
    per_block = OUT_SIDE * OUT_SIDE
    shape = (2 * per_block,) * 2
    out_row = lax.broadcasted_iota(jnp.int32, shape, 0)
    in_row = lax.broadcasted_iota(jnp.int32, shape, 1)
    sent, kept = (out_row, in_row) if to_sent else (in_row, out_row)
    target_core = (sent // (2 * unit)) % 2
    within = sent // (4 * unit) * (2 * unit) + sent % (2 * unit)
    return (within + jnp.where(target_core == core, 0, per_block) == kept).astype(jnp.bfloat16)


def act_kernel(offsets, chips, unit, last, facts_ref, own_ref, other_ref, *refs):
    *before, slope_ref, out_ref = refs
    pre = own_ref[...] + other_ref[...]
    width = pre.shape[1] // len(offsets)
    live = live_rows(facts_ref, pre.shape[0], unit)
    sigma = jax.nn.sigmoid(pre)
    slope_ref[...] = sigma * (1.0 + pre * (1.0 - sigma)) * live
    act = (pre * sigma * live).astype(jnp.bfloat16)
    total = before[0][...].astype(jnp.float32) if last else 0.0
    for place, offset in enumerate(offsets):
        columns = block_columns(facts_ref, offset, chips, width)
        piece = act[:, place * width : (place + 1) * width]
        total += jnp.dot(piece, columns, preferred_element_type=jnp.float32)
    total = total.astype(jnp.bfloat16)
    if last:
        matrix = exchange_matrix(facts_ref[0], unit, True)
        total = jnp.dot(matrix, total, preferred_element_type=jnp.float32).astype(jnp.bfloat16)
    out_ref[...] = total


def token_kernel(offsets, chips, unit, facts_ref, act_ref, *refs):
    count = len(offsets)
    blocks, refs = refs[:count], refs[count:]
    keep_ref, send_ref, *buffers, sems = refs
    copies = [
        pltpu.make_async_copy(ref, buffer, sems.at[place])
        for place, (ref, buffer) in enumerate(zip(blocks, buffers))
    ]
    for copy in copies:
        copy.start()
    width = buffers[0].shape[0]
    matrix = exchange_matrix(facts_ref[0], unit, False)
    act = jnp.dot(matrix, act_ref[...], preferred_element_type=jnp.float32).astype(jnp.bfloat16)
    pieces = [
        contract_last(act, block_columns(facts_ref, offset, chips, width)).astype(jnp.bfloat16)
        for offset in offsets
    ]
    for copy in copies:
        copy.wait()
    total = stacked_dot(pieces, [buffer[...] for buffer in buffers])
    rows = keep_ref.shape[0]
    keep_ref[...] = total[:rows]
    send_ref[...] = total[rows:].astype(jnp.bfloat16)


def block_products(kernel, left, blocks):
    rows = 2 * OUT_SIDE * OUT_SIDE
    return whole_call(kernel, f32(rows, len(blocks) * blocks[0].shape[0]), [])(*left, *blocks)


def facts_call(kernel, outs, facts, operands, cost=FREE):
    return pl.pallas_call(
        kernel,
        out_shape=outs,
        in_specs=vmem_specs(len(operands)),
        compiler_params=pltpu.CompilerParams(vmem_limit_bytes=VMEM_BYTES),
        cost_estimate=cost,
    )(facts, *operands)


def add_gradients(facts, terms, slopes, pieces, blocks, before, unit, parts, last):
    rows = terms[0].shape[0] // 2
    kernel = functools.partial(totals_kernel, pieces, unit, parts, not before)
    outs = ()
    for lanes in parts:
        shape = rows, lanes.stop - lanes.start
        outs += f32(*shape), (bf16 if last else f32)(*shape)
    return tuple(facts_call(kernel, outs, facts, (*terms, *slopes, *blocks, *before)))


def act_and_slope(facts, terms, offsets, chips, before, unit):
    rows, columns = terms[0].shape
    kernel = functools.partial(act_kernel, offsets, chips, unit, bool(before))
    outs = f32(rows, columns), bf16(rows, columns // len(offsets) * chips)
    return facts_call(kernel, outs, facts, (*terms, *before))


def token_products(facts, act, offsets, chips, blocks, unit):
    rows, columns = act.shape[0] // 2, blocks[0].shape[1]
    return pl.pallas_call(
        functools.partial(token_kernel, offsets, chips, unit),
        out_shape=(f32(rows, columns), bf16(rows, columns)),
        in_specs=vmem_specs(1) + [pl.BlockSpec(memory_space=pl.ANY)] * len(blocks),
        scratch_shapes=[pltpu.VMEM(block.shape, block.dtype) for block in blocks]
        + [pltpu.SemaphoreType.DMA((len(blocks),))],
        compiler_params=pltpu.CompilerParams(vmem_limit_bytes=VMEM_BYTES),
        cost_estimate=FREE,
    )(facts, act, *blocks)


def chips_exchange(value):
    count = lax.axis_size("ctx")
    groups = [list(range(core, count, 2)) for core in range(2)]
    return lax.all_to_all(
        value, "ctx", split_axis=0, concat_axis=0, tiled=True, axis_index_groups=groups
    )


def per_device(
    features,
    group_kernel,
    squeeze_in,
    squeeze_out,
    sampler_kernel,
    readout_kernel,
    frame_clip,
    clip_keep,
    token_cotangent,
):
    chans = features.shape[2]
    count = lax.axis_size("ctx")
    steps, unit = count // 4, OUT_SIDE * OUT_SIDE // count
    flat_sampler = sampler_kernel.reshape(sampler_kernel.shape[0], 8 * chans)
    chips = count // 2
    s_up, s_down = ring_send(flat_sampler, 1), ring_send(flat_sampler, -1)
    group_kernel = jnp.swapaxes(group_kernel, 1, 2)
    squeeze_in = squeeze_in.T
    facts = facts_of(frame_clip, clip_keep)

    conv, padded, squeezed = conv_forward(features, group_kernel, squeeze_in)
    squeezed = sum_tp(squeezed)
    even, odd, excite = hidden_frames(conv, padded, squeezed, squeeze_out)
    halo = shifted(odd, "ctx", 1)

    s_up, s_down = [flat_sampler, s_up], [flat_sampler, s_down]
    s_up[1], s_down[1], even, readout_kernel = tie(s_up[1], s_down[1], even, readout_kernel)
    for step in range(2, steps):
        s_up.append(ring_send(s_up[-1], 1))
        s_down.append(ring_send(s_down[-1], -1))
        if step == 2:
            halo, s_up[2], s_down[2] = tie(halo, s_up[2], s_down[2])
            r_down = [readout_kernel, ring_send(readout_kernel, -1)]
            patches = take_patches(facts, halo, even)
            patches = order_rows(facts, patches, swap_cores(patches), unit)
    held = tie(s_up[-1], s_down[-1], token_cotangent, readout_kernel)
    s_up[-1], s_down[-1], token_cotangent, readout_kernel = held
    back = chips_exchange(token_cotangent)
    back = (back, swap_cores(back))
    s_last = ring_send(s_up[-1], 1)
    r_up = [readout_kernel, ring_send(readout_kernel, 1)]
    samplers = [flat_sampler] + [block for pair in zip(s_up[1:], s_down[1:]) for block in pair]
    offsets = ring_offsets(chips)
    count = 2 * steps - 3
    first_pre = tp_terms(block_products(pre_kernel, (patches,), samplers[:count]))
    r_down[1], s_last, *first_pre = tie(r_down[1], s_last, *first_pre)
    first_slope, first_act = act_and_slope(facts, first_pre, offsets[:count], chips, (), unit)
    last_pre = block_products(pre_kernel, (patches,), [*samplers[count:], s_last])
    last_slope, act = act_and_slope(
        facts, tp_terms(last_pre), offsets[count:], chips, (first_act,), unit
    )
    slopes = first_slope, last_slope
    r_up[1], act = tie(r_up[1], act)
    for step in range(1, steps - 2):
        r_down.append(ring_send(r_down[-1], -1))
        r_up.append(ring_send(r_up[-1], 1))
    r_down.append(ring_send(r_down[-1], -1))
    early = r_down[: steps - 1]
    sums = block_products(back_kernel, back, early)
    r_up[-1], act, *terms = tie(r_up[-1], chips_exchange(act), *tp_terms(sums))
    r_up.append(ring_send(r_up[-1], 1))
    halo_lanes, even_lanes = slice(0, 4 * chans), slice(4 * chans, 8 * chans)
    both = halo_lanes, even_lanes
    pieces = [(0, 2 * step) for step in range(steps - 1)]
    blocks = [flat_sampler] + s_down[1 : steps - 1]
    grads = add_gradients(facts, terms, slopes, pieces, blocks, (), unit, both, False)
    middle = r_up[1 : steps - 1] + [r_down[steps - 1]]
    r_down.append(ring_send(r_down[-1], -1))
    terms = tp_terms(block_products(back_kernel, back, middle))
    pieces = [(0, 2 * step - 1) for step in range(1, steps - 1)] + [(1, 1)]
    blocks = s_up[1 : steps - 1] + [s_down[steps - 1]]
    grads = add_gradients(facts, terms, slopes, pieces, blocks, grads, unit, both, False)

    late_up, late_down, *grads = tie(r_up[-1], r_down[-1], *grads)
    terms = tp_terms(block_products(back_kernel, back, [late_up, late_down]))
    pieces, blocks = [(1, 0), (1, 2)], [s_up[-1], s_last]
    halo_own, halo_mate = add_gradients(
        facts, terms, slopes, pieces, blocks, grads[:2], unit, (halo_lanes,), True
    )
    halo_mate, first_term = tie(halo_mate, terms[0])
    even_own, even_mate = add_gradients(
        facts, (first_term, terms[1]), slopes, pieces, blocks, grads[2:], unit, (even_lanes,), True
    )
    lead, facts_late = return_patches(facts, halo_own, swap_cores(halo_mate), chans, jnp.bfloat16)
    grad_odd = shifted(lead, "ctx", -1)
    grad_even, facts_late = return_patches(
        facts_late, even_own, swap_cores(even_mate), chans, jnp.float32
    )
    places = [*range(steps - 1), *range(-1, 1 - steps, -1), steps - 1, 1 - steps, steps]
    tokens = token_products(
        facts_late, act, places, chips, [*early, *middle, late_up, late_down], unit
    )
    grad_relaxed = sum_tp(excite_grad(grad_even, grad_odd, conv, excite, squeeze_out))
    llm_tokens = (tokens[0] + swap_cores(tokens[1]).astype(jnp.float32)).astype(jnp.bfloat16)
    grad_features = conv_backward(
        grad_even, grad_odd, conv, excite, squeezed, grad_relaxed, squeeze_in,
        dense_weights(facts_late, group_kernel), group_kernel.shape[1],
    )
    return (llm_tokens, grad_features)


def solution(mesh):
    placed = (
        P("ctx", None, "tp"),
        P(None, "tp", None),
        P("tp", None),
        P(None, "tp"),
        P("ctx", None, "tp"),
        P("ctx", "tp"),
        P(),
        P(),
        P("ctx", "tp"),
    )
    return jax.shard_map(
        per_device,
        mesh=mesh,
        in_specs=placed,
        out_specs=(P("ctx", "tp"), P("ctx", None, "tp")),
        check_vma=False,
    )
```

```python
import functools

import jax
import jax.numpy as jnp
from jax import lax
from jax.experimental import pallas as pl
from jax.experimental.pallas import tpu as pltpu
from jax.sharding import PartitionSpec as P

SIDE = 14
OUT_SIDE = 8
WIDE = 16
FRAME_ROWS = WIDE * WIDE
EDGE = 8
LANES = 128
WINDOW = 256
VMEM_BYTES = 16 * 2**20
FREE = pl.CostEstimate(flops=0, bytes_accessed=0, transcendentals=0)


def whole_call(kernel, outs, scratch, cost=FREE):
    return pl.pallas_call(
        kernel,
        out_shape=outs,
        scratch_shapes=scratch,
        compiler_params=pltpu.CompilerParams(vmem_limit_bytes=VMEM_BYTES),
        cost_estimate=cost,
    )


def contract_last(left, right):
    return lax.dot_general(
        left, right, (((1,), (1,)), ((), ())), preferred_element_type=jnp.float32
    )


def contract_exact(left, right):
    return lax.dot_general(
        left,
        right,
        (((1,), (1,)), ((), ())),
        precision=lax.Precision.HIGHEST,
        preferred_element_type=jnp.float32,
    )


def silu_slope(values):
    sigma = jax.nn.sigmoid(values)
    return sigma * (1.0 + values * (1.0 - sigma))


def inside(rows):
    row = lax.broadcasted_iota(jnp.int32, (rows, 1), 0)
    across, down = row & (WIDE - 1), (row // WIDE) & (WIDE - 1)
    good = (across >= 1) & (across <= SIDE) & (down >= 1) & (down <= SIDE)
    return good.astype(jnp.float32)


def channel_blocks(chans, width):
    span = 4 * width
    blocks = []
    for low in range(0, chans, span):
        high = min(chans, low + span)
        blocks.append((low, high, low // LANES * LANES, min(chans, -(-high // LANES) * LANES)))
    return blocks


def block_tools(block, width):
    low, high, start, end = block
    size = end - start
    out_row = lax.broadcasted_iota(jnp.int32, (size, width), 0) + start
    within = lax.broadcasted_iota(jnp.int32, (size, width), 1)
    lane = lax.broadcasted_iota(jnp.int32, (size, size), 1) + start
    row = lax.broadcasted_iota(jnp.int32, (size, size), 0) + start
    spread = jnp.zeros((size, width), jnp.float32)
    same = jnp.zeros((size, size), jnp.float32)
    for first in range(low, high, width):
        spread += (out_row == within + first).astype(jnp.float32)
        in_lane = (lane >= first) & (lane < first + width)
        in_row = (row >= first) & (row < first + width)
        same += (in_lane & in_row).astype(jnp.float32)
    return spread.astype(jnp.bfloat16), same


def dense_tap(group_ref, tap, block, spread, same):
    _, _, start, end = block
    full = jnp.dot(spread, group_ref[tap, :, start:end], preferred_element_type=jnp.float32)
    return (full * same).astype(jnp.bfloat16)


def store_shifts(wide_ref, shift_ref, sign):
    rows = shift_ref.shape[1]
    for col in range(3):
        at = EDGE + sign * (col - 1)
        chans = wide_ref.shape[1]
        shift_ref[col, :, 0:chans] = wide_ref[at : at + rows, :].astype(jnp.bfloat16)
        if shift_ref.shape[2] > chans:
            blank = jnp.zeros((rows, shift_ref.shape[2] - chans), jnp.bfloat16)
            shift_ref[col, :, chans:] = blank


def conv_kernel(feat_ref, group_ref, squeeze_ref, *refs):
    conv_ref, pad_ref, sq_ref, flat_ref, wide_ref, shift_ref = refs
    frames, _, chans = feat_ref.shape
    width = group_ref.shape[1]
    rows = frames * FRAME_ROWS
    wide_ref[...] = jnp.zeros_like(wide_ref)
    for frame in range(frames):
        flat_ref[...] = feat_ref[frame].astype(jnp.float32)
        for y in range(SIDE):
            at = EDGE + frame * FRAME_ROWS + (y + 1) * WIDE + 1
            wide_ref[at : at + SIDE, :] = flat_ref[y * SIDE : (y + 1) * SIDE, :]
    store_shifts(wide_ref, shift_ref, 1)
    pad_ref[...] = shift_ref[1]
    conv_ref[...] = jnp.zeros_like(conv_ref)
    body = rows - 2 * WIDE
    for block in channel_blocks(chans, width):
        _, _, start, end = block
        spread, same = block_tools(block, width)
        total = jnp.zeros((body, end - start), jnp.float32)
        for tap in range(9):
            down, across = divmod(tap, 3)
            weights = dense_tap(group_ref, tap, block, spread, same)
            source = shift_ref[across, down * WIDE : down * WIDE + body, start:end]
            total += contract_last(source, weights)
        conv_ref[WIDE : WIDE + body, start:end] += total
    conv = conv_ref[...] * inside(rows)
    conv_ref[...] = conv
    active = conv * jax.nn.sigmoid(conv)
    pooled = jnp.concatenate(
        [
            jnp.sum(active[f * FRAME_ROWS : (f + 1) * FRAME_ROWS], axis=0, keepdims=True)
            for f in range(frames)
        ],
        axis=0,
    ) * (1.0 / (SIDE * SIDE))
    sq_ref[...] = contract_exact(pooled, squeeze_ref[...].astype(jnp.float32))


def hidden_kernel(conv_ref, pad_ref, sq_ref, expand_ref, even_ref, odd_ref, excite_ref):
    squeezed = sq_ref[...]
    relaxed = squeezed * jax.nn.sigmoid(squeezed)
    excite = jax.nn.sigmoid(
        jnp.dot(relaxed, expand_ref[...].astype(jnp.float32), precision=lax.Precision.HIGHEST)
    )
    excite_ref[...] = excite
    for frame, out_ref in enumerate((even_ref, odd_ref)):
        rows = slice(frame * FRAME_ROWS, (frame + 1) * FRAME_ROWS)
        conv = conv_ref[rows, :]
        active = conv * jax.nn.sigmoid(conv)
        hidden = pad_ref[rows, :].astype(jnp.float32) + active * excite[frame : frame + 1]
        out_ref[...] = hidden.astype(jnp.bfloat16)


def select_rows(to_patches):
    shape = (FRAME_ROWS, FRAME_ROWS)
    out_row = lax.broadcasted_iota(jnp.int32, shape, 0)
    in_row = lax.broadcasted_iota(jnp.int32, shape, 1)
    patch_row, frame_row = (out_row, in_row) if to_patches else (in_row, out_row)
    down, across = patch_row >> 7, (patch_row >> 6) & 1
    a, b = (patch_row >> 3) & 7, patch_row & 7
    return ((2 * a + down) * WIDE + 2 * b + across == frame_row).astype(jnp.float32)


def facts_kernel(clip_ref, keep_ref, out_ref):
    shard = lax.axis_index("ctx")
    frames = clip_ref.shape[0]
    out_ref[0] = shard % 2
    for block in range(2):
        pair = shard // 2 * 2 + block
        clip = clip_ref[2 * pair]
        start = jnp.int32(0)
        for other in range(0, frames, 2):
            start += jnp.where(clip_ref[other] < clip, 1, 0)
        out_ref[1 + block] = keep_ref[clip] - (pair - start) * (OUT_SIDE * OUT_SIDE)
    before = clip_ref[jnp.maximum(2 * shard - 1, 0)]
    chip, chips = shard // 2, lax.axis_size("ctx") // 2
    out_ref[4] = jnp.where(chip % 2 == 0, chip // 2, chips - 1 - chip // 2)
    out_ref[3] = jnp.where((shard > 0) & (before == clip_ref[2 * shard]), 1, 0)


def token_place(row, core, unit):
    per_block = OUT_SIDE * OUT_SIDE
    within = row % per_block
    block = (within // unit) % 2
    target_core = jnp.where(row < per_block, core, 1 - core)
    return block, unit * (2 * (within // (2 * unit)) + target_core) + within % unit


def reorder_matrix(core, unit, to_sent):
    shape = (2 * OUT_SIDE * OUT_SIDE,) * 2
    out_row = lax.broadcasted_iota(jnp.int32, shape, 0)
    in_row = lax.broadcasted_iota(jnp.int32, shape, 1)
    sent, natural = (out_row, in_row) if to_sent else (in_row, out_row)
    block, token = token_place(sent, core, unit)
    source = jnp.where(block == core, 0, OUT_SIDE * OUT_SIDE) + token
    return (source == natural).astype(jnp.bfloat16)


def order_kernel(unit, facts_ref, own_ref, mate_ref, out_ref):
    rows = jnp.concatenate([own_ref[...], mate_ref[...]], axis=0)
    matrix = reorder_matrix(facts_ref[0], unit, True)
    out_ref[...] = jnp.dot(matrix, rows, preferred_element_type=jnp.float32).astype(jnp.bfloat16)


def patch_kernel(facts_ref, halo_ref, even_ref, out_ref):
    chans = halo_ref.shape[1]
    per_frame = OUT_SIDE * OUT_SIDE
    select = select_rows(True).astype(jnp.bfloat16)
    for frame, source in enumerate((halo_ref, even_ref)):
        rows = jnp.dot(select, source[...], preferred_element_type=jnp.float32)
        if frame == 0:
            rows = rows * facts_ref[3].astype(jnp.float32)
        rows = rows.astype(jnp.bfloat16)
        for tap in range(4):
            at = (frame * 4 + tap) * chans
            out_ref[:, at : at + chans] = rows[tap * per_frame : (tap + 1) * per_frame]


def unpatch_kernel(facts_ref, own_ref, mate_ref, out_ref, facts_out_ref):
    for place in range(facts_ref.shape[0]):
        facts_out_ref[place] = facts_ref[place]
    chans = out_ref.shape[1]
    rows = own_ref[...] + mate_ref[...].astype(jnp.float32)
    pieces = [rows[:, tap * chans : (tap + 1) * chans] for tap in range(4)]
    rows = jnp.concatenate(pieces, axis=0)
    select = select_rows(False).astype(jnp.bfloat16)
    coarse = rows.astype(jnp.bfloat16)
    frame = jnp.dot(select, coarse, preferred_element_type=jnp.float32)
    if out_ref.dtype == jnp.bfloat16:
        frame = frame * facts_ref[3].astype(jnp.float32)
    else:
        rest = (rows - coarse.astype(jnp.float32)).astype(jnp.bfloat16)
        frame += jnp.dot(select, rest, preferred_element_type=jnp.float32)
    out_ref[...] = (frame * inside(FRAME_ROWS)).astype(out_ref.dtype)


def excite_grad_kernel(even_ref, odd_ref, conv_ref, excite_ref, expand_ref, out_ref):
    sums = []
    for frame, grad_ref in enumerate((even_ref, odd_ref)):
        conv = conv_ref[frame * FRAME_ROWS : (frame + 1) * FRAME_ROWS, :]
        active = conv * jax.nn.sigmoid(conv)
        sums.append(jnp.sum(grad_ref[...].astype(jnp.float32) * active, axis=0, keepdims=True))
    excite = excite_ref[...]
    inner = jnp.concatenate(sums, axis=0) * excite * (1.0 - excite)
    out_ref[...] = contract_exact(inner, expand_ref[...].astype(jnp.float32))


def conv_grad_kernel(
    width, even_ref, odd_ref, conv_ref, excite_ref, sq_ref, relaxed_ref, squeeze_ref, *refs
):
    *dense_refs, out_ref, flat_ref, wide_ref, shift_ref, grad_ref = refs
    frames, _, chans = out_ref.shape
    rows = frames * FRAME_ROWS
    grad_squeezed = relaxed_ref[...] * silu_slope(sq_ref[...])
    pooled = jnp.dot(
        grad_squeezed, squeeze_ref[...].astype(jnp.float32), precision=lax.Precision.HIGHEST
    ) * (1.0 / (SIDE * SIDE))
    wide_ref[0:EDGE, :] = jnp.zeros((EDGE, chans), jnp.float32)
    wide_ref[EDGE + rows :, :] = jnp.zeros((EDGE, chans), jnp.float32)
    good = inside(FRAME_ROWS)
    for frame, source in enumerate((even_ref, odd_ref)):
        at = frame * FRAME_ROWS
        grad = source[...].astype(jnp.float32)
        grad_ref[at : at + FRAME_ROWS, :] = grad
        active = grad * excite_ref[frame : frame + 1, :] + pooled[frame : frame + 1]
        slope = silu_slope(conv_ref[at : at + FRAME_ROWS, :])
        wide_ref[EDGE + at : EDGE + at + FRAME_ROWS, :] = active * slope * good
    store_shifts(wide_ref, shift_ref, -1)
    body = rows - 2 * WIDE
    for block, dense_ref in zip(channel_blocks(chans, width), dense_refs):
        start = block[2]
        sources = []
        for tap in range(9):
            down, across = divmod(tap, 3)
            at = (2 - down) * WIDE
            sources.append(shift_ref[across, at : at + body, start : start + WINDOW])
        total = jnp.dot(
            jnp.concatenate(sources, axis=1), dense_ref[...], preferred_element_type=jnp.float32
        )
        end = min(chans, start + WINDOW)
        grad_ref[WIDE : WIDE + body, start:end] += total[:, : end - start]
    for frame in range(frames):
        for y in range(SIDE):
            at = frame * FRAME_ROWS + (y + 1) * WIDE + 1
            flat_ref[y * SIDE : (y + 1) * SIDE, :] = grad_ref[at : at + SIDE, :]
        out_ref[frame] = flat_ref[...].astype(jnp.bfloat16)


def f32(*shape):
    return jax.ShapeDtypeStruct(shape, jnp.float32)


def bf16(*shape):
    return jax.ShapeDtypeStruct(shape, jnp.bfloat16)


def conv_forward(features, group_kernel, squeeze_in):
    frames, cells, chans = features.shape
    rows = frames * FRAME_ROWS
    return whole_call(
        conv_kernel,
        (f32(rows, chans), bf16(rows, chans), f32(frames, squeeze_in.shape[0])),
        [
            pltpu.VMEM((cells, chans), jnp.float32),
            pltpu.VMEM((rows + 2 * EDGE, chans), jnp.float32),
            pltpu.VMEM((3, rows, chans), jnp.bfloat16),
        ],
    )(features, group_kernel, squeeze_in)


def hidden_frames(conv, padded, squeezed, squeeze_out):
    rows, chans = conv.shape
    return whole_call(
        hidden_kernel,
        (bf16(FRAME_ROWS, chans), bf16(FRAME_ROWS, chans), f32(rows // FRAME_ROWS, chans)),
        [],
    )(conv, padded, squeezed, squeeze_out)


def vmem_specs(count):
    return [pl.BlockSpec(memory_space=pltpu.SMEM)] + [pl.BlockSpec(memory_space=pltpu.VMEM)] * count


def facts_of(frame_clip, clip_keep):
    smem = pl.BlockSpec(memory_space=pltpu.SMEM)
    return pl.pallas_call(
        facts_kernel,
        out_shape=jax.ShapeDtypeStruct((5,), jnp.int32),
        in_specs=[smem, smem],
        out_specs=smem,
        cost_estimate=FREE,
    )(frame_clip, clip_keep)


def order_rows(facts, own, mate, unit):
    rows, columns = own.shape
    return pl.pallas_call(
        functools.partial(order_kernel, unit),
        out_shape=bf16(2 * rows, columns),
        in_specs=vmem_specs(2),
        compiler_params=pltpu.CompilerParams(vmem_limit_bytes=VMEM_BYTES),
        cost_estimate=FREE,
    )(facts, own, mate)


def take_patches(facts, halo, even):
    chans = even.shape[1]
    return pl.pallas_call(
        patch_kernel,
        out_shape=bf16(OUT_SIDE * OUT_SIDE, 8 * chans),
        in_specs=vmem_specs(2),
        compiler_params=pltpu.CompilerParams(vmem_limit_bytes=VMEM_BYTES),
        cost_estimate=FREE,
    )(facts, halo, even)


def return_patches(facts, own, mate, chans, dtype):
    return pl.pallas_call(
        unpatch_kernel,
        out_shape=(
            jax.ShapeDtypeStruct((FRAME_ROWS, chans), dtype),
            jax.ShapeDtypeStruct(facts.shape, jnp.int32),
        ),
        in_specs=vmem_specs(2),
        out_specs=vmem_specs(1)[::-1],
        compiler_params=pltpu.CompilerParams(vmem_limit_bytes=VMEM_BYTES),
        cost_estimate=FREE,
    )(facts, own, mate)


def excite_grad(even, odd, conv, excite, squeeze_out):
    rows, chans = conv.shape
    return whole_call(
        excite_grad_kernel,
        f32(rows // FRAME_ROWS, squeeze_out.shape[0]),
        [],
    )(even, odd, conv, excite, squeeze_out)


def conv_backward(even, odd, conv, excite, squeezed, grad_relaxed, squeeze_in, dense, width):
    rows, chans = conv.shape
    frames = rows // FRAME_ROWS
    lanes = channel_blocks(chans, width)[-1][2] + WINDOW
    return whole_call(
        functools.partial(conv_grad_kernel, width),
        bf16(frames, SIDE * SIDE, chans),
        [
            pltpu.VMEM((SIDE * SIDE, chans), jnp.float32),
            pltpu.VMEM((rows + 2 * EDGE, chans), jnp.float32),
            pltpu.VMEM((3, rows, lanes), jnp.bfloat16),
            pltpu.VMEM((rows, chans), jnp.float32),
        ],
        pl.CostEstimate(flops=rows * chans * 9216, bytes_accessed=16 * rows * chans, transcendentals=0),
    )(even, odd, conv, excite, squeezed, grad_relaxed, squeeze_in, *dense)


def dense_kernel(facts_ref, group_ref, *dense_refs):
    _, width, chans = group_ref.shape
    for block, dense_ref in zip(channel_blocks(chans, width), dense_refs):
        low, high, start, _ = block
        end = min(chans, start + WINDOW)
        spread, same = block_tools((low, high, start, start + WINDOW), width)
        dense_ref[...] = jnp.zeros_like(dense_ref)
        for tap in range(9):
            full = jnp.dot(spread, group_ref[tap, :, start:end], preferred_element_type=jnp.float32)
            rows = slice(tap * WINDOW, (tap + 1) * WINDOW)
            dense_ref[rows, 0 : end - start] = (full * same[:, : end - start]).astype(jnp.bfloat16)


def dense_weights(facts, group_kernel):
    _, width, chans = group_kernel.shape
    outs = (bf16(9 * WINDOW, WINDOW),) * len(channel_blocks(chans, width))
    return facts_call(dense_kernel, outs, facts, (group_kernel,))


def shifted(value, axis, by):
    count = lax.axis_size(axis)
    pairs = [(i, i + by) for i in range(count) if 0 <= i + by < count]
    return lax.ppermute(value, axis, pairs)


def ring_order(chips):
    return list(range(0, chips, 2)) + list(range(1, chips, 2))[::-1]


def ring_pairs(count, by):
    order = ring_order(count // 2)
    pairs = []
    for place, chip in enumerate(order):
        target = order[(place + by) % len(order)]
        pairs += [(2 * chip, 2 * target), (2 * chip + 1, 2 * target + 1)]
    return pairs


def swap_cores(value):
    return lax.ppermute(value, "ctx", [(i, i ^ 1) for i in range(lax.axis_size("ctx"))])


def tp_terms(value):
    size = lax.axis_size("tp")
    reach, other = 1, None
    while reach < size:
        value = value if other is None else value + other
        other = lax.ppermute(value, "tp", [(i, i ^ reach) for i in range(size)])
        reach *= 2
    return value, jnp.zeros_like(value) if other is None else other


def sum_tp(value):
    value, other = tp_terms(value)
    return value + other


def ring_send(value, by):
    return lax.ppermute(value, "ctx", ring_pairs(lax.axis_size("ctx"), by))


def tie(*values):
    return lax.optimization_barrier(values)


def stacked_contract(left, blocks):
    blocks = [ref[...] for ref in blocks]
    if blocks[0].shape[0] % 8 == 0:
        blocks = [jnp.concatenate(blocks, axis=0)]
    return jnp.concatenate([contract_last(left, block) for block in blocks], axis=1)


def pre_kernel(patch_ref, *refs):
    *blocks, out_ref = refs
    out_ref[...] = stacked_contract(patch_ref[...], blocks)


def back_kernel(keep_ref, send_ref, *refs):
    *blocks, out_ref = refs
    back = jnp.concatenate([keep_ref[...], send_ref[...]], axis=0)
    out_ref[...] = stacked_contract(back, blocks)


def live_rows(facts_ref, rows, unit):
    block, token = token_place(
        lax.broadcasted_iota(jnp.int32, (rows, 1), 0), facts_ref[0], unit
    )
    return (token < jnp.where(block == 0, facts_ref[1], facts_ref[2])).astype(jnp.float32)


def stacked_dot(pieces, blocks):
    if blocks[0].shape[0] % 8 == 0:
        pieces = [jnp.concatenate(pieces, axis=1)]
        blocks = [jnp.concatenate(blocks, axis=0)]
    total = 0.0
    for piece, block in zip(pieces, blocks):
        total += jnp.dot(piece, block, preferred_element_type=jnp.float32)
    return total


def totals_kernel(pieces, unit, parts, first, facts_ref, *refs):
    grad_act = refs[0][...] + refs[1][...]
    count = len(pieces)
    slopes, blocks = refs[2:4], refs[4 : 4 + count]
    before, after = refs[4 + count : -2 * len(parts)], refs[-2 * len(parts) :]
    rows, width = grad_act.shape[0], blocks[0].shape[0]
    slope = jnp.concatenate(
        [slopes[source][:, index * width : (index + 1) * width] for source, index in pieces], axis=1
    )
    factor = jnp.dot(
        reorder_matrix(facts_ref[0], unit, False),
        (grad_act * slope).astype(jnp.bfloat16),
        preferred_element_type=jnp.float32,
    ).astype(jnp.bfloat16)
    factors = [factor[:, place * width : (place + 1) * width] for place in range(count)]
    for part, lanes in enumerate(parts):
        total = stacked_dot(factors, [ref[:, lanes] for ref in blocks])
        for half in range(2):
            value = total[half * rows // 2 : (half + 1) * rows // 2]
            value = value if first else before[2 * part + half][...] + value
            ref = after[2 * part + half]
            ref[...] = value.astype(ref.dtype)


def ring_offsets(chips):
    offsets = [0]
    for step in range(1, chips // 2):
        offsets += [-step, step]
    return offsets + [chips // 2]


def block_columns(facts_ref, offset, chips, width):
    shape = (width, chips * width)
    place = (facts_ref[4] + offset + chips) % chips
    column = lax.broadcasted_iota(jnp.int32, shape, 1)
    return (column == lax.broadcasted_iota(jnp.int32, shape, 0) + place * width).astype(jnp.bfloat16)


def exchange_matrix(core, unit, to_sent):
    per_block = OUT_SIDE * OUT_SIDE
    shape = (2 * per_block,) * 2
    out_row = lax.broadcasted_iota(jnp.int32, shape, 0)
    in_row = lax.broadcasted_iota(jnp.int32, shape, 1)
    sent, kept = (out_row, in_row) if to_sent else (in_row, out_row)
    target_core = (sent // (2 * unit)) % 2
    within = sent // (4 * unit) * (2 * unit) + sent % (2 * unit)
    return (within + jnp.where(target_core == core, 0, per_block) == kept).astype(jnp.bfloat16)


def act_kernel(offsets, chips, unit, last, facts_ref, own_ref, other_ref, *refs):
    *before, slope_ref, out_ref = refs
    pre = own_ref[...] + other_ref[...]
    width = pre.shape[1] // len(offsets)
    live = live_rows(facts_ref, pre.shape[0], unit)
    sigma = jax.nn.sigmoid(pre)
    slope_ref[...] = sigma * (1.0 + pre * (1.0 - sigma)) * live
    act = (pre * sigma * live).astype(jnp.bfloat16)
    total = before[0][...].astype(jnp.float32) if last else 0.0
    for place, offset in enumerate(offsets):
        columns = block_columns(facts_ref, offset, chips, width)
        piece = act[:, place * width : (place + 1) * width]
        total += jnp.dot(piece, columns, preferred_element_type=jnp.float32)
    total = total.astype(jnp.bfloat16)
    if last:
        matrix = exchange_matrix(facts_ref[0], unit, True)
        total = jnp.dot(matrix, total, preferred_element_type=jnp.float32).astype(jnp.bfloat16)
    out_ref[...] = total


def token_kernel(offsets, chips, unit, facts_ref, act_ref, *refs):
    count = len(offsets)
    blocks, refs = refs[:count], refs[count:]
    keep_ref, send_ref, *buffers, sems = refs
    copies = [
        pltpu.make_async_copy(ref, buffer, sems.at[place])
        for place, (ref, buffer) in enumerate(zip(blocks, buffers))
    ]
    for copy in copies:
        copy.start()
    width = buffers[0].shape[0]
    matrix = exchange_matrix(facts_ref[0], unit, False)
    act = jnp.dot(matrix, act_ref[...], preferred_element_type=jnp.float32).astype(jnp.bfloat16)
    pieces = [
        contract_last(act, block_columns(facts_ref, offset, chips, width)).astype(jnp.bfloat16)
        for offset in offsets
    ]
    for copy in copies:
        copy.wait()
    total = stacked_dot(pieces, [buffer[...] for buffer in buffers])
    rows = keep_ref.shape[0]
    keep_ref[...] = total[:rows]
    send_ref[...] = total[rows:].astype(jnp.bfloat16)


def block_products(kernel, left, blocks):
    rows = 2 * OUT_SIDE * OUT_SIDE
    return whole_call(kernel, f32(rows, len(blocks) * blocks[0].shape[0]), [])(*left, *blocks)


def facts_call(kernel, outs, facts, operands, cost=FREE):
    return pl.pallas_call(
        kernel,
        out_shape=outs,
        in_specs=vmem_specs(len(operands)),
        compiler_params=pltpu.CompilerParams(vmem_limit_bytes=VMEM_BYTES),
        cost_estimate=cost,
    )(facts, *operands)


def add_gradients(facts, terms, slopes, pieces, blocks, before, unit, parts, last):
    rows = terms[0].shape[0] // 2
    kernel = functools.partial(totals_kernel, pieces, unit, parts, not before)
    outs = ()
    for lanes in parts:
        shape = rows, lanes.stop - lanes.start
        outs += f32(*shape), (bf16 if last else f32)(*shape)
    return tuple(facts_call(kernel, outs, facts, (*terms, *slopes, *blocks, *before)))


def act_and_slope(facts, terms, offsets, chips, before, unit):
    rows, columns = terms[0].shape
    kernel = functools.partial(act_kernel, offsets, chips, unit, bool(before))
    outs = f32(rows, columns), bf16(rows, columns // len(offsets) * chips)
    return facts_call(kernel, outs, facts, (*terms, *before))


def token_products(facts, act, offsets, chips, blocks, unit):
    rows, columns = act.shape[0] // 2, blocks[0].shape[1]
    return pl.pallas_call(
        functools.partial(token_kernel, offsets, chips, unit),
        out_shape=(f32(rows, columns), bf16(rows, columns)),
        in_specs=vmem_specs(1) + [pl.BlockSpec(memory_space=pl.ANY)] * len(blocks),
        scratch_shapes=[pltpu.VMEM(block.shape, block.dtype) for block in blocks]
        + [pltpu.SemaphoreType.DMA((len(blocks),))],
        compiler_params=pltpu.CompilerParams(vmem_limit_bytes=VMEM_BYTES),
        cost_estimate=FREE,
    )(facts, act, *blocks)


def chips_exchange(value):
    count = lax.axis_size("ctx")
    groups = [list(range(core, count, 2)) for core in range(2)]
    return lax.all_to_all(
        value, "ctx", split_axis=0, concat_axis=0, tiled=True, axis_index_groups=groups
    )


def per_device(
    features,
    group_kernel,
    squeeze_in,
    squeeze_out,
    sampler_kernel,
    readout_kernel,
    frame_clip,
    clip_keep,
    token_cotangent,
):
    chans = features.shape[2]
    count = lax.axis_size("ctx")
    steps, unit = count // 4, OUT_SIDE * OUT_SIDE // count
    flat_sampler = sampler_kernel.reshape(sampler_kernel.shape[0], 8 * chans)
    chips = count // 2
    s_up, s_down = ring_send(flat_sampler, 1), ring_send(flat_sampler, -1)
    group_kernel = jnp.swapaxes(group_kernel, 1, 2)
    squeeze_in = squeeze_in.T
    facts = facts_of(frame_clip, clip_keep)

    conv, padded, squeezed = conv_forward(features, group_kernel, squeeze_in)
    squeezed = sum_tp(squeezed)
    even, odd, excite = hidden_frames(conv, padded, squeezed, squeeze_out)
    halo = shifted(odd, "ctx", 1)

    s_up, s_down = [flat_sampler, s_up], [flat_sampler, s_down]
    s_up[1], s_down[1], even, readout_kernel = tie(s_up[1], s_down[1], even, readout_kernel)
    for step in range(2, steps):
        s_up.append(ring_send(s_up[-1], 1))
        s_down.append(ring_send(s_down[-1], -1))
        if step == 2:
            halo, s_up[2], s_down[2] = tie(halo, s_up[2], s_down[2])
            r_down = [readout_kernel, ring_send(readout_kernel, -1)]
            patches = take_patches(facts, halo, even)
            patches = order_rows(facts, patches, swap_cores(patches), unit)
    held = tie(s_up[-1], s_down[-1], token_cotangent, readout_kernel)
    s_up[-1], s_down[-1], token_cotangent, readout_kernel = held
    back = chips_exchange(token_cotangent)
    back = (back, swap_cores(back))
    s_last = ring_send(s_up[-1], 1)
    r_up = [readout_kernel, ring_send(readout_kernel, 1)]
    samplers = [flat_sampler] + [block for pair in zip(s_up[1:], s_down[1:]) for block in pair]
    offsets = ring_offsets(chips)
    count = 2 * steps - 3
    first_pre = tp_terms(block_products(pre_kernel, (patches,), samplers[:count]))
    r_down[1], s_last, *first_pre = tie(r_down[1], s_last, *first_pre)
    first_slope, first_act = act_and_slope(facts, first_pre, offsets[:count], chips, (), unit)
    last_pre = block_products(pre_kernel, (patches,), [*samplers[count:], s_last])
    last_slope, act = act_and_slope(
        facts, tp_terms(last_pre), offsets[count:], chips, (first_act,), unit
    )
    slopes = first_slope, last_slope
    r_up[1], act = tie(r_up[1], chips_exchange(act))
    for step in range(1, steps - 2):
        r_down.append(ring_send(r_down[-1], -1))
        r_up.append(ring_send(r_up[-1], 1))
    r_down.append(ring_send(r_down[-1], -1))
    early = r_down[: steps - 1]
    sums = block_products(back_kernel, back, early)
    r_up[-1], *terms = tie(r_up[-1], *tp_terms(sums))
    r_up.append(ring_send(r_up[-1], 1))
    halo_lanes, even_lanes = slice(0, 4 * chans), slice(4 * chans, 8 * chans)
    both = halo_lanes, even_lanes
    pieces = [(0, 2 * step) for step in range(steps - 1)]
    blocks = [flat_sampler] + s_down[1 : steps - 1]
    grads = add_gradients(facts, terms, slopes, pieces, blocks, (), unit, both, False)
    middle = r_up[1 : steps - 1] + [r_down[steps - 1]]
    r_down.append(ring_send(r_down[-1], -1))
    terms = tp_terms(block_products(back_kernel, back, middle))
    pieces = [(0, 2 * step - 1) for step in range(1, steps - 1)] + [(1, 1)]
    blocks = s_up[1 : steps - 1] + [s_down[steps - 1]]
    grads = add_gradients(facts, terms, slopes, pieces, blocks, grads, unit, both, False)

    late_up, late_down, *grads = tie(r_up[-1], r_down[-1], *grads)
    sums, act = tie(block_products(back_kernel, back, [late_up, late_down]), act)
    terms = tp_terms(sums)
    places = [*range(steps - 1), *range(-1, 1 - steps, -1), steps - 1, 1 - steps, steps]
    tokens = token_products(
        facts, act, places, chips, [*early, *middle, late_up, late_down], unit
    )
    other_term, *tokens = tie(terms[1], *tokens)
    terms = terms[0], other_term
    llm_tokens = (tokens[0] + swap_cores(tokens[1]).astype(jnp.float32)).astype(jnp.bfloat16)
    pieces, blocks = [(1, 0), (1, 2)], [s_up[-1], s_last]
    halo_own, halo_mate = add_gradients(
        facts, terms, slopes, pieces, blocks, grads[:2], unit, (halo_lanes,), True
    )
    halo_mate, first_term = tie(halo_mate, terms[0])
    even_own, even_mate = add_gradients(
        facts, (first_term, terms[1]), slopes, pieces, blocks, grads[2:], unit, (even_lanes,), True
    )
    lead, facts_late = return_patches(facts, halo_own, swap_cores(halo_mate), chans, jnp.bfloat16)
    grad_odd = shifted(lead, "ctx", -1)
    grad_even, facts_late = return_patches(
        facts_late, even_own, swap_cores(even_mate), chans, jnp.float32
    )
    llm_tokens, grad_odd = tie(llm_tokens, grad_odd)
    grad_relaxed = sum_tp(excite_grad(grad_even, grad_odd, conv, excite, squeeze_out))
    grad_features = conv_backward(
        grad_even, grad_odd, conv, excite, squeezed, grad_relaxed, squeeze_in,
        dense_weights(facts_late, group_kernel), group_kernel.shape[1],
    )
    return (llm_tokens, grad_features)


def solution(mesh):
    placed = (
        P("ctx", None, "tp"),
        P(None, "tp", None),
        P("tp", None),
        P(None, "tp"),
        P("ctx", None, "tp"),
        P("ctx", "tp"),
        P(),
        P(),
        P("ctx", "tp"),
    )
    return jax.shard_map(
        per_device,
        mesh=mesh,
        in_specs=placed,
        out_specs=(P("ctx", "tp"), P("ctx", None, "tp")),
        check_vma=False,
    )
```
